32 devices in a mesh: pts: 8 (over z, y), loc: 4 (over x, core).
Axes of the slice: x: 2, y: 2, z: 4, core: 2. Of those that a mesh axis runs over, the one named last changes fastest.
Arguments:
- points: bfloat16 [32768, 64], P(('pts', 'loc'))
- lengths: int32 [9], replicated, may hold values from 1024 to 8192, as said below
- neighbours_one: int32 [32768, 20], P(('pts', 'loc')), may hold values from 0 to 8191, as said below
- neighbours_two: int32 [32768, 20], P(('pts', 'loc')), may hold values from 0 to 8191, as said below
- weight_one: bfloat16 [128, 128], replicated, may hold values from -0.5 to 0.5
- gain_one: float32 [128], replicated, may hold values from 0.5 to 2
- shift_one: float32 [128], replicated, may hold values from -2.5 to 2.5
- weight_two: bfloat16 [256, 256], replicated, may hold values from -0.375 to 0.375
- gain_two: float32 [256], replicated, may hold values from 0.5 to 2
- shift_two: float32 [256], replicated, may hold values from -2.5 to 2.5
- cotangent: bfloat16 [32768, 256], P(('pts', 'loc')), may hold values from -6 to 6
Outputs:
- act_one: bfloat16 [32768, 128], P(('pts', 'loc'))
- act_two: bfloat16 [32768, 256], P(('pts', 'loc'))
- grad_points: float32 [32768, 64], P(('pts', 'loc'))
- grad_weight_one: float32 [128, 128], replicated
- grad_gain_one: float32 [128], replicated
- grad_shift_one: float32 [128], replicated
- grad_weight_two: float32 [256, 256], replicated
- grad_gain_two: float32 [256], replicated
- grad_shift_two: float32 [256], replicated
The draws below stay inside these ranges and needn't reach their ends.
Inputs may be any that keep to these rules, and one draw needn't show every extreme that they name: `lengths`: exactly 3 lines of 8192 positions (b * 8192 to (b + 1) * 8192 - 1, which lines drawn from the seed) are each one cloud of 8192 points; each other line holds 6 clouds of 1024 points or more. No cloud crosses a line's end. `neighbours_one`: each entry is an index within the point's own cloud. For a point of a cloud that fills a line, the neighbours lie anywhere in the line, and of the 20480 entries of one device's points exactly 2560 fall on each device of that line; for a point of any other cloud every neighbour is stored on the point's own device. `neighbours_two`: as for neighbours_one, drawn independently.
All inputs are finite; a program needn't handle non-finite values.
Results may differ from the reference program's by a relative error of at most 0.009.
Values may be sent and summed in bfloat16 or wider, within the bound.
No kernel may reach another device: no remote copies, remote signals or barrier semaphores. Data moves between devices by JAX's collectives and lax.ppermute only.
A program may use at most 192 MiB of HBM per device.

```python
import math
import jax
import jax.numpy as jnp
from jax import lax

C0 = 64
C1 = 128
C2 = 256
K = 20
PTS_DEV = 1024
BASE_LEN = 1024
TOTAL = 32768
MAXLEN = 8192
NBIG = 3
SMALL_LINE = 6
NCLOUD = 9
CAP = 2560
N_PTS = 8
N_LOC = 4


def cloud_lengths(key):
    key = jax.random.fold_in(key, 101)
    spare = MAXLEN - SMALL_LINE * BASE_LEN
    line_order = jax.random.permutation(jax.random.fold_in(key, 1), N_LOC)
    filled = line_order < NBIG
    cut_points = jnp.sort(jax.random.randint(jax.random.fold_in(key, 2), (N_LOC, SMALL_LINE - 1), 0, spare + 1), axis=1)
    bounds = jnp.concatenate([jnp.zeros((N_LOC, 1), jnp.int32), cut_points.astype(jnp.int32), jnp.full((N_LOC, 1), spare, jnp.int32)], axis=1)
    smaller = BASE_LEN + bounds[:, 1:] - bounds[:, :-1]
    first_column = jnp.where(filled, MAXLEN, smaller[:, 0])
    remaining = jnp.where(filled[:, None], 0, smaller[:, 1:])
    table = jnp.concatenate([first_column[:, None], remaining], axis=1).reshape(-1).astype(jnp.int32)
    keeping = jnp.argsort((table == 0).astype(jnp.int32), stable=True)
    return table[keeping][:NCLOUD].astype(jnp.int32)


def neighbour_lists(key, salt):
    lengths = cloud_lengths(key)
    key = jax.random.fold_in(key, salt)
    slot_count = PTS_DEV * K
    cloud_ends = jnp.cumsum(lengths).astype(jnp.int32)
    cloud_starts = cloud_ends - lengths

    def one_device(device):
        device_key = jax.random.fold_in(key, device)
        pts_place = device // N_LOC
        loc_place = device % N_LOC
        device_first = loc_place * MAXLEN + pts_place * PTS_DEV
        position = device_first + jnp.arange(PTS_DEV, dtype=jnp.int32)
        cloud_number = jnp.searchsorted(cloud_ends, position, side='right')
        cloud_begin = jnp.repeat(cloud_starts[cloud_number], K)
        cloud_size = jnp.repeat(lengths[cloud_number], K)
        slot_spot = jax.random.permutation(jax.random.fold_in(device_key, 1), slot_count)
        owner = slot_spot // CAP
        wide_index = owner * PTS_DEV + jax.random.randint(jax.random.fold_in(device_key, 2), (slot_count,), 0, PTS_DEV)
        lower = jnp.maximum(cloud_begin, device_first)
        upper = jnp.minimum(cloud_begin + cloud_size, device_first + PTS_DEV)
        narrow = lower + jax.random.randint(jax.random.fold_in(device_key, 3), (slot_count,), 0, upper - lower)
        chosen = jnp.where(cloud_size == MAXLEN, wide_index, narrow - cloud_begin)
        return chosen.astype(jnp.int32).reshape(PTS_DEV, K)
    return jax.vmap(one_device)(jnp.arange(N_PTS * N_LOC, dtype=jnp.int32)).reshape(TOTAL, K)


def draw_lengths(key, part):
    return cloud_lengths(key)


def draw_neighbours_one(key, part):
    return neighbour_lists(key, 211)


def draw_neighbours_two(key, part):
    return neighbour_lists(key, 307)


def draw_points(key, part):
    key = jax.random.fold_in(key, 7)
    row_scale = 10.0 ** jax.random.uniform(jax.random.fold_in(key, 1), (TOTAL, 1), jnp.float32)
    column_scale = 10.0 ** (0.5 * jax.random.uniform(jax.random.fold_in(key, 2), (1, C0), jnp.float32))
    rising = 3.0 ** (jnp.arange(TOTAL, dtype=jnp.float32)[:, None] / TOTAL)
    basis = jax.random.normal(jax.random.fold_in(key, 3), (TOTAL, C0), jnp.float32)
    return (basis * row_scale * column_scale * rising * 0.15).astype(jnp.bfloat16)


def shard_levels(own_key, shape, cuts, smallest, top_value):
    def one(dim, blocks):
        draws = jax.random.uniform(jax.random.fold_in(jax.random.fold_in(own_key, 6), dim), (blocks,), jnp.float32, smallest / len(cuts), top_value / len(cuts))
        return jnp.repeat(jnp.exp(draws), shape[dim] // blocks).reshape((-1,) + (1,) * (len(shape) - dim - 1))

    factor_of = one(*cuts[0])
    for cut in cuts[1:]:
        factor_of = factor_of * one(*cut)
    return factor_of


def normal_values(own_key, dims, width, most, cuts=(), kind=jnp.bfloat16):
    result = jax.random.normal(own_key, dims, jnp.float32) * width
    if len(cuts) > 0:
        result = shard_levels(own_key, dims, cuts, -0.22, 0.18) * result
    return jnp.clip(result, min=-most, max=most).astype(kind)


def setup_inputs(seed: int = 0) -> dict:
    splits = jax.random.split(jax.random.key(seed), 12)
    return {
        "points": draw_points(jax.random.fold_in(splits[11], 71), 0),
        "lengths": draw_lengths(jax.random.fold_in(splits[11], 71), 0),
        "neighbours_one": draw_neighbours_one(jax.random.fold_in(splits[11], 71), 0),
        "neighbours_two": draw_neighbours_two(jax.random.fold_in(splits[11], 71), 0),
        "weight_one": normal_values(splits[4], (2 * C0, C1), (2 * C0) ** -0.5, 0.5),
        "gain_one": jnp.clip(jnp.exp(jax.random.uniform(splits[5], (C1,), jnp.float32, math.log(0.5), math.log(2.0))), 0.5, 2.0),
        "shift_one": normal_values(splits[6], (C1,), 0.5, 2.5, (), jnp.float32),
        "weight_two": normal_values(splits[7], (2 * C1, C2), (2 * C1) ** -0.5, 0.375),
        "gain_two": jnp.clip(jnp.exp(jax.random.uniform(splits[8], (C2,), jnp.float32, math.log(0.5), math.log(2.0))), 0.5, 2.0),
        "shift_two": normal_values(splits[9], (C2,), 0.5, 2.5, (), jnp.float32),
        "cotangent": normal_values(splits[10], (TOTAL, C2), 1.0, 6.0, ((0, 32),)),
    }


@jax.custom_vjp
def low(v):
    return lax.optimization_barrier(v.astype(jnp.bfloat16)).astype(jnp.float32)

@jax.custom_vjp
def low_back(v):
    return v

def low_keep(v):
    return (low(v), None)

def low_pass(kept, grad):
    return (grad,)

def back_keep(v):
    return (v, None)

def back_low(kept, grad):
    return (low(grad),)
low.defvjp(low_keep, low_pass)
low_back.defvjp(back_keep, back_low)
EPS = 1e-05

def storage_rows(lengths, neighbours):
    cloud_ends = jnp.cumsum(lengths).astype(jnp.int32)
    cloud_starts = (cloud_ends - lengths).astype(jnp.int32)
    stored = jnp.arange(TOTAL, dtype=jnp.int32)
    device = stored // PTS_DEV
    position = device % N_LOC * MAXLEN + device // N_LOC * PTS_DEV + stored % PTS_DEV
    cloud_number = jnp.searchsorted(cloud_ends, position, side='right').astype(jnp.int32)
    target = (cloud_starts[cloud_number][:, None] + neighbours).astype(jnp.int32)
    line = target // MAXLEN
    within = target % MAXLEN
    return ((within // PTS_DEV * N_LOC + line) * PTS_DEV + within % PTS_DEV).astype(jnp.int32)

def edge_layer(inputs, row_table, weight, norm_gain, norm_shift):
    values = low(inputs)
    in_width = values.shape[1]
    row_blocks = row_table.reshape(-1, PTS_DEV, K)
    value_blocks = values.reshape(-1, PTS_DEV, in_width)

    def project(pieces):
        near_rows, own_values = pieces
        beside = low_back(values[near_rows])
        centre = jnp.broadcast_to(own_values[:, None, :], beside.shape)
        edge_rows = low(jnp.concatenate([centre, beside - centre], axis=2))
        return jnp.einsum('pkc,cd->pkd', edge_rows, weight, precision=lax.Precision.HIGHEST)
    mixed_rows = low_back(lax.map(jax.checkpoint(project), (row_blocks, value_blocks)))
    average = lax.optimization_barrier(jnp.mean(mixed_rows, axis=(0, 1, 2)))
    spread = lax.optimization_barrier(jnp.mean(jnp.square(mixed_rows - average), axis=(0, 1, 2)))
    inverse_std = lax.rsqrt(spread + EPS)

    def finish(mixed_block):
        shifted = norm_gain * ((mixed_block - average) * inverse_std) + norm_shift
        return jax.nn.logsumexp(jax.nn.silu(shifted), axis=1) - math.log(K)
    pooled = lax.map(jax.checkpoint(finish), mixed_rows)
    return pooled.reshape(TOTAL, -1)

def reference(points, lengths, neighbours_one, neighbours_two, weight_one, gain_one, shift_one, weight_two, gain_two, shift_two, cotangent):
    rows_one = storage_rows(lengths, neighbours_one)
    rows_two = storage_rows(lengths, neighbours_two)

    def forward(inputs, w_first, g_first, s_first, w_second, g_second, s_second):
        pooled_one = edge_layer(inputs, rows_one, w_first, g_first, s_first)
        pooled_two = edge_layer(pooled_one, rows_two, w_second, g_second, s_second)
        return (pooled_one, pooled_two)
    primal = (points.astype(jnp.float32), weight_one.astype(jnp.float32), gain_one, shift_one, weight_two.astype(jnp.float32), gain_two, shift_two)
    outputs, pull_back = jax.vjp(forward, *primal)
    pooled_one, pooled_two = outputs
    grads = pull_back((jnp.zeros_like(pooled_one), cotangent.astype(jnp.float32)))
    return (pooled_one.astype(jnp.bfloat16), pooled_two.astype(jnp.bfloat16), grads[0], grads[1], grads[2], grads[3], grads[4], grads[5], grads[6])
```

```python
import functools
import math

import jax
import jax.numpy as jnp
from jax import lax
from jax.experimental import pallas as pl
from jax.experimental.pallas import tpu as pltpu
from jax.sharding import PartitionSpec as P

EPS = 1e-05
BLOCK = 128
GROUP = 32
VMEM_LIMIT = 56 * 1024 * 1024
BOTH = ("pts", "loc")

f32 = jnp.float32
bf16 = jnp.bfloat16


def params():
    return pltpu.CompilerParams(vmem_limit_bytes=VMEM_LIMIT)


def vmem():
    return pl.BlockSpec(memory_space=pltpu.VMEM)


def smem():
    return pl.BlockSpec(memory_space=pltpu.SMEM)


def fold_rows(x):
    return jnp.sum(x.reshape(x.shape[0] // 8, 8, x.shape[1]), axis=0)


def dot(a, b):
    return jnp.dot(a, b, preferred_element_type=f32)


def dot_t(a, b):
    return lax.dot_general(a, b, (((1,), (1,)), ((), ())), preferred_element_type=f32)


def gather_kernel(idx_ref, table_ref, own_ref, w_ref, diff_ref, stat_ref, tab, picked):
    near, rows, c = diff_ref.shape
    d = w_ref.shape[1]
    total = table_ref.shape[0]

    def widen(i, _):
        at = pl.ds(pl.multiple_of(i * 256, 256), 256)
        tab[at, :] = table_ref[at, :].astype(f32)
        return 0

    lax.fori_loop(0, total // 256, widen, 0)

    def pick(b, _):
        base = pl.multiple_of(b * 8, 8)
        for k in range(near):
            for j in range(8):
                i = idx_ref[k, base + j]
                picked[k, pl.ds(base + j, 1), :] = tab[pl.ds(i, 1), :]
        return 0

    lax.fori_loop(0, rows // 8, pick, 0)

    def subtract(b, total_sums):
        at = pl.ds(pl.multiple_of(b * BLOCK, BLOCK), BLOCK)
        own = own_ref[at, :].astype(f32)
        own_sum, diff_sum = total_sums
        for k in range(near):
            diff = (picked[k, at, :] - own).astype(bf16)
            diff_ref[k, at, :] = diff
            diff_sum = diff_sum + fold_rows(diff.astype(f32))
        return (own_sum + fold_rows(own), diff_sum)

    zero = jnp.zeros((8, c), f32)
    own_sum, diff_sum = lax.fori_loop(0, rows // BLOCK, subtract, (zero, zero))
    weight = w_ref[...].astype(f32)
    both = jnp.dot(
        own_sum * float(near), weight[:c], precision=lax.Precision.HIGHEST, preferred_element_type=f32
    ) + jnp.dot(diff_sum, weight[c:], precision=lax.Precision.HIGHEST, preferred_element_type=f32)
    mean = jnp.sum(both, axis=0, keepdims=True) * (1.0 / (rows * near))

    def deviate(b, m2):
        at = pl.ds(pl.multiple_of(b * BLOCK, BLOCK), BLOCK)
        centre = dot(own_ref[at, :], w_ref[:c, :]) - mean
        for k in range(near):
            z = dot(diff_ref[k, at, :], w_ref[c:, :]) + centre
            m2 = m2 + fold_rows(z * z)
        return m2

    m2 = lax.fori_loop(0, rows // BLOCK, deviate, jnp.zeros((8, d), f32))
    stat_ref[0:1, :] = mean
    stat_ref[1:2, :] = jnp.sum(m2, axis=0, keepdims=True)


def gather_rows(index, table, own, weight):
    near, rows = index.shape
    c, d = own.shape[1], weight.shape[1]
    return pl.pallas_call(
        gather_kernel,
        out_shape=(
            jax.ShapeDtypeStruct((near, rows, c), bf16),
            jax.ShapeDtypeStruct((2, d), f32),
        ),
        in_specs=[smem(), vmem(), vmem(), vmem()],
        out_specs=(vmem(), vmem()),
        scratch_shapes=[
            pltpu.VMEM((table.shape[0], c), f32),
            pltpu.VMEM((near, rows, c), f32),
        ],
        compiler_params=params(),
        name="gather_rows",
    )(index, table, own, weight)


def moments(stat, edges_each):
    devices = stat.shape[0]
    means = stat[:, 0, :]
    mean = jnp.sum(means, axis=0, keepdims=True) * (1.0 / devices)
    off = means - mean
    m2 = jnp.sum(stat[:, 1, :], axis=0, keepdims=True) + edges_each * jnp.sum(
        off * off, axis=0, keepdims=True
    )
    return mean, lax.rsqrt(m2 * (1.0 / (edges_each * devices)) + EPS)


def pool_kernel(
    mode, edges_each, diff_ref, own_ref, w_ref, stat_ref, gain_ref, shift_ref, *refs
):
    near, block, c = diff_ref.shape
    d = w_ref.shape[1]
    if mode == "forward":
        pooled_ref, mixed, centre = refs
    elif mode == "slope":
        slope_ref, sum_ref, moment_ref, mixed, centre = refs
    else:
        cot_ref, pooled_ref, slope_ref, sums_ref, mixed, centre = refs
    mean, inv = moments(stat_ref[...], edges_each)
    half_scale = gain_ref[...] * inv * 0.5
    centre[...] = (dot(own_ref[...], w_ref[:c, :]) - mean) * half_scale + shift_ref[...] * 0.5
    mixed[...] = dot(diff_ref[...].reshape(near * block, c), w_ref[c:, :]).reshape(near, block, d)
    if mode == "full":

        @pl.when(pl.program_id(0) == 0)
        def _():
            sums_ref[...] = jnp.zeros_like(sums_ref)

    for lane in range(0, d, 128):
        lanes = pl.ds(lane, 128)
        scale = jnp.broadcast_to(half_scale[:, lane : lane + 128], (8, 128))

        def step(b, carry, lanes=lanes, scale=scale):
            at = pl.ds(pl.multiple_of(b * 8, 8), 8)
            offset = centre[at, lanes]
            one_plus, active, halves = [], [], []
            for k in range(near):
                half = mixed[k, at, lanes] * scale + offset
                t = 1.0 + jnp.tanh(half)
                one_plus.append(t)
                halves.append(half)
                active.append(half * t)
            top = functools.reduce(jnp.maximum, active)
            powers = [jnp.exp(a - top) for a in active]
            total = functools.reduce(jnp.add, powers)
            if mode != "slope":
                pooled = top + jnp.log(total) - math.log(near)
                pooled_ref[at, lanes] = pooled.astype(pooled_ref.dtype)
            if mode == "forward":
                return carry
            factor = 0.5 / total
            if mode == "full":
                factor = factor * cot_ref[at, lanes].astype(f32)
            slope_sum = jnp.zeros((8, 128), f32)
            slope_moment = jnp.zeros((8, 128), f32)
            for k in range(near):
                slope = (powers[k] * factor) * (
                    one_plus[k] * ((halves[k] + halves[k] + 1.0) - active[k])
                )
                slope_ref[k, at, lanes] = slope
                slope_sum = slope_sum + slope
                slope_moment = slope_moment + slope * halves[k]
            if mode == "slope":
                sum_ref[at, lanes] = slope_sum
                moment_ref[at, lanes] = slope_moment
                return carry
            return (carry[0] + slope_sum, carry[1] + slope_moment)

        zero = jnp.zeros((8, 128), f32)
        carry = lax.fori_loop(0, block // 8, step, (zero, zero))
        if mode == "full":
            sums_ref[0:1, lanes] += jnp.sum(carry[0], axis=0, keepdims=True)
            sums_ref[1:2, lanes] += jnp.sum(carry[1], axis=0, keepdims=True)


def pool(mode, diff, own, weight, stat, gain, shift, cot=None):
    near, rows, c = diff.shape
    d = weight.shape[1]
    whole = lambda x: pl.BlockSpec(x.shape, lambda b: (0,) * x.ndim)
    by_block = lambda width: pl.BlockSpec((BLOCK, width), lambda b: (b, 0))
    by_edge = lambda width: pl.BlockSpec((near, BLOCK, width), lambda b: (0, b, 0))
    gain, shift = gain.reshape(1, d), shift.reshape(1, d)
    inputs = [diff, own, weight, stat, gain, shift]
    in_specs = [by_edge(c), by_block(c), whole(weight), whole(stat), whole(gain), whole(shift)]
    row_out = lambda kind: (jax.ShapeDtypeStruct((rows, d), kind), by_block(d))
    slope_out = (jax.ShapeDtypeStruct((near, rows, d), f32), by_edge(d))
    if mode == "forward":
        outs = [row_out(bf16)]
    elif mode == "slope":
        outs = [slope_out, row_out(f32), row_out(f32)]
    else:
        inputs.append(cot)
        in_specs.append(by_block(d))
        outs = [
            row_out(bf16),
            slope_out,
            (jax.ShapeDtypeStruct((2, d), f32), pl.BlockSpec((2, d), lambda b: (0, 0))),
        ]
    result = pl.pallas_call(
        functools.partial(pool_kernel, mode, float(near * rows)),
        grid=(rows // BLOCK,),
        out_shape=tuple(o[0] for o in outs),
        in_specs=in_specs,
        out_specs=tuple(o[1] for o in outs),
        scratch_shapes=[pltpu.VMEM((near, BLOCK, d), f32), pltpu.VMEM((BLOCK, d), f32)],
        compiler_params=params(),
        name="pool_" + mode,
    )(*inputs)
    return result if len(outs) > 1 else result[0]


def scatter_kernel(
    edges_each,
    idx_ref,
    slope_ref,
    upstream_ref,
    diff_ref,
    own_ref,
    w_ref,
    stat_ref,
    gain_ref,
    shift_ref,
    grads_ref,
    same_ref,
    dz_ref,
    dz_sum_ref,
    centre_ref,
    line_ref,
    mixed,
    constant,
    spread,
    line,
):
    near, block, c = diff_ref.shape
    d = w_ref.shape[1]
    step_id = pl.program_id(0)
    total = line.shape[0]
    edges = edges_each * stat_ref.shape[0]

    @pl.when(step_id == 0)
    def _():
        def clear(i, _):
            line[pl.ds(pl.multiple_of(i * 256, 256), 256), :] = jnp.zeros((256, c), f32)
            return 0

        lax.fori_loop(0, total // 256, clear, 0)

    mean, inv = moments(stat_ref[...], edges_each)
    gain = gain_ref[...]
    sums = jnp.sum(grads_ref[...], axis=0)
    grad_shift = sums[0:1]
    grad_gain = (2.0 * sums[1:2] - shift_ref[...] * grad_shift) / gain
    alpha = gain * inv
    rate = alpha * inv * grad_gain * (1.0 / edges)
    constant[...] = alpha * grad_shift * (1.0 / edges) + rate * (
        dot(own_ref[...], w_ref[:c, :]) - mean
    )
    mixed[...] = dot(diff_ref[...].reshape(near * block, c), w_ref[c:, :]).reshape(near, block, d)

    for lane in range(0, d, 128):
        lanes = pl.ds(lane, 128)
        wide_alpha = jnp.broadcast_to(alpha[:, lane : lane + 128], (16, 128))
        wide_rate = jnp.broadcast_to(rate[:, lane : lane + 128], (16, 128))

        def step(b, _, lanes=lanes, wide_alpha=wide_alpha, wide_rate=wide_rate):
            at = pl.ds(pl.multiple_of(b * 16, 16), 16)
            offset = constant[at, lanes]
            factor = wide_alpha
            if upstream_ref is not None:
                factor = factor * upstream_ref[at, lanes]
            dz_sum = jnp.zeros((16, 128), f32)
            for k in range(near):
                dz = (
                    factor * slope_ref[k, at, lanes].astype(f32)
                    - offset
                    - wide_rate * mixed[k, at, lanes]
                ).astype(bf16)
                dz_ref[k, at, lanes] = dz
                dz_sum = dz_sum + dz.astype(f32)
            dz_sum_ref[at, lanes] = dz_sum
            return 0

        lax.fori_loop(0, block // 16, step, 0)

    weight = w_ref[...].astype(f32)
    centre_ref[...] = lax.dot_general(
        dz_sum_ref[...],
        weight[:c] - weight[c:],
        (((1,), (1,)), ((), ())),
        precision=lax.Precision.HIGHEST,
        preferred_element_type=f32,
    )
    back = dot_t(dz_ref[...].reshape(near * block, d), w_ref[c:, :]).astype(bf16)
    back = back.reshape(near, block, c)
    for k in range(near):
        spread[k] = dot(same_ref[k], back[k])

    def scatter(k, _):
        first = step_id * block
        for g in range(0, block, GROUP):
            places = [idx_ref[k, first + (g + j)] for j in range(GROUP)]
            old = [line[pl.ds(places[j], 1), :] for j in range(GROUP)]
            new = [old[j] + spread[k, pl.ds(g + j, 1), :] for j in range(GROUP)]
            for j in range(GROUP):
                line[pl.ds(places[j], 1), :] = new[j]
        return 0

    lax.fori_loop(0, near, scatter, 0)

    @pl.when(step_id == pl.num_programs(0) - 1)
    def _():
        def narrow(i, _):
            at = pl.ds(pl.multiple_of(i * 256, 256), 256)
            line_ref[at, :] = line[at, :].astype(bf16)
            return 0

        lax.fori_loop(0, total // 256, narrow, 0)


def scatter_grads(index, slope, upstream, diff, own, weight, stat, gain, shift, grads, same, total):
    near, rows, c = diff.shape
    d = weight.shape[1]
    whole = lambda x: pl.BlockSpec(x.shape, lambda b: (0,) * x.ndim)
    by_block = lambda width: pl.BlockSpec((BLOCK, width), lambda b: (b, 0))
    by_edge = lambda width: pl.BlockSpec((near, BLOCK, width), lambda b: (0, b, 0))
    gain, shift = gain.reshape(1, d), shift.reshape(1, d)
    inputs = [index, slope, upstream, diff, own, weight, stat, gain, shift, grads, same]
    in_specs = [
        smem(),
        by_edge(d),
        by_block(d),
        by_edge(c),
        by_block(c),
        whole(weight),
        whole(stat),
        whole(gain),
        whole(shift),
        whole(grads),
        by_edge(BLOCK),
    ]
    body = functools.partial(scatter_kernel, float(near * rows))
    if upstream is None:
        del inputs[2], in_specs[2]
        inner = body
        body = lambda i, s, *rest: inner(i, s, None, *rest)
    return pl.pallas_call(
        body,
        grid=(rows // BLOCK,),
        out_shape=(
            jax.ShapeDtypeStruct((near, rows, d), bf16),
            jax.ShapeDtypeStruct((rows, d), f32),
            jax.ShapeDtypeStruct((rows, c), f32),
            jax.ShapeDtypeStruct((total, c), bf16),
        ),
        in_specs=in_specs,
        out_specs=(
            by_edge(d),
            by_block(d),
            by_block(c),
            pl.BlockSpec((total, c), lambda b: (0, 0)),
        ),
        scratch_shapes=[
            pltpu.VMEM((near, BLOCK, d), f32),
            pltpu.VMEM((BLOCK, d), f32),
            pltpu.VMEM((near, BLOCK, c), f32),
            pltpu.VMEM((total, c), f32),
        ],
        compiler_params=params(),
        name="scatter_grads",
    )(*inputs)


def same_target(index):
    near, rows = index.shape
    blocks = index.reshape(near, rows // BLOCK, BLOCK)
    group = jnp.arange(BLOCK, dtype=jnp.int32) // GROUP
    equal = (blocks[:, :, :, None] == blocks[:, :, None, :]) & (group[:, None] == group[None, :])
    return equal.astype(bf16).reshape(near, rows, BLOCK)


def everyone(x):
    devices = lax.axis_size(BOTH)
    copies = jnp.broadcast_to(x[None], (devices,) + x.shape)
    return lax.all_to_all(copies, BOTH, split_axis=0, concat_axis=0, tiled=True)


def owners_sum(line, centre):
    places = lax.axis_size("pts")
    parts = lax.all_to_all(
        line.reshape(places, -1, line.shape[1]), "pts", split_axis=0, concat_axis=0, tiled=True
    )
    return centre + jnp.sum(parts.astype(f32), axis=0)


def weight_grad(diff, own, dz, dz_sum):
    near, rows, c = diff.shape
    first = jnp.dot(
        own.astype(f32).T, dz_sum, precision=lax.Precision.HIGHEST, preferred_element_type=f32
    )
    second = jnp.einsum("kgc,kgd->cd", diff, dz, preferred_element_type=f32)
    return jnp.concatenate([first, second], axis=0)


def per_device(
    points,
    lengths,
    neighbours_one,
    neighbours_two,
    weight_one,
    gain_one,
    shift_one,
    weight_two,
    gain_two,
    shift_two,
    cotangent,
):
    line_devices = lax.axis_size("pts")
    row_count = points.shape[0]
    line_length = line_devices * row_count
    table_one = lax.all_gather(points, "pts", axis=0, tiled=True)

    cloud_ends = jnp.cumsum(lengths)
    cloud_starts = cloud_ends - lengths
    line_first = lax.axis_index("loc") * line_length
    position = (
        line_first + lax.axis_index("pts") * row_count + jnp.arange(row_count, dtype=jnp.int32)
    )
    begins = (position[:, None] >= cloud_starts[None, :]) & (position[:, None] < cloud_ends[None, :])
    begin = jnp.sum(jnp.where(begins, cloud_starts[None, :], 0), axis=1) - line_first
    index_one = neighbours_one.T + begin[None, :]
    index_two = neighbours_two.T + begin[None, :]
    same_one = same_target(index_one)
    same_two = same_target(index_two)

    diff_one, stat_one = gather_rows(index_one, table_one, points, weight_one)
    stat_one = everyone(stat_one)
    act_one = pool("forward", diff_one, points, weight_one, stat_one, gain_one, shift_one)
    table_two = lax.all_gather(act_one, "pts", axis=0, tiled=True)
    slope_one, slope_sum, slope_moment = pool(
        "slope", diff_one, points, weight_one, stat_one, gain_one, shift_one
    )
    diff_two, stat_two = gather_rows(index_two, table_two, act_one, weight_two)
    stat_two = everyone(stat_two)
    act_two, slope_two, sums_two = pool(
        "full", diff_two, act_one, weight_two, stat_two, gain_two, shift_two, cotangent
    )
    sums_two = everyone(sums_two)
    dz_two, dz_sum_two, centre_two, line_two = scatter_grads(
        index_two,
        slope_two,
        None,
        diff_two,
        act_one,
        weight_two,
        stat_two,
        gain_two,
        shift_two,
        sums_two,
        same_two,
        line_length,
    )
    grad_first = owners_sum(line_two, centre_two)
    sums_one = jnp.stack(
        [jnp.sum(grad_first * slope_sum, axis=0), jnp.sum(grad_first * slope_moment, axis=0)]
    )
    sums_one = everyone(sums_one)
    dz_one, dz_sum_one, centre_one, line_one = scatter_grads(
        index_one,
        slope_one,
        grad_first,
        diff_one,
        points,
        weight_one,
        stat_one,
        gain_one,
        shift_one,
        sums_one,
        same_one,
        line_length,
    )
    grad_points = owners_sum(line_one, centre_one)
    weight_part_two = weight_grad(diff_two, act_one, dz_two, dz_sum_two)
    weight_part_one = weight_grad(diff_one, points, dz_one, dz_sum_one)
    grad_weight_two = lax.psum(weight_part_two, BOTH)
    grad_weight_one = lax.psum(weight_part_one, BOTH)

    def norm_grads(sums, gain, shift):
        sums = jnp.sum(sums, axis=0)
        return (2.0 * sums[1] - shift * sums[0]) / gain, sums[0]

    grad_gain_one, grad_shift_one = norm_grads(sums_one, gain_one, shift_one)
    grad_gain_two, grad_shift_two = norm_grads(sums_two, gain_two, shift_two)
    return (
        act_one,
        act_two,
        grad_points,
        grad_weight_one,
        grad_gain_one,
        grad_shift_one,
        grad_weight_two,
        grad_gain_two,
        grad_shift_two,
    )


def solution(mesh):
    rows, copied = P(("pts", "loc"), None), P()
    in_specs = (rows, copied, rows, rows) + (copied,) * 6 + (rows,)
    out_specs = (rows, rows, rows) + (copied,) * 6
    return jax.shard_map(
        per_device, mesh=mesh, in_specs=in_specs, out_specs=out_specs, check_vma=False
    )
```

```python
import functools
import math

import jax
import jax.numpy as jnp
from jax import lax
from jax.experimental import pallas as pl
from jax.experimental.pallas import tpu as pltpu
from jax.sharding import PartitionSpec as P

EPS = 1e-05
BLOCK = 128
GROUP = 16
UNROLL = 64
LANES = 128
VMEM_LIMIT = 56 * 1024 * 1024
BOTH = ("pts", "loc")

f32 = jnp.float32
bf16 = jnp.bfloat16


def params():
    return pltpu.CompilerParams(vmem_limit_bytes=VMEM_LIMIT)


def vmem():
    return pl.BlockSpec(memory_space=pltpu.VMEM)


def smem():
    return pl.BlockSpec(memory_space=pltpu.SMEM)


def fold_rows(x):
    return jnp.sum(x.reshape(x.shape[0] // 8, 8, x.shape[1]), axis=0)


def dot(a, b):
    return jnp.dot(a, b, preferred_element_type=f32)


def dot_t(a, b):
    return lax.dot_general(a, b, (((1,), (1,)), ((), ())), preferred_element_type=f32)


def gather_kernel(idx_ref, table_ref, out_ref):
    k = pl.program_id(0)

    def pick(b, _):
        base = b * UNROLL
        for j in range(UNROLL):
            out_ref[base + j] = table_ref[idx_ref[k, base + j]]
        return 0

    lax.fori_loop(0, out_ref.shape[0] // UNROLL, pick, 0)


def gather_rows(index, table):
    near, rows = index.shape
    total, c = table.shape
    wide = jnp.pad(table.astype(f32), ((0, 0), (0, LANES - c))).reshape(total, 1, LANES)
    picked = pl.pallas_call(
        gather_kernel,
        grid=(near,),
        out_shape=jax.ShapeDtypeStruct((near * rows, 1, LANES), f32),
        in_specs=[smem(), pl.BlockSpec((total, 1, LANES), lambda k: (0, 0, 0))],
        out_specs=pl.BlockSpec((rows, 1, LANES), lambda k: (k, 0, 0)),
        compiler_params=params(),
        name="gather_rows",
    )(index, wide)
    return picked.reshape(near, rows, LANES)


def edge_kernel(picked_ref, own_ref, w_ref, diff_ref, stat_ref, pivot, sums, square):
    near, block, c = diff_ref.shape
    d = w_ref.shape[1]
    step_id = pl.program_id(0)
    own = own_ref[...].astype(f32)
    own_sum = fold_rows(own) * float(near)
    diff_sum = jnp.zeros((8, c), f32)
    for k in range(near):
        diff = (picked_ref[k, :, :c] - own).astype(bf16)
        diff_ref[k] = diff
        diff_sum = diff_sum + fold_rows(diff.astype(f32))

    def project(own_sum, diff_sum):
        weight = w_ref[...].astype(f32)
        exact = functools.partial(
            jnp.dot, precision=lax.Precision.HIGHEST, preferred_element_type=f32
        )
        both = exact(own_sum, weight[:c]) + exact(diff_sum, weight[c:])
        return jnp.sum(both, axis=0, keepdims=True)

    @pl.when(step_id == 0)
    def _():
        pivot[...] = project(own_sum, diff_sum) * (1.0 / (near * block))
        sums[...] = jnp.zeros_like(sums)
        square[...] = jnp.zeros_like(square)

    sums[0] += own_sum
    sums[1] += diff_sum
    centre = dot(own_ref[...], w_ref[:c, :]) - pivot[...]
    weight = w_ref[c:, :]
    total = square[...]
    for k in range(near):
        z = dot(diff_ref[k], weight) + centre
        total = total + fold_rows(z * z)
    square[...] = total

    @pl.when(step_id == pl.num_programs(0) - 1)
    def _():
        count = float(near * block * pl.num_programs(0))
        mean = project(sums[0], sums[1]) / count
        off = mean - pivot[...]
        stat_ref[0:1, :] = mean
        stat_ref[1:2, :] = jnp.sum(square[...], axis=0, keepdims=True) - count * off * off


def edge_stats(picked, own, weight):
    near, rows, _ = picked.shape
    c, d = own.shape[1], weight.shape[1]
    return pl.pallas_call(
        edge_kernel,
        grid=(rows // BLOCK,),
        out_shape=(
            jax.ShapeDtypeStruct((near, rows, c), bf16),
            jax.ShapeDtypeStruct((2, d), f32),
        ),
        in_specs=[
            pl.BlockSpec((near, BLOCK, LANES), lambda b: (0, b, 0)),
            pl.BlockSpec((BLOCK, c), lambda b: (b, 0)),
            pl.BlockSpec(weight.shape, lambda b: (0, 0)),
        ],
        out_specs=(
            pl.BlockSpec((near, BLOCK, c), lambda b: (0, b, 0)),
            pl.BlockSpec((2, d), lambda b: (0, 0)),
        ),
        scratch_shapes=[
            pltpu.VMEM((1, d), f32),
            pltpu.VMEM((2, 8, c), f32),
            pltpu.VMEM((8, d), f32),
        ],
        compiler_params=params(),
        name="edge_stats",
    )(picked, own, weight)


def moments(stat, edges_each):
    devices = stat.shape[0]
    means = stat[:, 0, :]
    mean = jnp.sum(means, axis=0, keepdims=True) * (1.0 / devices)
    off = means - mean
    m2 = jnp.sum(stat[:, 1, :], axis=0, keepdims=True) + edges_each * jnp.sum(
        off * off, axis=0, keepdims=True
    )
    return mean, lax.rsqrt(m2 * (1.0 / (edges_each * devices)) + EPS)


def pool_kernel(
    mode, edges_each, diff_ref, own_ref, w_ref, stat_ref, gain_ref, shift_ref, *refs
):
    near, block, c = diff_ref.shape
    d = w_ref.shape[1]
    if mode == "forward":
        pooled_ref, mixed, centre = refs
    elif mode == "slope":
        slope_ref, sum_ref, moment_ref, mixed, centre = refs
    else:
        cot_ref, pooled_ref, slope_ref, sums_ref, mixed, centre = refs
    mean, inv = moments(stat_ref[...], edges_each)
    half_scale = gain_ref[...] * inv * 0.5
    centre[...] = (dot(own_ref[...], w_ref[:c, :]) - mean) * half_scale + shift_ref[...] * 0.5
    mixed[...] = dot(diff_ref[...].reshape(near * block, c), w_ref[c:, :]).reshape(near, block, d)
    if mode == "full":

        @pl.when(pl.program_id(0) == 0)
        def _():
            sums_ref[...] = jnp.zeros_like(sums_ref)

    for lane in range(0, d, 128):
        lanes = pl.ds(lane, 128)
        scale = jnp.broadcast_to(half_scale[:, lane : lane + 128], (8, 128))

        def step(b, carry, lanes=lanes, scale=scale):
            at = pl.ds(pl.multiple_of(b * 8, 8), 8)
            offset = centre[at, lanes]
            one_plus, active, halves = [], [], []
            for k in range(near):
                half = mixed[k, at, lanes] * scale + offset
                t = 1.0 + jnp.tanh(half)
                one_plus.append(t)
                halves.append(half)
                active.append(half * t)
            top = functools.reduce(jnp.maximum, active)
            powers = [jnp.exp(a - top) for a in active]
            total = functools.reduce(jnp.add, powers)
            if mode != "slope":
                pooled = top + jnp.log(total) - math.log(near)
                pooled_ref[at, lanes] = pooled.astype(pooled_ref.dtype)
            if mode == "forward":
                return carry
            factor = 0.5 / total
            if mode == "full":
                factor = factor * cot_ref[at, lanes].astype(f32)
            slope_sum = jnp.zeros((8, 128), f32)
            slope_moment = jnp.zeros((8, 128), f32)
            for k in range(near):
                slope = (powers[k] * factor) * (
                    one_plus[k] * ((halves[k] + halves[k] + 1.0) - active[k])
                )
                slope_ref[k, at, lanes] = slope
                slope_sum = slope_sum + slope
                slope_moment = slope_moment + slope * halves[k]
            if mode == "slope":
                sum_ref[at, lanes] = slope_sum
                moment_ref[at, lanes] = slope_moment
                return carry
            return (carry[0] + slope_sum, carry[1] + slope_moment)

        zero = jnp.zeros((8, 128), f32)
        carry = lax.fori_loop(0, block // 8, step, (zero, zero))
        if mode == "full":
            sums_ref[0:1, lanes] += jnp.sum(carry[0], axis=0, keepdims=True)
            sums_ref[1:2, lanes] += jnp.sum(carry[1], axis=0, keepdims=True)


def pool(mode, diff, own, weight, stat, gain, shift, cot=None):
    near, rows, c = diff.shape
    d = weight.shape[1]
    whole = lambda x: pl.BlockSpec(x.shape, lambda b: (0,) * x.ndim)
    by_block = lambda width: pl.BlockSpec((BLOCK, width), lambda b: (b, 0))
    by_edge = lambda width: pl.BlockSpec((near, BLOCK, width), lambda b: (0, b, 0))
    gain, shift = gain.reshape(1, d), shift.reshape(1, d)
    inputs = [diff, own, weight, stat, gain, shift]
    in_specs = [by_edge(c), by_block(c), whole(weight), whole(stat), whole(gain), whole(shift)]
    row_out = lambda kind: (jax.ShapeDtypeStruct((rows, d), kind), by_block(d))
    slope_out = (jax.ShapeDtypeStruct((near, rows, d), f32), by_edge(d))
    if mode == "forward":
        outs = [row_out(bf16)]
    elif mode == "slope":
        outs = [slope_out, row_out(f32), row_out(f32)]
    else:
        inputs.append(cot)
        in_specs.append(by_block(d))
        outs = [
            row_out(bf16),
            slope_out,
            (jax.ShapeDtypeStruct((2, d), f32), pl.BlockSpec((2, d), lambda b: (0, 0))),
        ]
    result = pl.pallas_call(
        functools.partial(pool_kernel, mode, float(near * rows)),
        grid=(rows // BLOCK,),
        out_shape=tuple(o[0] for o in outs),
        in_specs=in_specs,
        out_specs=tuple(o[1] for o in outs),
        scratch_shapes=[pltpu.VMEM((near, BLOCK, d), f32), pltpu.VMEM((BLOCK, d), f32)],
        compiler_params=params(),
        name="pool_" + mode,
    )(*inputs)
    return result if len(outs) > 1 else result[0]


def grads_kernel(
    edges_each,
    with_weight,
    slope_ref,
    upstream_ref,
    diff_ref,
    own_ref,
    w_ref,
    back_ref,
    stat_ref,
    gain_ref,
    shift_ref,
    grads_ref,
    same_ref,
    dz_ref,
    dz_sum_ref,
    centre_ref,
    spread_ref,
    *refs,
):
    near, block, c = diff_ref.shape
    d = w_ref.shape[1]
    mixed, constant = refs[-2:]
    edges = edges_each * stat_ref.shape[0]
    mean, inv = moments(stat_ref[...], edges_each)
    gain = gain_ref[...]
    sums = jnp.sum(grads_ref[...], axis=0)
    grad_shift = sums[0:1]
    grad_gain = (2.0 * sums[1:2] - shift_ref[...] * grad_shift) / gain
    alpha = gain * inv
    rate = alpha * inv * grad_gain * (1.0 / edges)
    constant[...] = alpha * grad_shift * (1.0 / edges) + rate * (
        dot(own_ref[...], w_ref[:c, :]) - mean
    )
    mixed[...] = dot(diff_ref[...].reshape(near * block, c), w_ref[c:, :]).reshape(near, block, d)

    for lane in range(0, d, 128):
        lanes = pl.ds(lane, 128)
        wide_alpha = jnp.broadcast_to(alpha[:, lane : lane + 128], (16, 128))
        wide_rate = jnp.broadcast_to(rate[:, lane : lane + 128], (16, 128))

        def step(b, _, lanes=lanes, wide_alpha=wide_alpha, wide_rate=wide_rate):
            at = pl.ds(pl.multiple_of(b * 16, 16), 16)
            offset = constant[at, lanes]
            factor = wide_alpha
            if upstream_ref is not None:
                factor = factor * upstream_ref[at, lanes]
            dz_sum = jnp.zeros((16, 128), f32)
            for k in range(near):
                dz = (
                    factor * slope_ref[k, at, lanes] - offset - wide_rate * mixed[k, at, lanes]
                ).astype(bf16)
                dz_ref[k, at, lanes] = dz
                dz_sum = dz_sum + dz.astype(f32)
            dz_sum_ref[at, lanes] = dz_sum
            return 0

        lax.fori_loop(0, block // 16, step, 0)

    weight = w_ref[...].astype(f32)
    centre_ref[...] = lax.dot_general(
        dz_sum_ref[...],
        weight[:c] - weight[c:],
        (((1,), (1,)), ((), ())),
        precision=lax.Precision.HIGHEST,
        preferred_element_type=f32,
    )
    flat = dz_ref[...].reshape(near * block, d)
    back = dot_t(flat, back_ref[...]).astype(bf16).reshape(near, block, LANES)
    for k in range(near):
        spread_ref[k] = dot(same_ref[k], back[k])
    if with_weight:
        weight_ref = refs[0]

        @pl.when(pl.program_id(0) == 0)
        def _():
            weight_ref[...] = jnp.zeros_like(weight_ref)

        weight_ref[:c, :] += lax.dot_general(
            own_ref[...].astype(f32),
            dz_sum_ref[...],
            (((0,), (0,)), ((), ())),
            precision=lax.Precision.HIGHEST,
            preferred_element_type=f32,
        )
        weight_ref[c:, :] += lax.dot_general(
            diff_ref[...].reshape(near * block, c),
            flat,
            (((0,), (0,)), ((), ())),
            preferred_element_type=f32,
        )


def edge_grads(slope, upstream, diff, own, weight, stat, gain, shift, grads, same, with_weight):
    near, rows, c = diff.shape
    d = weight.shape[1]
    whole = lambda x: pl.BlockSpec(x.shape, lambda b: (0,) * x.ndim)
    by_block = lambda width: pl.BlockSpec((BLOCK, width), lambda b: (b, 0))
    by_edge = lambda width: pl.BlockSpec((near, BLOCK, width), lambda b: (0, b, 0))
    gain, shift = gain.reshape(1, d), shift.reshape(1, d)
    back = jnp.pad(weight[c:], ((0, LANES - c), (0, 0)))
    inputs = [slope, upstream, diff, own, weight, back, stat, gain, shift, grads, same]
    in_specs = [
        by_edge(d),
        by_block(d),
        by_edge(c),
        by_block(c),
        whole(weight),
        whole(back),
        whole(stat),
        whole(gain),
        whole(shift),
        whole(grads),
        by_edge(BLOCK),
    ]
    body = functools.partial(grads_kernel, float(near * rows), with_weight)
    if upstream is None:
        del inputs[1], in_specs[1]
        inner = body
        body = lambda s, *rest: inner(s, None, *rest)
    outs = [
        (jax.ShapeDtypeStruct((near, rows, d), bf16), by_edge(d)),
        (jax.ShapeDtypeStruct((rows, d), f32), by_block(d)),
        (jax.ShapeDtypeStruct((rows, c), f32), by_block(c)),
        (jax.ShapeDtypeStruct((near, rows, LANES), f32), by_edge(LANES)),
    ]
    if with_weight:
        outs.append((jax.ShapeDtypeStruct((2 * c, d), f32), whole(weight)))
    return pl.pallas_call(
        body,
        grid=(rows // BLOCK,),
        out_shape=tuple(o[0] for o in outs),
        in_specs=in_specs,
        out_specs=tuple(o[1] for o in outs),
        scratch_shapes=[pltpu.VMEM((near, BLOCK, d), f32), pltpu.VMEM((BLOCK, d), f32)],
        compiler_params=params(),
        name="edge_grads",
    )(*inputs)


def scatter_kernel(idx_ref, spread_ref, zero_ref, out_ref, even, odd):
    k = pl.program_id(0)

    @pl.when(k == 0)
    def _():
        pltpu.sync_copy(zero_ref, even)
        pltpu.sync_copy(zero_ref, odd)

    def step(b, _):
        base = b * (2 * GROUP)
        for half, line in enumerate((even, odd)):
            first = base + half * GROUP
            new = [line[idx_ref[k, first + j]] + spread_ref[first + j] for j in range(GROUP)]
            for j in range(GROUP):
                line[idx_ref[k, first + j]] = new[j]
        return 0

    lax.fori_loop(0, spread_ref.shape[0] // (2 * GROUP), step, 0)

    @pl.when(k == pl.num_programs(0) - 1)
    def _():
        pltpu.sync_copy(even, out_ref.at[0])
        pltpu.sync_copy(odd, out_ref.at[1])


def scatter_grads(index, spread, total):
    near, rows = index.shape
    spread = spread.reshape(near * rows, 1, LANES)
    return pl.pallas_call(
        scatter_kernel,
        grid=(near,),
        out_shape=jax.ShapeDtypeStruct((2, total, 1, LANES), f32),
        in_specs=[
            smem(),
            pl.BlockSpec((rows, 1, LANES), lambda k: (k, 0, 0)),
            pl.BlockSpec(memory_space=pl.ANY),
        ],
        out_specs=pl.BlockSpec(memory_space=pl.ANY),
        scratch_shapes=[pltpu.VMEM((total, 1, LANES), f32)] * 2,
        compiler_params=params(),
        name="scatter_grads",
    )(index, spread, jnp.zeros((total, 1, LANES), f32)).reshape(2, total, LANES)


def same_target(index):
    near, rows = index.shape
    blocks = index.reshape(near, rows // BLOCK, BLOCK)
    group = jnp.arange(BLOCK, dtype=jnp.int32) // GROUP
    equal = (blocks[:, :, :, None] == blocks[:, :, None, :]) & (group[:, None] == group[None, :])
    return equal.astype(bf16).reshape(near, rows, BLOCK)


def everyone(x):
    devices = lax.axis_size(BOTH)
    copies = jnp.broadcast_to(x[None], (devices,) + x.shape)
    return lax.all_to_all(copies, BOTH, split_axis=0, concat_axis=0, tiled=True)


def owners_sum(halves, centre):
    places = lax.axis_size("pts")
    rows, c = centre.shape
    line = (halves[0, :, :c] + halves[1, :, :c]).astype(bf16).reshape(places, rows, c)
    parts = lax.all_to_all(line, "pts", split_axis=0, concat_axis=0, tiled=True)
    return centre + jnp.sum(parts.astype(f32), axis=0)


def line_table(values):
    copies = jnp.broadcast_to(values[None], (lax.axis_size("pts"),) + values.shape)
    table = lax.all_to_all(copies, "pts", split_axis=0, concat_axis=0, tiled=True)
    return table.reshape(-1, values.shape[1])


def sum_everywhere(x):
    devices = lax.axis_size(BOTH)
    shares = x.reshape(devices, x.shape[0] // devices, x.shape[1])
    parts = lax.all_to_all(shares, BOTH, split_axis=0, concat_axis=0, tiled=True)
    return everyone(jnp.sum(parts, axis=0)).reshape(x.shape)


def weight_grad(diff, own, dz, dz_sum):
    first = jnp.dot(
        own.astype(f32).T, dz_sum, precision=lax.Precision.HIGHEST, preferred_element_type=f32
    )
    second = jnp.einsum("kgc,kgd->cd", diff, dz, preferred_element_type=f32)
    return jnp.concatenate([first, second], axis=0)


def per_device(
    points,
    lengths,
    neighbours_one,
    neighbours_two,
    weight_one,
    gain_one,
    shift_one,
    weight_two,
    gain_two,
    shift_two,
    cotangent,
):
    line_devices = lax.axis_size("pts")
    row_count = points.shape[0]
    line_length = line_devices * row_count
    table_one = line_table(points)

    cloud_ends = jnp.cumsum(lengths)
    cloud_starts = cloud_ends - lengths
    line_first = lax.axis_index("loc") * line_length
    position = (
        line_first + lax.axis_index("pts") * row_count + jnp.arange(row_count, dtype=jnp.int32)
    )
    begins = (position[:, None] >= cloud_starts[None, :]) & (position[:, None] < cloud_ends[None, :])
    begin = jnp.sum(jnp.where(begins, cloud_starts[None, :], 0), axis=1) - line_first
    index_one = neighbours_one.T + begin[None, :]
    index_two = neighbours_two.T + begin[None, :]
    same_one = same_target(index_one)
    same_two = same_target(index_two)

    diff_one, stat_one = edge_stats(gather_rows(index_one, table_one), points, weight_one)
    stat_one = everyone(stat_one)
    act_one = pool("forward", diff_one, points, weight_one, stat_one, gain_one, shift_one)
    table_two = lax.all_gather(act_one, "pts", axis=0, tiled=True)
    slope_one, slope_sum, slope_moment = pool(
        "slope", diff_one, points, weight_one, stat_one, gain_one, shift_one
    )
    diff_two, stat_two = edge_stats(gather_rows(index_two, table_two), act_one, weight_two)
    stat_two = everyone(stat_two)
    act_two, slope_two, sums_two = pool(
        "full", diff_two, act_one, weight_two, stat_two, gain_two, shift_two, cotangent
    )
    sums_two = everyone(sums_two)
    dz_two, dz_sum_two, centre_two, spread_two = edge_grads(
        slope_two,
        None,
        diff_two,
        act_one,
        weight_two,
        stat_two,
        gain_two,
        shift_two,
        sums_two,
        same_two,
        False,
    )
    line_two = scatter_grads(index_two, spread_two, line_length)
    line_two, dz_two, dz_sum_two = lax.optimization_barrier((line_two, dz_two, dz_sum_two))
    weight_part_two = weight_grad(diff_two, act_one, dz_two, dz_sum_two)
    grad_first = owners_sum(line_two, centre_two)
    sums_one = jnp.stack(
        [jnp.sum(grad_first * slope_sum, axis=0), jnp.sum(grad_first * slope_moment, axis=0)]
    )
    sums_one = everyone(sums_one)
    _, _, centre_one, spread_one, weight_part_one = edge_grads(
        slope_one,
        grad_first,
        diff_one,
        points,
        weight_one,
        stat_one,
        gain_one,
        shift_one,
        sums_one,
        same_one,
        True,
    )
    parts = jnp.concatenate([weight_part_two.reshape(-1, LANES), weight_part_one], axis=0)
    parts = sum_everywhere(parts)
    grad_weight_two = parts[: -weight_one.shape[0]].reshape(weight_two.shape)
    grad_weight_one = parts[-weight_one.shape[0] :]
    line_one = scatter_grads(index_one, spread_one, line_length)
    grad_points = owners_sum(line_one, centre_one)

    def norm_grads(sums, gain, shift):
        sums = jnp.sum(sums, axis=0)
        return (2.0 * sums[1] - shift * sums[0]) / gain, sums[0]

    grad_gain_one, grad_shift_one = norm_grads(sums_one, gain_one, shift_one)
    grad_gain_two, grad_shift_two = norm_grads(sums_two, gain_two, shift_two)
    return (
        act_one,
        act_two,
        grad_points,
        grad_weight_one,
        grad_gain_one,
        grad_shift_one,
        grad_weight_two,
        grad_gain_two,
        grad_shift_two,
    )


def solution(mesh):
    rows, copied = P(("pts", "loc"), None), P()
    in_specs = (rows, copied, rows, rows) + (copied,) * 6 + (rows,)
    out_specs = (rows, rows, rows) + (copied,) * 6
    return jax.shard_map(
        per_device, mesh=mesh, in_specs=in_specs, out_specs=out_specs, check_vma=False
    )
```

```python
import functools
import math

import jax
import jax.numpy as jnp
from jax import lax
from jax.experimental import pallas as pl
from jax.experimental.pallas import tpu as pltpu
from jax.sharding import PartitionSpec as P

EPS = 1e-05
BLOCK = 128
GROUP = 16
LANES = 128
MIB = 1024 * 1024
BOTH = ("pts", "loc")

f32 = jnp.float32
bf16 = jnp.bfloat16


def params(mebibytes):
    return pltpu.CompilerParams(vmem_limit_bytes=mebibytes * MIB)


def smem():
    return pl.BlockSpec(memory_space=pltpu.SMEM)


def fold_rows(x):
    return jnp.sum(x.reshape(x.shape[0] // 8, 8, x.shape[1]), axis=0)


def dot(a, b):
    return jnp.dot(a, b, preferred_element_type=f32)


def dot_t(a, b):
    return lax.dot_general(a, b, (((1,), (1,)), ((), ())), preferred_element_type=f32)


def gather_kernel(idx_ref, table_ref, out_ref):
    lines = out_ref.shape[0] // LANES
    first = pl.program_id(0) * lines

    def pick(b, _):
        base = b * LANES
        for g in range(0, LANES, GROUP):
            rows = [table_ref[idx_ref[first + b, g + j]] for j in range(GROUP)]
            for j in range(GROUP):
                out_ref[base + (g + j)] = rows[j]
        return 0

    lax.fori_loop(0, lines, pick, 0)


def gather_rows(index, table):
    near, rows = index.shape
    total, c = table.shape
    wide = jnp.pad(table.astype(f32), ((0, 0), (0, LANES - c))).reshape(total, 1, LANES)
    picked = pl.pallas_call(
        gather_kernel,
        grid=(near,),
        out_shape=jax.ShapeDtypeStruct((near * rows, 1, LANES), f32),
        in_specs=[smem(), pl.BlockSpec((total, 1, LANES), lambda k: (0, 0, 0))],
        out_specs=pl.BlockSpec((rows, 1, LANES), lambda k: (k, 0, 0)),
        compiler_params=params(total * LANES * 8 // MIB + 4),
        name="gather_rows",
    )(index.reshape(-1, LANES), wide)
    return picked.reshape(near, rows, LANES)


def edge_kernel(picked_ref, own_ref, w_ref, diff_ref, stat_ref, pivot, sums, square):
    near, block, c = diff_ref.shape
    d = w_ref.shape[1]
    step_id = pl.program_id(0)
    own = own_ref[...].astype(f32)
    own_sum = fold_rows(own) * float(near)
    diff_sum = jnp.zeros((8, c), f32)
    for k in range(near):
        diff = (picked_ref[k, :, :c] - own).astype(bf16)
        diff_ref[k] = diff
        diff_sum = diff_sum + fold_rows(diff.astype(f32))

    def project(own_sum, diff_sum):
        weight = w_ref[...].astype(f32)
        exact = functools.partial(
            jnp.dot, precision=lax.Precision.HIGHEST, preferred_element_type=f32
        )
        both = exact(own_sum, weight[:c]) + exact(diff_sum, weight[c:])
        return jnp.sum(both, axis=0, keepdims=True)

    @pl.when(step_id == 0)
    def _():
        pivot[...] = project(own_sum, diff_sum) * (1.0 / (near * block))
        sums[...] = jnp.zeros_like(sums)
        square[...] = jnp.zeros_like(square)

    sums[0] += own_sum
    sums[1] += diff_sum
    centre = dot(own_ref[...], w_ref[:c, :]) - pivot[...]
    weight = w_ref[c:, :]
    total = square[...]
    for k in range(near):
        z = dot(diff_ref[k], weight) + centre
        total = total + fold_rows(z * z)
    square[...] = total

    @pl.when(step_id == pl.num_programs(0) - 1)
    def _():
        count = float(near * block * pl.num_programs(0))
        mean = project(sums[0], sums[1]) / count
        off = mean - pivot[...]
        stat_ref[0:1, :] = mean
        stat_ref[1:2, :] = jnp.sum(square[...], axis=0, keepdims=True) - count * off * off


def edge_stats(picked, own, weight):
    near, rows, _ = picked.shape
    c, d = own.shape[1], weight.shape[1]
    return pl.pallas_call(
        edge_kernel,
        grid=(rows // BLOCK,),
        out_shape=(
            jax.ShapeDtypeStruct((near, rows, c), bf16),
            jax.ShapeDtypeStruct((2, d), f32),
        ),
        in_specs=[
            pl.BlockSpec((near, BLOCK, LANES), lambda b: (0, b, 0)),
            pl.BlockSpec((BLOCK, c), lambda b: (b, 0)),
            pl.BlockSpec(weight.shape, lambda b: (0, 0)),
        ],
        out_specs=(
            pl.BlockSpec((near, BLOCK, c), lambda b: (0, b, 0)),
            pl.BlockSpec((2, d), lambda b: (0, 0)),
        ),
        scratch_shapes=[
            pltpu.VMEM((1, d), f32),
            pltpu.VMEM((2, 8, c), f32),
            pltpu.VMEM((8, d), f32),
        ],
        compiler_params=params(12),
        name="edge_stats",
    )(picked, own, weight)


def moments(stat, edges_each):
    devices = stat.shape[0]
    means = stat[:, 0, :]
    mean = jnp.sum(means, axis=0, keepdims=True) * (1.0 / devices)
    off = means - mean
    m2 = jnp.sum(stat[:, 1, :], axis=0, keepdims=True) + edges_each * jnp.sum(
        off * off, axis=0, keepdims=True
    )
    return mean, lax.rsqrt(m2 * (1.0 / (edges_each * devices)) + EPS)


def pool_kernel(
    mode, edges_each, diff_ref, own_ref, w_ref, stat_ref, gain_ref, shift_ref, *refs
):
    near, block, c = diff_ref.shape
    d = w_ref.shape[1]
    if mode == "forward":
        pooled_ref, mixed, centre = refs
    elif mode == "slope":
        slope_ref, sum_ref, moment_ref, mixed, centre = refs
    else:
        cot_ref, pooled_ref, slope_ref, sums_ref, mixed, centre = refs
    mean, inv = moments(stat_ref[...], edges_each)
    half_scale = gain_ref[...] * inv * 0.5
    centre[...] = (dot(own_ref[...], w_ref[:c, :]) - mean) * half_scale + shift_ref[...] * 0.5
    mixed[...] = dot(diff_ref[...].reshape(near * block, c), w_ref[c:, :]).reshape(near, block, d)
    if mode == "full":

        @pl.when(pl.program_id(0) == 0)
        def _():
            sums_ref[...] = jnp.zeros_like(sums_ref)

    for lane in range(0, d, 128):
        lanes = pl.ds(lane, 128)
        scale = jnp.broadcast_to(half_scale[:, lane : lane + 128], (8, 128))

        def step(b, carry, lanes=lanes, scale=scale):
            at = pl.ds(pl.multiple_of(b * 8, 8), 8)
            offset = centre[at, lanes]
            one_plus, active, halves = [], [], []
            for k in range(near):
                half = mixed[k, at, lanes] * scale + offset
                t = 1.0 + jnp.tanh(half)
                one_plus.append(t)
                halves.append(half)
                active.append(half * t)
            top = functools.reduce(jnp.maximum, active)
            powers = [jnp.exp(a - top) for a in active]
            total = functools.reduce(jnp.add, powers)
            if mode != "slope":
                pooled = top + jnp.log(total) - math.log(near)
                pooled_ref[at, lanes] = pooled.astype(pooled_ref.dtype)
            if mode == "forward":
                return carry
            factor = 0.5 / total
            if mode == "full":
                factor = factor * cot_ref[at, lanes].astype(f32)
            slope_sum = jnp.zeros((8, 128), f32)
            slope_moment = jnp.zeros((8, 128), f32)
            for k in range(near):
                slope = (powers[k] * factor) * (
                    one_plus[k] * ((halves[k] + halves[k] + 1.0) - active[k])
                )
                slope_ref[k, at, lanes] = slope
                slope_sum = slope_sum + slope
                slope_moment = slope_moment + slope * halves[k]
            if mode == "slope":
                sum_ref[at, lanes] = slope_sum
                moment_ref[at, lanes] = slope_moment
                return carry
            return (carry[0] + slope_sum, carry[1] + slope_moment)

        zero = jnp.zeros((8, 128), f32)
        carry = lax.fori_loop(0, block // 8, step, (zero, zero))
        if mode == "full":
            sums_ref[0:1, lanes] += jnp.sum(carry[0], axis=0, keepdims=True)
            sums_ref[1:2, lanes] += jnp.sum(carry[1], axis=0, keepdims=True)


def pool(mode, diff, own, weight, stat, gain, shift, cot=None):
    near, rows, c = diff.shape
    d = weight.shape[1]
    whole = lambda x: pl.BlockSpec(x.shape, lambda b: (0,) * x.ndim)
    by_block = lambda width: pl.BlockSpec((BLOCK, width), lambda b: (b, 0))
    by_edge = lambda width: pl.BlockSpec((near, BLOCK, width), lambda b: (0, b, 0))
    gain, shift = gain.reshape(1, d), shift.reshape(1, d)
    inputs = [diff, own, weight, stat, gain, shift]
    in_specs = [by_edge(c), by_block(c), whole(weight), whole(stat), whole(gain), whole(shift)]
    row_out = lambda kind: (jax.ShapeDtypeStruct((rows, d), kind), by_block(d))
    slope_out = (jax.ShapeDtypeStruct((near, rows, d), f32), by_edge(d))
    if mode == "forward":
        outs = [row_out(bf16)]
    elif mode == "slope":
        outs = [slope_out, row_out(f32), row_out(f32)]
    else:
        inputs.append(cot)
        in_specs.append(by_block(d))
        outs = [
            row_out(bf16),
            slope_out,
            (jax.ShapeDtypeStruct((2, d), f32), pl.BlockSpec((2, d), lambda b: (0, 0))),
        ]
    result = pl.pallas_call(
        functools.partial(pool_kernel, mode, float(near * rows)),
        grid=(rows // BLOCK,),
        out_shape=tuple(o[0] for o in outs),
        in_specs=in_specs,
        out_specs=tuple(o[1] for o in outs),
        scratch_shapes=[pltpu.VMEM((near, BLOCK, d), f32), pltpu.VMEM((BLOCK, d), f32)],
        compiler_params=params(16),
        name="pool_" + mode,
    )(*inputs)
    return result if len(outs) > 1 else result[0]


def grads_kernel(
    edges_each,
    with_weight,
    slope_ref,
    upstream_ref,
    diff_ref,
    own_ref,
    w_ref,
    back_ref,
    stat_ref,
    gain_ref,
    shift_ref,
    grads_ref,
    same_ref,
    dz_ref,
    dz_sum_ref,
    centre_ref,
    spread_ref,
    *refs,
):
    near, block, c = diff_ref.shape
    d = w_ref.shape[1]
    mixed, constant = refs[-2:]
    edges = edges_each * stat_ref.shape[0]
    mean, inv = moments(stat_ref[...], edges_each)
    gain = gain_ref[...]
    sums = jnp.sum(grads_ref[...], axis=0)
    grad_shift = sums[0:1]
    grad_gain = (2.0 * sums[1:2] - shift_ref[...] * grad_shift) / gain
    alpha = gain * inv
    rate = alpha * inv * grad_gain * (1.0 / edges)
    constant[...] = alpha * grad_shift * (1.0 / edges) + rate * (
        dot(own_ref[...], w_ref[:c, :]) - mean
    )
    mixed[...] = dot(diff_ref[...].reshape(near * block, c), w_ref[c:, :]).reshape(near, block, d)

    for lane in range(0, d, 128):
        lanes = pl.ds(lane, 128)
        wide_alpha = jnp.broadcast_to(alpha[:, lane : lane + 128], (16, 128))
        wide_rate = jnp.broadcast_to(rate[:, lane : lane + 128], (16, 128))

        def step(b, _, lanes=lanes, wide_alpha=wide_alpha, wide_rate=wide_rate):
            at = pl.ds(pl.multiple_of(b * 16, 16), 16)
            offset = constant[at, lanes]
            factor = wide_alpha
            if upstream_ref is not None:
                factor = factor * upstream_ref[at, lanes]
            dz_sum = jnp.zeros((16, 128), f32)
            for k in range(near):
                dz = (
                    factor * slope_ref[k, at, lanes] - offset - wide_rate * mixed[k, at, lanes]
                ).astype(bf16)
                dz_ref[k, at, lanes] = dz
                dz_sum = dz_sum + dz.astype(f32)
            dz_sum_ref[at, lanes] = dz_sum
            return 0

        lax.fori_loop(0, block // 16, step, 0)

    weight = w_ref[...].astype(f32)
    centre_ref[...] = lax.dot_general(
        dz_sum_ref[...],
        weight[:c] - weight[c:],
        (((1,), (1,)), ((), ())),
        precision=lax.Precision.HIGHEST,
        preferred_element_type=f32,
    )
    flat = dz_ref[...].reshape(near * block, d)
    back = dot_t(flat, back_ref[...]).astype(bf16).reshape(near, block, LANES)
    for k in range(near):
        spread_ref[k] = dot(same_ref[k], back[k])
    if with_weight:
        weight_ref = refs[0]

        @pl.when(pl.program_id(0) == 0)
        def _():
            weight_ref[...] = jnp.zeros_like(weight_ref)

        weight_ref[:c, :] += lax.dot_general(
            own_ref[...].astype(f32),
            dz_sum_ref[...],
            (((0,), (0,)), ((), ())),
            precision=lax.Precision.HIGHEST,
            preferred_element_type=f32,
        )
        weight_ref[c:, :] += lax.dot_general(
            diff_ref[...].reshape(near * block, c),
            flat,
            (((0,), (0,)), ((), ())),
            preferred_element_type=f32,
        )


def edge_grads(slope, upstream, diff, own, weight, stat, gain, shift, grads, same, with_weight):
    near, rows, c = diff.shape
    d = weight.shape[1]
    whole = lambda x: pl.BlockSpec(x.shape, lambda b: (0,) * x.ndim)
    by_block = lambda width: pl.BlockSpec((BLOCK, width), lambda b: (b, 0))
    by_edge = lambda width: pl.BlockSpec((near, BLOCK, width), lambda b: (0, b, 0))
    gain, shift = gain.reshape(1, d), shift.reshape(1, d)
    back = jnp.pad(weight[c:], ((0, LANES - c), (0, 0)))
    inputs = [slope, upstream, diff, own, weight, back, stat, gain, shift, grads, same]
    in_specs = [
        by_edge(d),
        by_block(d),
        by_edge(c),
        by_block(c),
        whole(weight),
        whole(back),
        whole(stat),
        whole(gain),
        whole(shift),
        whole(grads),
        by_edge(BLOCK),
    ]
    body = functools.partial(grads_kernel, float(near * rows), with_weight)
    if upstream is None:
        del inputs[1], in_specs[1]
        inner = body
        body = lambda s, *rest: inner(s, None, *rest)
    outs = [
        (jax.ShapeDtypeStruct((near, rows, d), bf16), by_edge(d)),
        (jax.ShapeDtypeStruct((rows, d), f32), by_block(d)),
        (jax.ShapeDtypeStruct((rows, c), f32), by_block(c)),
        (jax.ShapeDtypeStruct((near, rows, LANES), f32), by_edge(LANES)),
    ]
    if with_weight:
        outs.append((jax.ShapeDtypeStruct((2 * c, d), f32), whole(weight)))
    return pl.pallas_call(
        body,
        grid=(rows // BLOCK,),
        out_shape=tuple(o[0] for o in outs),
        in_specs=in_specs,
        out_specs=tuple(o[1] for o in outs),
        scratch_shapes=[pltpu.VMEM((near, BLOCK, d), f32), pltpu.VMEM((BLOCK, d), f32)],
        compiler_params=params(24),
        name="edge_grads",
    )(*inputs)


def scatter_kernel(idx_ref, spread_ref, zero_ref, out_ref, even, odd, sems):
    k = pl.program_id(0)
    lines = spread_ref.shape[0] // LANES
    piece = zero_ref.shape[0]
    pieces = even.shape[0] // piece

    @pl.when(k == 0)
    def _():
        copies = [
            pltpu.make_async_copy(
                zero_ref, line.at[pl.ds(i * piece, piece)], sems.at[half * pieces + i]
            )
            for half, line in enumerate((even, odd))
            for i in range(pieces)
        ]
        for copy in copies:
            copy.start()
        for copy in copies:
            copy.wait()

    def step(b, _):
        at = k * lines + b
        base = b * LANES
        for g in range(0, LANES, GROUP):
            line = (even, odd)[g // GROUP % 2]
            new = [
                line[idx_ref[at, g + j]] + spread_ref[base + (g + j)] for j in range(GROUP)
            ]
            for j in range(GROUP):
                line[idx_ref[at, g + j]] = new[j]
        return 0

    lax.fori_loop(0, lines, step, 0)

    @pl.when(k == pl.num_programs(0) - 1)
    def _():
        copies = [
            pltpu.make_async_copy(line, out_ref.at[half], sems.at[half])
            for half, line in enumerate((even, odd))
        ]
        for copy in copies:
            copy.start()
        for copy in copies:
            copy.wait()


def scatter_grads(index, spread, total):
    near, rows = index.shape
    spread = spread.reshape(near * rows, 1, LANES)
    return pl.pallas_call(
        scatter_kernel,
        grid=(near,),
        out_shape=jax.ShapeDtypeStruct((2, total, 1, LANES), f32),
        in_specs=[
            smem(),
            pl.BlockSpec((rows, 1, LANES), lambda k: (k, 0, 0)),
            pl.BlockSpec(memory_space=pl.ANY),
        ],
        out_specs=pl.BlockSpec(memory_space=pl.ANY),
        scratch_shapes=[pltpu.VMEM((total, 1, LANES), f32)] * 2
        + [pltpu.SemaphoreType.DMA((2 * total // rows,))],
        compiler_params=params(total * LANES * 8 // MIB + 4),
        name="scatter_grads",
    )(index.reshape(-1, LANES), spread, jnp.zeros((rows, 1, LANES), f32)).reshape(2, total, LANES)


def same_target(index):
    near, rows = index.shape
    blocks = index.reshape(near, rows // BLOCK, BLOCK)
    group = jnp.arange(BLOCK, dtype=jnp.int32) // GROUP
    equal = (blocks[:, :, :, None] == blocks[:, :, None, :]) & (group[:, None] == group[None, :])
    return equal.astype(bf16).reshape(near, rows, BLOCK)


def everyone(x):
    devices = lax.axis_size(BOTH)
    copies = jnp.broadcast_to(x[None], (devices,) + x.shape)
    return lax.all_to_all(copies, BOTH, split_axis=0, concat_axis=0, tiled=True)


def owners_sum(halves, centre):
    places = lax.axis_size("pts")
    rows, c = centre.shape
    line = (halves[0, :, :c] + halves[1, :, :c]).astype(bf16).reshape(places, rows, c)
    parts = lax.all_to_all(line, "pts", split_axis=0, concat_axis=0, tiled=True)
    return centre + jnp.sum(parts.astype(f32), axis=0)


def line_table(values):
    copies = jnp.broadcast_to(values[None], (lax.axis_size("pts"),) + values.shape)
    table = lax.all_to_all(copies, "pts", split_axis=0, concat_axis=0, tiled=True)
    return table.reshape(-1, values.shape[1])


def weight_grad(diff, own, dz, dz_sum):
    first = jnp.dot(
        own.astype(f32).T, dz_sum, precision=lax.Precision.HIGHEST, preferred_element_type=f32
    )
    second = jnp.einsum("kgc,kgd->cd", diff, dz, preferred_element_type=f32)
    return jnp.concatenate([first, second], axis=0)


def per_device(
    points,
    lengths,
    neighbours_one,
    neighbours_two,
    weight_one,
    gain_one,
    shift_one,
    weight_two,
    gain_two,
    shift_two,
    cotangent,
):
    line_devices = lax.axis_size("pts")
    row_count = points.shape[0]
    line_length = line_devices * row_count
    table_one = line_table(points)

    cloud_ends = jnp.cumsum(lengths)
    cloud_starts = cloud_ends - lengths
    line_first = lax.axis_index("loc") * line_length
    position = (
        line_first + lax.axis_index("pts") * row_count + jnp.arange(row_count, dtype=jnp.int32)
    )
    begins = (position[:, None] >= cloud_starts[None, :]) & (position[:, None] < cloud_ends[None, :])
    begin = jnp.sum(jnp.where(begins, cloud_starts[None, :], 0), axis=1) - line_first
    index_one = neighbours_one.T + begin[None, :]
    index_two = neighbours_two.T + begin[None, :]
    same_one = same_target(index_one)
    same_two = same_target(index_two)

    diff_one, stat_one = edge_stats(gather_rows(index_one, table_one), points, weight_one)
    stat_one = everyone(stat_one)
    act_one = pool("forward", diff_one, points, weight_one, stat_one, gain_one, shift_one)
    table_two = lax.all_gather(act_one, "pts", axis=0, tiled=True)
    slope_one, slope_sum, slope_moment = pool(
        "slope", diff_one, points, weight_one, stat_one, gain_one, shift_one
    )
    diff_two, stat_two = edge_stats(gather_rows(index_two, table_two), act_one, weight_two)
    stat_two = everyone(stat_two)
    act_two, slope_two, sums_two = pool(
        "full", diff_two, act_one, weight_two, stat_two, gain_two, shift_two, cotangent
    )
    sums_two = everyone(sums_two)
    dz_two, dz_sum_two, centre_two, spread_two = edge_grads(
        slope_two,
        None,
        diff_two,
        act_one,
        weight_two,
        stat_two,
        gain_two,
        shift_two,
        sums_two,
        same_two,
        False,
    )
    line_two = scatter_grads(index_two, spread_two, line_length)
    line_two, dz_two, dz_sum_two = lax.optimization_barrier((line_two, dz_two, dz_sum_two))
    grad_weight_two = lax.psum(weight_grad(diff_two, act_one, dz_two, dz_sum_two), BOTH)
    grad_first = owners_sum(line_two, centre_two)
    sums_one = jnp.stack(
        [jnp.sum(grad_first * slope_sum, axis=0), jnp.sum(grad_first * slope_moment, axis=0)]
    )
    sums_one = everyone(sums_one)
    _, _, centre_one, spread_one, weight_part_one = edge_grads(
        slope_one,
        grad_first,
        diff_one,
        points,
        weight_one,
        stat_one,
        gain_one,
        shift_one,
        sums_one,
        same_one,
        True,
    )
    grad_weight_two, weight_part_one = lax.optimization_barrier((grad_weight_two, weight_part_one))
    grad_weight_one = lax.psum(weight_part_one, BOTH)
    line_one = scatter_grads(index_one, spread_one, line_length)
    grad_points = owners_sum(line_one, centre_one)

    def norm_grads(sums, gain, shift):
        sums = jnp.sum(sums, axis=0)
        return (2.0 * sums[1] - shift * sums[0]) / gain, sums[0]

    grad_gain_one, grad_shift_one = norm_grads(sums_one, gain_one, shift_one)
    grad_gain_two, grad_shift_two = norm_grads(sums_two, gain_two, shift_two)
    return (
        act_one,
        act_two,
        grad_points,
        grad_weight_one,
        grad_gain_one,
        grad_shift_one,
        grad_weight_two,
        grad_gain_two,
        grad_shift_two,
    )


def solution(mesh):
    rows, copied = P(("pts", "loc"), None), P()
    in_specs = (rows, copied, rows, rows) + (copied,) * 6 + (rows,)
    out_specs = (rows, rows, rows) + (copied,) * 6
    return jax.shard_map(
        per_device, mesh=mesh, in_specs=in_specs, out_specs=out_specs, check_vma=False
    )
```

```python
import functools
import math

import jax
import jax.numpy as jnp
from jax import lax
from jax.experimental import pallas as pl
from jax.experimental.pallas import tpu as pltpu
from jax.sharding import PartitionSpec as P

EPS = 1e-05
BLOCK = 128
GROUP = 8
LANES = 128
MIB = 1024 * 1024
BOTH = ("pts", "loc")

f32 = jnp.float32
bf16 = jnp.bfloat16


def params(mebibytes):
    return pltpu.CompilerParams(vmem_limit_bytes=mebibytes * MIB)


def smem():
    return pl.BlockSpec(memory_space=pltpu.SMEM)


def fold_rows(x):
    return jnp.sum(x.reshape(x.shape[0] // 8, 8, x.shape[1]), axis=0)


def dot(a, b):
    return jnp.dot(a, b, preferred_element_type=f32)


def dot_t(a, b):
    return lax.dot_general(a, b, (((1,), (1,)), ((), ())), preferred_element_type=f32)


def gather_kernel(idx_ref, table_ref, out_ref):
    lines = out_ref.shape[0] // LANES
    first = pl.program_id(0) * lines

    def pick(b, _):
        base = b * LANES
        for g in range(0, LANES, GROUP):
            rows = [table_ref[idx_ref[first + b, g + j]] for j in range(GROUP)]
            for j in range(GROUP):
                out_ref[base + (g + j)] = rows[j]
        return 0

    lax.fori_loop(0, lines, pick, 0)


def gather_rows(index, table):
    near, rows = index.shape
    total, c = table.shape
    wide = jnp.pad(table.astype(f32), ((0, 0), (0, LANES - c))).reshape(total, 1, LANES)
    picked = pl.pallas_call(
        gather_kernel,
        grid=(near,),
        out_shape=jax.ShapeDtypeStruct((near * rows, 1, LANES), f32),
        in_specs=[smem(), pl.BlockSpec((total, 1, LANES), lambda k: (0, 0, 0))],
        out_specs=pl.BlockSpec((rows, 1, LANES), lambda k: (k, 0, 0)),
        compiler_params=params(total * LANES * 8 // MIB + 4),
        name="gather_rows",
    )(index.reshape(-1, LANES), wide)
    return picked.reshape(near, rows, LANES)


def edge_kernel(picked_ref, own_ref, w_ref, diff_ref, stat_ref, pivot, sums, square):
    near, block, c = diff_ref.shape
    d = w_ref.shape[1]
    step_id = pl.program_id(0)
    own = own_ref[...].astype(f32)
    own_sum = fold_rows(own) * float(near)
    diff_sum = jnp.zeros((8, c), f32)
    for k in range(near):
        diff = (picked_ref[k, :, :c] - own).astype(bf16)
        diff_ref[k] = diff
        diff_sum = diff_sum + fold_rows(diff.astype(f32))

    def project(own_sum, diff_sum):
        weight = w_ref[...].astype(f32)
        exact = functools.partial(
            jnp.dot, precision=lax.Precision.HIGHEST, preferred_element_type=f32
        )
        both = exact(own_sum, weight[:c]) + exact(diff_sum, weight[c:])
        return jnp.sum(both, axis=0, keepdims=True)

    @pl.when(step_id == 0)
    def _():
        pivot[...] = project(own_sum, diff_sum) * (1.0 / (near * block))
        sums[...] = jnp.zeros_like(sums)
        square[...] = jnp.zeros_like(square)

    sums[0] += own_sum
    sums[1] += diff_sum
    centre = dot(own_ref[...], w_ref[:c, :]) - pivot[...]
    weight = w_ref[c:, :]
    total = square[...]
    for k in range(near):
        z = dot(diff_ref[k], weight) + centre
        total = total + fold_rows(z * z)
    square[...] = total

    @pl.when(step_id == pl.num_programs(0) - 1)
    def _():
        count = float(near * block * pl.num_programs(0))
        mean = project(sums[0], sums[1]) / count
        off = mean - pivot[...]
        stat_ref[0:1, :] = mean
        stat_ref[1:2, :] = jnp.sum(square[...], axis=0, keepdims=True) - count * off * off


def edge_stats(picked, own, weight):
    near, rows, _ = picked.shape
    c, d = own.shape[1], weight.shape[1]
    return pl.pallas_call(
        edge_kernel,
        grid=(rows // BLOCK,),
        out_shape=(
            jax.ShapeDtypeStruct((near, rows, c), bf16),
            jax.ShapeDtypeStruct((2, d), f32),
        ),
        in_specs=[
            pl.BlockSpec((near, BLOCK, LANES), lambda b: (0, b, 0)),
            pl.BlockSpec((BLOCK, c), lambda b: (b, 0)),
            pl.BlockSpec(weight.shape, lambda b: (0, 0)),
        ],
        out_specs=(
            pl.BlockSpec((near, BLOCK, c), lambda b: (0, b, 0)),
            pl.BlockSpec((2, d), lambda b: (0, 0)),
        ),
        scratch_shapes=[
            pltpu.VMEM((1, d), f32),
            pltpu.VMEM((2, 8, c), f32),
            pltpu.VMEM((8, d), f32),
        ],
        compiler_params=params(12),
        name="edge_stats",
    )(picked, own, weight)


def moments(stat, edges_each):
    devices = stat.shape[0]
    means = stat[:, 0, :]
    mean = jnp.sum(means, axis=0, keepdims=True) * (1.0 / devices)
    off = means - mean
    m2 = jnp.sum(stat[:, 1, :], axis=0, keepdims=True) + edges_each * jnp.sum(
        off * off, axis=0, keepdims=True
    )
    return mean, lax.rsqrt(m2 * (1.0 / (edges_each * devices)) + EPS)


def pool_kernel(
    last, edges_each, diff_ref, own_ref, w_ref, stat_ref, gain_ref, shift_ref, *refs
):
    near, block, c = diff_ref.shape
    d = w_ref.shape[1]
    if last:
        cot_ref, pooled_ref, slope_ref, sums_ref, mixed, centre, upstream = refs
        upstream[...] = cot_ref[...].astype(f32)
    else:
        pooled_ref, slope_ref, sum_ref, moment_ref, mixed, centre = refs
    mean, inv = moments(stat_ref[...], edges_each)
    half_scale = gain_ref[...] * inv * 0.5
    centre[...] = (dot(own_ref[...], w_ref[:c, :]) - mean) * half_scale + shift_ref[...] * 0.5
    mixed[...] = dot(diff_ref[...].reshape(near * block, c), w_ref[c:, :]).reshape(near, block, d)
    if last:

        @pl.when(pl.program_id(0) == 0)
        def _():
            sums_ref[...] = jnp.zeros_like(sums_ref)

    for lane in range(0, d, 128):
        lanes = pl.ds(lane, 128)
        scale = jnp.broadcast_to(half_scale[:, lane : lane + 128], (8, 128))

        def step(b, carry, lanes=lanes, scale=scale):
            at = pl.ds(pl.multiple_of(b * 8, 8), 8)
            offset = centre[at, lanes]
            one_plus, active, halves = [], [], []
            for k in range(near):
                half = mixed[k, at, lanes] * scale + offset
                t = 1.0 + jnp.tanh(half)
                one_plus.append(t)
                halves.append(half)
                active.append(half * t)
            top = functools.reduce(jnp.maximum, active)
            powers = [jnp.exp(a - top) for a in active]
            total = functools.reduce(jnp.add, powers)
            pooled = top + jnp.log(total) - math.log(near)
            centre[at, lanes] = pooled
            factor = 0.5 / total
            if last:
                factor = factor * upstream[at, lanes]
            slope_sum = jnp.zeros((8, 128), f32)
            slope_moment = jnp.zeros((8, 128), f32)
            for k in range(near):
                slope = (powers[k] * factor) * (
                    one_plus[k] * ((halves[k] + halves[k] + 1.0) - active[k])
                )
                slope_ref[k, at, lanes] = slope
                slope_sum = slope_sum + slope
                slope_moment = slope_moment + slope * halves[k]
            if not last:
                sum_ref[at, lanes] = slope_sum
                moment_ref[at, lanes] = slope_moment
                return carry
            return (carry[0] + slope_sum, carry[1] + slope_moment)

        zero = jnp.zeros((8, 128), f32)
        carry = lax.fori_loop(0, block // 8, step, (zero, zero))
        if last:
            sums_ref[0:1, lanes] += jnp.sum(carry[0], axis=0, keepdims=True)
            sums_ref[1:2, lanes] += jnp.sum(carry[1], axis=0, keepdims=True)
    pooled_ref[...] = centre[...].astype(bf16)


def pool(diff, own, weight, stat, gain, shift, cot=None):
    near, rows, c = diff.shape
    d = weight.shape[1]
    whole = lambda x: pl.BlockSpec(x.shape, lambda b: (0,) * x.ndim)
    by_block = lambda width: pl.BlockSpec((BLOCK, width), lambda b: (b, 0))
    by_edge = lambda width: pl.BlockSpec((near, BLOCK, width), lambda b: (0, b, 0))
    gain, shift = gain.reshape(1, d), shift.reshape(1, d)
    inputs = [diff, own, weight, stat, gain, shift]
    in_specs = [by_edge(c), by_block(c), whole(weight), whole(stat), whole(gain), whole(shift)]
    row_out = lambda kind: (jax.ShapeDtypeStruct((rows, d), kind), by_block(d))
    outs = [row_out(bf16), (jax.ShapeDtypeStruct((near, rows, d), f32), by_edge(d))]
    if cot is None:
        outs += [row_out(f32), row_out(f32)]
    else:
        inputs.append(cot)
        in_specs.append(by_block(d))
        outs.append((jax.ShapeDtypeStruct((2, d), f32), pl.BlockSpec((2, d), lambda b: (0, 0))))
    return pl.pallas_call(
        functools.partial(pool_kernel, cot is not None, float(near * rows)),
        grid=(rows // BLOCK,),
        out_shape=tuple(o[0] for o in outs),
        in_specs=in_specs,
        out_specs=tuple(o[1] for o in outs),
        scratch_shapes=[pltpu.VMEM((near, BLOCK, d), f32)]
        + [pltpu.VMEM((BLOCK, d), f32)] * (1 if cot is None else 2),
        compiler_params=params(52),
        name="pool",
    )(*inputs)


def grads_kernel(
    edges_each,
    with_weight,
    slope_ref,
    upstream_ref,
    diff_ref,
    own_ref,
    w_ref,
    back_ref,
    stat_ref,
    gain_ref,
    shift_ref,
    grads_ref,
    same_ref,
    dz_ref,
    dz_sum_ref,
    centre_ref,
    spread_ref,
    *refs,
):
    near, block, c = diff_ref.shape
    d = w_ref.shape[1]
    mixed, constant = refs[-2:]
    edges = edges_each * stat_ref.shape[0]
    mean, inv = moments(stat_ref[...], edges_each)
    gain = gain_ref[...]
    sums = jnp.sum(grads_ref[...], axis=0)
    grad_shift = sums[0:1]
    grad_gain = (2.0 * sums[1:2] - shift_ref[...] * grad_shift) / gain
    alpha = gain * inv
    rate = alpha * inv * grad_gain * (1.0 / edges)
    constant[...] = alpha * grad_shift * (1.0 / edges) + rate * (
        dot(own_ref[...], w_ref[:c, :]) - mean
    )
    mixed[...] = dot(diff_ref[...].reshape(near * block, c), w_ref[c:, :]).reshape(near, block, d)

    for lane in range(0, d, 128):
        lanes = pl.ds(lane, 128)
        wide_alpha = jnp.broadcast_to(alpha[:, lane : lane + 128], (16, 128))
        wide_rate = jnp.broadcast_to(rate[:, lane : lane + 128], (16, 128))

        def step(b, _, lanes=lanes, wide_alpha=wide_alpha, wide_rate=wide_rate):
            at = pl.ds(pl.multiple_of(b * 16, 16), 16)
            offset = constant[at, lanes]
            factor = wide_alpha
            if upstream_ref is not None:
                factor = factor * upstream_ref[at, lanes]
            dz_sum = jnp.zeros((16, 128), f32)
            for k in range(near):
                dz = (
                    factor * slope_ref[k, at, lanes] - offset - wide_rate * mixed[k, at, lanes]
                ).astype(bf16)
                dz_ref[k, at, lanes] = dz
                dz_sum = dz_sum + dz.astype(f32)
            dz_sum_ref[at, lanes] = dz_sum
            return 0

        lax.fori_loop(0, block // 16, step, 0)

    weight = w_ref[...].astype(f32)
    centre_ref[...] = lax.dot_general(
        dz_sum_ref[...],
        weight[:c] - weight[c:],
        (((1,), (1,)), ((), ())),
        precision=lax.Precision.HIGHEST,
        preferred_element_type=f32,
    )
    flat = dz_ref[...].reshape(near * block, d)
    back = dot_t(flat, back_ref[...]).astype(bf16).reshape(near, block, LANES)
    for k in range(near):
        spread_ref[k] = dot(same_ref[k], back[k])
    if with_weight:
        weight_ref = refs[0]

        @pl.when(pl.program_id(0) == 0)
        def _():
            weight_ref[...] = jnp.zeros_like(weight_ref)

        weight_ref[:c, :] += lax.dot_general(
            own_ref[...].astype(f32),
            dz_sum_ref[...],
            (((0,), (0,)), ((), ())),
            precision=lax.Precision.HIGHEST,
            preferred_element_type=f32,
        )
        weight_ref[c:, :] += lax.dot_general(
            diff_ref[...].reshape(near * block, c),
            flat,
            (((0,), (0,)), ((), ())),
            preferred_element_type=f32,
        )


def edge_grads(slope, upstream, diff, own, weight, stat, gain, shift, grads, same, with_weight):
    near, rows, c = diff.shape
    d = weight.shape[1]
    whole = lambda x: pl.BlockSpec(x.shape, lambda b: (0,) * x.ndim)
    by_block = lambda width: pl.BlockSpec((BLOCK, width), lambda b: (b, 0))
    by_edge = lambda width: pl.BlockSpec((near, BLOCK, width), lambda b: (0, b, 0))
    gain, shift = gain.reshape(1, d), shift.reshape(1, d)
    back = jnp.pad(weight[c:], ((0, LANES - c), (0, 0)))
    inputs = [slope, upstream, diff, own, weight, back, stat, gain, shift, grads, same]
    in_specs = [
        by_edge(d),
        by_block(d),
        by_edge(c),
        by_block(c),
        whole(weight),
        whole(back),
        whole(stat),
        whole(gain),
        whole(shift),
        whole(grads),
        by_edge(BLOCK),
    ]
    body = functools.partial(grads_kernel, float(near * rows), with_weight)
    if upstream is None:
        del inputs[1], in_specs[1]
        inner = body
        body = lambda s, *rest: inner(s, None, *rest)
    outs = [
        (jax.ShapeDtypeStruct((near, rows, d), bf16), by_edge(d)),
        (jax.ShapeDtypeStruct((rows, d), f32), by_block(d)),
        (jax.ShapeDtypeStruct((rows, c), f32), by_block(c)),
        (jax.ShapeDtypeStruct((near, rows, LANES), f32), by_edge(LANES)),
    ]
    if with_weight:
        outs.append((jax.ShapeDtypeStruct((2 * c, d), f32), whole(weight)))
    return pl.pallas_call(
        body,
        grid=(rows // BLOCK,),
        out_shape=tuple(o[0] for o in outs),
        in_specs=in_specs,
        out_specs=tuple(o[1] for o in outs),
        scratch_shapes=[pltpu.VMEM((near, BLOCK, d), f32), pltpu.VMEM((BLOCK, d), f32)],
        compiler_params=params(52),
        name="edge_grads",
    )(*inputs)


def scatter_kernel(idx_ref, spread_ref, zero_ref, out_ref, even, odd, sems):
    k = pl.program_id(0)
    lines = spread_ref.shape[0] // LANES
    piece = zero_ref.shape[0]
    pieces = even.shape[0] // piece

    @pl.when(k == 0)
    def _():
        copies = [
            pltpu.make_async_copy(
                zero_ref, line.at[pl.ds(i * piece, piece)], sems.at[half * pieces + i]
            )
            for half, line in enumerate((even, odd))
            for i in range(pieces)
        ]
        for copy in copies:
            copy.start()
        for copy in copies:
            copy.wait()

    def step(b, _):
        at = k * lines + b
        base = b * LANES
        for g in range(0, LANES, GROUP):
            line = (even, odd)[g // GROUP % 2]
            new = [
                line[idx_ref[at, g + j]] + spread_ref[base + (g + j)] for j in range(GROUP)
            ]
            for j in range(GROUP):
                line[idx_ref[at, g + j]] = new[j]
        return 0

    lax.fori_loop(0, lines, step, 0)

    @pl.when(k == pl.num_programs(0) - 1)
    def _():
        copies = [
            pltpu.make_async_copy(line, out_ref.at[half], sems.at[half])
            for half, line in enumerate((even, odd))
        ]
        for copy in copies:
            copy.start()
        for copy in copies:
            copy.wait()


def scatter_grads(index, spread, total):
    near, rows = index.shape
    spread = spread.reshape(near * rows, 1, LANES)
    return pl.pallas_call(
        scatter_kernel,
        grid=(near,),
        out_shape=jax.ShapeDtypeStruct((2, total, 1, LANES), f32),
        in_specs=[
            smem(),
            pl.BlockSpec((rows, 1, LANES), lambda k: (k, 0, 0)),
            pl.BlockSpec(memory_space=pl.ANY),
        ],
        out_specs=pl.BlockSpec(memory_space=pl.ANY),
        scratch_shapes=[pltpu.VMEM((total, 1, LANES), f32)] * 2
        + [pltpu.SemaphoreType.DMA((2 * total // rows,))],
        compiler_params=params(total * LANES * 8 // MIB + 4),
        name="scatter_grads",
    )(index.reshape(-1, LANES), spread, jnp.zeros((rows, 1, LANES), f32)).reshape(
        2, total // rows, rows, LANES
    )


def same_target(index):
    near, rows = index.shape
    blocks = index.reshape(near, rows // BLOCK, BLOCK)
    group = jnp.arange(BLOCK, dtype=jnp.int32) // GROUP
    equal = (blocks[:, :, :, None] == blocks[:, :, None, :]) & (group[:, None] == group[None, :])
    return equal.astype(bf16).reshape(near, rows, BLOCK)


def everyone(x):
    devices = lax.axis_size(BOTH)
    copies = jnp.broadcast_to(x[None], (devices,) + x.shape)
    return lax.all_to_all(copies, BOTH, split_axis=0, concat_axis=0, tiled=True)


def ring_moves(places):
    ring = list(range(0, places, 2)) + list(range(1, places, 2))[::-1]
    onward = [(ring[i], ring[(i + 1) % places]) for i in range(places)]
    return onward, [(b, a) for a, b in onward]


def ring_place(device, places):
    return jnp.where(device % 2 == 0, device // 2, places - 1 - device // 2)


def line_table(values):
    places = lax.axis_size("pts")
    onward, backward = ring_moves(places)
    rows, far = values.shape[0] // 2, places // 2
    behind, ahead = [values], [values]
    for _ in range(far - 1):
        behind.append(lax.ppermute(behind[-1], "pts", onward))
        ahead.append(lax.ppermute(ahead[-1], "pts", backward))
    farthest = [
        lax.ppermute(behind[-1][:rows], "pts", onward),
        lax.ppermute(ahead[-1][rows:], "pts", backward),
    ]
    return jnp.concatenate(behind + farthest + ahead[:0:-1], axis=0)


def owners_sum(halves, centre):
    places = lax.axis_size("pts")
    onward, backward = ring_moves(places)
    rows, c = centre.shape
    half, far = rows // 2, places // 2
    slot = lambda j, at=slice(None): halves[0, j, at, :c] + halves[1, j, at, :c]
    forth = slot(far, slice(0, half)).astype(bf16)
    back = slot(far, slice(half, rows)).astype(bf16)
    forth = lax.ppermute(forth, "pts", onward).astype(f32)
    back = lax.ppermute(back, "pts", backward).astype(f32)
    forth = jnp.pad(forth, ((0, half), (0, 0)))
    back = jnp.pad(back, ((half, 0), (0, 0)))
    for j in range(1, far):
        forth = lax.ppermute((forth + slot(far + j)).astype(bf16), "pts", onward).astype(f32)
        back = lax.ppermute((back + slot(far - j)).astype(bf16), "pts", backward).astype(f32)
    return centre + slot(0) + forth + back


def sum_everywhere(x):
    devices = lax.axis_size(BOTH)
    shares = x.reshape(devices, x.shape[0] // devices, x.shape[1])
    parts = lax.all_to_all(shares, BOTH, split_axis=0, concat_axis=0, tiled=True)
    return everyone(jnp.sum(parts, axis=0)).reshape(x.shape)


def weight_grad(diff, own, dz, dz_sum):
    first = jnp.dot(
        own.astype(f32).T, dz_sum, precision=lax.Precision.HIGHEST, preferred_element_type=f32
    )
    second = jnp.einsum("kgc,kgd->cd", diff, dz, preferred_element_type=f32)
    return jnp.concatenate([first, second], axis=0)


def per_device(
    points,
    lengths,
    neighbours_one,
    neighbours_two,
    weight_one,
    gain_one,
    shift_one,
    weight_two,
    gain_two,
    shift_two,
    cotangent,
):
    line_devices = lax.axis_size("pts")
    row_count = points.shape[0]
    line_length = line_devices * row_count
    table_one = line_table(points)

    cloud_ends = jnp.cumsum(lengths)
    cloud_starts = cloud_ends - lengths
    line_first = lax.axis_index("loc") * line_length
    position = (
        line_first + lax.axis_index("pts") * row_count + jnp.arange(row_count, dtype=jnp.int32)
    )
    begins = (position[:, None] >= cloud_starts[None, :]) & (position[:, None] < cloud_ends[None, :])
    begin = jnp.sum(jnp.where(begins, cloud_starts[None, :], 0), axis=1) - line_first
    here = ring_place(lax.axis_index("pts"), line_devices)

    def slot_rows(neighbours):
        within = neighbours.T + begin[None, :]
        slot = (here - ring_place(within // row_count, line_devices)) % line_devices
        return slot * row_count + within % row_count

    index_one = slot_rows(neighbours_one)
    index_two = slot_rows(neighbours_two)
    same_one = same_target(index_one)
    same_two = same_target(index_two)

    diff_one, stat_one = edge_stats(gather_rows(index_one, table_one), points, weight_one)
    stat_one = everyone(stat_one)
    act_one, slope_one, slope_sum, slope_moment = pool(
        diff_one, points, weight_one, stat_one, gain_one, shift_one
    )
    table_two = line_table(act_one)
    diff_two, stat_two = edge_stats(gather_rows(index_two, table_two), act_one, weight_two)
    stat_two = everyone(stat_two)
    act_two, slope_two, sums_two = pool(
        diff_two, act_one, weight_two, stat_two, gain_two, shift_two, cotangent
    )
    sums_two = everyone(sums_two)
    dz_two, dz_sum_two, centre_two, spread_two = edge_grads(
        slope_two,
        None,
        diff_two,
        act_one,
        weight_two,
        stat_two,
        gain_two,
        shift_two,
        sums_two,
        same_two,
        False,
    )
    line_two = scatter_grads(index_two, spread_two, line_length)
    line_two, dz_two, dz_sum_two = lax.optimization_barrier((line_two, dz_two, dz_sum_two))
    weight_part_two = weight_grad(diff_two, act_one, dz_two, dz_sum_two)
    grad_first = owners_sum(line_two, centre_two)
    sums_one = jnp.stack(
        [jnp.sum(grad_first * slope_sum, axis=0), jnp.sum(grad_first * slope_moment, axis=0)]
    )
    sums_one = everyone(sums_one)
    _, _, centre_one, spread_one, weight_part_one = edge_grads(
        slope_one,
        grad_first,
        diff_one,
        points,
        weight_one,
        stat_one,
        gain_one,
        shift_one,
        sums_one,
        same_one,
        True,
    )
    parts = jnp.concatenate([weight_part_two.reshape(-1, LANES), weight_part_one], axis=0)
    parts = sum_everywhere(parts)
    grad_weight_two = parts[: -weight_one.shape[0]].reshape(weight_two.shape)
    grad_weight_one = parts[-weight_one.shape[0] :]
    line_one = scatter_grads(index_one, spread_one, line_length)
    grad_points = owners_sum(line_one, centre_one)

    def norm_grads(sums, gain, shift):
        sums = jnp.sum(sums, axis=0)
        return (2.0 * sums[1] - shift * sums[0]) / gain, sums[0]

    grad_gain_one, grad_shift_one = norm_grads(sums_one, gain_one, shift_one)
    grad_gain_two, grad_shift_two = norm_grads(sums_two, gain_two, shift_two)
    return (
        act_one,
        act_two,
        grad_points,
        grad_weight_one,
        grad_gain_one,
        grad_shift_one,
        grad_weight_two,
        grad_gain_two,
        grad_shift_two,
    )


def solution(mesh):
    rows, copied = P(("pts", "loc"), None), P()
    in_specs = (rows, copied, rows, rows) + (copied,) * 6 + (rows,)
    out_specs = (rows, rows, rows) + (copied,) * 6
    return jax.shard_map(
        per_device, mesh=mesh, in_specs=in_specs, out_specs=out_specs, check_vma=False
    )
```

```python
import functools
import math

import jax
import jax.numpy as jnp
from jax import lax
from jax.experimental import pallas as pl
from jax.experimental.pallas import tpu as pltpu
from jax.sharding import PartitionSpec as P

EPS = 1e-05
BLOCK = 128
GROUP = 8
LANES = 128
MIB = 1024 * 1024
BOTH = ("pts", "loc")

f32 = jnp.float32
bf16 = jnp.bfloat16


def params():
    return pltpu.CompilerParams(vmem_limit_bytes=52 * MIB)


def lasting(microseconds):
    return pl.CostEstimate(flops=0, transcendentals=0, bytes_accessed=3_000_000 * microseconds)


def smem():
    return pl.BlockSpec(memory_space=pltpu.SMEM)


def fold_rows(x):
    return jnp.sum(x.reshape(x.shape[0] // 8, 8, x.shape[1]), axis=0)


def dot(a, b):
    return jnp.dot(a, b, preferred_element_type=f32)


def dot_t(a, b):
    return lax.dot_general(a, b, (((1,), (1,)), ((), ())), preferred_element_type=f32)


def edge_kernel(pieces, *refs):
    table_refs = refs[1 : 1 + pieces]
    idx_ref = refs[0]
    own_ref, w_ref, diff_ref, stat_ref, table, fresh, held, centre, pivot, sums, square = refs[
        1 + pieces :
    ]
    near, block, c = diff_ref.shape
    step_id = pl.program_id(0)
    last = pl.num_programs(0) - 1
    chunk = 4

    def project(own_sum, diff_sum):
        weight = w_ref[...].astype(f32)
        exact = functools.partial(
            jnp.dot, precision=lax.Precision.HIGHEST, preferred_element_type=f32
        )
        both = exact(own_sum, weight[:c]) + exact(diff_sum, weight[c:])
        return jnp.sum(both, axis=0, keepdims=True)

    @pl.when(step_id == 0)
    def _():
        first = 0
        for piece in table_refs:
            for r in range(0, piece.shape[0], 256):
                table[pl.ds(first + r, 256), :c] = piece[pl.ds(r, 256), :].astype(f32)
            first += piece.shape[0]
        sums[...] = jnp.zeros_like(sums)
        square[...] = jnp.zeros_like(square)

    @pl.when(step_id > 0)
    def _():
        for r in range(0, near * block, 256):
            held[pl.ds(r, 256), :] = fresh[pl.ds(r, 256), :]

    @pl.when(step_id == 1)
    def _():
        own = own_ref[...].astype(f32)
        diff_sum = jnp.zeros((8, c), f32)
        for k in range(near):
            diff_sum = diff_sum + fold_rows(held[pl.ds(k * block, block), :c] - own)
        own_sum = fold_rows(own) * float(near)
        pivot[...] = project(own_sum, diff_sum) * (1.0 / (near * block))

    def pick(k):
        base = pl.multiple_of(k * block, block)
        at = step_id * near + k
        for g in range(0, block, GROUP):
            rows = [table[pl.ds(idx_ref[at, g + j], 1), :] for j in range(GROUP)]
            for j in range(GROUP):
                fresh[pl.ds(base + (g + j), 1), :] = rows[j]

    def work(k, own, carry):
        diff_sum, total = carry
        at = pl.ds(pl.multiple_of(k * block, block), block)
        diff = (held[at, :c] - own).astype(bf16)
        diff_ref[k] = diff
        diff_sum = diff_sum + fold_rows(diff.astype(f32))
        z = dot(diff, w_ref[c:, :]) + centre[...]
        return diff_sum, total + fold_rows(z * z)

    @pl.when(step_id == 0)
    def _():
        def body(i, _):
            pick(i)
            return 0

        lax.fori_loop(0, near, body, 0)

    def finish(own, carry):
        sums[0] += fold_rows(own) * float(near)
        sums[1] += carry[0]
        square[...] += carry[1]

    def begin():
        centre[...] = dot(own_ref[...], w_ref[:c, :]) - pivot[...]
        zero = (jnp.zeros((8, c), f32), jnp.zeros_like(square[...]))
        return own_ref[...].astype(f32), zero

    @pl.when((step_id > 0) & (step_id < last))
    def _():
        own, zero = begin()

        def body(i, carry):
            for k in range(chunk):
                pick(i * chunk + k)
                carry = work(i * chunk + k, own_ref[...].astype(f32), carry)
            return carry

        finish(own, lax.fori_loop(0, near // chunk, body, zero))

    @pl.when(step_id == last)
    def _():
        own, carry = begin()
        for k in range(near):
            carry = work(k, own, carry)
        finish(own, carry)
        count = float(near * block * (pl.num_programs(0) - 1))
        mean = project(sums[0], sums[1]) / count
        off = mean - pivot[...]
        stat_ref[0:1, :] = mean
        stat_ref[1:2, :] = jnp.sum(square[...], axis=0, keepdims=True) - count * off * off


def edge_stats(index, pieces, own, weight):
    rows, c = own.shape
    d = weight.shape[1]
    blocks = rows // BLOCK
    near = index.shape[0] // blocks
    total = sum(piece.shape[0] for piece in pieces)
    before = lambda b: jnp.maximum(b - 1, 0)
    whole = lambda x: pl.BlockSpec(x.shape, lambda b: (0,) * x.ndim)
    return pl.pallas_call(
        functools.partial(edge_kernel, len(pieces)),
        grid=(blocks + 1,),
        out_shape=(
            jax.ShapeDtypeStruct((near, rows, c), bf16),
            jax.ShapeDtypeStruct((2, d), f32),
        ),
        in_specs=[smem()]
        + [whole(piece) for piece in pieces]
        + [pl.BlockSpec((BLOCK, c), lambda b: (before(b), 0)), whole(weight)],
        out_specs=(
            pl.BlockSpec((near, BLOCK, c), lambda b: (0, before(b), 0)),
            pl.BlockSpec((2, d), lambda b: (0, 0)),
        ),
        scratch_shapes=[
            pltpu.VMEM((total, LANES), f32),
            pltpu.VMEM((near * BLOCK, LANES), f32),
            pltpu.VMEM((near * BLOCK, LANES), f32),
            pltpu.VMEM((BLOCK, d), f32),
            pltpu.VMEM((1, d), f32),
            pltpu.VMEM((2, 8, c), f32),
            pltpu.VMEM((8, d), f32),
        ],
        compiler_params=params(),
        cost_estimate=lasting(22),
        name="edge_stats",
    )(index, *pieces, own, weight)


def moments(stat, edges_each):
    devices = stat.shape[0]
    means = stat[:, 0, :]
    mean = jnp.sum(means, axis=0, keepdims=True) * (1.0 / devices)
    off = means - mean
    m2 = jnp.sum(stat[:, 1, :], axis=0, keepdims=True) + edges_each * jnp.sum(
        off * off, axis=0, keepdims=True
    )
    return mean, lax.rsqrt(m2 * (1.0 / (edges_each * devices)) + EPS)


def pool_kernel(
    last, edges_each, diff_ref, own_ref, w_ref, stat_ref, gain_ref, shift_ref, *refs
):
    near, block, c = diff_ref.shape
    d = w_ref.shape[1]
    if last:
        cot_ref, pooled_ref, slope_ref, sums_ref, mixed, centre, upstream = refs
        upstream[...] = cot_ref[...].astype(f32)
    else:
        pooled_ref, slope_ref, sum_ref, moment_ref, mixed, centre = refs
    mean, inv = moments(stat_ref[...], edges_each)
    half_scale = gain_ref[...] * inv * 0.5
    centre[...] = (dot(own_ref[...], w_ref[:c, :]) - mean) * half_scale + shift_ref[...] * 0.5
    mixed[...] = dot(diff_ref[...].reshape(near * block, c), w_ref[c:, :]).reshape(near, block, d)
    if last:

        @pl.when(pl.program_id(0) == 0)
        def _():
            sums_ref[...] = jnp.zeros_like(sums_ref)

    for lane in range(0, d, 128):
        lanes = pl.ds(lane, 128)
        scale = jnp.broadcast_to(half_scale[:, lane : lane + 128], (8, 128))

        def step(b, carry, lanes=lanes, scale=scale):
            at = pl.ds(pl.multiple_of(b * 8, 8), 8)
            offset = centre[at, lanes]
            one_plus, active, halves = [], [], []
            for k in range(near):
                half = mixed[k, at, lanes] * scale + offset
                t = 1.0 + jnp.tanh(half)
                one_plus.append(t)
                halves.append(half)
                active.append(half * t)
            top = functools.reduce(jnp.maximum, active)
            powers = [jnp.exp(a - top) for a in active]
            total = functools.reduce(jnp.add, powers)
            pooled = top + jnp.log(total) - math.log(near)
            centre[at, lanes] = pooled
            factor = 0.5 / total
            if last:
                factor = factor * upstream[at, lanes]
            slope_sum = jnp.zeros((8, 128), f32)
            slope_moment = jnp.zeros((8, 128), f32)
            for k in range(near):
                slope = (powers[k] * factor) * (
                    one_plus[k] * ((halves[k] + halves[k] + 1.0) - active[k])
                )
                slope_ref[k, at, lanes] = slope
                slope_sum = slope_sum + slope
                slope_moment = slope_moment + slope * halves[k]
            if not last:
                sum_ref[at, lanes] = slope_sum
                moment_ref[at, lanes] = slope_moment
                return carry
            return (carry[0] + slope_sum, carry[1] + slope_moment)

        zero = jnp.zeros((8, 128), f32)
        carry = lax.fori_loop(0, block // 8, step, (zero, zero))
        if last:
            sums_ref[0:1, lanes] += jnp.sum(carry[0], axis=0, keepdims=True)
            sums_ref[1:2, lanes] += jnp.sum(carry[1], axis=0, keepdims=True)
    pooled_ref[...] = centre[...].astype(bf16)


def pool(diff, own, weight, stat, gain, shift, cot=None):
    near, rows, c = diff.shape
    d = weight.shape[1]
    whole = lambda x: pl.BlockSpec(x.shape, lambda b: (0,) * x.ndim)
    by_block = lambda width: pl.BlockSpec((BLOCK, width), lambda b: (b, 0))
    by_edge = lambda width: pl.BlockSpec((near, BLOCK, width), lambda b: (0, b, 0))
    gain, shift = gain.reshape(1, d), shift.reshape(1, d)
    inputs = [diff, own, weight, stat, gain, shift]
    in_specs = [by_edge(c), by_block(c), whole(weight), whole(stat), whole(gain), whole(shift)]
    row_out = lambda kind: (jax.ShapeDtypeStruct((rows, d), kind), by_block(d))
    outs = [row_out(bf16), (jax.ShapeDtypeStruct((near, rows, d), f32), by_edge(d))]
    if cot is None:
        outs += [row_out(f32), row_out(f32)]
    else:
        inputs.append(cot)
        in_specs.append(by_block(d))
        outs.append((jax.ShapeDtypeStruct((2, d), f32), pl.BlockSpec((2, d), lambda b: (0, 0))))
    return pl.pallas_call(
        functools.partial(pool_kernel, cot is not None, float(near * rows)),
        grid=(rows // BLOCK,),
        out_shape=tuple(o[0] for o in outs),
        in_specs=in_specs,
        out_specs=tuple(o[1] for o in outs),
        scratch_shapes=[pltpu.VMEM((near, BLOCK, d), f32)]
        + [pltpu.VMEM((BLOCK, d), f32)] * (1 if cot is None else 2),
        compiler_params=params(),
        cost_estimate=lasting(17 if cot is None else 32),
        name="pool",
    )(*inputs)


def grads_kernel(
    edges_each,
    with_weight,
    idx_ref,
    slope_ref,
    upstream_ref,
    diff_ref,
    own_ref,
    w_ref,
    back_ref,
    stat_ref,
    gain_ref,
    shift_ref,
    grads_ref,
    same_ref,
    zero_ref,
    *refs,
):
    near, block, c = diff_ref.shape
    d = w_ref.shape[1]
    if with_weight:
        centre_ref, line_ref, weight_ref, dz_ref = refs[:4]
    else:
        centre_ref, line_ref, dz_ref, all_sum_ref = refs[:4]
    dz_sum, factor, constant, fresh, held, even, odd, sems = refs[4:]
    step_id = pl.program_id(0)
    last = pl.num_programs(0) - 1
    chunk = 512 // d
    edges = edges_each * stat_ref.shape[0]
    mean, inv = moments(stat_ref[...], edges_each)
    gain = gain_ref[...]
    sums = jnp.sum(grads_ref[...], axis=0)
    grad_shift = sums[0:1]
    grad_gain = (2.0 * sums[1:2] - shift_ref[...] * grad_shift) / gain
    alpha = gain * inv
    rate = alpha * inv * grad_gain * (1.0 / edges)

    def zero_copies():
        piece = zero_ref.shape[0]
        pieces = even.shape[0] // piece
        return [
            pltpu.make_async_copy(
                zero_ref, line.at[pl.ds(i * piece, piece)], sems.at[half * pieces + i]
            )
            for half, line in enumerate((even, odd))
            for i in range(pieces)
        ]

    def begin():
        if upstream_ref is None:
            factor[...] = jnp.broadcast_to(alpha, factor.shape)
        else:
            factor[...] = upstream_ref[...] * alpha
        constant[...] = alpha * grad_shift * (1.0 / edges) + rate * (
            dot(own_ref[...], w_ref[:c, :]) - mean
        )
        dz_sum[...] = jnp.zeros_like(dz_sum)

    def work(i):
        ks = pl.ds(i * chunk, chunk)
        mixed = dot(diff_ref[ks].reshape(chunk * block, c), w_ref[c:, :])
        dzs = []
        total = dz_sum[...]
        for k in range(chunk):
            dz = (
                factor[...] * slope_ref[i * chunk + k]
                - constant[...]
                - rate * mixed[k * block : (k + 1) * block]
            ).astype(bf16)
            dz_ref[i * chunk + k] = dz
            total = total + dz.astype(f32)
            dzs.append(dz)
        dz_sum[...] = total
        back = dot_t(jnp.concatenate(dzs, axis=0), back_ref[...]).astype(bf16)
        for k in range(chunk):
            at = pl.ds(pl.multiple_of((i * chunk + k) * block, block), block)
            fresh[at, :] = dot(same_ref[i * chunk + k], back[k * block : (k + 1) * block])

    def finish():
        weight = w_ref[...].astype(f32)
        centre_ref[...] = lax.dot_general(
            dz_sum[...],
            weight[:c] - weight[c:],
            (((1,), (1,)), ((), ())),
            precision=lax.Precision.HIGHEST,
            preferred_element_type=f32,
        )
        if not with_weight:
            all_sum_ref[...] = dz_sum[...]
            return
        weight_ref[:c, :] += lax.dot_general(
            own_ref[...].astype(f32),
            dz_sum[...],
            (((0,), (0,)), ((), ())),
            precision=lax.Precision.HIGHEST,
            preferred_element_type=f32,
        )
        weight_ref[c:, :] += lax.dot_general(
            diff_ref[...].reshape(near * block, c),
            dz_ref[...].reshape(near * block, d),
            (((0,), (0,)), ((), ())),
            preferred_element_type=f32,
        )

    def add(i):
        for k in range(chunk):
            at = (step_id - 1) * near + i * chunk + k
            base = pl.multiple_of((i * chunk + k) * block, block)
            for g in range(0, block, GROUP):
                line = (even, odd)[g // GROUP % 2]
                new = [
                    line[pl.ds(idx_ref[at, g + j], 1), :] + held[pl.ds(base + (g + j), 1), :]
                    for j in range(GROUP)
                ]
                for j in range(GROUP):
                    line[pl.ds(idx_ref[at, g + j], 1), :] = new[j]

    @pl.when(step_id > 0)
    def _():
        for r in range(0, near * block, 256):
            held[pl.ds(r, 256), :] = fresh[pl.ds(r, 256), :]

    @pl.when(step_id == 0)
    def _():
        copies = zero_copies()
        for copy in copies:
            copy.start()
        if with_weight:
            weight_ref[...] = jnp.zeros_like(weight_ref)
        begin()

        def body(i, _):
            work(i)
            return 0

        lax.fori_loop(0, near // chunk, body, 0)
        finish()
        for copy in copies:
            copy.wait()

    @pl.when((step_id > 0) & (step_id < last))
    def _():
        begin()

        def body(i, _):
            add(i)
            work(i)
            return 0

        lax.fori_loop(0, near // chunk, body, 0)
        finish()

    @pl.when(step_id == last)
    def _():
        def body(i, _):
            add(i)
            return 0

        lax.fori_loop(0, near // chunk, body, 0)
        copies = [
            pltpu.make_async_copy(line, line_ref.at[half], sems.at[half])
            for half, line in enumerate((even, odd))
        ]
        for copy in copies:
            copy.start()
        for copy in copies:
            copy.wait()


def edge_grads(index, slope, upstream, diff, own, weight, stat, gain, shift, grads, same, total):
    near, rows, c = diff.shape
    d = weight.shape[1]
    blocks = rows // BLOCK
    with_weight = upstream is not None
    now = lambda b: jnp.minimum(b, blocks - 1)
    whole = lambda x: pl.BlockSpec(x.shape, lambda b: (0,) * x.ndim)
    by_block = lambda width: pl.BlockSpec((BLOCK, width), lambda b: (now(b), 0))
    by_edge = lambda width: pl.BlockSpec((near, BLOCK, width), lambda b: (0, now(b), 0))
    anywhere = pl.BlockSpec(memory_space=pl.ANY)
    gain, shift = gain.reshape(1, d), shift.reshape(1, d)
    back = jnp.pad(weight[c:], ((0, LANES - c), (0, 0)))
    zero = jnp.zeros((rows, LANES), f32)
    inputs = [index, slope, upstream, diff, own, weight, back, stat, gain, shift, grads, same, zero]
    in_specs = [
        smem(),
        by_edge(d),
        by_block(d),
        by_edge(c),
        by_block(c),
        whole(weight),
        whole(back),
        whole(stat),
        whole(gain),
        whole(shift),
        whole(grads),
        by_edge(BLOCK),
        anywhere,
    ]
    body = functools.partial(grads_kernel, float(near * rows), with_weight)
    outs = [
        (jax.ShapeDtypeStruct((rows, c), f32), by_block(c)),
        (jax.ShapeDtypeStruct((2, total, LANES), f32), anywhere),
    ]
    scratch = [
        pltpu.VMEM((BLOCK, d), f32),
        pltpu.VMEM((BLOCK, d), f32),
        pltpu.VMEM((BLOCK, d), f32),
        pltpu.VMEM((near * BLOCK, LANES), f32),
        pltpu.VMEM((near * BLOCK, LANES), f32),
        pltpu.VMEM((total, LANES), f32),
        pltpu.VMEM((total, LANES), f32),
        pltpu.SemaphoreType.DMA((2 * total // rows,)),
    ]
    if with_weight:
        outs.append((jax.ShapeDtypeStruct((2 * c, d), f32), whole(weight)))
        scratch.insert(0, pltpu.VMEM((near, BLOCK, d), bf16))
    else:
        del inputs[2], in_specs[2]
        inner = body
        body = lambda i, s, *rest: inner(i, s, None, *rest)
        outs.append((jax.ShapeDtypeStruct((near, rows, d), bf16), by_edge(d)))
        outs.append((jax.ShapeDtypeStruct((rows, d), f32), by_block(d)))
    result = pl.pallas_call(
        body,
        grid=(blocks + 1,),
        out_shape=tuple(o[0] for o in outs),
        in_specs=in_specs,
        out_specs=tuple(o[1] for o in outs),
        scratch_shapes=scratch,
        compiler_params=params(),
        cost_estimate=lasting(36),
        name="edge_grads",
    )(*inputs)
    return (result[0], result[1].reshape(2, total // rows, rows, LANES)) + tuple(result[2:])


def same_target(index):
    near, rows = index.shape
    blocks = index.reshape(near, rows // BLOCK, BLOCK)
    group = jnp.arange(BLOCK, dtype=jnp.int32) // GROUP
    equal = (blocks[:, :, :, None] == blocks[:, :, None, :]) & (group[:, None] == group[None, :])
    return equal.astype(bf16).reshape(near, rows, BLOCK)


def everyone(x):
    devices = lax.axis_size(BOTH)
    copies = jnp.broadcast_to(x[None], (devices,) + x.shape)
    return lax.all_to_all(copies, BOTH, split_axis=0, concat_axis=0, tiled=True)


def ring_moves(places):
    ring = list(range(0, places, 2)) + list(range(1, places, 2))[::-1]
    onward = [(ring[i], ring[(i + 1) % places]) for i in range(places)]
    return onward, [(b, a) for a, b in onward]


def ring_place(device, places):
    return jnp.where(device % 2 == 0, device // 2, places - 1 - device // 2)


def line_table(values):
    places = lax.axis_size("pts")
    onward, backward = ring_moves(places)
    rows, far = values.shape[0] // 2, places // 2
    behind, ahead = [values], [values]
    for _ in range(far - 1):
        behind.append(lax.ppermute(behind[-1], "pts", onward))
        ahead.append(lax.ppermute(ahead[-1], "pts", backward))
    farthest = [
        lax.ppermute(behind[-1][:rows], "pts", onward),
        lax.ppermute(ahead[-1][rows:], "pts", backward),
    ]
    return behind + farthest + ahead[:0:-1]


def owners_sum(halves, centre):
    places = lax.axis_size("pts")
    onward, backward = ring_moves(places)
    rows, c = centre.shape
    half, far = rows // 2, places // 2
    slot = lambda j, at=slice(None): halves[0, j, at, :c] + halves[1, j, at, :c]
    forth = slot(far, slice(0, half)).astype(bf16)
    back = slot(far, slice(half, rows)).astype(bf16)
    forth = lax.ppermute(forth, "pts", onward).astype(f32)
    back = lax.ppermute(back, "pts", backward).astype(f32)
    forth = jnp.pad(forth, ((0, half), (0, 0)))
    back = jnp.pad(back, ((half, 0), (0, 0)))
    for j in range(1, far):
        forth = lax.ppermute((forth + slot(far + j)).astype(bf16), "pts", onward).astype(f32)
        back = lax.ppermute((back + slot(far - j)).astype(bf16), "pts", backward).astype(f32)
    return centre + slot(0) + forth + back


def sum_everywhere(x):
    devices = lax.axis_size(BOTH)
    shares = x.reshape(devices, x.shape[0] // devices, x.shape[1])
    parts = lax.all_to_all(shares, BOTH, split_axis=0, concat_axis=0, tiled=True)
    return everyone(jnp.sum(parts, axis=0)).reshape(x.shape)


def weight_grad(diff, own, dz, dz_sum):
    first = jnp.dot(
        own.astype(f32).T, dz_sum, precision=lax.Precision.HIGHEST, preferred_element_type=f32
    )
    second = jnp.einsum("kgc,kgd->cd", diff, dz, preferred_element_type=f32)
    return jnp.concatenate([first, second], axis=0)


def per_device(
    points,
    lengths,
    neighbours_one,
    neighbours_two,
    weight_one,
    gain_one,
    shift_one,
    weight_two,
    gain_two,
    shift_two,
    cotangent,
):
    line_devices = lax.axis_size("pts")
    row_count = points.shape[0]
    line_length = line_devices * row_count
    table_one = line_table(points)

    cloud_ends = jnp.cumsum(lengths)
    cloud_starts = cloud_ends - lengths
    line_first = lax.axis_index("loc") * line_length
    position = (
        line_first + lax.axis_index("pts") * row_count + jnp.arange(row_count, dtype=jnp.int32)
    )
    begins = (position[:, None] >= cloud_starts[None, :]) & (position[:, None] < cloud_ends[None, :])
    begin = jnp.sum(jnp.where(begins, cloud_starts[None, :], 0), axis=1) - line_first
    here = ring_place(lax.axis_index("pts"), line_devices)

    def slot_rows(neighbours):
        within = neighbours.T + begin[None, :]
        slot = (here - ring_place(within // row_count, line_devices)) % line_devices
        return slot * row_count + within % row_count

    def by_blocks(index):
        blocks = index.reshape(index.shape[0], -1, BLOCK)
        return blocks.transpose(1, 0, 2).reshape(-1, BLOCK)

    index_one = slot_rows(neighbours_one)
    index_two = slot_rows(neighbours_two)
    order_one, order_two = by_blocks(index_one), by_blocks(index_two)
    same_one = same_target(index_one)
    same_two = same_target(index_two)

    diff_one, stat_one = edge_stats(order_one, table_one, points, weight_one)
    stat_one = everyone(stat_one)
    act_one, slope_one, slope_sum, slope_moment = pool(
        diff_one, points, weight_one, stat_one, gain_one, shift_one
    )
    table_two = line_table(act_one)
    diff_two, stat_two = edge_stats(order_two, table_two, act_one, weight_two)
    stat_two = everyone(stat_two)
    act_two, slope_two, sums_two = pool(
        diff_two, act_one, weight_two, stat_two, gain_two, shift_two, cotangent
    )
    sums_two = everyone(sums_two)
    centre_two, line_two, dz_two, dz_sum_two = edge_grads(
        order_two,
        slope_two,
        None,
        diff_two,
        act_one,
        weight_two,
        stat_two,
        gain_two,
        shift_two,
        sums_two,
        same_two,
        line_length,
    )
    grad_first = owners_sum(line_two, centre_two)
    sums_one = jnp.stack(
        [jnp.sum(grad_first * slope_sum, axis=0), jnp.sum(grad_first * slope_moment, axis=0)]
    )
    sums_one = everyone(sums_one)
    weight_part_two = weight_grad(diff_two, act_one, dz_two, dz_sum_two)
    centre_one, line_one, weight_part_one = edge_grads(
        order_one,
        slope_one,
        grad_first,
        diff_one,
        points,
        weight_one,
        stat_one,
        gain_one,
        shift_one,
        sums_one,
        same_one,
        line_length,
    )
    parts = jnp.concatenate([weight_part_two.reshape(-1, LANES), weight_part_one], axis=0)
    parts = sum_everywhere(parts)
    grad_weight_two = parts[: -weight_one.shape[0]].reshape(weight_two.shape)
    grad_weight_one = parts[-weight_one.shape[0] :]
    grad_points = owners_sum(line_one, centre_one)

    def norm_grads(sums, gain, shift):
        sums = jnp.sum(sums, axis=0)
        return (2.0 * sums[1] - shift * sums[0]) / gain, sums[0]

    grad_gain_one, grad_shift_one = norm_grads(sums_one, gain_one, shift_one)
    grad_gain_two, grad_shift_two = norm_grads(sums_two, gain_two, shift_two)
    return (
        act_one,
        act_two,
        grad_points,
        grad_weight_one,
        grad_gain_one,
        grad_shift_one,
        grad_weight_two,
        grad_gain_two,
        grad_shift_two,
    )


def solution(mesh):
    rows, copied = P(("pts", "loc"), None), P()
    in_specs = (rows, copied, rows, rows) + (copied,) * 6 + (rows,)
    out_specs = (rows, rows, rows) + (copied,) * 6
    return jax.shard_map(
        per_device, mesh=mesh, in_specs=in_specs, out_specs=out_specs, check_vma=False
    )
```

```python
import functools
import math

import jax
import jax.numpy as jnp
from jax import lax
from jax.experimental import pallas as pl
from jax.experimental.pallas import tpu as pltpu
from jax.sharding import PartitionSpec as P

EPS = 1e-05
BLOCK = 128
GROUP = 8
ROWS = 16
LANES = 128
MIB = 1024 * 1024
BOTH = ("pts", "loc")

f32 = jnp.float32
bf16 = jnp.bfloat16


def params():
    return pltpu.CompilerParams(vmem_limit_bytes=52 * MIB)


def lasting(microseconds):
    return pl.CostEstimate(flops=0, transcendentals=0, bytes_accessed=3_000_000 * microseconds)


def smem():
    return pl.BlockSpec(memory_space=pltpu.SMEM)


def fold_rows(x):
    return jnp.sum(x.reshape(x.shape[0] // 8, 8, x.shape[1]), axis=0)


def tree(op, terms):
    while len(terms) > 1:
        pairs = [op(a, b) for a, b in zip(terms[::2], terms[1::2])]
        terms = pairs + terms[len(pairs) * 2 :]
    return terms[0]


def dot(a, b):
    return jnp.dot(a, b, preferred_element_type=f32)


def dot_t(a, b):
    return lax.dot_general(a, b, (((1,), (1,)), ((), ())), preferred_element_type=f32)


def edge_kernel(pieces, *refs):
    table_refs = refs[1 : 1 + pieces]
    idx_ref = refs[0]
    own_ref, w_ref, diff_ref, stat_ref, table, fresh, held, centre, pivot, sums, square = refs[
        1 + pieces :
    ]
    near, block, c = diff_ref.shape
    step_id = pl.program_id(0)
    last = pl.num_programs(0) - 1
    chunk = 4

    def project(own_sum, diff_sum):
        weight = w_ref[...].astype(f32)
        exact = functools.partial(
            jnp.dot, precision=lax.Precision.HIGHEST, preferred_element_type=f32
        )
        both = exact(own_sum, weight[:c]) + exact(diff_sum, weight[c:])
        return jnp.sum(both, axis=0, keepdims=True)

    @pl.when(step_id == 0)
    def _():
        first = 0
        for piece in table_refs:
            for r in range(0, piece.shape[0], 256):
                table[pl.ds(first + r, 256), :c] = piece[pl.ds(r, 256), :].astype(f32)
            first += piece.shape[0]
        sums[...] = jnp.zeros_like(sums)
        square[...] = jnp.zeros_like(square)

    @pl.when(step_id > 0)
    def _():
        for r in range(0, near * block, 256):
            held[pl.ds(r, 256), :] = fresh[pl.ds(r, 256), :]

    @pl.when(step_id == 1)
    def _():
        own = own_ref[...].astype(f32)
        diff_sum = jnp.zeros((8, c), f32)
        for k in range(near):
            diff_sum = diff_sum + fold_rows(held[pl.ds(k * block, block), :c] - own)
        own_sum = fold_rows(own) * float(near)
        pivot[...] = project(own_sum, diff_sum) * (1.0 / (near * block))

    def pick(k):
        base = pl.multiple_of(k * block, block)
        at = step_id * near + k
        ready = None
        for g in range(0, block + GROUP, GROUP):
            rows = None
            if g < block:
                rows = [table[pl.ds(idx_ref[at, g + j], 1), :] for j in range(GROUP)]
            if ready is not None:
                for j in range(GROUP):
                    fresh[pl.ds(base + (g - GROUP + j), 1), :] = ready[j]
            ready = rows

    def work(k, own, carry):
        diff_sum, total = carry
        at = pl.ds(pl.multiple_of(k * block, block), block)
        diff = (held[at, :c] - own).astype(bf16)
        diff_ref[k] = diff
        diff_sum = diff_sum + fold_rows(diff.astype(f32))
        z = dot(diff, w_ref[c:, :]) + centre[...]
        return diff_sum, total + fold_rows(z * z)

    @pl.when(step_id == 0)
    def _():
        def body(i, _):
            pick(i)
            return 0

        lax.fori_loop(0, near, body, 0)

    def finish(own, carry):
        sums[0] += fold_rows(own) * float(near)
        sums[1] += carry[0]
        square[...] += carry[1]

    def begin():
        centre[...] = dot(own_ref[...], w_ref[:c, :]) - pivot[...]
        zero = (jnp.zeros((8, c), f32), jnp.zeros_like(square[...]))
        return own_ref[...].astype(f32), zero

    @pl.when((step_id > 0) & (step_id < last))
    def _():
        own, zero = begin()

        def body(i, carry):
            for k in range(chunk):
                pick(i * chunk + k)
                carry = work(i * chunk + k, own_ref[...].astype(f32), carry)
            return carry

        finish(own, lax.fori_loop(0, near // chunk, body, zero))

    @pl.when(step_id == last)
    def _():
        own, carry = begin()
        for k in range(near):
            carry = work(k, own, carry)
        finish(own, carry)
        count = float(near * block * (pl.num_programs(0) - 1))
        mean = project(sums[0], sums[1]) / count
        off = mean - pivot[...]
        stat_ref[0:1, :] = mean
        stat_ref[1:2, :] = jnp.sum(square[...], axis=0, keepdims=True) - count * off * off


def edge_stats(index, pieces, own, weight):
    rows, c = own.shape
    d = weight.shape[1]
    blocks = rows // BLOCK
    near = index.shape[0] // blocks
    total = sum(piece.shape[0] for piece in pieces)
    before = lambda b: jnp.maximum(b - 1, 0)
    whole = lambda x: pl.BlockSpec(x.shape, lambda b: (0,) * x.ndim)
    return pl.pallas_call(
        functools.partial(edge_kernel, len(pieces)),
        grid=(blocks + 1,),
        out_shape=(
            jax.ShapeDtypeStruct((near, rows, c), bf16),
            jax.ShapeDtypeStruct((2, d), f32),
        ),
        in_specs=[smem()]
        + [whole(piece) for piece in pieces]
        + [pl.BlockSpec((BLOCK, c), lambda b: (before(b), 0)), whole(weight)],
        out_specs=(
            pl.BlockSpec((near, BLOCK, c), lambda b: (0, before(b), 0)),
            pl.BlockSpec((2, d), lambda b: (0, 0)),
        ),
        scratch_shapes=[
            pltpu.VMEM((total, LANES), f32),
            pltpu.VMEM((near * BLOCK, LANES), f32),
            pltpu.VMEM((near * BLOCK, LANES), f32),
            pltpu.VMEM((BLOCK, d), f32),
            pltpu.VMEM((1, d), f32),
            pltpu.VMEM((2, 8, c), f32),
            pltpu.VMEM((8, d), f32),
        ],
        compiler_params=params(),
        cost_estimate=lasting(22),
        name="edge_stats",
    )(index, *pieces, own, weight)


def moments(stat, edges_each):
    devices = stat.shape[0]
    means = stat[:, 0, :]
    mean = jnp.sum(means, axis=0, keepdims=True) * (1.0 / devices)
    off = means - mean
    m2 = jnp.sum(stat[:, 1, :], axis=0, keepdims=True) + edges_each * jnp.sum(
        off * off, axis=0, keepdims=True
    )
    return mean, lax.rsqrt(m2 * (1.0 / (edges_each * devices)) + EPS)


def pool_kernel(
    last, edges_each, diff_ref, own_ref, w_ref, stat_ref, gain_ref, shift_ref, *refs
):
    near, block, c = diff_ref.shape
    d = w_ref.shape[1]
    if last:
        cot_ref, pooled_ref, slope_ref, sums_ref, mixed, centre, upstream = refs
        upstream[...] = cot_ref[...].astype(f32)
    else:
        pooled_ref, slope_ref, sum_ref, moment_ref, mixed, centre = refs
    mean, inv = moments(stat_ref[...], edges_each)
    half_scale = gain_ref[...] * inv * 0.5
    centre[...] = (dot(own_ref[...], w_ref[:c, :]) - mean) * half_scale + shift_ref[...] * 0.5
    mixed[...] = dot(diff_ref[...].reshape(near * block, c), w_ref[c:, :]).reshape(near, block, d)
    if last:

        @pl.when(pl.program_id(0) == 0)
        def _():
            sums_ref[...] = jnp.zeros_like(sums_ref)

    for lane in range(0, d, 128):
        lanes = pl.ds(lane, 128)
        scale = jnp.broadcast_to(half_scale[:, lane : lane + 128], (ROWS, 128))

        def step(b, carry, lanes=lanes, scale=scale):
            at = pl.ds(pl.multiple_of(b * ROWS, ROWS), ROWS)
            offset = centre[at, lanes]
            one_plus, active, halves = [], [], []
            for k in range(near):
                half = mixed[k, at, lanes] * scale + offset
                t = 1.0 + jnp.tanh(half)
                one_plus.append(t)
                halves.append(half)
                active.append(half * t)
            top = tree(jnp.maximum, active)
            powers = [jnp.exp(a - top) for a in active]
            total = tree(jnp.add, powers)
            pooled = top + jnp.log(total) - math.log(near)
            centre[at, lanes] = pooled
            factor = 0.5 / total
            if last:
                factor = factor * upstream[at, lanes]
            slopes = [
                (powers[k] * factor)
                * (one_plus[k] * ((halves[k] + halves[k] + 1.0) - active[k]))
                for k in range(near)
            ]
            for k in range(near):
                slope_ref[k, at, lanes] = slopes[k]
            slope_sum = tree(jnp.add, slopes)
            slope_moment = tree(jnp.add, [slopes[k] * halves[k] for k in range(near)])
            if not last:
                sum_ref[at, lanes] = slope_sum
                moment_ref[at, lanes] = slope_moment
                return carry
            return (carry[0] + slope_sum, carry[1] + slope_moment)

        zero = jnp.zeros((ROWS, 128), f32)
        carry = lax.fori_loop(0, block // ROWS, step, (zero, zero))
        if last:
            sums_ref[0:1, lanes] += jnp.sum(carry[0], axis=0, keepdims=True)
            sums_ref[1:2, lanes] += jnp.sum(carry[1], axis=0, keepdims=True)
    pooled_ref[...] = centre[...].astype(bf16)


def pool(diff, own, weight, stat, gain, shift, cot=None):
    near, rows, c = diff.shape
    d = weight.shape[1]
    whole = lambda x: pl.BlockSpec(x.shape, lambda b: (0,) * x.ndim)
    by_block = lambda width: pl.BlockSpec((BLOCK, width), lambda b: (b, 0))
    by_edge = lambda width: pl.BlockSpec((near, BLOCK, width), lambda b: (0, b, 0))
    gain, shift = gain.reshape(1, d), shift.reshape(1, d)
    inputs = [diff, own, weight, stat, gain, shift]
    in_specs = [by_edge(c), by_block(c), whole(weight), whole(stat), whole(gain), whole(shift)]
    row_out = lambda kind: (jax.ShapeDtypeStruct((rows, d), kind), by_block(d))
    outs = [row_out(bf16), (jax.ShapeDtypeStruct((near, rows, d), f32), by_edge(d))]
    if cot is None:
        outs += [row_out(f32), row_out(f32)]
    else:
        inputs.append(cot)
        in_specs.append(by_block(d))
        outs.append((jax.ShapeDtypeStruct((2, d), f32), pl.BlockSpec((2, d), lambda b: (0, 0))))
    return pl.pallas_call(
        functools.partial(pool_kernel, cot is not None, float(near * rows)),
        grid=(rows // BLOCK,),
        out_shape=tuple(o[0] for o in outs),
        in_specs=in_specs,
        out_specs=tuple(o[1] for o in outs),
        scratch_shapes=[pltpu.VMEM((near, BLOCK, d), f32)]
        + [pltpu.VMEM((BLOCK, d), f32)] * (1 if cot is None else 2),
        compiler_params=params(),
        cost_estimate=lasting(17 if cot is None else 32),
        name="pool",
    )(*inputs)


def grads_kernel(
    edges_each,
    with_weight,
    slope_ref,
    upstream_ref,
    diff_ref,
    own_ref,
    w_ref,
    back_ref,
    stat_ref,
    gain_ref,
    shift_ref,
    grads_ref,
    same_ref,
    dz_ref,
    dz_sum_ref,
    centre_ref,
    spread_ref,
    *refs,
):
    near, block, c = diff_ref.shape
    d = w_ref.shape[1]
    mixed, constant = refs[-2:]
    edges = edges_each * stat_ref.shape[0]
    mean, inv = moments(stat_ref[...], edges_each)
    gain = gain_ref[...]
    sums = jnp.sum(grads_ref[...], axis=0)
    grad_shift = sums[0:1]
    grad_gain = (2.0 * sums[1:2] - shift_ref[...] * grad_shift) / gain
    alpha = gain * inv
    rate = alpha * inv * grad_gain * (1.0 / edges)
    constant[...] = alpha * grad_shift * (1.0 / edges) + rate * (
        dot(own_ref[...], w_ref[:c, :]) - mean
    )
    mixed[...] = dot(diff_ref[...].reshape(near * block, c), w_ref[c:, :]).reshape(near, block, d)

    for lane in range(0, d, 128):
        lanes = pl.ds(lane, 128)
        wide_alpha = jnp.broadcast_to(alpha[:, lane : lane + 128], (16, 128))
        wide_rate = jnp.broadcast_to(rate[:, lane : lane + 128], (16, 128))

        def step(b, _, lanes=lanes, wide_alpha=wide_alpha, wide_rate=wide_rate):
            at = pl.ds(pl.multiple_of(b * 16, 16), 16)
            offset = constant[at, lanes]
            factor = wide_alpha
            if upstream_ref is not None:
                factor = factor * upstream_ref[at, lanes]
            dz_sum = jnp.zeros((16, 128), f32)
            for k in range(near):
                dz = (
                    factor * slope_ref[k, at, lanes] - offset - wide_rate * mixed[k, at, lanes]
                ).astype(bf16)
                dz_ref[k, at, lanes] = dz
                dz_sum = dz_sum + dz.astype(f32)
            dz_sum_ref[at, lanes] = dz_sum
            return 0

        lax.fori_loop(0, block // 16, step, 0)

    weight = w_ref[...].astype(f32)
    centre_ref[...] = lax.dot_general(
        dz_sum_ref[...],
        weight[:c] - weight[c:],
        (((1,), (1,)), ((), ())),
        precision=lax.Precision.HIGHEST,
        preferred_element_type=f32,
    )
    flat = dz_ref[...].reshape(near * block, d)
    back = dot_t(flat, back_ref[...]).astype(bf16).reshape(near, block, LANES)
    for k in range(near):
        spread_ref[k] = dot(same_ref[k], back[k])
    if with_weight:
        weight_ref = refs[0]

        @pl.when(pl.program_id(0) == 0)
        def _():
            weight_ref[...] = jnp.zeros_like(weight_ref)

        weight_ref[:c, :] += lax.dot_general(
            own_ref[...].astype(f32),
            dz_sum_ref[...],
            (((0,), (0,)), ((), ())),
            precision=lax.Precision.HIGHEST,
            preferred_element_type=f32,
        )
        weight_ref[c:, :] += lax.dot_general(
            diff_ref[...].reshape(near * block, c),
            flat,
            (((0,), (0,)), ((), ())),
            preferred_element_type=f32,
        )


def edge_grads(slope, upstream, diff, own, weight, stat, gain, shift, grads, same, with_weight):
    near, rows, c = diff.shape
    d = weight.shape[1]
    whole = lambda x: pl.BlockSpec(x.shape, lambda b: (0,) * x.ndim)
    by_block = lambda width: pl.BlockSpec((BLOCK, width), lambda b: (b, 0))
    by_edge = lambda width: pl.BlockSpec((near, BLOCK, width), lambda b: (0, b, 0))
    gain, shift = gain.reshape(1, d), shift.reshape(1, d)
    back = jnp.pad(weight[c:], ((0, LANES - c), (0, 0)))
    inputs = [slope, upstream, diff, own, weight, back, stat, gain, shift, grads, same]
    in_specs = [
        by_edge(d),
        by_block(d),
        by_edge(c),
        by_block(c),
        whole(weight),
        whole(back),
        whole(stat),
        whole(gain),
        whole(shift),
        whole(grads),
        by_edge(BLOCK),
    ]
    body = functools.partial(grads_kernel, float(near * rows), with_weight)
    if upstream is None:
        del inputs[1], in_specs[1]
        inner = body
        body = lambda s, *rest: inner(s, None, *rest)
    outs = [
        (jax.ShapeDtypeStruct((near, rows, d), bf16), by_edge(d)),
        (jax.ShapeDtypeStruct((rows, d), f32), by_block(d)),
        (jax.ShapeDtypeStruct((rows, c), f32), by_block(c)),
        (jax.ShapeDtypeStruct((near, rows, LANES), f32), by_edge(LANES)),
    ]
    if with_weight:
        outs.append((jax.ShapeDtypeStruct((2 * c, d), f32), whole(weight)))
    return pl.pallas_call(
        body,
        grid=(rows // BLOCK,),
        out_shape=tuple(o[0] for o in outs),
        in_specs=in_specs,
        out_specs=tuple(o[1] for o in outs),
        scratch_shapes=[pltpu.VMEM((near, BLOCK, d), f32), pltpu.VMEM((BLOCK, d), f32)],
        compiler_params=params(),
        cost_estimate=lasting(22),
        name="edge_grads",
    )(*inputs)


def scatter_kernel(idx_ref, spread_ref, zero_ref, out_ref, even, odd, sems):
    k = pl.program_id(0)
    lines = spread_ref.shape[0] // LANES
    piece = zero_ref.shape[0]
    pieces = even.shape[0] // piece

    @pl.when(k == 0)
    def _():
        copies = [
            pltpu.make_async_copy(
                zero_ref, line.at[pl.ds(i * piece, piece)], sems.at[half * pieces + i]
            )
            for half, line in enumerate((even, odd))
            for i in range(pieces)
        ]
        for copy in copies:
            copy.start()
        for copy in copies:
            copy.wait()

    def step(b, _):
        at = k * lines + b
        base = b * LANES
        def store(line, places, rows):
            for place, row in zip(places, rows):
                line[place] = row

        ready = None
        for g in range(0, LANES, GROUP):
            line = (even, odd)[g // GROUP % 2]
            places = [idx_ref[at, g + j] for j in range(GROUP)]
            rows = [line[places[j]] + spread_ref[base + (g + j)] for j in range(GROUP)]
            if ready is not None:
                store(*ready)
            ready = (line, places, rows)
        store(*ready)
        return 0

    lax.fori_loop(0, lines, step, 0)

    @pl.when(k == pl.num_programs(0) - 1)
    def _():
        copies = [
            pltpu.make_async_copy(line, out_ref.at[half], sems.at[half])
            for half, line in enumerate((even, odd))
        ]
        for copy in copies:
            copy.start()
        for copy in copies:
            copy.wait()


def scatter_grads(index, spread, total):
    near, rows = index.shape
    spread = spread.reshape(near * rows, 1, LANES)
    return pl.pallas_call(
        scatter_kernel,
        grid=(near,),
        out_shape=jax.ShapeDtypeStruct((2, total, 1, LANES), f32),
        in_specs=[
            smem(),
            pl.BlockSpec((rows, 1, LANES), lambda k: (k, 0, 0)),
            pl.BlockSpec(memory_space=pl.ANY),
        ],
        out_specs=pl.BlockSpec(memory_space=pl.ANY),
        scratch_shapes=[pltpu.VMEM((total, 1, LANES), f32)] * 2
        + [pltpu.SemaphoreType.DMA((2 * total // rows,))],
        compiler_params=params(),
        cost_estimate=lasting(25),
        name="scatter_grads",
    )(index.reshape(-1, LANES), spread, jnp.zeros((rows, 1, LANES), f32)).reshape(
        2, total // rows, rows, LANES
    )


def same_target(index):
    near, rows = index.shape
    blocks = index.reshape(near, rows // BLOCK, BLOCK)
    group = jnp.arange(BLOCK, dtype=jnp.int32) // GROUP
    equal = (blocks[:, :, :, None] == blocks[:, :, None, :]) & (group[:, None] == group[None, :])
    return equal.astype(bf16).reshape(near, rows, BLOCK)


def copies(x):
    return jnp.broadcast_to(x[None], (lax.axis_size(BOTH),) + x.shape)


def shared(x):
    devices = lax.axis_size(BOTH)
    return x.reshape(devices, x.shape[0] // devices, x.shape[1])


def exchange(shares):
    return lax.all_to_all(shares, BOTH, split_axis=0, concat_axis=0, tiled=True)


def everyone(x):
    return exchange(copies(x))


def meet(x):
    return jnp.sum(exchange(shared(x)), axis=0)


def ring_moves(places):
    ring = list(range(0, places, 2)) + list(range(1, places, 2))[::-1]
    onward = [(ring[i], ring[(i + 1) % places]) for i in range(places)]
    return onward, [(b, a) for a, b in onward]


def ring_place(device, places):
    return jnp.where(device % 2 == 0, device // 2, places - 1 - device // 2)


def line_table(values):
    places = lax.axis_size("pts")
    onward, backward = ring_moves(places)
    rows, far = values.shape[0] // 2, places // 2
    behind, ahead = [values], [values]
    for _ in range(far - 1):
        behind.append(lax.ppermute(behind[-1], "pts", onward))
        ahead.append(lax.ppermute(ahead[-1], "pts", backward))
    farthest = [
        lax.ppermute(behind[-1][:rows], "pts", onward),
        lax.ppermute(ahead[-1][rows:], "pts", backward),
    ]
    return behind + farthest + ahead[:0:-1]


def owners_sum(halves, centre):
    places = lax.axis_size("pts")
    onward, backward = ring_moves(places)
    rows, c = centre.shape
    half, far = rows // 2, places // 2
    slot = lambda j, at=slice(None): halves[0, j, at, :c] + halves[1, j, at, :c]
    forth = slot(far, slice(0, half)).astype(bf16)
    back = slot(far, slice(half, rows)).astype(bf16)
    forth = lax.ppermute(forth, "pts", onward).astype(f32)
    back = lax.ppermute(back, "pts", backward).astype(f32)
    forth = jnp.pad(forth, ((0, half), (0, 0)))
    back = jnp.pad(back, ((half, 0), (0, 0)))
    for j in range(1, far):
        forth = lax.ppermute((forth + slot(far + j)).astype(bf16), "pts", onward).astype(f32)
        back = lax.ppermute((back + slot(far - j)).astype(bf16), "pts", backward).astype(f32)
    return centre + slot(0) + forth + back


def weight_grad(diff, own, dz, dz_sum):
    first = jnp.dot(
        own.astype(f32).T, dz_sum, precision=lax.Precision.HIGHEST, preferred_element_type=f32
    )
    second = jnp.einsum("kgc,kgd->cd", diff, dz, preferred_element_type=f32)
    return jnp.concatenate([first, second], axis=0)


def per_device(
    points,
    lengths,
    neighbours_one,
    neighbours_two,
    weight_one,
    gain_one,
    shift_one,
    weight_two,
    gain_two,
    shift_two,
    cotangent,
):
    line_devices = lax.axis_size("pts")
    row_count = points.shape[0]
    line_length = line_devices * row_count
    table_one = line_table(points)

    cloud_ends = jnp.cumsum(lengths)
    cloud_starts = cloud_ends - lengths
    line_first = lax.axis_index("loc") * line_length
    position = (
        line_first + lax.axis_index("pts") * row_count + jnp.arange(row_count, dtype=jnp.int32)
    )
    begins = (position[:, None] >= cloud_starts[None, :]) & (position[:, None] < cloud_ends[None, :])
    begin = jnp.sum(jnp.where(begins, cloud_starts[None, :], 0), axis=1) - line_first
    here = ring_place(lax.axis_index("pts"), line_devices)

    def slot_rows(neighbours):
        within = neighbours.T + begin[None, :]
        slot = (here - ring_place(within // row_count, line_devices)) % line_devices
        return slot * row_count + within % row_count

    def by_blocks(index):
        blocks = index.reshape(index.shape[0], -1, BLOCK)
        return blocks.transpose(1, 0, 2).reshape(-1, BLOCK)

    index_one = slot_rows(neighbours_one)
    index_two = slot_rows(neighbours_two)
    order_one, order_two = by_blocks(index_one), by_blocks(index_two)
    same_one = same_target(index_one)
    same_two = same_target(index_two)

    diff_one, stat_one = edge_stats(order_one, table_one, points, weight_one)
    stat_one = everyone(stat_one)
    act_one, slope_one, slope_sum, slope_moment = pool(
        diff_one, points, weight_one, stat_one, gain_one, shift_one
    )
    table_two = line_table(act_one)
    diff_two, stat_two = edge_stats(order_two, table_two, act_one, weight_two)
    stat_two = everyone(stat_two)
    act_two, slope_two, sums_two = pool(
        diff_two, act_one, weight_two, stat_two, gain_two, shift_two, cotangent
    )
    sums_two = everyone(sums_two)
    dz_two, dz_sum_two, centre_two, spread_two = edge_grads(
        slope_two,
        None,
        diff_two,
        act_one,
        weight_two,
        stat_two,
        gain_two,
        shift_two,
        sums_two,
        same_two,
        False,
    )
    line_two = scatter_grads(index_two, spread_two, line_length)
    line_two, dz_two, dz_sum_two = lax.optimization_barrier((line_two, dz_two, dz_sum_two))
    weight_part_two = weight_grad(diff_two, act_one, dz_two, dz_sum_two)
    grad_first = owners_sum(line_two, centre_two)
    sums_one = jnp.stack(
        [jnp.sum(grad_first * slope_sum, axis=0), jnp.sum(grad_first * slope_moment, axis=0)]
    )
    sums_one = everyone(sums_one)
    parts_two = meet(weight_part_two.reshape(-1, LANES))
    _, _, centre_one, spread_one, weight_part_one = edge_grads(
        slope_one,
        grad_first,
        diff_one,
        points,
        weight_one,
        stat_one,
        gain_one,
        shift_one,
        sums_one,
        same_one,
        True,
    )
    shares = jnp.concatenate([copies(parts_two), shared(weight_part_one)], axis=1)
    shares = exchange(shares)
    grad_weight_two = shares[:, : parts_two.shape[0]].reshape(weight_two.shape)
    parts_one = jnp.sum(shares[:, parts_two.shape[0] :], axis=0)
    line_one = scatter_grads(index_one, spread_one, line_length)
    grad_weight_one = everyone(parts_one).reshape(weight_one.shape)
    grad_points = owners_sum(line_one, centre_one)

    def norm_grads(sums, gain, shift):
        sums = jnp.sum(sums, axis=0)
        return (2.0 * sums[1] - shift * sums[0]) / gain, sums[0]

    grad_gain_one, grad_shift_one = norm_grads(sums_one, gain_one, shift_one)
    grad_gain_two, grad_shift_two = norm_grads(sums_two, gain_two, shift_two)
    return (
        act_one,
        act_two,
        grad_points,
        grad_weight_one,
        grad_gain_one,
        grad_shift_one,
        grad_weight_two,
        grad_gain_two,
        grad_shift_two,
    )


def solution(mesh):
    rows, copied = P(("pts", "loc"), None), P()
    in_specs = (rows, copied, rows, rows) + (copied,) * 6 + (rows,)
    out_specs = (rows, rows, rows) + (copied,) * 6
    return jax.shard_map(
        per_device, mesh=mesh, in_specs=in_specs, out_specs=out_specs, check_vma=False
    )
```

```python
import functools
import math

import jax
import jax.numpy as jnp
from jax import lax
from jax.experimental import pallas as pl
from jax.experimental.pallas import tpu as pltpu
from jax.sharding import PartitionSpec as P

EPS = 1e-05
BLOCK = 128
GROUP = 8
ROWS = 32
CHUNK = 5
LANES = 128
MIB = 1024 * 1024
BOTH = ("pts", "loc")

f32 = jnp.float32
bf16 = jnp.bfloat16


def params():
    return pltpu.CompilerParams(vmem_limit_bytes=52 * MIB)


def lasting(microseconds):
    return pl.CostEstimate(flops=0, transcendentals=0, bytes_accessed=3_000_000 * microseconds)


def smem():
    return pl.BlockSpec(memory_space=pltpu.SMEM)


def fold_rows(x):
    return jnp.sum(x.reshape(x.shape[0] // 8, 8, x.shape[1]), axis=0)


def tree(op, terms):
    while len(terms) > 1:
        pairs = [op(a, b) for a, b in zip(terms[::2], terms[1::2])]
        terms = pairs + terms[len(pairs) * 2 :]
    return terms[0]


def dot(a, b):
    return jnp.dot(a, b, preferred_element_type=f32)


def dot_t(a, b):
    return lax.dot_general(a, b, (((1,), (1,)), ((), ())), preferred_element_type=f32)


def edge_kernel(pieces, *refs):
    table_refs = refs[1 : 1 + pieces]
    idx_ref = refs[0]
    own_ref, w_ref, diff_ref, stat_ref, table, fresh, held, centre, pivot, sums, square = refs[
        1 + pieces :
    ]
    near, block, c = diff_ref.shape
    step_id = pl.program_id(0)
    last = pl.num_programs(0) - 1
    chunk = 4

    def project(own_sum, diff_sum):
        weight = w_ref[...].astype(f32)
        exact = functools.partial(
            jnp.dot, precision=lax.Precision.HIGHEST, preferred_element_type=f32
        )
        both = exact(own_sum, weight[:c]) + exact(diff_sum, weight[c:])
        return jnp.sum(both, axis=0, keepdims=True)

    @pl.when(step_id == 0)
    def _():
        first = 0
        for piece in table_refs:
            for r in range(0, piece.shape[0], 256):
                table[pl.ds(first + r, 256), :c] = piece[pl.ds(r, 256), :].astype(f32)
            first += piece.shape[0]
        sums[...] = jnp.zeros_like(sums)
        square[...] = jnp.zeros_like(square)

    @pl.when(step_id > 0)
    def _():
        for r in range(0, near * block, 256):
            held[pl.ds(r, 256), :] = fresh[pl.ds(r, 256), :]

    @pl.when(step_id == 1)
    def _():
        own = own_ref[...].astype(f32)
        diff_sum = jnp.zeros((8, c), f32)
        for k in range(near):
            diff_sum = diff_sum + fold_rows(held[pl.ds(k * block, block), :c] - own)
        own_sum = fold_rows(own) * float(near)
        pivot[...] = project(own_sum, diff_sum) * (1.0 / (near * block))

    def pick(k):
        base = pl.multiple_of(k * block, block)
        at = step_id * near + k
        ready = None
        for g in range(0, block + GROUP, GROUP):
            rows = None
            if g < block:
                rows = [table[pl.ds(idx_ref[at, g + j], 1), :] for j in range(GROUP)]
            if ready is not None:
                for j in range(GROUP):
                    fresh[pl.ds(base + (g - GROUP + j), 1), :] = ready[j]
            ready = rows

    def work(k, own, carry):
        diff_sum, total = carry
        at = pl.ds(pl.multiple_of(k * block, block), block)
        diff = (held[at, :c] - own).astype(bf16)
        diff_ref[k] = diff
        diff_sum = diff_sum + fold_rows(diff.astype(f32))
        z = dot(diff, w_ref[c:, :]) + centre[...]
        return diff_sum, total + fold_rows(z * z)

    @pl.when(step_id == 0)
    def _():
        def body(i, _):
            pick(i)
            return 0

        lax.fori_loop(0, near, body, 0)

    def finish(own, carry):
        sums[0] += fold_rows(own) * float(near)
        sums[1] += carry[0]
        square[...] += carry[1]

    def begin():
        centre[...] = dot(own_ref[...], w_ref[:c, :]) - pivot[...]
        zero = (jnp.zeros((8, c), f32), jnp.zeros_like(square[...]))
        return own_ref[...].astype(f32), zero

    @pl.when((step_id > 0) & (step_id < last))
    def _():
        own, zero = begin()

        def body(i, carry):
            for k in range(chunk):
                pick(i * chunk + k)
                carry = work(i * chunk + k, own_ref[...].astype(f32), carry)
            return carry

        finish(own, lax.fori_loop(0, near // chunk, body, zero))

    @pl.when(step_id == last)
    def _():
        own, carry = begin()
        for k in range(near):
            carry = work(k, own, carry)
        finish(own, carry)
        count = float(near * block * (pl.num_programs(0) - 1))
        mean = project(sums[0], sums[1]) / count
        off = mean - pivot[...]
        stat_ref[0:1, :] = mean
        stat_ref[1:2, :] = jnp.sum(square[...], axis=0, keepdims=True) - count * off * off


def edge_stats(index, pieces, own, weight):
    rows, c = own.shape
    d = weight.shape[1]
    blocks = rows // BLOCK
    near = index.shape[0] // blocks
    total = sum(piece.shape[0] for piece in pieces)
    before = lambda b: jnp.maximum(b - 1, 0)
    whole = lambda x: pl.BlockSpec(x.shape, lambda b: (0,) * x.ndim)
    return pl.pallas_call(
        functools.partial(edge_kernel, len(pieces)),
        grid=(blocks + 1,),
        out_shape=(
            jax.ShapeDtypeStruct((near, rows, c), bf16),
            jax.ShapeDtypeStruct((2, d), f32),
        ),
        in_specs=[smem()]
        + [whole(piece) for piece in pieces]
        + [pl.BlockSpec((BLOCK, c), lambda b: (before(b), 0)), whole(weight)],
        out_specs=(
            pl.BlockSpec((near, BLOCK, c), lambda b: (0, before(b), 0)),
            pl.BlockSpec((2, d), lambda b: (0, 0)),
        ),
        scratch_shapes=[
            pltpu.VMEM((total, LANES), f32),
            pltpu.VMEM((near * BLOCK, LANES), f32),
            pltpu.VMEM((near * BLOCK, LANES), f32),
            pltpu.VMEM((BLOCK, d), f32),
            pltpu.VMEM((1, d), f32),
            pltpu.VMEM((2, 8, c), f32),
            pltpu.VMEM((8, d), f32),
        ],
        compiler_params=params(),
        cost_estimate=lasting(22),
        name="edge_stats",
    )(index, *pieces, own, weight)


def moments(stat, edges_each):
    devices = stat.shape[0]
    means = stat[:, 0, :]
    mean = jnp.sum(means, axis=0, keepdims=True) * (1.0 / devices)
    off = means - mean
    m2 = jnp.sum(stat[:, 1, :], axis=0, keepdims=True) + edges_each * jnp.sum(
        off * off, axis=0, keepdims=True
    )
    return mean, lax.rsqrt(m2 * (1.0 / (edges_each * devices)) + EPS)


def pool_kernel(
    last, edges_each, diff_ref, own_ref, w_ref, stat_ref, gain_ref, shift_ref, *refs
):
    near, block, c = diff_ref.shape
    d = w_ref.shape[1]
    if last:
        cot_ref, pooled_ref, slope_ref, sums_ref, mixed, centre, upstream = refs
        upstream[...] = cot_ref[...].astype(f32)
    else:
        pooled_ref, slope_ref, sum_ref, moment_ref, mixed, centre = refs
    mean, inv = moments(stat_ref[...], edges_each)
    half_scale = gain_ref[...] * inv * 0.5
    centre[...] = (dot(own_ref[...], w_ref[:c, :]) - mean) * half_scale + shift_ref[...] * 0.5
    mixed[...] = dot(diff_ref[...].reshape(near * block, c), w_ref[c:, :]).reshape(near, block, d)
    if last:

        @pl.when(pl.program_id(0) == 0)
        def _():
            sums_ref[...] = jnp.zeros_like(sums_ref)

    for lane in range(0, d, 128):
        lanes = pl.ds(lane, 128)
        scale = jnp.broadcast_to(half_scale[:, lane : lane + 128], (ROWS, 128))

        def step(b, carry, lanes=lanes, scale=scale):
            at = pl.ds(pl.multiple_of(b * ROWS, ROWS), ROWS)
            offset = centre[at, lanes]
            one_plus, active, halves = [], [], []
            for k in range(near):
                half = mixed[k, at, lanes] * scale + offset
                t = 1.0 + jnp.tanh(half)
                one_plus.append(t)
                halves.append(half)
                active.append(half * t)
            top = tree(jnp.maximum, active)
            powers = [jnp.exp(a - top) for a in active]
            total = tree(jnp.add, powers)
            pooled = top + jnp.log(total) - math.log(near)
            centre[at, lanes] = pooled
            factor = 0.5 / total
            if last:
                factor = factor * upstream[at, lanes]
            slopes = [
                (powers[k] * factor)
                * (one_plus[k] * ((halves[k] + halves[k] + 1.0) - active[k]))
                for k in range(near)
            ]
            for k in range(near):
                slope_ref[k, at, lanes] = slopes[k]
            slope_sum = tree(jnp.add, slopes)
            slope_moment = tree(jnp.add, [slopes[k] * halves[k] for k in range(near)])
            if not last:
                sum_ref[at, lanes] = slope_sum
                moment_ref[at, lanes] = slope_moment
                return carry
            return (carry[0] + slope_sum, carry[1] + slope_moment)

        zero = jnp.zeros((ROWS, 128), f32)
        carry = lax.fori_loop(0, block // ROWS, step, (zero, zero))
        if last:
            sums_ref[0:1, lanes] += jnp.sum(carry[0], axis=0, keepdims=True)
            sums_ref[1:2, lanes] += jnp.sum(carry[1], axis=0, keepdims=True)
    pooled_ref[...] = centre[...].astype(bf16)


def pool(diff, own, weight, stat, gain, shift, cot=None):
    near, rows, c = diff.shape
    d = weight.shape[1]
    whole = lambda x: pl.BlockSpec(x.shape, lambda b: (0,) * x.ndim)
    by_block = lambda width: pl.BlockSpec((BLOCK, width), lambda b: (b, 0))
    by_edge = lambda width: pl.BlockSpec((near, BLOCK, width), lambda b: (0, b, 0))
    gain, shift = gain.reshape(1, d), shift.reshape(1, d)
    inputs = [diff, own, weight, stat, gain, shift]
    in_specs = [by_edge(c), by_block(c), whole(weight), whole(stat), whole(gain), whole(shift)]
    row_out = lambda kind: (jax.ShapeDtypeStruct((rows, d), kind), by_block(d))
    outs = [row_out(bf16), (jax.ShapeDtypeStruct((near, rows, d), f32), by_edge(d))]
    if cot is None:
        outs += [row_out(f32), row_out(f32)]
    else:
        inputs.append(cot)
        in_specs.append(by_block(d))
        outs.append((jax.ShapeDtypeStruct((2, d), f32), pl.BlockSpec((2, d), lambda b: (0, 0))))
    return pl.pallas_call(
        functools.partial(pool_kernel, cot is not None, float(near * rows)),
        grid=(rows // BLOCK,),
        out_shape=tuple(o[0] for o in outs),
        in_specs=in_specs,
        out_specs=tuple(o[1] for o in outs),
        scratch_shapes=[pltpu.VMEM((near, BLOCK, d), f32)]
        + [pltpu.VMEM((BLOCK, d), f32)] * (1 if cot is None else 2),
        compiler_params=params(),
        cost_estimate=lasting(17 if cot is None else 32),
        name="pool",
    )(*inputs)


def grads_kernel(
    edges_each,
    idx_ref,
    slope_ref,
    upstream_ref,
    diff_ref,
    own_ref,
    w_ref,
    back_ref,
    stat_ref,
    gain_ref,
    shift_ref,
    grads_ref,
    same_ref,
    zero_ref,
    centre_ref,
    weight_ref,
    line_ref,
    dz_sum,
    factor,
    constant,
    weight_sum,
    fresh,
    held,
    even,
    odd,
    sems,
):
    near, block, c = diff_ref.shape
    d = w_ref.shape[1]
    step_id = pl.program_id(0)
    last = pl.num_programs(0) - 1
    total = even.shape[0]

    def zero_copies():
        piece = zero_ref.shape[0]
        pieces = total // piece
        return [
            pltpu.make_async_copy(
                zero_ref, line.at[pl.ds(i * piece, piece)], sems.at[half * pieces + i]
            )
            for half, line in enumerate((even, odd))
            for i in range(pieces)
        ]

    def add(k, ready):
        at = (step_id - 1) * near + k
        base = pl.multiple_of(k * block, block)
        for g in range(0, block, GROUP):
            line = (even, odd)[g // GROUP % 2]
            places = [pl.ds(idx_ref[at, g + j], 1) for j in range(GROUP)]
            rows = [line[places[j], :] + held[pl.ds(base + (g + j), 1), :] for j in range(GROUP)]
            store(ready)
            ready = (line, places, rows)
        return ready

    def store(ready):
        if ready is not None:
            line, places, rows = ready
            for place, row in zip(places, rows):
                line[place, :] = row

    def work(adding):
        edges = edges_each * stat_ref.shape[0]
        mean, inv = moments(stat_ref[...], edges_each)
        gain = gain_ref[...]
        sums = jnp.sum(grads_ref[...], axis=0)
        grad_shift = sums[0:1]
        grad_gain = (2.0 * sums[1:2] - shift_ref[...] * grad_shift) / gain
        alpha = gain * inv
        rate = alpha * inv * grad_gain * (1.0 / edges)
        if upstream_ref is None:
            factor[...] = jnp.broadcast_to(alpha, factor.shape)
        else:
            factor[...] = upstream_ref[...] * alpha
        constant[...] = alpha * grad_shift * (1.0 / edges) + rate * (
            dot(own_ref[...], w_ref[:c, :]) - mean
        )
        dz_sum[...] = jnp.zeros_like(dz_sum)
        weight_sum[...] = jnp.zeros_like(weight_sum)

        def part(i, _):
            first = i * CHUNK
            mixed, dzs, backs = {}, {}, {}
            ready = None
            for k in range(CHUNK + 3):
                if adding and k < CHUNK:
                    ready = add(first + k, ready)
                if k < CHUNK:
                    mixed[k] = dot(diff_ref[first + k], w_ref[c:, :])
                p = k - 1
                if 0 <= p < CHUNK:
                    dzs[p] = (
                        factor[...] * slope_ref[first + p] - constant[...] - rate * mixed.pop(p)
                    ).astype(bf16)
                    dz_sum[...] += dzs[p].astype(f32)
                p = k - 2
                if 0 <= p < CHUNK:
                    dz = dzs.pop(p)
                    backs[p] = dot_t(dz, back_ref[...]).astype(bf16)
                    weight_sum[...] += lax.dot_general(
                        diff_ref[first + p],
                        dz,
                        (((0,), (0,)), ((), ())),
                        preferred_element_type=f32,
                    )
                p = k - 3
                if 0 <= p < CHUNK:
                    at = pl.multiple_of((first + p) * block, block)
                    fresh[pl.ds(at, block), :] = dot(same_ref[first + p], backs.pop(p))
            store(ready)
            return 0

        lax.fori_loop(0, near // CHUNK, part, 0)
        exact = functools.partial(
            lax.dot_general, precision=lax.Precision.HIGHEST, preferred_element_type=f32
        )
        wide = w_ref[...].astype(f32)
        centre_ref[...] = exact(dz_sum[...], wide[:c] - wide[c:], (((1,), (1,)), ((), ())))
        weight_ref[:c, :] += exact(own_ref[...].astype(f32), dz_sum[...], (((0,), (0,)), ((), ())))
        weight_ref[c:, :] += weight_sum[...]

    @pl.when(step_id > 0)
    def _():
        for r in range(0, near * block, 256):
            held[pl.ds(r, 256), :] = fresh[pl.ds(r, 256), :]

    @pl.when(step_id == 0)
    def _():
        copies = zero_copies()
        for copy in copies:
            copy.start()
        weight_ref[...] = jnp.zeros_like(weight_ref)
        work(False)
        for copy in copies:
            copy.wait()

    @pl.when((step_id > 0) & (step_id < last))
    def _():
        work(True)

    @pl.when(step_id == last)
    def _():
        def rest(k, _):
            store(add(k, None))
            return 0

        lax.fori_loop(0, near, rest, 0)

        def join(i, _):
            at = pl.ds(pl.multiple_of(i * 256, 256), 256)
            even[at, :] = even[at, :] + odd[at, :]
            return 0

        lax.fori_loop(0, total // 256, join, 0)
        pltpu.sync_copy(even, line_ref)


def edge_grads(index, slope, upstream, diff, own, weight, stat, gain, shift, grads, same, total):
    near, rows, c = diff.shape
    d = weight.shape[1]
    blocks = rows // BLOCK
    now = lambda b: jnp.minimum(b, blocks - 1)
    whole = lambda x: pl.BlockSpec(x.shape, lambda b: (0,) * x.ndim)
    by_block = lambda width: pl.BlockSpec((BLOCK, width), lambda b: (now(b), 0))
    by_edge = lambda width: pl.BlockSpec((near, BLOCK, width), lambda b: (0, now(b), 0))
    anywhere = pl.BlockSpec(memory_space=pl.ANY)
    gain, shift = gain.reshape(1, d), shift.reshape(1, d)
    back = jnp.pad(weight[c:], ((0, LANES - c), (0, 0)))
    zero = jnp.zeros((rows, LANES), f32)
    inputs = [index, slope, upstream, diff, own, weight, back, stat, gain, shift, grads, same, zero]
    in_specs = [
        smem(),
        by_edge(d),
        by_block(d),
        by_edge(c),
        by_block(c),
        whole(weight),
        whole(back),
        whole(stat),
        whole(gain),
        whole(shift),
        whole(grads),
        by_edge(BLOCK),
        anywhere,
    ]
    body = functools.partial(grads_kernel, float(near * rows))
    if upstream is None:
        del inputs[2], in_specs[2]
        inner = body
        body = lambda i, s, *rest: inner(i, s, None, *rest)
    return pl.pallas_call(
        body,
        grid=(blocks + 1,),
        out_shape=(
            jax.ShapeDtypeStruct((rows, c), f32),
            jax.ShapeDtypeStruct((2 * c, d), f32),
            jax.ShapeDtypeStruct((total, LANES), f32),
        ),
        in_specs=in_specs,
        out_specs=(by_block(c), whole(weight), anywhere),
        scratch_shapes=[
            pltpu.VMEM((BLOCK, d), f32),
            pltpu.VMEM((BLOCK, d), f32),
            pltpu.VMEM((BLOCK, d), f32),
            pltpu.VMEM((c, d), f32),
            pltpu.VMEM((near * BLOCK, LANES), f32),
            pltpu.VMEM((near * BLOCK, LANES), f32),
            pltpu.VMEM((total, LANES), f32),
            pltpu.VMEM((total, LANES), f32),
            pltpu.SemaphoreType.DMA((2 * total // rows,)),
        ],
        compiler_params=params(),
        cost_estimate=lasting(35),
        name="edge_grads",
    )(*inputs)


def same_target(index):
    near, rows = index.shape
    blocks = index.reshape(near, rows // BLOCK, BLOCK)
    group = jnp.arange(BLOCK, dtype=jnp.int32) // GROUP
    equal = (blocks[:, :, :, None] == blocks[:, :, None, :]) & (group[:, None] == group[None, :])
    return equal.astype(bf16).reshape(near, rows, BLOCK)


def copies(x):
    return jnp.broadcast_to(x[None], (lax.axis_size(BOTH),) + x.shape)


def shared(x):
    devices = lax.axis_size(BOTH)
    return x.reshape(devices, x.shape[0] // devices, x.shape[1])


def exchange(shares):
    return lax.all_to_all(shares, BOTH, split_axis=0, concat_axis=0, tiled=True)


def everyone(x):
    return exchange(copies(x))


def meet(x):
    return jnp.sum(exchange(shared(x)), axis=0)


def ring_moves(places):
    ring = list(range(0, places, 2)) + list(range(1, places, 2))[::-1]
    onward = [(ring[i], ring[(i + 1) % places]) for i in range(places)]
    return onward, [(b, a) for a, b in onward]


def ring_place(device, places):
    return jnp.where(device % 2 == 0, device // 2, places - 1 - device // 2)


def line_table(values):
    places = lax.axis_size("pts")
    onward, backward = ring_moves(places)
    rows, far = values.shape[0] // 2, places // 2
    behind, ahead = [values], [values]
    for _ in range(far - 1):
        behind.append(lax.ppermute(behind[-1], "pts", onward))
        ahead.append(lax.ppermute(ahead[-1], "pts", backward))
    farthest = [
        lax.ppermute(behind[-1][:rows], "pts", onward),
        lax.ppermute(ahead[-1][rows:], "pts", backward),
    ]
    return behind + farthest + ahead[:0:-1]


def owners_sum(line, centre, beside):
    places = lax.axis_size("pts")
    onward, backward = ring_moves(places)
    rows, c = centre.shape
    half, far = rows // 2, places // 2

    def slot(j, first=0, count=rows):
        return line[j * rows + first : j * rows + first + count, :c]

    forth = lax.ppermute(slot(far, 0, half).astype(bf16), "pts", onward).astype(f32)
    back = lax.ppermute(slot(far, half, half).astype(bf16), "pts", backward).astype(f32)
    forth = jnp.pad(forth, ((0, half), (0, 0)))
    back = jnp.pad(back, ((half, 0), (0, 0)))
    for j in range(1, far):
        forth, back = (forth + slot(far + j)).astype(bf16), (back + slot(far - j)).astype(bf16)
        if j == 2:
            forth, back, beside = lax.optimization_barrier((forth, back, beside))
        else:
            forth, back = lax.optimization_barrier((forth, back))
        forth = lax.ppermute(forth, "pts", onward).astype(f32)
        back = lax.ppermute(back, "pts", backward).astype(f32)
    return centre + slot(0) + forth + back, beside


def per_device(
    points,
    lengths,
    neighbours_one,
    neighbours_two,
    weight_one,
    gain_one,
    shift_one,
    weight_two,
    gain_two,
    shift_two,
    cotangent,
):
    line_devices = lax.axis_size("pts")
    row_count = points.shape[0]
    line_length = line_devices * row_count
    table_one = line_table(points)

    cloud_ends = jnp.cumsum(lengths)
    cloud_starts = cloud_ends - lengths
    line_first = lax.axis_index("loc") * line_length
    position = (
        line_first + lax.axis_index("pts") * row_count + jnp.arange(row_count, dtype=jnp.int32)
    )
    begins = (position[:, None] >= cloud_starts[None, :]) & (position[:, None] < cloud_ends[None, :])
    begin = jnp.sum(jnp.where(begins, cloud_starts[None, :], 0), axis=1) - line_first
    here = ring_place(lax.axis_index("pts"), line_devices)

    def slot_rows(neighbours):
        within = neighbours.T + begin[None, :]
        slot = (here - ring_place(within // row_count, line_devices)) % line_devices
        return slot * row_count + within % row_count

    def by_blocks(index):
        blocks = index.reshape(index.shape[0], -1, BLOCK)
        return blocks.transpose(1, 0, 2).reshape(-1, BLOCK)

    index_one = slot_rows(neighbours_one)
    index_two = slot_rows(neighbours_two)
    order_one, order_two = by_blocks(index_one), by_blocks(index_two)
    same_one = same_target(index_one)
    same_two = same_target(index_two)

    diff_one, stat_one = edge_stats(order_one, table_one, points, weight_one)
    stat_one = everyone(stat_one)
    act_one, slope_one, slope_sum, slope_moment = pool(
        diff_one, points, weight_one, stat_one, gain_one, shift_one
    )
    table_two = line_table(act_one)
    diff_two, stat_two = edge_stats(order_two, table_two, act_one, weight_two)
    stat_two = everyone(stat_two)
    act_two, slope_two, sums_two = pool(
        diff_two, act_one, weight_two, stat_two, gain_two, shift_two, cotangent
    )
    sums_two = everyone(sums_two)
    centre_two, weight_part_two, line_two = edge_grads(
        order_two,
        slope_two,
        None,
        diff_two,
        act_one,
        weight_two,
        stat_two,
        gain_two,
        shift_two,
        sums_two,
        same_two,
        line_length,
    )
    shares = shared(weight_part_two.reshape(-1, LANES))
    grad_first, shares = owners_sum(line_two, centre_two, exchange(shares))
    parts_two = jnp.sum(shares, axis=0)
    sums_one = jnp.stack(
        [jnp.sum(grad_first * slope_sum, axis=0), jnp.sum(grad_first * slope_moment, axis=0)]
    )
    sums_one = everyone(sums_one)
    centre_one, weight_part_one, line_one = edge_grads(
        order_one,
        slope_one,
        grad_first,
        diff_one,
        points,
        weight_one,
        stat_one,
        gain_one,
        shift_one,
        sums_one,
        same_one,
        line_length,
    )
    shares = jnp.concatenate([copies(parts_two), shared(weight_part_one)], axis=1)
    grad_points, shares = owners_sum(line_one, centre_one, exchange(shares))
    grad_weight_two = shares[:, : parts_two.shape[0]].reshape(weight_two.shape)
    parts_one = jnp.sum(shares[:, parts_two.shape[0] :], axis=0)
    grad_weight_one = everyone(parts_one).reshape(weight_one.shape)

    def norm_grads(sums, gain, shift):
        sums = jnp.sum(sums, axis=0)
        return (2.0 * sums[1] - shift * sums[0]) / gain, sums[0]

    grad_gain_one, grad_shift_one = norm_grads(sums_one, gain_one, shift_one)
    grad_gain_two, grad_shift_two = norm_grads(sums_two, gain_two, shift_two)
    return (
        act_one,
        act_two,
        grad_points,
        grad_weight_one,
        grad_gain_one,
        grad_shift_one,
        grad_weight_two,
        grad_gain_two,
        grad_shift_two,
    )


def solution(mesh):
    rows, copied = P(("pts", "loc"), None), P()
    in_specs = (rows, copied, rows, rows) + (copied,) * 6 + (rows,)
    out_specs = (rows, rows, rows) + (copied,) * 6
    return jax.shard_map(
        per_device, mesh=mesh, in_specs=in_specs, out_specs=out_specs, check_vma=False
    )
```

```python
import functools
import math

import jax
import jax.numpy as jnp
from jax import lax
from jax.experimental import pallas as pl
from jax.experimental.pallas import tpu as pltpu
from jax.sharding import PartitionSpec as P

EPS = 1e-05
BLOCK = 128
GROUP = 8
ROWS = 16
AHEAD = 4
LANES = 128
MIB = 1024 * 1024
BOTH = ("pts", "loc")

f32 = jnp.float32
bf16 = jnp.bfloat16


def params():
    return pltpu.CompilerParams(vmem_limit_bytes=52 * MIB)


def lasting(microseconds):
    return pl.CostEstimate(flops=0, transcendentals=0, bytes_accessed=3_000_000 * microseconds)


def smem():
    return pl.BlockSpec(memory_space=pltpu.SMEM)


def fold_rows(x):
    return jnp.sum(x.reshape(x.shape[0] // 8, 8, x.shape[1]), axis=0)


def tree(op, terms):
    while len(terms) > 1:
        pairs = [op(a, b) for a, b in zip(terms[::2], terms[1::2])]
        terms = pairs + terms[len(pairs) * 2 :]
    return terms[0]


def dot(a, b):
    return jnp.dot(a, b, preferred_element_type=f32)


def dot_t(a, b):
    return lax.dot_general(a, b, (((1,), (1,)), ((), ())), preferred_element_type=f32)


def edge_kernel(pieces, *refs):
    table_refs = refs[1 : 1 + pieces]
    idx_ref = refs[0]
    own_ref, w_ref, diff_ref, stat_ref, table, fresh, held, centre, pivot, sums, square = refs[
        1 + pieces :
    ]
    near, block, c = diff_ref.shape
    step_id = pl.program_id(0)
    last = pl.num_programs(0) - 1
    chunk = 4

    def project(own_sum, diff_sum):
        weight = w_ref[...].astype(f32)
        exact = functools.partial(
            jnp.dot, precision=lax.Precision.HIGHEST, preferred_element_type=f32
        )
        both = exact(own_sum, weight[:c]) + exact(diff_sum, weight[c:])
        return jnp.sum(both, axis=0, keepdims=True)

    @pl.when(step_id == 0)
    def _():
        first = 0
        for piece in table_refs:
            for r in range(0, piece.shape[0], 256):
                table[pl.ds(first + r, 256), :c] = piece[pl.ds(r, 256), :].astype(f32)
            first += piece.shape[0]
        sums[...] = jnp.zeros_like(sums)
        square[...] = jnp.zeros_like(square)

    @pl.when(step_id > 0)
    def _():
        for r in range(0, near * block, 256):
            held[pl.ds(r, 256), :] = fresh[pl.ds(r, 256), :]

    @pl.when(step_id == 1)
    def _():
        own = own_ref[...].astype(f32)
        diff_sum = jnp.zeros((8, c), f32)
        for k in range(near):
            diff_sum = diff_sum + fold_rows(held[pl.ds(k * block, block), :c] - own)
        own_sum = fold_rows(own) * float(near)
        pivot[...] = project(own_sum, diff_sum) * (1.0 / (near * block))

    def pick(k):
        base = pl.multiple_of(k * block, block)
        at = step_id * near + k
        rows = []
        for e in range(block + GROUP):
            if e < block:
                rows.append(table[pl.ds(idx_ref[at, e], 1), :])
            if e >= GROUP:
                fresh[pl.ds(base + (e - GROUP), 1), :] = rows[e - GROUP]

    def work(k, own, carry):
        diff_sum, total = carry
        at = pl.ds(pl.multiple_of(k * block, block), block)
        diff = (held[at, :c] - own).astype(bf16)
        diff_ref[k] = diff
        diff_sum = diff_sum + fold_rows(diff.astype(f32))
        z = dot(diff, w_ref[c:, :]) + centre[...]
        return diff_sum, total + fold_rows(z * z)

    @pl.when(step_id == 0)
    def _():
        def body(i, _):
            pick(i)
            return 0

        lax.fori_loop(0, near, body, 0)

    def finish(own, carry):
        sums[0] += fold_rows(own) * float(near)
        sums[1] += carry[0]
        square[...] += carry[1]

    def begin():
        centre[...] = dot(own_ref[...], w_ref[:c, :]) - pivot[...]
        zero = (jnp.zeros((8, c), f32), jnp.zeros_like(square[...]))
        return own_ref[...].astype(f32), zero

    @pl.when((step_id > 0) & (step_id < last))
    def _():
        own, zero = begin()

        def body(i, carry):
            for k in range(chunk):
                pick(i * chunk + k)
                carry = work(i * chunk + k, own_ref[...].astype(f32), carry)
            return carry

        finish(own, lax.fori_loop(0, near // chunk, body, zero))

    @pl.when(step_id == last)
    def _():
        own, carry = begin()
        for k in range(near):
            carry = work(k, own, carry)
        finish(own, carry)
        count = float(near * block * (pl.num_programs(0) - 1))
        mean = project(sums[0], sums[1]) / count
        off = mean - pivot[...]
        stat_ref[0:1, :] = mean
        stat_ref[1:2, :] = jnp.sum(square[...], axis=0, keepdims=True) - count * off * off


def edge_stats(index, pieces, own, weight):
    rows, c = own.shape
    d = weight.shape[1]
    blocks = rows // BLOCK
    near = index.shape[0] // blocks
    total = sum(piece.shape[0] for piece in pieces)
    before = lambda b: jnp.maximum(b - 1, 0)
    whole = lambda x: pl.BlockSpec(x.shape, lambda b: (0,) * x.ndim)
    return pl.pallas_call(
        functools.partial(edge_kernel, len(pieces)),
        grid=(blocks + 1,),
        out_shape=(
            jax.ShapeDtypeStruct((near, rows, c), bf16),
            jax.ShapeDtypeStruct((2, d), f32),
        ),
        in_specs=[smem()]
        + [whole(piece) for piece in pieces]
        + [pl.BlockSpec((BLOCK, c), lambda b: (before(b), 0)), whole(weight)],
        out_specs=(
            pl.BlockSpec((near, BLOCK, c), lambda b: (0, before(b), 0)),
            pl.BlockSpec((2, d), lambda b: (0, 0)),
        ),
        scratch_shapes=[
            pltpu.VMEM((total, LANES), f32),
            pltpu.VMEM((near * BLOCK, LANES), f32),
            pltpu.VMEM((near * BLOCK, LANES), f32),
            pltpu.VMEM((BLOCK, d), f32),
            pltpu.VMEM((1, d), f32),
            pltpu.VMEM((2, 8, c), f32),
            pltpu.VMEM((8, d), f32),
        ],
        compiler_params=params(),
        cost_estimate=lasting(22),
        name="edge_stats",
    )(index, *pieces, own, weight)


def moments(stat, edges_each):
    devices = stat.shape[0]
    means = stat[:, 0, :]
    mean = jnp.sum(means, axis=0, keepdims=True) * (1.0 / devices)
    off = means - mean
    m2 = jnp.sum(stat[:, 1, :], axis=0, keepdims=True) + edges_each * jnp.sum(
        off * off, axis=0, keepdims=True
    )
    return mean, lax.rsqrt(m2 * (1.0 / (edges_each * devices)) + EPS)


def pool_kernel(
    last, edges_each, diff_ref, own_ref, w_ref, stat_ref, gain_ref, shift_ref, *refs
):
    near, block, c = diff_ref.shape
    d = w_ref.shape[1]
    if last:
        cot_ref, pooled_ref, slope_ref, sums_ref, mixed, centre, upstream = refs
        upstream[...] = cot_ref[...].astype(f32)
    else:
        pooled_ref, slope_ref, sum_ref, moment_ref, mixed, centre = refs
    mean, inv = moments(stat_ref[...], edges_each)
    half_scale = gain_ref[...] * inv * 0.5
    centre[...] = (dot(own_ref[...], w_ref[:c, :]) - mean) * half_scale + shift_ref[...] * 0.5
    mixed[...] = dot(diff_ref[...].reshape(near * block, c), w_ref[c:, :]).reshape(near, block, d)
    if last:

        @pl.when(pl.program_id(0) == 0)
        def _():
            sums_ref[...] = jnp.zeros_like(sums_ref)

    for lane in range(0, d, 128):
        lanes = pl.ds(lane, 128)
        scale = jnp.broadcast_to(half_scale[:, lane : lane + 128], (ROWS, 128))

        def step(b, carry, lanes=lanes, scale=scale):
            at = pl.ds(pl.multiple_of(b * ROWS, ROWS), ROWS)
            offset = centre[at, lanes]
            active, bends = [], []
            for k in range(near):
                half = mixed[k, at, lanes] * scale + offset
                t = 1.0 + jnp.tanh(half)
                a = half * t
                active.append(a)
                bends.append(t * ((half + half + 1.0) - a))
            top = tree(jnp.maximum, active)
            powers = [jnp.exp(a - top) for a in active]
            total = tree(jnp.add, powers)
            pooled = top + jnp.log(total) - math.log(near)
            centre[at, lanes] = pooled
            factor = 0.5 / total
            if last:
                factor = factor * upstream[at, lanes]
            halves = [mixed[k, at, lanes] * scale + offset for k in range(near)]
            slopes = [(powers[k] * factor) * bends[k] for k in range(near)]
            slope_sum = tree(jnp.add, slopes)
            slope_moment = tree(jnp.add, [slopes[k] * halves[k] for k in range(near)])
            for k in range(near):
                slope_ref[k, at, lanes] = slopes[k]
            if not last:
                sum_ref[at, lanes] = slope_sum
                moment_ref[at, lanes] = slope_moment
                return carry
            return (carry[0] + slope_sum, carry[1] + slope_moment)

        zero = jnp.zeros((ROWS, 128), f32)
        carry = lax.fori_loop(0, block // ROWS, step, (zero, zero))
        if last:
            sums_ref[0:1, lanes] += jnp.sum(carry[0], axis=0, keepdims=True)
            sums_ref[1:2, lanes] += jnp.sum(carry[1], axis=0, keepdims=True)
    pooled_ref[...] = centre[...].astype(bf16)


def pool(diff, own, weight, stat, gain, shift, cot=None):
    near, rows, c = diff.shape
    d = weight.shape[1]
    whole = lambda x: pl.BlockSpec(x.shape, lambda b: (0,) * x.ndim)
    by_block = lambda width: pl.BlockSpec((BLOCK, width), lambda b: (b, 0))
    by_edge = lambda width: pl.BlockSpec((near, BLOCK, width), lambda b: (0, b, 0))
    gain, shift = gain.reshape(1, d), shift.reshape(1, d)
    inputs = [diff, own, weight, stat, gain, shift]
    in_specs = [by_edge(c), by_block(c), whole(weight), whole(stat), whole(gain), whole(shift)]
    row_out = lambda kind: (jax.ShapeDtypeStruct((rows, d), kind), by_block(d))
    outs = [row_out(bf16), (jax.ShapeDtypeStruct((near, rows, d), f32), by_edge(d))]
    if cot is None:
        outs += [row_out(f32), row_out(f32)]
    else:
        inputs.append(cot)
        in_specs.append(by_block(d))
        outs.append((jax.ShapeDtypeStruct((2, d), f32), pl.BlockSpec((2, d), lambda b: (0, 0))))
    return pl.pallas_call(
        functools.partial(pool_kernel, cot is not None, float(near * rows)),
        grid=(rows // BLOCK,),
        out_shape=tuple(o[0] for o in outs),
        in_specs=in_specs,
        out_specs=tuple(o[1] for o in outs),
        scratch_shapes=[pltpu.VMEM((near, BLOCK, d), f32)]
        + [pltpu.VMEM((BLOCK, d), f32)] * (1 if cot is None else 2),
        compiler_params=params(),
        cost_estimate=lasting(17 if cot is None else 32),
        name="pool",
    )(*inputs)


def grads_kernel(
    edges_each,
    with_weight,
    slope_ref,
    upstream_ref,
    diff_ref,
    own_ref,
    w_ref,
    back_ref,
    stat_ref,
    gain_ref,
    shift_ref,
    grads_ref,
    same_ref,
    *refs,
):
    near, block, c = diff_ref.shape
    d = w_ref.shape[1]
    if with_weight:
        centre_ref, spread_ref, weight_ref, dz_ref, dz_sum_ref = refs[:-2]
    else:
        dz_ref, dz_sum_ref, centre_ref, spread_ref = refs[:-2]
    mixed, constant = refs[-2:]
    edges = edges_each * stat_ref.shape[0]
    mean, inv = moments(stat_ref[...], edges_each)
    gain = gain_ref[...]
    sums = jnp.sum(grads_ref[...], axis=0)
    grad_shift = sums[0:1]
    grad_gain = (2.0 * sums[1:2] - shift_ref[...] * grad_shift) / gain
    alpha = gain * inv
    rate = alpha * inv * grad_gain * (1.0 / edges)
    constant[...] = alpha * grad_shift * (1.0 / edges) + rate * (
        dot(own_ref[...], w_ref[:c, :]) - mean
    )
    mixed[...] = dot(diff_ref[...].reshape(near * block, c), w_ref[c:, :]).reshape(near, block, d)

    for lane in range(0, d, 128):
        lanes = pl.ds(lane, 128)
        wide_alpha = jnp.broadcast_to(alpha[:, lane : lane + 128], (16, 128))
        wide_rate = jnp.broadcast_to(rate[:, lane : lane + 128], (16, 128))

        def step(b, _, lanes=lanes, wide_alpha=wide_alpha, wide_rate=wide_rate):
            at = pl.ds(pl.multiple_of(b * 16, 16), 16)
            offset = constant[at, lanes]
            factor = wide_alpha
            if upstream_ref is not None:
                factor = factor * upstream_ref[at, lanes]
            load = lambda k: (slope_ref[k, at, lanes], mixed[k, at, lanes])
            loaded = [load(k) for k in range(AHEAD)]
            dzs = []
            for k in range(near):
                if k + AHEAD < near:
                    loaded.append(load(k + AHEAD))
                slope, mix = loaded[k]
                dzs.append((factor * slope - offset - wide_rate * mix).astype(bf16))
                if k >= AHEAD:
                    dz_ref[k - AHEAD, at, lanes] = dzs[k - AHEAD]
            for k in range(near - AHEAD, near):
                dz_ref[k, at, lanes] = dzs[k]
            dz_sum = tree(jnp.add, [dz.astype(f32) for dz in dzs])
            dz_sum_ref[at, lanes] = dz_sum
            return 0

        lax.fori_loop(0, block // 16, step, 0)

    weight = w_ref[...].astype(f32)
    centre_ref[...] = lax.dot_general(
        dz_sum_ref[...],
        weight[:c] - weight[c:],
        (((1,), (1,)), ((), ())),
        precision=lax.Precision.HIGHEST,
        preferred_element_type=f32,
    )
    flat = dz_ref[...].reshape(near * block, d)
    back = dot_t(flat, back_ref[...]).astype(bf16).reshape(near, block, LANES)
    for k in range(near):
        spread_ref[k] = dot(same_ref[k], back[k])
    if with_weight:

        @pl.when(pl.program_id(0) == 0)
        def _():
            weight_ref[...] = jnp.zeros_like(weight_ref)

        weight_ref[:c, :] += lax.dot_general(
            own_ref[...].astype(f32),
            dz_sum_ref[...],
            (((0,), (0,)), ((), ())),
            precision=lax.Precision.HIGHEST,
            preferred_element_type=f32,
        )
        weight_ref[c:, :] += lax.dot_general(
            diff_ref[...].reshape(near * block, c),
            flat,
            (((0,), (0,)), ((), ())),
            preferred_element_type=f32,
        )


def edge_grads(slope, upstream, diff, own, weight, stat, gain, shift, grads, same, with_weight):
    near, rows, c = diff.shape
    d = weight.shape[1]
    whole = lambda x: pl.BlockSpec(x.shape, lambda b: (0,) * x.ndim)
    by_block = lambda width: pl.BlockSpec((BLOCK, width), lambda b: (b, 0))
    by_edge = lambda width: pl.BlockSpec((near, BLOCK, width), lambda b: (0, b, 0))
    gain, shift = gain.reshape(1, d), shift.reshape(1, d)
    back = jnp.pad(weight[c:], ((0, LANES - c), (0, 0)))
    inputs = [slope, upstream, diff, own, weight, back, stat, gain, shift, grads, same]
    in_specs = [
        by_edge(d),
        by_block(d),
        by_edge(c),
        by_block(c),
        whole(weight),
        whole(back),
        whole(stat),
        whole(gain),
        whole(shift),
        whole(grads),
        by_edge(BLOCK),
    ]
    body = functools.partial(grads_kernel, float(near * rows), with_weight)
    if upstream is None:
        del inputs[1], in_specs[1]
        inner = body
        body = lambda s, *rest: inner(s, None, *rest)
    outs = [
        (jax.ShapeDtypeStruct((rows, c), f32), by_block(c)),
        (jax.ShapeDtypeStruct((near, rows, LANES), f32), by_edge(LANES)),
    ]
    scratch = [pltpu.VMEM((near, BLOCK, d), f32), pltpu.VMEM((BLOCK, d), f32)]
    if with_weight:
        outs.append((jax.ShapeDtypeStruct((2 * c, d), f32), whole(weight)))
        scratch = [pltpu.VMEM((near, BLOCK, d), bf16), pltpu.VMEM((BLOCK, d), f32)] + scratch
    else:
        outs = [
            (jax.ShapeDtypeStruct((near, rows, d), bf16), by_edge(d)),
            (jax.ShapeDtypeStruct((rows, d), f32), by_block(d)),
        ] + outs
    return pl.pallas_call(
        body,
        grid=(rows // BLOCK,),
        out_shape=tuple(o[0] for o in outs),
        in_specs=in_specs,
        out_specs=tuple(o[1] for o in outs),
        scratch_shapes=scratch,
        compiler_params=params(),
        cost_estimate=lasting(22),
        name="edge_grads",
    )(*inputs)


def scatter_kernel(idx_ref, spread_ref, zero_ref, line_ref, first_ref, even, odd, sems):
    near, block, _ = spread_ref.shape
    c = first_ref.shape[1]
    step_id = pl.program_id(0)
    total = even.shape[0]
    piece = zero_ref.shape[0]

    @pl.when(step_id == 0)
    def _():
        pieces = total // piece
        copies = [
            pltpu.make_async_copy(
                zero_ref, line.at[pl.ds(i * piece, piece)], sems.at[half * pieces + i]
            )
            for half, line in enumerate((even, odd))
            for i in range(pieces)
        ]
        for copy in copies:
            copy.start()
        for copy in copies:
            copy.wait()

    def add(k, _):
        at = step_id * near + k
        held = []
        for e in range(block + GROUP):
            if e < block:
                line = (even, odd)[e // GROUP % 2]
                place = pl.ds(idx_ref[at, e], 1)
                held.append((line, place, line[place, :] + spread_ref[k, pl.ds(e, 1), :]))
            if e >= GROUP:
                line, place, row = held[e - GROUP]
                line[place, :] = row
        return 0

    lax.fori_loop(0, near, add, 0)

    @pl.when(step_id == pl.num_programs(0) - 1)
    def _():
        def join(i, _):
            at = pl.ds(pl.multiple_of(i * 256, 256), 256)
            even[at, :] = even[at, :] + odd[at, :]
            return 0

        lax.fori_loop(0, total // 256, join, 0)
        copy = pltpu.make_async_copy(even, line_ref, sems.at[0])
        copy.start()
        first_ref[...] = even[pl.ds(total // 2, piece), :c].astype(bf16)
        copy.wait()


def scatter_grads(order, spread, total, c):
    near, rows, _ = spread.shape
    anywhere = pl.BlockSpec(memory_space=pl.ANY)
    return pl.pallas_call(
        scatter_kernel,
        grid=(rows // BLOCK,),
        out_shape=(
            jax.ShapeDtypeStruct((total, LANES), f32),
            jax.ShapeDtypeStruct((rows, c), bf16),
        ),
        in_specs=[
            smem(),
            pl.BlockSpec((near, BLOCK, LANES), lambda b: (0, b, 0)),
            anywhere,
        ],
        out_specs=(anywhere, pl.BlockSpec((rows, c), lambda b: (0, 0))),
        scratch_shapes=[pltpu.VMEM((total, LANES), f32)] * 2
        + [pltpu.SemaphoreType.DMA((2 * total // rows,))],
        compiler_params=params(),
        cost_estimate=lasting(20),
        name="scatter_grads",
    )(order, spread, jnp.zeros((rows, LANES), f32))


def same_target(index):
    near, rows = index.shape
    blocks = index.reshape(near, rows // BLOCK, BLOCK)
    group = jnp.arange(BLOCK, dtype=jnp.int32) // GROUP
    equal = (blocks[:, :, :, None] == blocks[:, :, None, :]) & (group[:, None] == group[None, :])
    return equal.astype(bf16).reshape(near, rows, BLOCK)


def copies(x):
    return jnp.broadcast_to(x[None], (lax.axis_size(BOTH),) + x.shape)


def shared(x):
    devices = lax.axis_size(BOTH)
    return x.reshape(devices, x.shape[0] // devices, x.shape[1])


def exchange(shares):
    return lax.all_to_all(shares, BOTH, split_axis=0, concat_axis=0, tiled=True)


def everyone(x):
    return exchange(copies(x))


def ring_moves(places):
    ring = list(range(0, places, 2)) + list(range(1, places, 2))[::-1]
    onward = [(ring[i], ring[(i + 1) % places]) for i in range(places)]
    return onward, [(b, a) for a, b in onward]


def ring_place(device, places):
    return jnp.where(device % 2 == 0, device // 2, places - 1 - device // 2)


def line_table(values):
    places = lax.axis_size("pts")
    onward, backward = ring_moves(places)
    rows, far = values.shape[0] // 2, places // 2
    behind, ahead = [values], [values]
    for _ in range(far - 1):
        behind.append(lax.ppermute(behind[-1], "pts", onward))
        ahead.append(lax.ppermute(ahead[-1], "pts", backward))
    farthest = [
        lax.ppermute(behind[-1][:rows], "pts", onward),
        lax.ppermute(ahead[-1][rows:], "pts", backward),
    ]
    return behind + farthest + ahead[:0:-1]


def owners_sum(line, first, centre, beside):
    places = lax.axis_size("pts")
    onward, backward = ring_moves(places)
    rows, c = centre.shape
    half, far = rows // 2, places // 2

    def slot(j):
        return line[j * rows : (j + 1) * rows, :c]

    forth = lax.ppermute(first[:half], "pts", onward).astype(f32)
    back = lax.ppermute(first[half:], "pts", backward).astype(f32)
    forth = jnp.pad(forth, ((0, half), (0, 0)))
    back = jnp.pad(back, ((half, 0), (0, 0)))
    for j in range(1, far):
        forth, back = (forth + slot(far + j)).astype(bf16), (back + slot(far - j)).astype(bf16)
        if j == 2:
            forth, back, beside = lax.optimization_barrier((forth, back, beside))
        else:
            forth, back = lax.optimization_barrier((forth, back))
        forth = lax.ppermute(forth, "pts", onward).astype(f32)
        back = lax.ppermute(back, "pts", backward).astype(f32)
    return centre + slot(0) + forth + back, beside


def weight_grad(diff, own, dz, dz_sum):
    first = jnp.dot(
        own.astype(f32).T, dz_sum, precision=lax.Precision.HIGHEST, preferred_element_type=f32
    )
    second = jnp.einsum("kgc,kgd->cd", diff, dz, preferred_element_type=f32)
    return jnp.concatenate([first, second], axis=0)


def per_device(
    points,
    lengths,
    neighbours_one,
    neighbours_two,
    weight_one,
    gain_one,
    shift_one,
    weight_two,
    gain_two,
    shift_two,
    cotangent,
):
    line_devices = lax.axis_size("pts")
    row_count = points.shape[0]
    line_length = line_devices * row_count
    table_one = line_table(points)

    cloud_ends = jnp.cumsum(lengths)
    cloud_starts = cloud_ends - lengths
    line_first = lax.axis_index("loc") * line_length
    position = (
        line_first + lax.axis_index("pts") * row_count + jnp.arange(row_count, dtype=jnp.int32)
    )
    begins = (position[:, None] >= cloud_starts[None, :]) & (position[:, None] < cloud_ends[None, :])
    begin = jnp.sum(jnp.where(begins, cloud_starts[None, :], 0), axis=1) - line_first
    here = ring_place(lax.axis_index("pts"), line_devices)

    def slot_rows(neighbours):
        within = neighbours.T + begin[None, :]
        slot = (here - ring_place(within // row_count, line_devices)) % line_devices
        return slot * row_count + within % row_count

    def by_blocks(index):
        blocks = index.reshape(index.shape[0], -1, BLOCK)
        return blocks.transpose(1, 0, 2).reshape(-1, BLOCK)

    index_one = slot_rows(neighbours_one)
    index_two = slot_rows(neighbours_two)
    order_one, order_two = by_blocks(index_one), by_blocks(index_two)
    same_one = same_target(index_one)
    same_two = same_target(index_two)

    diff_one, stat_one = edge_stats(order_one, table_one, points, weight_one)
    stat_one = everyone(stat_one)
    act_one, slope_one, slope_sum, slope_moment = pool(
        diff_one, points, weight_one, stat_one, gain_one, shift_one
    )
    table_two = line_table(act_one)
    diff_two, stat_two = edge_stats(order_two, table_two, act_one, weight_two)
    stat_two = everyone(stat_two)
    act_two, slope_two, sums_two = pool(
        diff_two, act_one, weight_two, stat_two, gain_two, shift_two, cotangent
    )
    sums_two = everyone(sums_two)
    dz_two, dz_sum_two, centre_two, spread_two = edge_grads(
        slope_two,
        None,
        diff_two,
        act_one,
        weight_two,
        stat_two,
        gain_two,
        shift_two,
        sums_two,
        same_two,
        False,
    )
    line_two, first_two = scatter_grads(order_two, spread_two, line_length, act_one.shape[1])
    grad_first, _ = owners_sum(line_two, first_two, centre_two, None)
    grad_first, dz_two, dz_sum_two = lax.optimization_barrier((grad_first, dz_two, dz_sum_two))
    weight_part_two = weight_grad(diff_two, act_one, dz_two, dz_sum_two)
    sums_one = jnp.stack(
        [jnp.sum(grad_first * slope_sum, axis=0), jnp.sum(grad_first * slope_moment, axis=0)]
    )
    sums_one = everyone(sums_one)
    centre_one, spread_one, weight_part_one = edge_grads(
        slope_one,
        grad_first,
        diff_one,
        points,
        weight_one,
        stat_one,
        gain_one,
        shift_one,
        sums_one,
        same_one,
        True,
    )
    weights = jnp.concatenate([weight_part_two.reshape(-1, LANES), weight_part_one], axis=0)
    shares = exchange(shared(weights))
    line_one, first_one = scatter_grads(order_one, spread_one, line_length, points.shape[1])
    shares, first_one = lax.optimization_barrier((shares, first_one))
    weights = everyone(jnp.sum(shares, axis=0))
    grad_points, weights = owners_sum(line_one, first_one, centre_one, weights)
    weights = weights.reshape(-1, LANES)
    grad_weight_two = weights[: -weight_one.shape[0]].reshape(weight_two.shape)
    grad_weight_one = weights[-weight_one.shape[0] :]

    def norm_grads(sums, gain, shift):
        sums = jnp.sum(sums, axis=0)
        return (2.0 * sums[1] - shift * sums[0]) / gain, sums[0]

    grad_gain_one, grad_shift_one = norm_grads(sums_one, gain_one, shift_one)
    grad_gain_two, grad_shift_two = norm_grads(sums_two, gain_two, shift_two)
    return (
        act_one,
        act_two,
        grad_points,
        grad_weight_one,
        grad_gain_one,
        grad_shift_one,
        grad_weight_two,
        grad_gain_two,
        grad_shift_two,
    )


def solution(mesh):
    rows, copied = P(("pts", "loc"), None), P()
    in_specs = (rows, copied, rows, rows) + (copied,) * 6 + (rows,)
    out_specs = (rows, rows, rows) + (copied,) * 6
    return jax.shard_map(
        per_device, mesh=mesh, in_specs=in_specs, out_specs=out_specs, check_vma=False
    )
```

```python
import functools
import math

import jax
import jax.numpy as jnp
from jax import lax
from jax.experimental import pallas as pl
from jax.experimental.pallas import tpu as pltpu
from jax.sharding import PartitionSpec as P

EPS = 1e-05
BLOCK = 128
GROUP = 8
ROWS = 16
AHEAD = 4
LOG2E = 1.0 / math.log(2.0)
LANES = 128
MIB = 1024 * 1024
BOTH = ("pts", "loc")

f32 = jnp.float32
bf16 = jnp.bfloat16


def params():
    return pltpu.CompilerParams(vmem_limit_bytes=52 * MIB)


def lasting(microseconds):
    return pl.CostEstimate(flops=0, transcendentals=0, bytes_accessed=3_000_000 * microseconds)


def smem():
    return pl.BlockSpec(memory_space=pltpu.SMEM)


def fold_rows(x):
    return jnp.sum(x.reshape(x.shape[0] // 8, 8, x.shape[1]), axis=0)


def tree(op, terms):
    while len(terms) > 1:
        pairs = [op(a, b) for a, b in zip(terms[::2], terms[1::2])]
        terms = pairs + terms[len(pairs) * 2 :]
    return terms[0]


def dot(a, b):
    return jnp.dot(a, b, preferred_element_type=f32)


def dot_t(a, b):
    return lax.dot_general(a, b, (((1,), (1,)), ((), ())), preferred_element_type=f32)


def edge_kernel(pieces, *refs):
    table_refs = refs[1 : 1 + pieces]
    idx_ref = refs[0]
    own_ref, w_ref, diff_ref, stat_ref, table, fresh, held, centre, pivot, sums, square = refs[
        1 + pieces :
    ]
    near, block, c = diff_ref.shape
    step_id = pl.program_id(0)
    last = pl.num_programs(0) - 1
    chunk = 4

    def project(own_sum, diff_sum):
        weight = w_ref[...].astype(f32)
        exact = functools.partial(
            jnp.dot, precision=lax.Precision.HIGHEST, preferred_element_type=f32
        )
        both = exact(own_sum, weight[:c]) + exact(diff_sum, weight[c:])
        return jnp.sum(both, axis=0, keepdims=True)

    @pl.when(step_id == 0)
    def _():
        first = 0
        for piece in table_refs:
            for r in range(0, piece.shape[0], 256):
                table[pl.ds(first + r, 256), :c] = piece[pl.ds(r, 256), :].astype(f32)
            first += piece.shape[0]
        sums[...] = jnp.zeros_like(sums)
        square[...] = jnp.zeros_like(square)

    @pl.when(step_id > 0)
    def _():
        for r in range(0, near * block, 256):
            held[pl.ds(r, 256), :] = fresh[pl.ds(r, 256), :]

    @pl.when(step_id == 1)
    def _():
        own = own_ref[...].astype(f32)
        diff_sum = jnp.zeros((8, c), f32)
        for k in range(near):
            diff_sum = diff_sum + fold_rows(held[pl.ds(k * block, block), :c] - own)
        own_sum = fold_rows(own) * float(near)
        pivot[...] = project(own_sum, diff_sum) * (1.0 / (near * block))

    def pick(k):
        base = pl.multiple_of(k * block, block)
        at = step_id * near + k
        rows = []
        for e in range(block + GROUP):
            if e < block:
                rows.append(table[pl.ds(idx_ref[at, e], 1), :])
            if e >= GROUP:
                fresh[pl.ds(base + (e - GROUP), 1), :] = rows[e - GROUP]

    def work(k, own, carry):
        diff_sum, total = carry
        at = pl.ds(pl.multiple_of(k * block, block), block)
        diff = (held[at, :c] - own).astype(bf16)
        diff_ref[k] = diff
        diff_sum = diff_sum + fold_rows(diff.astype(f32))
        z = dot(diff, w_ref[c:, :]) + centre[...]
        return diff_sum, total + fold_rows(z * z)

    @pl.when(step_id == 0)
    def _():
        def body(i, _):
            pick(i)
            return 0

        lax.fori_loop(0, near, body, 0)

    def finish(own, carry):
        sums[0] += fold_rows(own) * float(near)
        sums[1] += carry[0]
        square[...] += carry[1]

    def begin():
        centre[...] = dot(own_ref[...], w_ref[:c, :]) - pivot[...]
        zero = (jnp.zeros((8, c), f32), jnp.zeros_like(square[...]))
        return own_ref[...].astype(f32), zero

    @pl.when((step_id > 0) & (step_id < last))
    def _():
        own, zero = begin()

        def body(i, carry):
            for k in range(chunk):
                pick(i * chunk + k)
                carry = work(i * chunk + k, own_ref[...].astype(f32), carry)
            return carry

        finish(own, lax.fori_loop(0, near // chunk, body, zero))

    @pl.when(step_id == last)
    def _():
        own, carry = begin()
        for k in range(near):
            carry = work(k, own, carry)
        finish(own, carry)
        count = float(near * block * (pl.num_programs(0) - 1))
        mean = project(sums[0], sums[1]) / count
        off = mean - pivot[...]
        stat_ref[0:1, :] = mean
        stat_ref[1:2, :] = jnp.sum(square[...], axis=0, keepdims=True) - count * off * off


def edge_stats(index, pieces, own, weight):
    rows, c = own.shape
    d = weight.shape[1]
    blocks = rows // BLOCK
    near = index.shape[0] // blocks
    total = sum(piece.shape[0] for piece in pieces)
    before = lambda b: jnp.maximum(b - 1, 0)
    whole = lambda x: pl.BlockSpec(x.shape, lambda b: (0,) * x.ndim)
    return pl.pallas_call(
        functools.partial(edge_kernel, len(pieces)),
        grid=(blocks + 1,),
        out_shape=(
            jax.ShapeDtypeStruct((near, rows, c), bf16),
            jax.ShapeDtypeStruct((2, d), f32),
        ),
        in_specs=[smem()]
        + [whole(piece) for piece in pieces]
        + [pl.BlockSpec((BLOCK, c), lambda b: (before(b), 0)), whole(weight)],
        out_specs=(
            pl.BlockSpec((near, BLOCK, c), lambda b: (0, before(b), 0)),
            pl.BlockSpec((2, d), lambda b: (0, 0)),
        ),
        scratch_shapes=[
            pltpu.VMEM((total, LANES), f32),
            pltpu.VMEM((near * BLOCK, LANES), f32),
            pltpu.VMEM((near * BLOCK, LANES), f32),
            pltpu.VMEM((BLOCK, d), f32),
            pltpu.VMEM((1, d), f32),
            pltpu.VMEM((2, 8, c), f32),
            pltpu.VMEM((8, d), f32),
        ],
        compiler_params=params(),
        cost_estimate=lasting(22),
        name="edge_stats",
    )(index, *pieces, own, weight)


def moments(stat, edges_each):
    devices = stat.shape[0]
    means = stat[:, 0, :]
    mean = jnp.sum(means, axis=0, keepdims=True) * (1.0 / devices)
    off = means - mean
    m2 = jnp.sum(stat[:, 1, :], axis=0, keepdims=True) + edges_each * jnp.sum(
        off * off, axis=0, keepdims=True
    )
    return mean, lax.rsqrt(m2 * (1.0 / (edges_each * devices)) + EPS)


def pool_kernel(
    last, edges_each, diff_ref, own_ref, w_ref, stat_ref, norm_ref, *refs
):
    near, block, c = diff_ref.shape
    d = w_ref.shape[1]
    if last:
        cot_ref, pooled_ref, slope_ref, sums_ref, mixed, centre, upstream = refs
        upstream[...] = cot_ref[...].astype(f32)
    else:
        pooled_ref, slope_ref, sum_ref, moment_ref, mixed, centre = refs
    mean, inv = moments(stat_ref[...], edges_each)
    half_scale = norm_ref[0:1, :] * inv * 0.5
    centre[...] = (dot(own_ref[...], w_ref[:c, :]) - mean) * half_scale + norm_ref[1:2, :] * 0.5
    mixed[...] = dot(diff_ref[...].reshape(near * block, c), w_ref[c:, :]).reshape(near, block, d)
    if last:

        @pl.when(pl.program_id(0) == 0)
        def _():
            sums_ref[...] = jnp.zeros_like(sums_ref)

    for lane in range(0, d, 128):
        lanes = pl.ds(lane, 128)
        scale = jnp.broadcast_to(half_scale[:, lane : lane + 128], (ROWS, 128))

        def step(b, carry, lanes=lanes, scale=scale):
            at = pl.ds(pl.multiple_of(b * ROWS, ROWS), ROWS)
            offset = centre[at, lanes]
            active, bends = [], []
            for k in range(near):
                half = mixed[k, at, lanes] * scale + offset
                t = 1.0 + jnp.tanh(half)
                a = half * t
                active.append(a)
                bends.append(t * ((half + half + 1.0) - a))
            top = tree(jnp.maximum, active)
            powers = [jnp.exp2((a - top) * LOG2E) for a in active]
            total = tree(jnp.add, powers)
            pooled = top + jnp.log(total) - math.log(near)
            centre[at, lanes] = pooled
            factor = 0.5 / total
            if last:
                factor = factor * upstream[at, lanes]
            halves = [mixed[k, at, lanes] * scale + offset for k in range(near)]
            slopes = [(powers[k] * factor) * bends[k] for k in range(near)]
            slope_sum = tree(jnp.add, slopes)
            slope_moment = tree(jnp.add, [slopes[k] * halves[k] for k in range(near)])
            for k in range(near):
                slope_ref[k, at, lanes] = slopes[k]
            if not last:
                sum_ref[at, lanes] = slope_sum
                moment_ref[at, lanes] = slope_moment
                return carry
            return (carry[0] + slope_sum, carry[1] + slope_moment)

        zero = jnp.zeros((ROWS, 128), f32)
        carry = lax.fori_loop(0, block // ROWS, step, (zero, zero))
        if last:
            sums_ref[0:1, lanes] += jnp.sum(carry[0], axis=0, keepdims=True)
            sums_ref[1:2, lanes] += jnp.sum(carry[1], axis=0, keepdims=True)
    pooled_ref[...] = centre[...].astype(bf16)


def pool(diff, own, weight, stat, norm, cot=None):
    near, rows, c = diff.shape
    d = weight.shape[1]
    whole = lambda x: pl.BlockSpec(x.shape, lambda b: (0,) * x.ndim)
    by_block = lambda width: pl.BlockSpec((BLOCK, width), lambda b: (b, 0))
    by_edge = lambda width: pl.BlockSpec((near, BLOCK, width), lambda b: (0, b, 0))
    inputs = [diff, own, weight, stat, norm]
    in_specs = [by_edge(c), by_block(c), whole(weight), whole(stat), whole(norm)]
    row_out = lambda kind: (jax.ShapeDtypeStruct((rows, d), kind), by_block(d))
    outs = [row_out(bf16), (jax.ShapeDtypeStruct((near, rows, d), f32), by_edge(d))]
    if cot is None:
        outs += [row_out(f32), row_out(f32)]
    else:
        inputs.append(cot)
        in_specs.append(by_block(d))
        outs.append((jax.ShapeDtypeStruct((2, d), f32), pl.BlockSpec((2, d), lambda b: (0, 0))))
    return pl.pallas_call(
        functools.partial(pool_kernel, cot is not None, float(near * rows)),
        grid=(rows // BLOCK,),
        out_shape=tuple(o[0] for o in outs),
        in_specs=in_specs,
        out_specs=tuple(o[1] for o in outs),
        scratch_shapes=[pltpu.VMEM((near, BLOCK, d), f32)]
        + [pltpu.VMEM((BLOCK, d), f32)] * (1 if cot is None else 2),
        compiler_params=params(),
        cost_estimate=lasting(17 if cot is None else 32),
        name="pool",
    )(*inputs)


def grads_kernel(
    edges_each,
    with_weight,
    slope_ref,
    upstream_ref,
    diff_ref,
    own_ref,
    w_ref,
    back_ref,
    stat_ref,
    norm_ref,
    grads_ref,
    same_ref,
    *refs,
):
    near, block, c = diff_ref.shape
    d = w_ref.shape[1]
    if with_weight:
        centre_ref, spread_ref, weight_ref, dz_ref, dz_sum_ref = refs[:-2]
    else:
        dz_ref, dz_sum_ref, centre_ref, spread_ref = refs[:-2]
    mixed, constant = refs[-2:]
    edges = edges_each * stat_ref.shape[0]
    mean, inv = moments(stat_ref[...], edges_each)
    gain = norm_ref[0:1, :]
    sums = jnp.sum(grads_ref[...], axis=0)
    grad_shift = sums[0:1]
    grad_gain = (2.0 * sums[1:2] - norm_ref[1:2, :] * grad_shift) / gain
    alpha = gain * inv
    rate = alpha * inv * grad_gain * (1.0 / edges)
    constant[...] = alpha * grad_shift * (1.0 / edges) + rate * (
        dot(own_ref[...], w_ref[:c, :]) - mean
    )
    mixed[...] = dot(diff_ref[...].reshape(near * block, c), w_ref[c:, :]).reshape(near, block, d)

    for lane in range(0, d, 128):
        lanes = pl.ds(lane, 128)
        wide_alpha = jnp.broadcast_to(alpha[:, lane : lane + 128], (16, 128))
        wide_rate = jnp.broadcast_to(rate[:, lane : lane + 128], (16, 128))

        def step(b, _, lanes=lanes, wide_alpha=wide_alpha, wide_rate=wide_rate):
            at = pl.ds(pl.multiple_of(b * 16, 16), 16)
            offset = constant[at, lanes]
            factor = wide_alpha
            if upstream_ref is not None:
                factor = factor * upstream_ref[at, lanes]
            load = lambda k: (slope_ref[k, at, lanes], mixed[k, at, lanes])
            loaded = [load(k) for k in range(AHEAD)]
            dzs = []
            for k in range(near):
                if k + AHEAD < near:
                    loaded.append(load(k + AHEAD))
                slope, mix = loaded[k]
                dzs.append((factor * slope - offset - wide_rate * mix).astype(bf16))
                if k >= AHEAD:
                    dz_ref[k - AHEAD, at, lanes] = dzs[k - AHEAD]
            for k in range(near - AHEAD, near):
                dz_ref[k, at, lanes] = dzs[k]
            dz_sum = tree(jnp.add, [dz.astype(f32) for dz in dzs])
            dz_sum_ref[at, lanes] = dz_sum
            return 0

        lax.fori_loop(0, block // 16, step, 0)

    weight = w_ref[...].astype(f32)
    centre_ref[...] = lax.dot_general(
        dz_sum_ref[...],
        weight[:c] - weight[c:],
        (((1,), (1,)), ((), ())),
        precision=lax.Precision.HIGHEST,
        preferred_element_type=f32,
    )
    flat = dz_ref[...].reshape(near * block, d)
    back = dot_t(flat, back_ref[...]).astype(bf16).reshape(near, block, LANES)
    for k in range(near):
        spread_ref[k] = dot(same_ref[k], back[k])
    if with_weight:

        @pl.when(pl.program_id(0) == 0)
        def _():
            weight_ref[...] = jnp.zeros_like(weight_ref)

        weight_ref[:c, :] += lax.dot_general(
            own_ref[...].astype(f32),
            dz_sum_ref[...],
            (((0,), (0,)), ((), ())),
            precision=lax.Precision.HIGHEST,
            preferred_element_type=f32,
        )
        weight_ref[c:, :] += lax.dot_general(
            diff_ref[...].reshape(near * block, c),
            flat,
            (((0,), (0,)), ((), ())),
            preferred_element_type=f32,
        )


def edge_grads(slope, upstream, diff, own, weight, stat, norm, grads, same, with_weight):
    near, rows, c = diff.shape
    d = weight.shape[1]
    whole = lambda x: pl.BlockSpec(x.shape, lambda b: (0,) * x.ndim)
    by_block = lambda width: pl.BlockSpec((BLOCK, width), lambda b: (b, 0))
    by_edge = lambda width: pl.BlockSpec((near, BLOCK, width), lambda b: (0, b, 0))
    back = jnp.pad(weight[c:], ((0, LANES - c), (0, 0)))
    inputs = [slope, upstream, diff, own, weight, back, stat, norm, grads, same]
    in_specs = [
        by_edge(d),
        by_block(d),
        by_edge(c),
        by_block(c),
        whole(weight),
        whole(back),
        whole(stat),
        whole(norm),
        whole(grads),
        by_edge(BLOCK),
    ]
    body = functools.partial(grads_kernel, float(near * rows), with_weight)
    if upstream is None:
        del inputs[1], in_specs[1]
        inner = body
        body = lambda s, *rest: inner(s, None, *rest)
    outs = [
        (jax.ShapeDtypeStruct((rows, c), f32), by_block(c)),
        (jax.ShapeDtypeStruct((near, rows, LANES), f32), by_edge(LANES)),
    ]
    scratch = [pltpu.VMEM((near, BLOCK, d), f32), pltpu.VMEM((BLOCK, d), f32)]
    if with_weight:
        outs.append((jax.ShapeDtypeStruct((2 * c, d), f32), whole(weight)))
        scratch = [pltpu.VMEM((near, BLOCK, d), bf16), pltpu.VMEM((BLOCK, d), f32)] + scratch
    else:
        outs = [
            (jax.ShapeDtypeStruct((near, rows, d), bf16), by_edge(d)),
            (jax.ShapeDtypeStruct((rows, d), f32), by_block(d)),
        ] + outs
    return pl.pallas_call(
        body,
        grid=(rows // BLOCK,),
        out_shape=tuple(o[0] for o in outs),
        in_specs=in_specs,
        out_specs=tuple(o[1] for o in outs),
        scratch_shapes=scratch,
        compiler_params=params(),
        cost_estimate=lasting(22),
        name="edge_grads",
    )(*inputs)


def scatter_kernel(sends, rows, idx_ref, spread_ref, line_ref, *refs):
    near, block, _ = spread_ref.shape
    send_refs = refs[: len(sends)]
    even, odd, sem = refs[len(sends) :]
    step_id = pl.program_id(0)
    total = even.shape[0]

    @pl.when(step_id == 0)
    def _():
        def clear(i, _):
            at = pl.ds(pl.multiple_of(i * 256, 256), 256)
            even[at, :] = jnp.zeros((256, LANES), f32)
            odd[at, :] = jnp.zeros((256, LANES), f32)
            return 0

        lax.fori_loop(0, total // 256, clear, 0)

    def add(k, _):
        at = step_id * near + k
        held = []
        for e in range(block + GROUP):
            if e < block:
                line = (even, odd)[e // GROUP % 2]
                place = pl.ds(idx_ref[at, e], 1)
                held.append((line, place, line[place, :] + spread_ref[k, pl.ds(e, 1), :]))
            if e >= GROUP:
                line, place, row = held[e - GROUP]
                line[place, :] = row
        return 0

    lax.fori_loop(0, near, add, 0)

    @pl.when(step_id == pl.num_programs(0) - 1)
    def _():
        def join(i, _):
            at = pl.ds(pl.multiple_of(i * 256, 256), 256)
            even[at, :] = even[at, :] + odd[at, :]
            return 0

        lax.fori_loop(0, total // 256, join, 0)
        copy = pltpu.make_async_copy(even, line_ref, sem)
        copy.start()
        for send_ref, slots in zip(send_refs, sends):
            for i, slot in enumerate(slots):
                values = even[pl.ds(slot * rows, rows), : send_ref.shape[1]]
                send_ref[pl.ds(i * rows, rows), :] = values.astype(bf16)
        copy.wait()


def scatter_grads(order, spread, total, c, sends):
    near, rows, _ = spread.shape
    shapes = [(len(slots) * rows, c) for slots in sends]
    anywhere = pl.BlockSpec(memory_space=pl.ANY)
    return pl.pallas_call(
        functools.partial(scatter_kernel, sends, rows),
        grid=(rows // BLOCK,),
        out_shape=(jax.ShapeDtypeStruct((total, LANES), f32),)
        + tuple(jax.ShapeDtypeStruct(shape, bf16) for shape in shapes),
        in_specs=[smem(), pl.BlockSpec((near, BLOCK, LANES), lambda b: (0, b, 0))],
        out_specs=(anywhere,) + tuple(pl.BlockSpec(shape, lambda b: (0, 0)) for shape in shapes),
        scratch_shapes=[pltpu.VMEM((total, LANES), f32)] * 2 + [pltpu.SemaphoreType.DMA],
        compiler_params=params(),
        cost_estimate=lasting(20),
        name="scatter_grads",
    )(order, spread)


def same_target(index):
    near, rows = index.shape
    blocks = index.reshape(near, rows // BLOCK, BLOCK)
    group = jnp.arange(BLOCK, dtype=jnp.int32) // GROUP
    equal = (blocks[:, :, :, None] == blocks[:, :, None, :]) & (group[:, None] == group[None, :])
    return equal.astype(bf16).reshape(near, rows, BLOCK)


def copies(x):
    return jnp.broadcast_to(x[None], (lax.axis_size(BOTH),) + x.shape)


def shared(x):
    devices = lax.axis_size(BOTH)
    return x.reshape(devices, x.shape[0] // devices, x.shape[1])


def exchange(shares):
    return lax.all_to_all(shares, BOTH, split_axis=0, concat_axis=0, tiled=True)


def everyone(x):
    return exchange(copies(x))


def ring_moves(places):
    ring = list(range(0, places, 2)) + list(range(1, places, 2))[::-1]
    onward = [(ring[i], ring[(i + 1) % places]) for i in range(places)]
    return onward, [(b, a) for a, b in onward]


def ring_place(device, places):
    return jnp.where(device % 2 == 0, device // 2, places - 1 - device // 2)


def ring_jumps(places):
    onward, backward = ring_moves(places)
    twice = lambda moves: [(a, dict(moves)[b]) for a, b in moves]
    return twice(onward), twice(backward)


def line_table(values):
    places = lax.axis_size("pts")
    onward, backward = ring_moves(places)
    rows, far = values.shape[0] // 2, places // 2
    behind, ahead = [values], [values]
    for _ in range(far - 1):
        behind.append(lax.ppermute(behind[-1], "pts", onward))
        ahead.append(lax.ppermute(ahead[-1], "pts", backward))
    farthest = [
        lax.ppermute(behind[-1][:rows], "pts", onward),
        lax.ppermute(ahead[-1][rows:], "pts", backward),
    ]
    return behind + farthest + ahead[:0:-1]


def short_table(values):
    if lax.axis_size("pts") != 8:
        return line_table(values)
    onward, backward = ring_moves(8)
    far_onward, far_backward = ring_jumps(8)
    rows = values.shape[0] // 2
    behind_two = lax.ppermute(values, "pts", far_onward)
    ahead_two = lax.ppermute(values, "pts", far_backward)
    behind_one = lax.ppermute(values, "pts", onward)
    ahead_one = lax.ppermute(values, "pts", backward)
    farthest = [
        lax.ppermute(behind_two[:rows], "pts", far_onward),
        lax.ppermute(ahead_two[rows:], "pts", far_backward),
    ]
    behind_three = lax.ppermute(behind_two, "pts", onward)
    ahead_three = lax.ppermute(ahead_two, "pts", backward)
    return (
        [values, behind_one, behind_two, behind_three]
        + farthest
        + [ahead_three, ahead_two, ahead_one]
    )


def owners_sum(line, sends, centre):
    places = lax.axis_size("pts")
    onward, backward = ring_moves(places)
    rows, c = centre.shape
    half, far = rows // 2, places // 2
    (first,) = sends

    def slot(j):
        return line[j * rows : (j + 1) * rows, :c]

    forth = lax.ppermute(first[:half], "pts", onward).astype(f32)
    back = lax.ppermute(first[half:], "pts", backward).astype(f32)
    forth = jnp.pad(forth, ((0, half), (0, 0)))
    back = jnp.pad(back, ((half, 0), (0, 0)))
    for j in range(1, far):
        forth, back = (forth + slot(far + j)).astype(bf16), (back + slot(far - j)).astype(bf16)
        forth, back = lax.optimization_barrier((forth, back))
        forth = lax.ppermute(forth, "pts", onward).astype(f32)
        back = lax.ppermute(back, "pts", backward).astype(f32)
    return centre + slot(0) + forth + back


def short_sends(places):
    return [[7, 5], [1, 3], [4]] if places == 8 else [[places // 2]]


def short_sum(line, sends, centre):
    if lax.axis_size("pts") != 8:
        return owners_sum(line, sends, centre)
    onward, backward = ring_moves(8)
    far_onward, far_backward = ring_jumps(8)
    rows, c = centre.shape
    half = rows // 2
    slot = lambda j: line[j * rows : (j + 1) * rows, :c]
    ahead, behind, farthest = sends
    forth_far = lax.ppermute(farthest[:half], "pts", far_onward).astype(f32)
    back_far = lax.ppermute(farthest[half:], "pts", far_backward).astype(f32)
    forth = lax.ppermute(ahead, "pts", onward).astype(f32)
    back = lax.ppermute(behind, "pts", backward).astype(f32)
    forth_two = (slot(6) + forth[rows:] + jnp.pad(forth_far, ((0, half), (0, 0)))).astype(bf16)
    back_two = (slot(2) + back[rows:] + jnp.pad(back_far, ((half, 0), (0, 0)))).astype(bf16)
    forth_two, back_two = lax.optimization_barrier((forth_two, back_two))
    forth_two = lax.ppermute(forth_two, "pts", far_onward).astype(f32)
    back_two = lax.ppermute(back_two, "pts", far_backward).astype(f32)
    return centre + slot(0) + forth[:rows] + back[:rows] + forth_two + back_two


def weight_grad(diff, own, dz, dz_sum):
    first = jnp.dot(
        own.astype(f32).T, dz_sum, precision=lax.Precision.HIGHEST, preferred_element_type=f32
    )
    second = jnp.einsum("kgc,kgd->cd", diff, dz, preferred_element_type=f32)
    return jnp.concatenate([first, second], axis=0)


def per_device(
    points,
    lengths,
    neighbours_one,
    neighbours_two,
    weight_one,
    gain_one,
    shift_one,
    weight_two,
    gain_two,
    shift_two,
    cotangent,
):
    line_devices = lax.axis_size("pts")
    row_count = points.shape[0]
    line_length = line_devices * row_count
    table_one = short_table(points)

    norm_one, norm_two = jnp.stack([gain_one, shift_one]), jnp.stack([gain_two, shift_two])

    cloud_ends = jnp.cumsum(lengths)
    cloud_starts = cloud_ends - lengths
    line_first = lax.axis_index("loc") * line_length
    position = (
        line_first + lax.axis_index("pts") * row_count + jnp.arange(row_count, dtype=jnp.int32)
    )
    begins = (position[:, None] >= cloud_starts[None, :]) & (position[:, None] < cloud_ends[None, :])
    begin = jnp.sum(jnp.where(begins, cloud_starts[None, :], 0), axis=1) - line_first
    here = ring_place(lax.axis_index("pts"), line_devices)

    def slot_rows(neighbours):
        within = neighbours.T + begin[None, :]
        slot = (here - ring_place(within // row_count, line_devices)) % line_devices
        return slot * row_count + within % row_count

    def by_blocks(index):
        blocks = index.reshape(index.shape[0], -1, BLOCK)
        return blocks.transpose(1, 0, 2).reshape(-1, BLOCK)

    index_one = slot_rows(neighbours_one)
    index_two = slot_rows(neighbours_two)
    order_one, order_two = by_blocks(index_one), by_blocks(index_two)
    same_one = same_target(index_one)
    same_two = same_target(index_two)

    diff_one, stat_one = edge_stats(order_one, table_one, points, weight_one)
    stat_one = everyone(stat_one)
    act_one, slope_one, slope_sum, slope_moment = pool(
        diff_one, points, weight_one, stat_one, norm_one
    )
    table_two = line_table(act_one)
    diff_two, stat_two = edge_stats(order_two, table_two, act_one, weight_two)
    stat_two = everyone(stat_two)
    act_two, slope_two, sums_two = pool(
        diff_two, act_one, weight_two, stat_two, norm_two, cotangent
    )
    sums_two = everyone(sums_two)
    dz_two, dz_sum_two, centre_two, spread_two = edge_grads(
        slope_two,
        None,
        diff_two,
        act_one,
        weight_two,
        stat_two,
        norm_two,
        sums_two,
        same_two,
        False,
    )
    line_two, *sends_two = scatter_grads(
        order_two, spread_two, line_length, act_one.shape[1], [[line_devices // 2]]
    )
    grad_first = owners_sum(line_two, sends_two, centre_two)
    grad_first, dz_two, dz_sum_two = lax.optimization_barrier((grad_first, dz_two, dz_sum_two))
    weight_part_two = weight_grad(diff_two, act_one, dz_two, dz_sum_two)
    sums_one = jnp.stack(
        [jnp.sum(grad_first * slope_sum, axis=0), jnp.sum(grad_first * slope_moment, axis=0)]
    )
    sums_one = everyone(sums_one)
    centre_one, spread_one, weight_part_one = edge_grads(
        slope_one,
        grad_first,
        diff_one,
        points,
        weight_one,
        stat_one,
        norm_one,
        sums_one,
        same_one,
        True,
    )
    weights = jnp.concatenate([weight_part_two.reshape(-1, LANES), weight_part_one], axis=0)
    shares = exchange(shared(weights))
    line_one, *sends_one = scatter_grads(
        order_one, spread_one, line_length, points.shape[1], short_sends(line_devices)
    )
    shares, line_one, *sends_one = lax.optimization_barrier((shares, line_one, *sends_one))
    weights = everyone(jnp.sum(shares, axis=0))
    grad_points = short_sum(line_one, sends_one, centre_one)
    weights = weights.reshape(-1, LANES)
    grad_weight_two = weights[: -weight_one.shape[0]].reshape(weight_two.shape)
    grad_weight_one = weights[-weight_one.shape[0] :]

    def norm_grads(sums, gain, shift):
        sums = jnp.sum(sums, axis=0)
        return (2.0 * sums[1] - shift * sums[0]) / gain, sums[0]

    grad_gain_one, grad_shift_one = norm_grads(sums_one, gain_one, shift_one)
    grad_gain_two, grad_shift_two = norm_grads(sums_two, gain_two, shift_two)
    return (
        act_one,
        act_two,
        grad_points,
        grad_weight_one,
        grad_gain_one,
        grad_shift_one,
        grad_weight_two,
        grad_gain_two,
        grad_shift_two,
    )


def solution(mesh):
    rows, copied = P(("pts", "loc"), None), P()
    in_specs = (rows, copied, rows, rows) + (copied,) * 6 + (rows,)
    out_specs = (rows, rows, rows) + (copied,) * 6
    return jax.shard_map(
        per_device, mesh=mesh, in_specs=in_specs, out_specs=out_specs, check_vma=False
    )
```

```python
import functools
import math

import jax
import jax.numpy as jnp
from jax import lax
from jax.experimental import pallas as pl
from jax.experimental.pallas import tpu as pltpu
from jax.sharding import PartitionSpec as P

EPS = 1e-05
BLOCK = 128
GROUP = 8
ROWS = 16
AHEAD = 4
LOG2E = 1.0 / math.log(2.0)
LANES = 128
MIB = 1024 * 1024
BOTH = ("pts", "loc")

f32 = jnp.float32
bf16 = jnp.bfloat16


def params():
    return pltpu.CompilerParams(vmem_limit_bytes=52 * MIB)


def lasting(microseconds):
    return pl.CostEstimate(flops=0, transcendentals=0, bytes_accessed=3_000_000 * microseconds)


def smem():
    return pl.BlockSpec(memory_space=pltpu.SMEM)


def fold_rows(x):
    return jnp.sum(x.reshape(x.shape[0] // 8, 8, x.shape[1]), axis=0)


def tree(op, terms):
    while len(terms) > 1:
        pairs = [op(a, b) for a, b in zip(terms[::2], terms[1::2])]
        terms = pairs + terms[len(pairs) * 2 :]
    return terms[0]


def dot(a, b):
    return jnp.dot(a, b, preferred_element_type=f32)


def dot_t(a, b):
    return lax.dot_general(a, b, (((1,), (1,)), ((), ())), preferred_element_type=f32)


def edge_kernel(pieces, *refs):
    table_refs = refs[1 : 1 + pieces]
    idx_ref = refs[0]
    own_ref, w_ref, diff_ref, stat_ref, table, fresh, held, centre, pivot, sums, square = refs[
        1 + pieces :
    ]
    near, block, c = diff_ref.shape
    step_id = pl.program_id(0)
    last = pl.num_programs(0) - 1
    chunk = 4

    def project(own_sum, diff_sum):
        weight = w_ref[...].astype(f32)
        exact = functools.partial(
            jnp.dot, precision=lax.Precision.HIGHEST, preferred_element_type=f32
        )
        both = exact(own_sum, weight[:c]) + exact(diff_sum, weight[c:])
        return jnp.sum(both, axis=0, keepdims=True)

    @pl.when(step_id == 0)
    def _():
        first = 0
        for piece in table_refs:
            for r in range(0, piece.shape[0], 256):
                table[pl.ds(first + r, 256), :c] = piece[pl.ds(r, 256), :].astype(f32)
            first += piece.shape[0]
        sums[...] = jnp.zeros_like(sums)
        square[...] = jnp.zeros_like(square)

    @pl.when(step_id > 0)
    def _():
        for r in range(0, near * block, 256):
            held[pl.ds(r, 256), :] = fresh[pl.ds(r, 256), :]

    @pl.when(step_id == 1)
    def _():
        own = own_ref[...].astype(f32)
        diff_sum = jnp.zeros((8, c), f32)
        for k in range(near):
            diff_sum = diff_sum + fold_rows(held[pl.ds(k * block, block), :c] - own)
        own_sum = fold_rows(own) * float(near)
        pivot[...] = project(own_sum, diff_sum) * (1.0 / (near * block))

    def pick(k):
        base = pl.multiple_of(k * block, block)
        at = step_id * near + k
        rows = []
        for e in range(block + GROUP):
            if e < block:
                rows.append(table[pl.ds(idx_ref[at, e], 1), :])
            if e >= GROUP:
                fresh[pl.ds(base + (e - GROUP), 1), :] = rows[e - GROUP]

    def work(k, own, carry):
        diff_sum, total = carry
        at = pl.ds(pl.multiple_of(k * block, block), block)
        diff = (held[at, :c] - own).astype(bf16)
        diff_ref[k] = diff
        diff_sum = diff_sum + fold_rows(diff.astype(f32))
        z = dot(diff, w_ref[c:, :]) + centre[...]
        return diff_sum, total + fold_rows(z * z)

    @pl.when(step_id == 0)
    def _():
        def body(i, _):
            pick(i)
            return 0

        lax.fori_loop(0, near, body, 0)

    def finish(own, carry):
        sums[0] += fold_rows(own) * float(near)
        sums[1] += carry[0]
        square[...] += carry[1]

    def begin():
        centre[...] = dot(own_ref[...], w_ref[:c, :]) - pivot[...]
        zero = (jnp.zeros((8, c), f32), jnp.zeros_like(square[...]))
        return own_ref[...].astype(f32), zero

    @pl.when((step_id > 0) & (step_id < last))
    def _():
        own, zero = begin()

        def body(i, carry):
            for k in range(chunk):
                pick(i * chunk + k)
                carry = work(i * chunk + k, own_ref[...].astype(f32), carry)
            return carry

        finish(own, lax.fori_loop(0, near // chunk, body, zero))

    @pl.when(step_id == last)
    def _():
        own, carry = begin()
        for k in range(near):
            carry = work(k, own, carry)
        finish(own, carry)
        count = float(near * block * (pl.num_programs(0) - 1))
        mean = project(sums[0], sums[1]) / count
        off = mean - pivot[...]
        stat_ref[0:1, :] = mean
        stat_ref[1:2, :] = jnp.sum(square[...], axis=0, keepdims=True) - count * off * off


def edge_stats(index, pieces, own, weight):
    rows, c = own.shape
    d = weight.shape[1]
    blocks = rows // BLOCK
    near = index.shape[0] // blocks
    total = sum(piece.shape[0] for piece in pieces)
    before = lambda b: jnp.maximum(b - 1, 0)
    whole = lambda x: pl.BlockSpec(x.shape, lambda b: (0,) * x.ndim)
    return pl.pallas_call(
        functools.partial(edge_kernel, len(pieces)),
        grid=(blocks + 1,),
        out_shape=(
            jax.ShapeDtypeStruct((near, rows, c), bf16),
            jax.ShapeDtypeStruct((2, d), f32),
        ),
        in_specs=[smem()]
        + [whole(piece) for piece in pieces]
        + [pl.BlockSpec((BLOCK, c), lambda b: (before(b), 0)), whole(weight)],
        out_specs=(
            pl.BlockSpec((near, BLOCK, c), lambda b: (0, before(b), 0)),
            pl.BlockSpec((2, d), lambda b: (0, 0)),
        ),
        scratch_shapes=[
            pltpu.VMEM((total, LANES), f32),
            pltpu.VMEM((near * BLOCK, LANES), f32),
            pltpu.VMEM((near * BLOCK, LANES), f32),
            pltpu.VMEM((BLOCK, d), f32),
            pltpu.VMEM((1, d), f32),
            pltpu.VMEM((2, 8, c), f32),
            pltpu.VMEM((8, d), f32),
        ],
        compiler_params=params(),
        cost_estimate=lasting(22),
        name="edge_stats",
    )(index, *pieces, own, weight)


def moments(stat, edges_each):
    devices = stat.shape[0]
    means = stat[:, 0, :]
    mean = jnp.sum(means, axis=0, keepdims=True) * (1.0 / devices)
    off = means - mean
    m2 = jnp.sum(stat[:, 1, :], axis=0, keepdims=True) + edges_each * jnp.sum(
        off * off, axis=0, keepdims=True
    )
    return mean, lax.rsqrt(m2 * (1.0 / (edges_each * devices)) + EPS)


def pool_kernel(
    last, edges_each, diff_ref, own_ref, w_ref, stat_ref, norm_ref, *refs
):
    near, block, c = diff_ref.shape
    d = w_ref.shape[1]
    if last:
        cot_ref, pooled_ref, slope_ref, sums_ref, mixed, centre, upstream = refs
        upstream[...] = cot_ref[...].astype(f32)
    else:
        pooled_ref, slope_ref, sum_ref, moment_ref, mixed, centre = refs
    mean, inv = moments(stat_ref[...], edges_each)
    half_scale = norm_ref[0:1, :] * inv * 0.5
    centre[...] = (dot(own_ref[...], w_ref[:c, :]) - mean) * half_scale + norm_ref[1:2, :] * 0.5
    mixed[...] = dot(diff_ref[...].reshape(near * block, c), w_ref[c:, :]).reshape(near, block, d)
    if last:

        @pl.when(pl.program_id(0) == 0)
        def _():
            sums_ref[...] = jnp.zeros_like(sums_ref)

    for lane in range(0, d, 128):
        lanes = pl.ds(lane, 128)
        scale = jnp.broadcast_to(half_scale[:, lane : lane + 128], (ROWS, 128))

        def step(b, carry, lanes=lanes, scale=scale):
            at = pl.ds(pl.multiple_of(b * ROWS, ROWS), ROWS)
            offset = centre[at, lanes]
            active, bends = [], []
            for k in range(near):
                half = mixed[k, at, lanes] * scale + offset
                bent = jnp.tanh(half)
                t = 1.0 + bent
                a = half * t
                active.append(a)
                bends.append(t + a * (1.0 - bent))
            top = tree(jnp.maximum, active)
            powers = [jnp.exp2((a - top) * LOG2E) for a in active]
            total = tree(jnp.add, powers)
            pooled = top + jnp.log(total) - math.log(near)
            centre[at, lanes] = pooled
            factor = 0.5 / total
            if last:
                factor = factor * upstream[at, lanes]
            halves = [mixed[k, at, lanes] * scale + offset for k in range(near)]
            slopes = [(powers[k] * factor) * bends[k] for k in range(near)]
            slope_sum = tree(jnp.add, slopes)
            slope_moment = tree(jnp.add, [slopes[k] * halves[k] for k in range(near)])
            for k in range(near):
                slope_ref[k, at, lanes] = slopes[k]
            if not last:
                sum_ref[at, lanes] = slope_sum
                moment_ref[at, lanes] = slope_moment
                return carry
            return (carry[0] + slope_sum, carry[1] + slope_moment)

        zero = jnp.zeros((ROWS, 128), f32)
        carry = lax.fori_loop(0, block // ROWS, step, (zero, zero))
        if last:
            sums_ref[0:1, lanes] += jnp.sum(carry[0], axis=0, keepdims=True)
            sums_ref[1:2, lanes] += jnp.sum(carry[1], axis=0, keepdims=True)
    pooled_ref[...] = centre[...].astype(bf16)


def pool(diff, own, weight, stat, norm, cot=None):
    near, rows, c = diff.shape
    d = weight.shape[1]
    whole = lambda x: pl.BlockSpec(x.shape, lambda b: (0,) * x.ndim)
    by_block = lambda width: pl.BlockSpec((BLOCK, width), lambda b: (b, 0))
    by_edge = lambda width: pl.BlockSpec((near, BLOCK, width), lambda b: (0, b, 0))
    inputs = [diff, own, weight, stat, norm]
    in_specs = [by_edge(c), by_block(c), whole(weight), whole(stat), whole(norm)]
    row_out = lambda kind: (jax.ShapeDtypeStruct((rows, d), kind), by_block(d))
    outs = [row_out(bf16), (jax.ShapeDtypeStruct((near, rows, d), f32), by_edge(d))]
    if cot is None:
        outs += [row_out(f32), row_out(f32)]
    else:
        inputs.append(cot)
        in_specs.append(by_block(d))
        outs.append((jax.ShapeDtypeStruct((2, d), f32), pl.BlockSpec((2, d), lambda b: (0, 0))))
    return pl.pallas_call(
        functools.partial(pool_kernel, cot is not None, float(near * rows)),
        grid=(rows // BLOCK,),
        out_shape=tuple(o[0] for o in outs),
        in_specs=in_specs,
        out_specs=tuple(o[1] for o in outs),
        scratch_shapes=[pltpu.VMEM((near, BLOCK, d), f32)]
        + [pltpu.VMEM((BLOCK, d), f32)] * (1 if cot is None else 2),
        compiler_params=params(),
        cost_estimate=lasting(17 if cot is None else 32),
        name="pool",
    )(*inputs)


def grads_kernel(
    edges_each,
    inner,
    sends,
    idx_ref,
    slope_ref,
    upstream_ref,
    diff_ref,
    own_ref,
    w_ref,
    back_ref,
    stat_ref,
    norm_ref,
    grads_ref,
    same_ref,
    *refs,
):
    near, block, c = diff_ref.shape
    d = w_ref.shape[1]
    if inner:
        line_ref, dz_sum_ref, weight_ref, *send_refs, dz_ref = refs[:-7]
    else:
        line_ref, dz_sum_ref, dz_ref, *send_refs = refs[:-7]
    mixed, constant, fresh, held, even, odd, sem = refs[-7:]
    step_id = pl.program_id(0)
    last = pl.num_programs(0) - 1
    total, rows = even.shape[0], dz_sum_ref.shape[0]
    turns = block // 16 * (d // 128)
    share = near * block // turns

    def clear(i, _):
        at = pl.ds(pl.multiple_of(i * 256, 256), 256)
        even[at, :] = jnp.zeros((256, LANES), f32)
        odd[at, :] = jnp.zeros((256, LANES), f32)
        return 0

    def store(waiting, most):
        while len(waiting) > most:
            line, place, row = waiting.pop(0)
            line[place, :] = row

    def add(turn, edges, waiting):
        at = (step_id - 1) * turns + turn
        base = pl.multiple_of(turn * share, 16)
        for e in edges:
            line = (even, odd)[e // GROUP % 2]
            place = pl.ds(idx_ref[at, e], 1)
            waiting.append((line, place, line[place, :] + held[pl.ds(base + e, 1), :]))
            store(waiting, GROUP)

    def work(adding):
        edges = edges_each * stat_ref.shape[0]
        mean, inv = moments(stat_ref[...], edges_each)
        gain = norm_ref[0:1, :]
        sums = jnp.sum(grads_ref[...], axis=0)
        grad_shift = sums[0:1]
        grad_gain = (2.0 * sums[1:2] - norm_ref[1:2, :] * grad_shift) / gain
        alpha = gain * inv
        rate = alpha * inv * grad_gain * (1.0 / edges)
        constant[...] = alpha * grad_shift * (1.0 / edges) + rate * (
            dot(own_ref[...], w_ref[:c, :]) - mean
        )
        product = dot(diff_ref[...].reshape(near * block, c), w_ref[c:, :])
        mixed[...] = product.reshape(near, block, d)

        for lane in range(0, d, 128):
            lanes = pl.ds(lane, 128)
            wide_alpha = jnp.broadcast_to(alpha[:, lane : lane + 128], (16, 128))
            wide_rate = jnp.broadcast_to(rate[:, lane : lane + 128], (16, 128))

            def step(b, _, lane=lane, lanes=lanes, wide_alpha=wide_alpha, wide_rate=wide_rate):
                at = pl.ds(pl.multiple_of(b * 16, 16), 16)
                offset = constant[at, lanes]
                factor = wide_alpha
                if upstream_ref is not None:
                    factor = factor * upstream_ref[at, lanes]
                load = lambda k: (slope_ref[k, at, lanes], mixed[k, at, lanes])
                loaded = [load(k) for k in range(AHEAD)]
                dzs, waiting = [], []
                each = share // near
                for k in range(near):
                    if adding:
                        turn = lane // 128 * (block // 16) + b
                        add(turn, range(k * each, (k + 1) * each), waiting)
                    if k + AHEAD < near:
                        loaded.append(load(k + AHEAD))
                    slope, mix = loaded[k]
                    dzs.append((factor * slope - offset - wide_rate * mix).astype(bf16))
                    if k >= AHEAD:
                        dz_ref[k - AHEAD, at, lanes] = dzs[k - AHEAD]
                store(waiting, 0)
                for k in range(near - AHEAD, near):
                    dz_ref[k, at, lanes] = dzs[k]
                row = pl.multiple_of(step_id * block + b * 16, 16)
                dz_sum_ref[pl.ds(row, 16), lanes] = tree(jnp.add, [dz.astype(f32) for dz in dzs])
                return 0

            lax.fori_loop(0, block // 16, step, 0)

        flat = dz_ref[...].reshape(near * block, d)
        back = dot_t(flat, back_ref[...]).astype(bf16).reshape(near, block, LANES)
        for k in range(near):
            fresh[pl.ds(k * block, block), :] = dot(same_ref[k], back[k])
        if inner:
            weight_ref[...] += lax.dot_general(
                diff_ref[...].reshape(near * block, c),
                flat,
                (((0,), (0,)), ((), ())),
                preferred_element_type=f32,
            )

    @pl.when(step_id > 0)
    def _():
        for r in range(0, near * block, 256):
            held[pl.ds(r, 256), :] = fresh[pl.ds(r, 256), :]

    @pl.when(step_id == 0)
    def _():
        lax.fori_loop(0, total // 256, clear, 0)
        if inner:
            weight_ref[...] = jnp.zeros_like(weight_ref)
        work(False)

    @pl.when((step_id > 0) & (step_id < last))
    def _():
        work(True)

    @pl.when(step_id == last)
    def _():
        def rest(turn, _):
            waiting = []
            add(turn, range(share), waiting)
            store(waiting, 0)
            return 0

        lax.fori_loop(0, turns, rest, 0)

        def join(i, _):
            at = pl.ds(pl.multiple_of(i * 256, 256), 256)
            even[at, :] = even[at, :] + odd[at, :]
            return 0

        lax.fori_loop(0, total // 256, join, 0)
        copy = pltpu.make_async_copy(even, line_ref, sem)
        copy.start()
        for send_ref, slots in zip(send_refs, sends):
            for i, slot in enumerate(slots):
                values = even[pl.ds(slot * rows, rows), : send_ref.shape[1]]
                send_ref[pl.ds(i * rows, rows), :] = values.astype(bf16)
        copy.wait()


def edge_grads(order, slope, upstream, diff, own, weight, stat, norm, grads, same, total, sends):
    near, rows, c = diff.shape
    d = weight.shape[1]
    inner = upstream is not None
    blocks = rows // BLOCK
    now = lambda b: jnp.minimum(b, blocks - 1)
    whole = lambda x: pl.BlockSpec(x.shape, lambda b: (0,) * len(x.shape))
    by_block = lambda width: pl.BlockSpec((BLOCK, width), lambda b: (now(b), 0))
    by_edge = lambda width: pl.BlockSpec((near, BLOCK, width), lambda b: (0, now(b), 0))
    back = jnp.pad(weight[c:], ((0, LANES - c), (0, 0)))
    order = order.reshape(rows // 16 * (d // 128), -1)
    inputs = [order, slope, upstream, diff, own, weight, back, stat, norm, grads, same]
    in_specs = [
        smem(),
        by_edge(d),
        by_block(d),
        by_edge(c),
        by_block(c),
        whole(weight),
        whole(back),
        whole(stat),
        whole(norm),
        whole(grads),
        by_edge(BLOCK),
    ]
    body = functools.partial(grads_kernel, float(near * rows), inner, sends)
    if not inner:
        del inputs[2], in_specs[2]
        full = body
        body = lambda i, s, *rest: full(i, s, None, *rest)
    dz = jax.ShapeDtypeStruct((near, rows, d), bf16)
    dz_sum = jax.ShapeDtypeStruct((rows, d), f32)
    outs = [
        (jax.ShapeDtypeStruct((total, LANES), f32), pl.BlockSpec(memory_space=pl.ANY)),
        (dz_sum, whole(dz_sum)),
    ]
    scratch = [
        pltpu.VMEM((near, BLOCK, d), f32),
        pltpu.VMEM((BLOCK, d), f32),
        pltpu.VMEM((near * BLOCK, LANES), f32),
        pltpu.VMEM((near * BLOCK, LANES), f32),
        pltpu.VMEM((total, LANES), f32),
        pltpu.VMEM((total, LANES), f32),
        pltpu.SemaphoreType.DMA,
    ]
    if inner:
        part = jax.ShapeDtypeStruct((c, d), f32)
        outs.append((part, whole(part)))
        scratch.insert(0, pltpu.VMEM((near, BLOCK, d), bf16))
    else:
        outs.append((dz, by_edge(d)))
    for slots in sends:
        send = jax.ShapeDtypeStruct((len(slots) * rows, c), bf16)
        outs.append((send, whole(send)))
    return pl.pallas_call(
        body,
        grid=(blocks + 1,),
        out_shape=tuple(o[0] for o in outs),
        in_specs=in_specs,
        out_specs=tuple(o[1] for o in outs),
        scratch_shapes=scratch,
        compiler_params=params(),
        cost_estimate=lasting(40),
        name="edge_grads",
    )(*inputs)


def same_target(index):
    near, rows = index.shape
    blocks = index.reshape(near, rows // BLOCK, BLOCK)
    group = jnp.arange(BLOCK, dtype=jnp.int32) // GROUP
    equal = (blocks[:, :, :, None] == blocks[:, :, None, :]) & (group[:, None] == group[None, :])
    return equal.astype(bf16).reshape(near, rows, BLOCK)


def copies(x):
    return jnp.broadcast_to(x[None], (lax.axis_size(BOTH),) + x.shape)


def shared(x):
    devices = lax.axis_size(BOTH)
    return x.reshape(devices, x.shape[0] // devices, x.shape[1])


def exchange(shares):
    return lax.all_to_all(shares, BOTH, split_axis=0, concat_axis=0, tiled=True)


def everyone(x):
    return exchange(copies(x))


def ring_moves(places):
    ring = list(range(0, places, 2)) + list(range(1, places, 2))[::-1]
    onward = [(ring[i], ring[(i + 1) % places]) for i in range(places)]
    return onward, [(b, a) for a, b in onward]


def ring_place(device, places):
    return jnp.where(device % 2 == 0, device // 2, places - 1 - device // 2)


def ring_jumps(places):
    onward, backward = ring_moves(places)
    twice = lambda moves: [(a, dict(moves)[b]) for a, b in moves]
    return twice(onward), twice(backward)


def line_table(values):
    places = lax.axis_size("pts")
    onward, backward = ring_moves(places)
    rows, far = values.shape[0] // 2, places // 2
    behind, ahead = [values], [values]
    for _ in range(far - 1):
        behind.append(lax.ppermute(behind[-1], "pts", onward))
        ahead.append(lax.ppermute(ahead[-1], "pts", backward))
    farthest = [
        lax.ppermute(behind[-1][:rows], "pts", onward),
        lax.ppermute(ahead[-1][rows:], "pts", backward),
    ]
    return behind + farthest + ahead[:0:-1]


def owners_sum(line, sends, centre):
    places = lax.axis_size("pts")
    onward, backward = ring_moves(places)
    rows, c = centre.shape
    half, far = rows // 2, places // 2
    (first,) = sends

    def slot(j):
        return line[j * rows : (j + 1) * rows, :c]

    forth = lax.ppermute(first[:half], "pts", onward).astype(f32)
    back = lax.ppermute(first[half:], "pts", backward).astype(f32)
    forth = jnp.pad(forth, ((0, half), (0, 0)))
    back = jnp.pad(back, ((half, 0), (0, 0)))
    for j in range(1, far):
        forth, back = (forth + slot(far + j)).astype(bf16), (back + slot(far - j)).astype(bf16)
        forth, back = lax.optimization_barrier((forth, back))
        forth = lax.ppermute(forth, "pts", onward).astype(f32)
        back = lax.ppermute(back, "pts", backward).astype(f32)
    return centre + slot(0) + forth + back


def short_sends(places):
    return [[7, 5], [1, 3], [4]] if places == 8 else [[places // 2]]


def short_sum(line, sends, centre):
    if lax.axis_size("pts") != 8:
        return owners_sum(line, sends, centre)
    onward, backward = ring_moves(8)
    far_onward, far_backward = ring_jumps(8)
    rows, c = centre.shape
    half = rows // 2
    slot = lambda j: line[j * rows : (j + 1) * rows, :c]
    ahead, behind, farthest = sends
    forth_far = lax.ppermute(farthest[:half], "pts", far_onward).astype(f32)
    back_far = lax.ppermute(farthest[half:], "pts", far_backward).astype(f32)
    forth = lax.ppermute(ahead, "pts", onward).astype(f32)
    back = lax.ppermute(behind, "pts", backward).astype(f32)
    forth_two = (slot(6) + forth[rows:] + jnp.pad(forth_far, ((0, half), (0, 0)))).astype(bf16)
    back_two = (slot(2) + back[rows:] + jnp.pad(back_far, ((half, 0), (0, 0)))).astype(bf16)
    forth_two, back_two = lax.optimization_barrier((forth_two, back_two))
    forth_two = lax.ppermute(forth_two, "pts", far_onward).astype(f32)
    back_two = lax.ppermute(back_two, "pts", far_backward).astype(f32)
    return centre + slot(0) + forth[:rows] + back[:rows] + forth_two + back_two


def exact(a, b):
    return jnp.dot(a, b, precision=lax.Precision.HIGHEST, preferred_element_type=f32)


def centre_grad(dz_sum, weight):
    wide = weight.astype(f32)
    c = weight.shape[0] // 2
    return exact(dz_sum, (wide[:c] - wide[c:]).T)


def per_device(
    points,
    lengths,
    neighbours_one,
    neighbours_two,
    weight_one,
    gain_one,
    shift_one,
    weight_two,
    gain_two,
    shift_two,
    cotangent,
):
    line_devices = lax.axis_size("pts")
    row_count = points.shape[0]
    line_length = line_devices * row_count
    table_one = line_table(points)

    norm_one, norm_two = jnp.stack([gain_one, shift_one]), jnp.stack([gain_two, shift_two])

    cloud_ends = jnp.cumsum(lengths)
    cloud_starts = cloud_ends - lengths
    line_first = lax.axis_index("loc") * line_length
    position = (
        line_first + lax.axis_index("pts") * row_count + jnp.arange(row_count, dtype=jnp.int32)
    )
    begins = (position[:, None] >= cloud_starts[None, :]) & (position[:, None] < cloud_ends[None, :])
    begin = jnp.sum(jnp.where(begins, cloud_starts[None, :], 0), axis=1) - line_first
    here = ring_place(lax.axis_index("pts"), line_devices)

    def slot_rows(neighbours):
        within = neighbours.T + begin[None, :]
        slot = (here - ring_place(within // row_count, line_devices)) % line_devices
        return slot * row_count + within % row_count

    def by_blocks(index):
        blocks = index.reshape(index.shape[0], -1, BLOCK)
        return blocks.transpose(1, 0, 2).reshape(-1, BLOCK)

    index_one = slot_rows(neighbours_one)
    index_two = slot_rows(neighbours_two)
    order_one, order_two = by_blocks(index_one), by_blocks(index_two)
    same_one = same_target(index_one)
    same_two = same_target(index_two)

    diff_one, stat_one = edge_stats(order_one, table_one, points, weight_one)
    stat_one, order_two = lax.optimization_barrier((everyone(stat_one), order_two))
    act_one, slope_one, slope_sum, slope_moment = pool(
        diff_one, points, weight_one, stat_one, norm_one
    )
    table_two = line_table(act_one)
    diff_two, stat_two = edge_stats(order_two, table_two, act_one, weight_two)
    stat_two = everyone(stat_two)
    act_two, slope_two, sums_two = pool(
        diff_two, act_one, weight_two, stat_two, norm_two, cotangent
    )
    sums_two = everyone(sums_two)
    line_two, dz_sum_two, dz_two, *sends_two = edge_grads(
        order_two,
        slope_two,
        None,
        diff_two,
        act_one,
        weight_two,
        stat_two,
        norm_two,
        sums_two,
        same_two,
        line_length,
        [[line_devices // 2]],
    )
    grad_first = owners_sum(line_two, sends_two, centre_grad(dz_sum_two, weight_two))
    grad_first, dz_two, dz_sum_two = lax.optimization_barrier((grad_first, dz_two, dz_sum_two))
    first_two = exact(act_one.astype(f32).T, dz_sum_two)
    second_two = jnp.einsum("kgc,kgd->cd", diff_two, dz_two, preferred_element_type=f32)
    sums_one = jnp.stack(
        [jnp.sum(grad_first * slope_sum, axis=0), jnp.sum(grad_first * slope_moment, axis=0)]
    )
    sums_one = everyone(sums_one)
    line_one, dz_sum_one, second_one, *sends_one = edge_grads(
        order_one,
        slope_one,
        grad_first,
        diff_one,
        points,
        weight_one,
        stat_one,
        norm_one,
        sums_one,
        same_one,
        line_length,
        short_sends(line_devices),
    )
    first_one = exact(points.astype(f32).T, dz_sum_one)
    weights = jnp.concatenate(
        [first_two.reshape(-1, LANES), second_two.reshape(-1, LANES), first_one, second_one], axis=0
    )
    shares = exchange(shared(weights.astype(bf16)))
    weights = everyone(jnp.sum(shares.astype(f32), axis=0).astype(bf16))
    grad_points = short_sum(line_one, sends_one, centre_grad(dz_sum_one, weight_one))
    weights = weights.reshape(-1, LANES).astype(f32)
    grad_weight_two = weights[: -weight_one.shape[0]].reshape(weight_two.shape)
    grad_weight_one = weights[-weight_one.shape[0] :]

    def norm_grads(sums, gain, shift):
        sums = jnp.sum(sums, axis=0)
        return (2.0 * sums[1] - shift * sums[0]) / gain, sums[0]

    grad_gain_one, grad_shift_one = norm_grads(sums_one, gain_one, shift_one)
    grad_gain_two, grad_shift_two = norm_grads(sums_two, gain_two, shift_two)
    return (
        act_one,
        act_two,
        grad_points,
        grad_weight_one,
        grad_gain_one,
        grad_shift_one,
        grad_weight_two,
        grad_gain_two,
        grad_shift_two,
    )


def solution(mesh):
    rows, copied = P(("pts", "loc"), None), P()
    in_specs = (rows, copied, rows, rows) + (copied,) * 6 + (rows,)
    out_specs = (rows, rows, rows) + (copied,) * 6
    return jax.shard_map(
        per_device, mesh=mesh, in_specs=in_specs, out_specs=out_specs, check_vma=False
    )
```

```python
import functools
import math

import jax
import jax.numpy as jnp
from jax import lax
from jax.experimental import pallas as pl
from jax.experimental.pallas import tpu as pltpu
from jax.sharding import PartitionSpec as P

EPS = 1e-05
BLOCK = 128
GROUP = 8
ROWS = 16
AHEAD = 4
LOG2E = 1.0 / math.log(2.0)
LANES = 128
MIB = 1024 * 1024
BOTH = ("pts", "loc")

f32 = jnp.float32
bf16 = jnp.bfloat16


def params():
    return pltpu.CompilerParams(vmem_limit_bytes=52 * MIB)


def lasting(microseconds):
    return pl.CostEstimate(flops=0, transcendentals=0, bytes_accessed=3_000_000 * microseconds)


def smem():
    return pl.BlockSpec(memory_space=pltpu.SMEM)


def fold_rows(x):
    return jnp.sum(x.reshape(x.shape[0] // 8, 8, x.shape[1]), axis=0)


def tree(op, terms):
    while len(terms) > 1:
        pairs = [op(a, b) for a, b in zip(terms[::2], terms[1::2])]
        terms = pairs + terms[len(pairs) * 2 :]
    return terms[0]


def dot(a, b):
    return jnp.dot(a, b, preferred_element_type=f32)


def exact(a, b):
    return jnp.dot(a, b, precision=lax.Precision.HIGHEST, preferred_element_type=f32)


def dot_t(a, b):
    return lax.dot_general(a, b, (((1,), (1,)), ((), ())), preferred_element_type=f32)


def edge_kernel(pieces, *refs):
    table_refs = refs[1 : 1 + pieces]
    idx_ref = refs[0]
    own_ref, w_ref, diff_ref, stat_ref, table, centre, pivot, sums, square = refs[1 + pieces :]
    near, block, c = diff_ref.shape
    step_id = pl.program_id(0)
    last = pl.num_programs(0) - 1
    own_sum = fold_rows(own_ref[...].astype(f32)) * float(near)
    sublane = lax.broadcasted_iota(jnp.int32, (8, LANES), 0)
    zero = jnp.zeros((8, c), f32)
    none = jnp.zeros((8, w_ref.shape[1]), f32)

    def project(own_sum, diff_sum):
        weight = w_ref[...].astype(f32)
        both = exact(own_sum, weight[:c]) + exact(diff_sum, weight[c:])
        return jnp.sum(both, axis=0, keepdims=True)

    def pick(k, diff_sum):
        at = step_id * near + k
        for r in range(0, block, 16):
            halves = []
            for h in (r, r + 8):
                rows = None
                for j in range(8):
                    row = jnp.broadcast_to(table[pl.ds(idx_ref[at, h + j], 1), :], (8, LANES))
                    rows = row if j == 0 else jnp.where(sublane == j, row, rows)
                halves.append(rows[:, :c] - own_ref[pl.ds(r, 16), :].astype(f32)[h - r : h - r + 8])
            diff = jnp.concatenate(halves, axis=0).astype(bf16)
            diff_ref[k, pl.ds(r, 16), :] = diff
            diff_sum = diff_sum + fold_rows(diff.astype(f32))
        return diff_sum

    def deviate(k, total):
        z = dot(diff_ref[k], w_ref[c:, :]) + centre[...]
        return total + fold_rows(z * z)

    def add(diff_sum, total):
        sums[0] += own_sum
        sums[1] += diff_sum
        square[...] += total

    @pl.when(step_id == 0)
    def _():
        first = 0
        for piece in table_refs:
            for r in range(0, piece.shape[0], 256):
                table[pl.ds(first + r, 256), :c] = piece[pl.ds(r, 256), :].astype(f32)
            first += piece.shape[0]
        sums[...] = jnp.zeros_like(sums)
        square[...] = jnp.zeros_like(square)
        diff_sum = lax.fori_loop(0, near, pick, zero)
        pivot[...] = project(own_sum, diff_sum) * (1.0 / (near * block))
        centre[...] = dot(own_ref[...], w_ref[:c, :]) - pivot[...]
        add(diff_sum, lax.fori_loop(0, near, deviate, none))

    @pl.when(step_id > 0)
    def _():
        centre[...] = dot(own_ref[...], w_ref[:c, :]) - pivot[...]

        def both(k, carry):
            return pick(k, carry[0]), deviate(k - 1, carry[1])

        diff_sum, total = lax.fori_loop(1, near, both, (pick(0, zero), none))
        add(diff_sum, deviate(near - 1, total))

    @pl.when(step_id == last)
    def _():
        count = float(near * block * pl.num_programs(0))
        mean = project(sums[0], sums[1]) / count
        off = mean - pivot[...]
        stat_ref[0:1, :] = mean
        stat_ref[1:2, :] = jnp.sum(square[...], axis=0, keepdims=True) - count * off * off


def edge_stats(index, pieces, own, weight):
    rows, c = own.shape
    d = weight.shape[1]
    blocks = rows // BLOCK
    near = index.shape[0] // blocks
    total = sum(piece.shape[0] for piece in pieces)
    whole = lambda x: pl.BlockSpec(x.shape, lambda b: (0,) * x.ndim)
    return pl.pallas_call(
        functools.partial(edge_kernel, len(pieces)),
        grid=(blocks,),
        out_shape=(
            jax.ShapeDtypeStruct((near, rows, c), bf16),
            jax.ShapeDtypeStruct((2, d), f32),
        ),
        in_specs=[smem()]
        + [whole(piece) for piece in pieces]
        + [pl.BlockSpec((BLOCK, c), lambda b: (b, 0)), whole(weight)],
        out_specs=(
            pl.BlockSpec((near, BLOCK, c), lambda b: (0, b, 0)),
            pl.BlockSpec((2, d), lambda b: (0, 0)),
        ),
        scratch_shapes=[
            pltpu.VMEM((total, LANES), f32),
            pltpu.VMEM((BLOCK, d), f32),
            pltpu.VMEM((1, d), f32),
            pltpu.VMEM((2, 8, c), f32),
            pltpu.VMEM((8, d), f32),
        ],
        compiler_params=params(),
        cost_estimate=lasting(22),
        name="edge_stats",
    )(index, *pieces, own, weight)


def moments(stat, edges_each):
    devices = stat.shape[0]
    means = stat[:, 0, :]
    mean = jnp.sum(means, axis=0, keepdims=True) * (1.0 / devices)
    off = means - mean
    m2 = jnp.sum(stat[:, 1, :], axis=0, keepdims=True) + edges_each * jnp.sum(
        off * off, axis=0, keepdims=True
    )
    return mean, lax.rsqrt(m2 * (1.0 / (edges_each * devices)) + EPS)


def pool_kernel(
    last, edges_each, diff_ref, own_ref, w_ref, stat_ref, norm_ref, *refs
):
    near, block, c = diff_ref.shape
    d = w_ref.shape[1]
    if last:
        cot_ref, pooled_ref, slope_ref, sums_ref, mixed, centre, upstream = refs
        upstream[...] = cot_ref[...].astype(f32)
    else:
        pooled_ref, slope_ref, sum_ref, moment_ref, mixed, centre = refs
    mean, inv = moments(stat_ref[...], edges_each)
    half_scale = norm_ref[0:1, :] * inv * 0.5
    centre[...] = (dot(own_ref[...], w_ref[:c, :]) - mean) * half_scale + norm_ref[1:2, :] * 0.5
    mixed[...] = dot(diff_ref[...].reshape(near * block, c), w_ref[c:, :]).reshape(near, block, d)
    if last:

        @pl.when(pl.program_id(0) == 0)
        def _():
            sums_ref[...] = jnp.zeros_like(sums_ref)

    for lane in range(0, d, 128):
        lanes = pl.ds(lane, 128)
        scale = jnp.broadcast_to(half_scale[:, lane : lane + 128], (ROWS, 128))

        def step(b, carry, lanes=lanes, scale=scale):
            at = pl.ds(pl.multiple_of(b * ROWS, ROWS), ROWS)
            offset = centre[at, lanes]
            active, bends = [], []
            for k in range(near):
                half = mixed[k, at, lanes] * scale + offset
                bent = jnp.tanh(half)
                t = 1.0 + bent
                a = half * t
                active.append(a)
                bends.append(t + a * (1.0 - bent))
            top = tree(jnp.maximum, active)
            powers = [jnp.exp2((a - top) * LOG2E) for a in active]
            total = tree(jnp.add, powers)
            pooled = top + jnp.log(total) - math.log(near)
            centre[at, lanes] = pooled
            factor = 0.5 / total
            if last:
                factor = factor * upstream[at, lanes]
            halves = [mixed[k, at, lanes] * scale + offset for k in range(near)]
            slopes = [(powers[k] * factor) * bends[k] for k in range(near)]
            slope_sum = tree(jnp.add, slopes)
            slope_moment = tree(jnp.add, [slopes[k] * halves[k] for k in range(near)])
            for k in range(near):
                slope_ref[k, at, lanes] = slopes[k]
            if not last:
                sum_ref[at, lanes] = slope_sum
                moment_ref[at, lanes] = slope_moment
                return carry
            return (carry[0] + slope_sum, carry[1] + slope_moment)

        zero = jnp.zeros((ROWS, 128), f32)
        carry = lax.fori_loop(0, block // ROWS, step, (zero, zero))
        if last:
            sums_ref[0:1, lanes] += jnp.sum(carry[0], axis=0, keepdims=True)
            sums_ref[1:2, lanes] += jnp.sum(carry[1], axis=0, keepdims=True)
    pooled_ref[...] = centre[...].astype(bf16)


def pool(diff, own, weight, stat, norm, cot=None):
    near, rows, c = diff.shape
    d = weight.shape[1]
    whole = lambda x: pl.BlockSpec(x.shape, lambda b: (0,) * x.ndim)
    by_block = lambda width: pl.BlockSpec((BLOCK, width), lambda b: (b, 0))
    by_edge = lambda width: pl.BlockSpec((near, BLOCK, width), lambda b: (0, b, 0))
    inputs = [diff, own, weight, stat, norm]
    in_specs = [by_edge(c), by_block(c), whole(weight), whole(stat), whole(norm)]
    row_out = lambda kind: (jax.ShapeDtypeStruct((rows, d), kind), by_block(d))
    outs = [row_out(bf16), (jax.ShapeDtypeStruct((near, rows, d), f32), by_edge(d))]
    if cot is None:
        outs += [row_out(f32), row_out(f32)]
    else:
        inputs.append(cot)
        in_specs.append(by_block(d))
        outs.append((jax.ShapeDtypeStruct((2, d), f32), pl.BlockSpec((2, d), lambda b: (0, 0))))
    return pl.pallas_call(
        functools.partial(pool_kernel, cot is not None, float(near * rows)),
        grid=(rows // BLOCK,),
        out_shape=tuple(o[0] for o in outs),
        in_specs=in_specs,
        out_specs=tuple(o[1] for o in outs),
        scratch_shapes=[pltpu.VMEM((near, BLOCK, d), f32)]
        + [pltpu.VMEM((BLOCK, d), f32)] * (1 if cot is None else 2),
        compiler_params=params(),
        cost_estimate=lasting(17 if cot is None else 32),
        name="pool",
    )(*inputs)


def grads_kernel(
    edges_each,
    inner,
    sends,
    idx_ref,
    slope_ref,
    upstream_ref,
    diff_ref,
    own_ref,
    w_ref,
    back_ref,
    stat_ref,
    norm_ref,
    grads_ref,
    same_ref,
    *refs,
):
    near, block, c = diff_ref.shape
    d = w_ref.shape[1]
    if inner:
        line_ref, dz_sum_ref, weight_ref, *send_refs, dz_ref = refs[:-7]
    else:
        line_ref, dz_sum_ref, dz_ref, *send_refs = refs[:-7]
    mixed, constant, fresh, held, even, odd, sem = refs[-7:]
    step_id = pl.program_id(0)
    last = pl.num_programs(0) - 1
    total, rows = even.shape[0], dz_sum_ref.shape[0]
    turns = block // 16 * (d // 128)
    share = near * block // turns

    def clear(i, _):
        at = pl.ds(pl.multiple_of(i * 256, 256), 256)
        even[at, :] = jnp.zeros((256, LANES), f32)
        odd[at, :] = jnp.zeros((256, LANES), f32)
        return 0

    def store(waiting, most):
        while len(waiting) > most:
            line, place, row = waiting.pop(0)
            line[place, :] = row

    def add(turn, edges, waiting):
        at = (step_id - 1) * turns + turn
        base = pl.multiple_of(turn * share, 16)
        for e in edges:
            line = (even, odd)[e // GROUP % 2]
            if e % GROUP == 0:
                grads = held[pl.ds(base + e, GROUP), :]
            place = pl.ds(idx_ref[at, e], 1)
            row = grads[e % GROUP : e % GROUP + 1]
            waiting.append((line, place, line[place, :] + row))
            store(waiting, GROUP)

    def work(adding):
        edges = edges_each * stat_ref.shape[0]
        mean, inv = moments(stat_ref[...], edges_each)
        gain = norm_ref[0:1, :]
        sums = jnp.sum(grads_ref[...], axis=0)
        grad_shift = sums[0:1]
        grad_gain = (2.0 * sums[1:2] - norm_ref[1:2, :] * grad_shift) / gain
        alpha = gain * inv
        rate = alpha * inv * grad_gain * (1.0 / edges)
        constant[...] = alpha * grad_shift * (1.0 / edges) + rate * (
            dot(own_ref[...], w_ref[:c, :]) - mean
        )
        product = dot(diff_ref[...].reshape(near * block, c), w_ref[c:, :])
        mixed[...] = product.reshape(near, block, d)

        for lane in range(0, d, 128):
            lanes = pl.ds(lane, 128)
            wide_alpha = jnp.broadcast_to(alpha[:, lane : lane + 128], (16, 128))
            wide_rate = jnp.broadcast_to(rate[:, lane : lane + 128], (16, 128))

            def step(b, _, lane=lane, lanes=lanes, wide_alpha=wide_alpha, wide_rate=wide_rate):
                at = pl.ds(pl.multiple_of(b * 16, 16), 16)
                offset = constant[at, lanes]
                factor = wide_alpha
                if upstream_ref is not None:
                    factor = factor * upstream_ref[at, lanes]
                load = lambda k: (slope_ref[k, at, lanes], mixed[k, at, lanes])
                loaded = [load(k) for k in range(AHEAD)]
                dzs, waiting = [], []
                each = share // near
                for k in range(near):
                    if adding:
                        turn = lane // 128 * (block // 16) + b
                        add(turn, range(k * each, (k + 1) * each), waiting)
                    if k + AHEAD < near:
                        loaded.append(load(k + AHEAD))
                    slope, mix = loaded[k]
                    dzs.append((factor * slope - offset - wide_rate * mix).astype(bf16))
                    if k >= AHEAD:
                        dz_ref[k - AHEAD, at, lanes] = dzs[k - AHEAD]
                store(waiting, 0)
                for k in range(near - AHEAD, near):
                    dz_ref[k, at, lanes] = dzs[k]
                row = pl.multiple_of(step_id * block + b * 16, 16)
                dz_sum_ref[pl.ds(row, 16), lanes] = tree(jnp.add, [dz.astype(f32) for dz in dzs])
                return 0

            lax.fori_loop(0, block // 16, step, 0)

        flat = dz_ref[...].reshape(near * block, d)
        back = dot_t(flat, back_ref[...]).astype(bf16).reshape(near, block, LANES)
        for k in range(near):
            fresh[pl.ds(k * block, block), :] = dot(same_ref[k], back[k])
        if inner:
            weight_ref[...] += lax.dot_general(
                diff_ref[...].reshape(near * block, c),
                flat,
                (((0,), (0,)), ((), ())),
                preferred_element_type=f32,
            )

    @pl.when(step_id > 0)
    def _():
        for r in range(0, near * block, 256):
            held[pl.ds(r, 256), :] = fresh[pl.ds(r, 256), :]

    @pl.when(step_id == 0)
    def _():
        lax.fori_loop(0, total // 256, clear, 0)
        if inner:
            weight_ref[...] = jnp.zeros_like(weight_ref)
        work(False)

    @pl.when((step_id > 0) & (step_id < last))
    def _():
        work(True)

    @pl.when(step_id == last)
    def _():
        def rest(turn, _):
            waiting = []
            add(turn, range(share), waiting)
            store(waiting, 0)
            return 0

        lax.fori_loop(0, turns, rest, 0)

        def join(i, _):
            at = pl.ds(pl.multiple_of(i * 256, 256), 256)
            even[at, :] = even[at, :] + odd[at, :]
            return 0

        lax.fori_loop(0, total // 256, join, 0)
        copy = pltpu.make_async_copy(even, line_ref, sem)
        copy.start()
        for send_ref, slots in zip(send_refs, sends):
            for i, slot in enumerate(slots):
                values = even[pl.ds(slot * rows, rows), : send_ref.shape[1]]
                send_ref[pl.ds(i * rows, rows), :] = values.astype(bf16)
        copy.wait()


def edge_grads(order, slope, upstream, diff, own, weight, stat, norm, grads, same, total, sends):
    near, rows, c = diff.shape
    d = weight.shape[1]
    inner = upstream is not None
    blocks = rows // BLOCK
    now = lambda b: jnp.minimum(b, blocks - 1)
    whole = lambda x: pl.BlockSpec(x.shape, lambda b: (0,) * len(x.shape))
    by_block = lambda width: pl.BlockSpec((BLOCK, width), lambda b: (now(b), 0))
    by_edge = lambda width: pl.BlockSpec((near, BLOCK, width), lambda b: (0, now(b), 0))
    back = jnp.pad(weight[c:], ((0, LANES - c), (0, 0)))
    order = order.reshape(rows // 16 * (d // 128), -1)
    inputs = [order, slope, upstream, diff, own, weight, back, stat, norm, grads, same]
    in_specs = [
        smem(),
        by_edge(d),
        by_block(d),
        by_edge(c),
        by_block(c),
        whole(weight),
        whole(back),
        whole(stat),
        whole(norm),
        whole(grads),
        by_edge(BLOCK),
    ]
    body = functools.partial(grads_kernel, float(near * rows), inner, sends)
    if not inner:
        del inputs[2], in_specs[2]
        full = body
        body = lambda i, s, *rest: full(i, s, None, *rest)
    dz = jax.ShapeDtypeStruct((near, rows, d), bf16)
    dz_sum = jax.ShapeDtypeStruct((rows, d), f32)
    outs = [
        (jax.ShapeDtypeStruct((total, LANES), f32), pl.BlockSpec(memory_space=pl.ANY)),
        (dz_sum, whole(dz_sum)),
    ]
    scratch = [
        pltpu.VMEM((near, BLOCK, d), f32),
        pltpu.VMEM((BLOCK, d), f32),
        pltpu.VMEM((near * BLOCK, LANES), f32),
        pltpu.VMEM((near * BLOCK, LANES), f32),
        pltpu.VMEM((total, LANES), f32),
        pltpu.VMEM((total, LANES), f32),
        pltpu.SemaphoreType.DMA,
    ]
    if inner:
        part = jax.ShapeDtypeStruct((c, d), f32)
        outs.append((part, whole(part)))
        scratch.insert(0, pltpu.VMEM((near, BLOCK, d), bf16))
    else:
        outs.append((dz, by_edge(d)))
    for slots in sends:
        send = jax.ShapeDtypeStruct((len(slots) * rows, c), bf16)
        outs.append((send, whole(send)))
    return pl.pallas_call(
        body,
        grid=(blocks + 1,),
        out_shape=tuple(o[0] for o in outs),
        in_specs=in_specs,
        out_specs=tuple(o[1] for o in outs),
        scratch_shapes=scratch,
        compiler_params=params(),
        cost_estimate=lasting(40),
        name="edge_grads",
    )(*inputs)


def same_target(index):
    near, rows = index.shape
    blocks = index.reshape(near, rows // BLOCK, BLOCK)
    group = jnp.arange(BLOCK, dtype=jnp.int32) // GROUP
    equal = (blocks[:, :, :, None] == blocks[:, :, None, :]) & (group[:, None] == group[None, :])
    return equal.astype(bf16).reshape(near, rows, BLOCK)


def copies(x):
    return jnp.broadcast_to(x[None], (lax.axis_size(BOTH),) + x.shape)


def shared(x):
    devices = lax.axis_size(BOTH)
    return x.reshape(devices, x.shape[0] // devices, x.shape[1])


def exchange(shares):
    return lax.all_to_all(shares, BOTH, split_axis=0, concat_axis=0, tiled=True)


def everyone(x):
    return exchange(copies(x))


def ring_moves(places):
    ring = list(range(0, places, 2)) + list(range(1, places, 2))[::-1]
    onward = [(ring[i], ring[(i + 1) % places]) for i in range(places)]
    return onward, [(b, a) for a, b in onward]


def ring_place(device, places):
    return jnp.where(device % 2 == 0, device // 2, places - 1 - device // 2)


def ring_jumps(places):
    onward, backward = ring_moves(places)
    twice = lambda moves: [(a, dict(moves)[b]) for a, b in moves]
    return twice(onward), twice(backward)


def line_table(values):
    places = lax.axis_size("pts")
    onward, backward = ring_moves(places)
    rows, far = values.shape[0] // 2, places // 2
    behind, ahead = [values], [values]
    for _ in range(far - 1):
        behind.append(lax.ppermute(behind[-1], "pts", onward))
        ahead.append(lax.ppermute(ahead[-1], "pts", backward))
    farthest = [
        lax.ppermute(behind[-1][:rows], "pts", onward),
        lax.ppermute(ahead[-1][rows:], "pts", backward),
    ]
    return behind + farthest + ahead[:0:-1]


def owners_sum(line, sends, centre):
    places = lax.axis_size("pts")
    onward, backward = ring_moves(places)
    rows, c = centre.shape
    half, far = rows // 2, places // 2
    (first,) = sends

    def slot(j):
        return line[j * rows : (j + 1) * rows, :c]

    forth = lax.ppermute(first[:half], "pts", onward).astype(f32)
    back = lax.ppermute(first[half:], "pts", backward).astype(f32)
    forth = jnp.pad(forth, ((0, half), (0, 0)))
    back = jnp.pad(back, ((half, 0), (0, 0)))
    for j in range(1, far):
        forth, back = (forth + slot(far + j)).astype(bf16), (back + slot(far - j)).astype(bf16)
        forth, back = lax.optimization_barrier((forth, back))
        forth = lax.ppermute(forth, "pts", onward).astype(f32)
        back = lax.ppermute(back, "pts", backward).astype(f32)
    return centre + slot(0) + forth + back


def short_sends(places):
    return [[7, 5], [1, 3], [4]] if places == 8 else [[places // 2]]


def short_sum(line, sends, centre):
    if lax.axis_size("pts") != 8:
        return owners_sum(line, sends, centre)
    onward, backward = ring_moves(8)
    far_onward, far_backward = ring_jumps(8)
    rows, c = centre.shape
    half = rows // 2
    slot = lambda j: line[j * rows : (j + 1) * rows, :c]
    ahead, behind, farthest = sends
    forth_far = lax.ppermute(farthest[:half], "pts", far_onward).astype(f32)
    back_far = lax.ppermute(farthest[half:], "pts", far_backward).astype(f32)
    forth = lax.ppermute(ahead, "pts", onward).astype(f32)
    back = lax.ppermute(behind, "pts", backward).astype(f32)
    forth_two = (slot(6) + forth[rows:] + jnp.pad(forth_far, ((0, half), (0, 0)))).astype(bf16)
    back_two = (slot(2) + back[rows:] + jnp.pad(back_far, ((half, 0), (0, 0)))).astype(bf16)
    forth_two, back_two = lax.optimization_barrier((forth_two, back_two))
    forth_two = lax.ppermute(forth_two, "pts", far_onward).astype(f32)
    back_two = lax.ppermute(back_two, "pts", far_backward).astype(f32)
    return centre + slot(0) + forth[:rows] + back[:rows] + forth_two + back_two


def centre_grad(dz_sum, weight):
    wide = weight.astype(f32)
    c = weight.shape[0] // 2
    return exact(dz_sum, (wide[:c] - wide[c:]).T)


def per_device(
    points,
    lengths,
    neighbours_one,
    neighbours_two,
    weight_one,
    gain_one,
    shift_one,
    weight_two,
    gain_two,
    shift_two,
    cotangent,
):
    line_devices = lax.axis_size("pts")
    row_count = points.shape[0]
    line_length = line_devices * row_count
    table_one = line_table(points)

    norm_one, norm_two = jnp.stack([gain_one, shift_one]), jnp.stack([gain_two, shift_two])

    cloud_ends = jnp.cumsum(lengths)
    cloud_starts = cloud_ends - lengths
    line_first = lax.axis_index("loc") * line_length
    position = (
        line_first + lax.axis_index("pts") * row_count + jnp.arange(row_count, dtype=jnp.int32)
    )
    begins = (position[:, None] >= cloud_starts[None, :]) & (position[:, None] < cloud_ends[None, :])
    begin = jnp.sum(jnp.where(begins, cloud_starts[None, :], 0), axis=1) - line_first
    here = ring_place(lax.axis_index("pts"), line_devices)

    def slot_rows(neighbours):
        within = neighbours.T + begin[None, :]
        slot = (here - ring_place(within // row_count, line_devices)) % line_devices
        return slot * row_count + within % row_count

    def by_blocks(index):
        blocks = index.reshape(index.shape[0], -1, BLOCK)
        return blocks.transpose(1, 0, 2).reshape(-1, BLOCK)

    index_one = slot_rows(neighbours_one)
    index_two = slot_rows(neighbours_two)
    order_one, order_two = by_blocks(index_one), by_blocks(index_two)
    same_one = same_target(index_one)
    same_two = same_target(index_two)

    diff_one, stat_one = edge_stats(order_one, table_one, points, weight_one)
    stat_one, order_two = lax.optimization_barrier((everyone(stat_one), order_two))
    act_one, slope_one, slope_sum, slope_moment = pool(
        diff_one, points, weight_one, stat_one, norm_one
    )
    table_two = line_table(act_one)
    diff_two, stat_two = edge_stats(order_two, table_two, act_one, weight_two)
    stat_two = everyone(stat_two)
    act_two, slope_two, sums_two = pool(
        diff_two, act_one, weight_two, stat_two, norm_two, cotangent
    )
    sums_two = everyone(sums_two)
    line_two, dz_sum_two, dz_two, *sends_two = edge_grads(
        order_two,
        slope_two,
        None,
        diff_two,
        act_one,
        weight_two,
        stat_two,
        norm_two,
        sums_two,
        same_two,
        line_length,
        [[line_devices // 2]],
    )
    grad_first = owners_sum(line_two, sends_two, centre_grad(dz_sum_two, weight_two))
    grad_first, dz_two, dz_sum_two = lax.optimization_barrier((grad_first, dz_two, dz_sum_two))
    first_two = exact(act_one.astype(f32).T, dz_sum_two)
    second_two = jnp.einsum("kgc,kgd->cd", diff_two, dz_two, preferred_element_type=f32)
    sums_one = jnp.stack(
        [jnp.sum(grad_first * slope_sum, axis=0), jnp.sum(grad_first * slope_moment, axis=0)]
    )
    sums_one = everyone(sums_one)
    line_one, dz_sum_one, second_one, *sends_one = edge_grads(
        order_one,
        slope_one,
        grad_first,
        diff_one,
        points,
        weight_one,
        stat_one,
        norm_one,
        sums_one,
        same_one,
        line_length,
        short_sends(line_devices),
    )
    first_one = exact(points.astype(f32).T, dz_sum_one)
    weights = jnp.concatenate(
        [first_two.reshape(-1, LANES), second_two.reshape(-1, LANES), first_one, second_one], axis=0
    )
    shares = exchange(shared(weights.astype(bf16)))
    weights = everyone(jnp.sum(shares.astype(f32), axis=0).astype(bf16))
    grad_points = short_sum(line_one, sends_one, centre_grad(dz_sum_one, weight_one))
    weights = weights.reshape(-1, LANES).astype(f32)
    grad_weight_two = weights[: -weight_one.shape[0]].reshape(weight_two.shape)
    grad_weight_one = weights[-weight_one.shape[0] :]

    def norm_grads(sums, gain, shift):
        sums = jnp.sum(sums, axis=0)
        return (2.0 * sums[1] - shift * sums[0]) / gain, sums[0]

    grad_gain_one, grad_shift_one = norm_grads(sums_one, gain_one, shift_one)
    grad_gain_two, grad_shift_two = norm_grads(sums_two, gain_two, shift_two)
    return (
        act_one,
        act_two,
        grad_points,
        grad_weight_one,
        grad_gain_one,
        grad_shift_one,
        grad_weight_two,
        grad_gain_two,
        grad_shift_two,
    )


def solution(mesh):
    rows, copied = P(("pts", "loc"), None), P()
    in_specs = (rows, copied, rows, rows) + (copied,) * 6 + (rows,)
    out_specs = (rows, rows, rows) + (copied,) * 6
    return jax.shard_map(
        per_device, mesh=mesh, in_specs=in_specs, out_specs=out_specs, check_vma=False
    )
```

```python
import functools
import math

import jax
import jax.numpy as jnp
from jax import lax
from jax.experimental import pallas as pl
from jax.experimental.pallas import tpu as pltpu
from jax.sharding import PartitionSpec as P

EPS = 1e-05
BLOCK = 128
GROUP = 8
ROWS = 16
AHEAD = 4
LOG2E = 1.0 / math.log(2.0)
LANES = 128
MIB = 1024 * 1024
BOTH = ("pts", "loc")

f32 = jnp.float32
bf16 = jnp.bfloat16


def params():
    return pltpu.CompilerParams(vmem_limit_bytes=52 * MIB)


def lasting(microseconds):
    return pl.CostEstimate(flops=0, transcendentals=0, bytes_accessed=3_000_000 * microseconds)


def smem():
    return pl.BlockSpec(memory_space=pltpu.SMEM)


def fold_rows(x):
    return jnp.sum(x.reshape(x.shape[0] // 8, 8, x.shape[1]), axis=0)


def tree(op, terms):
    while len(terms) > 1:
        pairs = [op(a, b) for a, b in zip(terms[::2], terms[1::2])]
        terms = pairs + terms[len(pairs) * 2 :]
    return terms[0]


def dot(a, b):
    return jnp.dot(a, b, preferred_element_type=f32)


def exact(a, b):
    return jnp.dot(a, b, precision=lax.Precision.HIGHEST, preferred_element_type=f32)


def dot_t(a, b):
    return lax.dot_general(a, b, (((1,), (1,)), ((), ())), preferred_element_type=f32)


def edge_kernel(pieces, *refs):
    table_refs = refs[1 : 1 + pieces]
    idx_ref = refs[0]
    own_ref, w_ref, diff_ref, z_ref, stat_ref, pivot_ref, table, rows, centre, sums, square = refs[
        1 + pieces :
    ]
    near, block, c = diff_ref.shape
    step_id = pl.program_id(0)
    last = pl.num_programs(0) - 1
    chunk = 4

    def project(own_sum, diff_sum):
        weight = w_ref[...].astype(f32)
        both = exact(own_sum, weight[:c]) + exact(diff_sum, weight[c:])
        return jnp.sum(both, axis=0, keepdims=True)

    @pl.when(step_id == 0)
    def _():
        first = 0
        for piece in table_refs:
            for r in range(0, piece.shape[0], 256):
                table[pl.ds(first + r, 256), :c] = piece[pl.ds(r, 256), :].astype(f32)
            first += piece.shape[0]
        sums[...] = jnp.zeros_like(sums)
        square[...] = jnp.zeros_like(square)

    @pl.when(step_id == 1)
    def _():
        own = own_ref[...].astype(f32)
        diff_sum = jnp.zeros((8, c), f32)
        for k in range(near):
            diff_sum = diff_sum + fold_rows(rows[pl.ds(k * block, block), :c] - own)
        own_sum = fold_rows(own) * float(near)
        pivot_ref[...] = project(own_sum, diff_sum) * (1.0 / (near * block))

    def pick(k):
        base = pl.multiple_of(k * block, block)
        at = step_id * near + k
        waiting = []
        for e in range(block + GROUP):
            if e < block:
                waiting.append(table[pl.ds(idx_ref[at, e], 1), :])
            if e >= GROUP:
                rows[pl.ds(base + (e - GROUP), 1), :] = waiting[e - GROUP]

    def work(k, own, carry):
        diff_sum, total = carry
        at = pl.ds(pl.multiple_of(k * block, block), block)
        diff = (rows[at, :c] - own).astype(bf16)
        diff_ref[k] = diff
        diff_sum = diff_sum + fold_rows(diff.astype(f32))
        z = dot(diff, w_ref[c:, :]) + centre[...]
        z_ref[k] = z
        return diff_sum, total + fold_rows(z * z)

    @pl.when(step_id == 0)
    def _():
        def body(i, _):
            pick(i)
            return 0

        lax.fori_loop(0, near, body, 0)

    def finish(own, carry):
        sums[0] += fold_rows(own) * float(near)
        sums[1] += carry[0]
        square[...] += carry[1]

    def begin():
        centre[...] = dot(own_ref[...], w_ref[:c, :]) - pivot_ref[...]
        zero = (jnp.zeros((8, c), f32), jnp.zeros_like(square[...]))
        return own_ref[...].astype(f32), zero

    @pl.when((step_id > 0) & (step_id < last))
    def _():
        own, zero = begin()

        def body(i, carry):
            for k in range(chunk):
                carry = work(i * chunk + k, own_ref[...].astype(f32), carry)
                pick(i * chunk + k)
            return carry

        finish(own, lax.fori_loop(0, near // chunk, body, zero))

    @pl.when(step_id == last)
    def _():
        own, carry = begin()
        for k in range(near):
            carry = work(k, own, carry)
        finish(own, carry)
        count = float(near * block * (pl.num_programs(0) - 1))
        mean = project(sums[0], sums[1]) / count
        off = mean - pivot_ref[...]
        m2 = jnp.sum(square[...], axis=0, keepdims=True) - count * off * off
        stat_ref[...] = jnp.broadcast_to(jnp.concatenate([mean, m2], axis=0)[None], stat_ref.shape)


def edge_stats(index, pieces, own, weight):
    rows, c = own.shape
    d = weight.shape[1]
    blocks = rows // BLOCK
    near = index.shape[0] // blocks
    total = sum(piece.shape[0] for piece in pieces)
    before = lambda b: jnp.maximum(b - 1, 0)
    whole = lambda x: pl.BlockSpec(x.shape, lambda b: (0,) * len(x.shape))
    stat = jax.ShapeDtypeStruct((lax.axis_size(BOTH), 2, d), f32)
    pivot = jax.ShapeDtypeStruct((1, d), f32)
    return pl.pallas_call(
        functools.partial(edge_kernel, len(pieces)),
        grid=(blocks + 1,),
        out_shape=(
            jax.ShapeDtypeStruct((near, rows, c), bf16),
            jax.ShapeDtypeStruct((near, rows, d), f32),
            stat,
            pivot,
        ),
        in_specs=[smem()]
        + [whole(piece) for piece in pieces]
        + [pl.BlockSpec((BLOCK, c), lambda b: (before(b), 0)), whole(weight)],
        out_specs=(
            pl.BlockSpec((near, BLOCK, c), lambda b: (0, before(b), 0)),
            pl.BlockSpec((near, BLOCK, d), lambda b: (0, before(b), 0)),
            whole(stat),
            whole(pivot),
        ),
        scratch_shapes=[
            pltpu.VMEM((total, LANES), f32),
            pltpu.VMEM((near * BLOCK, LANES), f32),
            pltpu.VMEM((BLOCK, d), f32),
            pltpu.VMEM((2, 8, c), f32),
            pltpu.VMEM((8, d), f32),
        ],
        compiler_params=params(),
        cost_estimate=lasting(22),
        name="edge_stats",
    )(index, *pieces, own, weight)


def moments(stat, edges_each):
    devices = stat.shape[0]
    means = stat[:, 0, :]
    mean = jnp.sum(means, axis=0, keepdims=True) * (1.0 / devices)
    off = means - mean
    m2 = jnp.sum(stat[:, 1, :], axis=0, keepdims=True) + edges_each * jnp.sum(
        off * off, axis=0, keepdims=True
    )
    return mean, lax.rsqrt(m2 * (1.0 / (edges_each * devices)) + EPS)


def pool_kernel(last, edges_each, z_ref, stat_ref, pivot_ref, norm_ref, *refs):
    near, block, d = z_ref.shape
    if last:
        cot_ref, pooled_ref, slope_ref, sums_ref, sums = refs
    else:
        pooled_ref, slope_ref, sum_ref, moment_ref = refs
    mean, inv = moments(stat_ref[...], edges_each)
    half_scale = norm_ref[0:1, :] * inv * 0.5
    half_offset = (pivot_ref[...] - mean) * half_scale + norm_ref[1:2, :] * 0.5
    if last:

        @pl.when(pl.program_id(0) == 0)
        def _():
            sums[...] = jnp.zeros_like(sums)

    for lane in range(0, d, 128):
        lanes = pl.ds(lane, 128)
        scale = jnp.broadcast_to(half_scale[:, lane : lane + 128], (ROWS, 128))
        offset = jnp.broadcast_to(half_offset[:, lane : lane + 128], (ROWS, 128))

        def step(b, carry, lanes=lanes, scale=scale, offset=offset):
            at = pl.ds(pl.multiple_of(b * ROWS, ROWS), ROWS)
            active, bends = [], []
            for k in range(near):
                half = z_ref[k, at, lanes] * scale + offset
                bent = jnp.tanh(half)
                t = 1.0 + bent
                a = half * t
                active.append(a)
                bends.append(t + a * (1.0 - bent))
            top = tree(jnp.maximum, active)
            powers = [jnp.exp2((a - top) * LOG2E) for a in active]
            total = tree(jnp.add, powers)
            pooled = top + jnp.log(total) - math.log(near)
            pooled_ref[at, lanes] = pooled.astype(bf16)
            factor = 0.5 / total
            if last:
                factor = factor * cot_ref[at, lanes].astype(f32)
            halves = [z_ref[k, at, lanes] * scale + offset for k in range(near)]
            slopes = [(powers[k] * factor) * bends[k] for k in range(near)]
            slope_sum = tree(jnp.add, slopes)
            slope_moment = tree(jnp.add, [slopes[k] * halves[k] for k in range(near)])
            for k in range(near):
                slope_ref[k, at, lanes] = slopes[k]
            if not last:
                sum_ref[at, lanes] = slope_sum
                moment_ref[at, lanes] = slope_moment
                return carry
            return (carry[0] + slope_sum, carry[1] + slope_moment)

        zero = jnp.zeros((ROWS, 128), f32)
        carry = lax.fori_loop(0, block // ROWS, step, (zero, zero))
        if last:
            sums[0:1, lanes] += jnp.sum(carry[0], axis=0, keepdims=True)
            sums[1:2, lanes] += jnp.sum(carry[1], axis=0, keepdims=True)
    if last:

        @pl.when(pl.program_id(0) == pl.num_programs(0) - 1)
        def _():
            sums_ref[...] = jnp.broadcast_to(sums[...][None], sums_ref.shape)


def pool(z, stat, pivot, norm, cot=None):
    near, rows, d = z.shape
    whole = lambda x: pl.BlockSpec(x.shape, lambda b: (0,) * len(x.shape))
    by_block = pl.BlockSpec((BLOCK, d), lambda b: (b, 0))
    by_edge = pl.BlockSpec((near, BLOCK, d), lambda b: (0, b, 0))
    inputs = [z, stat, pivot, norm]
    in_specs = [by_edge, whole(stat), whole(pivot), whole(norm)]
    row_out = lambda kind: (jax.ShapeDtypeStruct((rows, d), kind), by_block)
    outs = [row_out(bf16), (jax.ShapeDtypeStruct((near, rows, d), f32), by_edge)]
    scratch = []
    if cot is None:
        outs += [row_out(f32), row_out(f32)]
    else:
        inputs.append(cot)
        in_specs.append(by_block)
        sums = jax.ShapeDtypeStruct(stat.shape, f32)
        outs.append((sums, whole(sums)))
        scratch.append(pltpu.VMEM((2, d), f32))
    return pl.pallas_call(
        functools.partial(pool_kernel, cot is not None, float(near * rows)),
        grid=(rows // BLOCK,),
        out_shape=tuple(o[0] for o in outs),
        in_specs=in_specs,
        out_specs=tuple(o[1] for o in outs),
        scratch_shapes=scratch,
        compiler_params=params(),
        cost_estimate=lasting(12 if cot is None else 20),
        name="pool",
    )(*inputs)


def grads_kernel(
    edges_each,
    inner,
    sends,
    idx_ref,
    slope_ref,
    z_ref,
    back_ref,
    stat_ref,
    pivot_ref,
    norm_ref,
    grads_ref,
    same_ref,
    *refs,
):
    near, block, d = slope_ref.shape
    if inner:
        upstream_ref, diff_ref, line_ref, dz_sum_ref, weight_ref, *send_refs, dz_ref = refs[:-4]
    else:
        line_ref, dz_sum_ref, dz_ref, *send_refs = refs[:-4]
    spread, even, odd, sem = refs[-4:]
    step_id = pl.program_id(0)
    last = pl.num_programs(0) - 1
    total, rows = even.shape[0], dz_sum_ref.shape[0]
    turns = block // 16 * (d // 128)
    share = near * block // turns

    def clear(i, _):
        at = pl.ds(pl.multiple_of(i * 256, 256), 256)
        even[at, :] = jnp.zeros((256, LANES), f32)
        odd[at, :] = jnp.zeros((256, LANES), f32)
        return 0

    def store(waiting, most):
        while len(waiting) > most:
            line, place, row = waiting.pop(0)
            line[place, :] = row

    def add(turn, edges, waiting):
        at = (step_id - 1) * turns + turn
        base = pl.multiple_of(turn * share, 16)
        for e in edges:
            line = (even, odd)[e // GROUP % 2]
            place = pl.ds(idx_ref[at, e], 1)
            waiting.append((line, place, line[place, :] + spread[pl.ds(base + e, 1), :]))
            store(waiting, GROUP)

    def work(adding):
        edges = edges_each * stat_ref.shape[0]
        mean, inv = moments(stat_ref[...], edges_each)
        gain = norm_ref[0:1, :]
        sums = jnp.sum(grads_ref[...], axis=0)
        grad_shift = sums[0:1]
        grad_gain = (2.0 * sums[1:2] - norm_ref[1:2, :] * grad_shift) / gain
        alpha = gain * inv
        rate = alpha * inv * grad_gain * (1.0 / edges)
        constant = alpha * grad_shift * (1.0 / edges) + rate * (pivot_ref[...] - mean)

        for lane in range(0, d, 128):
            lanes = pl.ds(lane, 128)
            wide = lambda x, lane=lane: jnp.broadcast_to(x[:, lane : lane + 128], (16, 128))
            wide_alpha, wide_rate, offset = wide(alpha), wide(rate), wide(constant)

            def step(
                b, _, lane=lane, lanes=lanes, wide_alpha=wide_alpha, wide_rate=wide_rate, offset=offset
            ):
                at = pl.ds(pl.multiple_of(b * 16, 16), 16)
                factor = wide_alpha
                if inner:
                    factor = factor * upstream_ref[at, lanes]
                load = lambda k: (slope_ref[k, at, lanes], z_ref[k, at, lanes])
                loaded = [load(k) for k in range(AHEAD)]
                dzs, waiting = [], []
                each = share // near
                for k in range(near):
                    if adding:
                        turn = lane // 128 * (block // 16) + b
                        add(turn, range(k * each, (k + 1) * each), waiting)
                    if k + AHEAD < near:
                        loaded.append(load(k + AHEAD))
                    slope, z = loaded[k]
                    dzs.append((factor * slope - offset - wide_rate * z).astype(bf16))
                    if k >= AHEAD:
                        dz_ref[k - AHEAD, at, lanes] = dzs[k - AHEAD]
                store(waiting, 0)
                for k in range(near - AHEAD, near):
                    dz_ref[k, at, lanes] = dzs[k]
                row = pl.multiple_of(step_id * block + b * 16, 16)
                dz_sum_ref[pl.ds(row, 16), lanes] = tree(jnp.add, [dz.astype(f32) for dz in dzs])
                return 0

            lax.fori_loop(0, block // 16, step, 0)

        flat = dz_ref[...].reshape(near * block, d)
        back = dot_t(flat, back_ref[...]).astype(bf16).reshape(near, block, LANES)
        for k in range(near):
            spread[pl.ds(k * block, block), :] = dot(same_ref[k], back[k])
        if inner:
            weight_ref[...] += lax.dot_general(
                diff_ref[...].reshape(near * block, diff_ref.shape[2]),
                flat,
                (((0,), (0,)), ((), ())),
                preferred_element_type=f32,
            )

    @pl.when(step_id == 0)
    def _():
        lax.fori_loop(0, total // 256, clear, 0)
        if inner:
            weight_ref[...] = jnp.zeros_like(weight_ref)
        work(False)

    @pl.when((step_id > 0) & (step_id < last))
    def _():
        work(True)

    @pl.when(step_id == last)
    def _():
        def rest(turn, _):
            waiting = []
            add(turn, range(share), waiting)
            store(waiting, 0)
            return 0

        lax.fori_loop(0, turns, rest, 0)

        def join(i, _):
            at = pl.ds(pl.multiple_of(i * 256, 256), 256)
            even[at, :] = even[at, :] + odd[at, :]
            return 0

        lax.fori_loop(0, total // 256, join, 0)
        copy = pltpu.make_async_copy(even, line_ref, sem)
        copy.start()
        for send_ref, slots in zip(send_refs, sends):
            for i, slot in enumerate(slots):
                values = even[pl.ds(slot * rows, rows), : send_ref.shape[1]]
                send_ref[pl.ds(i * rows, rows), :] = values.astype(bf16)
        copy.wait()


def edge_grads(order, slope, z, weight, stat, pivot, norm, grads, same, total, sends, inner=()):
    near, rows, d = slope.shape
    c = weight.shape[0] // 2
    blocks = rows // BLOCK
    now = lambda b: jnp.minimum(b, blocks - 1)
    whole = lambda x: pl.BlockSpec(x.shape, lambda b: (0,) * len(x.shape))
    by_block = lambda width: pl.BlockSpec((BLOCK, width), lambda b: (now(b), 0))
    by_edge = lambda width: pl.BlockSpec((near, BLOCK, width), lambda b: (0, now(b), 0))
    back = jnp.pad(weight[c:], ((0, LANES - c), (0, 0)))
    order = order.reshape(rows // 16 * (d // 128), -1)
    inputs = [order, slope, z, back, stat, pivot, norm, grads, same, *inner]
    in_specs = [
        smem(),
        by_edge(d),
        by_edge(d),
        whole(back),
        whole(stat),
        whole(pivot),
        whole(norm),
        whole(grads),
        by_edge(BLOCK),
    ]
    if inner:
        in_specs += [by_block(d), by_edge(c)]
    body = functools.partial(grads_kernel, float(near * rows), bool(inner), sends)
    dz = jax.ShapeDtypeStruct((near, rows, d), bf16)
    dz_sum = jax.ShapeDtypeStruct((rows, d), f32)
    outs = [
        (jax.ShapeDtypeStruct((total, LANES), f32), pl.BlockSpec(memory_space=pl.ANY)),
        (dz_sum, whole(dz_sum)),
    ]
    scratch = [
        pltpu.VMEM((near * BLOCK, LANES), f32),
        pltpu.VMEM((total, LANES), f32),
        pltpu.VMEM((total, LANES), f32),
        pltpu.SemaphoreType.DMA,
    ]
    if inner:
        part = jax.ShapeDtypeStruct((c, d), f32)
        outs.append((part, whole(part)))
        scratch.insert(0, pltpu.VMEM((near, BLOCK, d), bf16))
    else:
        outs.append((dz, by_edge(d)))
    for slots in sends:
        send = jax.ShapeDtypeStruct((len(slots) * rows, c), bf16)
        outs.append((send, whole(send)))
    return pl.pallas_call(
        body,
        grid=(blocks + 1,),
        out_shape=tuple(o[0] for o in outs),
        in_specs=in_specs,
        out_specs=tuple(o[1] for o in outs),
        scratch_shapes=scratch,
        compiler_params=params(),
        cost_estimate=lasting(40),
        name="edge_grads",
    )(*inputs)


def same_target(index):
    near, rows = index.shape
    blocks = index.reshape(near, rows // BLOCK, BLOCK)
    group = jnp.arange(BLOCK, dtype=jnp.int32) // GROUP
    equal = (blocks[:, :, :, None] == blocks[:, :, None, :]) & (group[:, None] == group[None, :])
    return equal.astype(bf16).reshape(near, rows, BLOCK)


def copies(x):
    return jnp.broadcast_to(x[None], (lax.axis_size(BOTH),) + x.shape)


def shared(x):
    devices = lax.axis_size(BOTH)
    return x.reshape(devices, x.shape[0] // devices, x.shape[1])


def exchange(shares):
    return lax.all_to_all(shares, BOTH, split_axis=0, concat_axis=0, tiled=True)


def everyone(x):
    return exchange(copies(x))


def ring_moves(places):
    ring = list(range(0, places, 2)) + list(range(1, places, 2))[::-1]
    onward = [(ring[i], ring[(i + 1) % places]) for i in range(places)]
    return onward, [(b, a) for a, b in onward]


def ring_place(device, places):
    return jnp.where(device % 2 == 0, device // 2, places - 1 - device // 2)


def ring_jumps(places):
    onward, backward = ring_moves(places)
    twice = lambda moves: [(a, dict(moves)[b]) for a, b in moves]
    return twice(onward), twice(backward)


def line_table(values):
    places = lax.axis_size("pts")
    onward, backward = ring_moves(places)
    rows, far = values.shape[0] // 2, places // 2
    behind, ahead = [values], [values]
    for _ in range(far - 1):
        behind.append(lax.ppermute(behind[-1], "pts", onward))
        ahead.append(lax.ppermute(ahead[-1], "pts", backward))
    farthest = [
        lax.ppermute(behind[-1][:rows], "pts", onward),
        lax.ppermute(ahead[-1][rows:], "pts", backward),
    ]
    return behind + farthest + ahead[:0:-1]


def owners_sum(line, sends, centre):
    places = lax.axis_size("pts")
    onward, backward = ring_moves(places)
    rows, c = centre.shape
    half, far = rows // 2, places // 2
    (first,) = sends

    def slot(j):
        return line[j * rows : (j + 1) * rows, :c]

    forth = lax.ppermute(first[:half], "pts", onward).astype(f32)
    back = lax.ppermute(first[half:], "pts", backward).astype(f32)
    forth = jnp.pad(forth, ((0, half), (0, 0)))
    back = jnp.pad(back, ((half, 0), (0, 0)))
    for j in range(1, far):
        forth, back = (forth + slot(far + j)).astype(bf16), (back + slot(far - j)).astype(bf16)
        forth, back = lax.optimization_barrier((forth, back))
        forth = lax.ppermute(forth, "pts", onward).astype(f32)
        back = lax.ppermute(back, "pts", backward).astype(f32)
    return centre + slot(0) + forth + back


def short_sends(places):
    return [[7, 5], [1, 3], [4]] if places == 8 else [[places // 2]]


def short_sum(line, sends, centre):
    if lax.axis_size("pts") != 8:
        return owners_sum(line, sends, centre)
    onward, backward = ring_moves(8)
    far_onward, far_backward = ring_jumps(8)
    rows, c = centre.shape
    half = rows // 2
    slot = lambda j: line[j * rows : (j + 1) * rows, :c]
    ahead, behind, farthest = sends
    forth_far = lax.ppermute(farthest[:half], "pts", far_onward).astype(f32)
    back_far = lax.ppermute(farthest[half:], "pts", far_backward).astype(f32)
    forth = lax.ppermute(ahead, "pts", onward).astype(f32)
    back = lax.ppermute(behind, "pts", backward).astype(f32)
    forth_two = (slot(6) + forth[rows:] + jnp.pad(forth_far, ((0, half), (0, 0)))).astype(bf16)
    back_two = (slot(2) + back[rows:] + jnp.pad(back_far, ((half, 0), (0, 0)))).astype(bf16)
    forth_two, back_two = lax.optimization_barrier((forth_two, back_two))
    forth_two = lax.ppermute(forth_two, "pts", far_onward).astype(f32)
    back_two = lax.ppermute(back_two, "pts", far_backward).astype(f32)
    return centre + slot(0) + forth[:rows] + back[:rows] + forth_two + back_two


def centre_grad(dz_sum, weight):
    wide = weight.astype(f32)
    c = weight.shape[0] // 2
    return exact(dz_sum, (wide[:c] - wide[c:]).T)


def per_device(
    points,
    lengths,
    neighbours_one,
    neighbours_two,
    weight_one,
    gain_one,
    shift_one,
    weight_two,
    gain_two,
    shift_two,
    cotangent,
):
    line_devices = lax.axis_size("pts")
    row_count = points.shape[0]
    line_length = line_devices * row_count
    table_one = line_table(points)

    norm_one, norm_two = jnp.stack([gain_one, shift_one]), jnp.stack([gain_two, shift_two])

    cloud_ends = jnp.cumsum(lengths)
    cloud_starts = cloud_ends - lengths
    line_first = lax.axis_index("loc") * line_length
    position = (
        line_first + lax.axis_index("pts") * row_count + jnp.arange(row_count, dtype=jnp.int32)
    )
    begins = (position[:, None] >= cloud_starts[None, :]) & (position[:, None] < cloud_ends[None, :])
    begin = jnp.sum(jnp.where(begins, cloud_starts[None, :], 0), axis=1) - line_first
    here = ring_place(lax.axis_index("pts"), line_devices)

    def slot_rows(neighbours):
        within = neighbours.T + begin[None, :]
        slot = (here - ring_place(within // row_count, line_devices)) % line_devices
        return slot * row_count + within % row_count

    def by_blocks(index):
        blocks = index.reshape(index.shape[0], -1, BLOCK)
        return blocks.transpose(1, 0, 2).reshape(-1, BLOCK)

    index_one = slot_rows(neighbours_one)
    index_two = slot_rows(neighbours_two)
    order_one, order_two = by_blocks(index_one), by_blocks(index_two)
    same_one = same_target(index_one)
    same_two = same_target(index_two)

    diff_one, z_one, stat_one, pivot_one = edge_stats(order_one, table_one, points, weight_one)
    stat_one, order_two = lax.optimization_barrier((exchange(stat_one), order_two))
    act_one, slope_one, slope_sum, slope_moment = pool(z_one, stat_one, pivot_one, norm_one)
    table_two = line_table(act_one)
    diff_two, z_two, stat_two, pivot_two = edge_stats(order_two, table_two, act_one, weight_two)
    stat_two = exchange(stat_two)
    act_two, slope_two, sums_two = pool(z_two, stat_two, pivot_two, norm_two, cotangent)
    sums_two = exchange(sums_two)
    line_two, dz_sum_two, dz_two, *sends_two = edge_grads(
        order_two,
        slope_two,
        z_two,
        weight_two,
        stat_two,
        pivot_two,
        norm_two,
        sums_two,
        same_two,
        line_length,
        [[line_devices // 2]],
    )
    grad_first = owners_sum(line_two, sends_two, centre_grad(dz_sum_two, weight_two))
    grad_first, dz_two, dz_sum_two = lax.optimization_barrier((grad_first, dz_two, dz_sum_two))
    first_two = exact(act_one.astype(f32).T, dz_sum_two)
    second_two = jnp.einsum("kgc,kgd->cd", diff_two, dz_two, preferred_element_type=f32)
    sums_one = jnp.stack(
        [jnp.sum(grad_first * slope_sum, axis=0), jnp.sum(grad_first * slope_moment, axis=0)]
    )
    sums_one = everyone(sums_one)
    line_one, dz_sum_one, second_one, *sends_one = edge_grads(
        order_one,
        slope_one,
        z_one,
        weight_one,
        stat_one,
        pivot_one,
        norm_one,
        sums_one,
        same_one,
        line_length,
        short_sends(line_devices),
        (grad_first, diff_one),
    )
    first_one = exact(points.astype(f32).T, dz_sum_one)
    weights = jnp.concatenate(
        [first_two.reshape(-1, LANES), second_two.reshape(-1, LANES), first_one, second_one], axis=0
    )
    shares = exchange(shared(weights.astype(bf16)))
    weights = everyone(jnp.sum(shares.astype(f32), axis=0).astype(bf16))
    grad_points = short_sum(line_one, sends_one, centre_grad(dz_sum_one, weight_one))
    weights = weights.reshape(-1, LANES).astype(f32)
    grad_weight_two = weights[: -weight_one.shape[0]].reshape(weight_two.shape)
    grad_weight_one = weights[-weight_one.shape[0] :]

    def norm_grads(sums, gain, shift):
        sums = jnp.sum(sums, axis=0)
        return (2.0 * sums[1] - shift * sums[0]) / gain, sums[0]

    grad_gain_one, grad_shift_one = norm_grads(sums_one, gain_one, shift_one)
    grad_gain_two, grad_shift_two = norm_grads(sums_two, gain_two, shift_two)
    return (
        act_one,
        act_two,
        grad_points,
        grad_weight_one,
        grad_gain_one,
        grad_shift_one,
        grad_weight_two,
        grad_gain_two,
        grad_shift_two,
    )


def solution(mesh):
    rows, copied = P(("pts", "loc"), None), P()
    in_specs = (rows, copied, rows, rows) + (copied,) * 6 + (rows,)
    out_specs = (rows, rows, rows) + (copied,) * 6
    return jax.shard_map(
        per_device, mesh=mesh, in_specs=in_specs, out_specs=out_specs, check_vma=False
    )
```

```python
import functools
import math

import jax
import jax.numpy as jnp
from jax import lax
from jax.experimental import pallas as pl
from jax.experimental.pallas import tpu as pltpu
from jax.sharding import PartitionSpec as P

EPS = 1e-05
BLOCK = 128
POOL_BLOCK = 256
GROUP = 8
ROWS = 16
AHEAD = 4
LOG2E = 1.0 / math.log(2.0)
LANES = 128
MIB = 1024 * 1024
BOTH = ("pts", "loc")

f32 = jnp.float32
bf16 = jnp.bfloat16


def params():
    return pltpu.CompilerParams(vmem_limit_bytes=52 * MIB)


def lasting(microseconds):
    return pl.CostEstimate(flops=0, transcendentals=0, bytes_accessed=3_000_000 * microseconds)


def smem():
    return pl.BlockSpec(memory_space=pltpu.SMEM)


def fold_rows(x):
    return jnp.sum(x.reshape(x.shape[0] // 8, 8, x.shape[1]), axis=0)


def tree(op, terms):
    while len(terms) > 1:
        pairs = [op(a, b) for a, b in zip(terms[::2], terms[1::2])]
        terms = pairs + terms[len(pairs) * 2 :]
    return terms[0]


def dot(a, b):
    return jnp.dot(a, b, preferred_element_type=f32)


def exact(a, b):
    return jnp.dot(a, b, precision=lax.Precision.HIGHEST, preferred_element_type=f32)


def dot_t(a, b):
    return lax.dot_general(a, b, (((1,), (1,)), ((), ())), preferred_element_type=f32)


def edge_kernel(pieces, *refs):
    table_refs = refs[1 : 1 + pieces]
    idx_ref = refs[0]
    own_ref, w_ref, diff_ref, z_ref, stat_ref, pivot_ref, table, rows, centre, sums, square = refs[
        1 + pieces :
    ]
    near, block, c = diff_ref.shape
    step_id = pl.program_id(0)
    last = pl.num_programs(0) - 1
    chunk = 4

    def project(own_sum, diff_sum):
        weight = w_ref[...].astype(f32)
        both = exact(own_sum, weight[:c]) + exact(diff_sum, weight[c:])
        return jnp.sum(both, axis=0, keepdims=True)

    @pl.when(step_id == 0)
    def _():
        first = 0
        for piece in table_refs:
            for r in range(0, piece.shape[0], 256):
                table[pl.ds(first + r, 256), :c] = piece[pl.ds(r, 256), :].astype(f32)
            first += piece.shape[0]
        sums[...] = jnp.zeros_like(sums)
        square[...] = jnp.zeros_like(square)

    @pl.when(step_id == 1)
    def _():
        own = own_ref[...].astype(f32)
        diff_sum = jnp.zeros((8, c), f32)
        for k in range(near):
            diff_sum = diff_sum + fold_rows(rows[pl.ds(k * block, block), :c] - own)
        own_sum = fold_rows(own) * float(near)
        pivot_ref[...] = project(own_sum, diff_sum) * (1.0 / (near * block))

    def pick(k):
        base = pl.multiple_of(k * block, block)
        at = step_id * near + k
        waiting = []
        for e in range(block + GROUP):
            if e < block:
                waiting.append(table[pl.ds(idx_ref[at, e], 1), :])
            if e >= GROUP:
                rows[pl.ds(base + (e - GROUP), 1), :] = waiting[e - GROUP]

    def work(k, own, carry):
        diff_sum, total = carry
        at = pl.ds(pl.multiple_of(k * block, block), block)
        diff = (rows[at, :c] - own).astype(bf16)
        diff_ref[k] = diff
        diff_sum = diff_sum + fold_rows(diff.astype(f32))
        z = dot(diff, w_ref[c:, :]) + centre[...]
        z_ref[k] = z
        return diff_sum, total + fold_rows(z * z)

    @pl.when(step_id == 0)
    def _():
        def body(i, _):
            pick(i)
            return 0

        lax.fori_loop(0, near, body, 0)

    def finish(own, carry):
        sums[0] += fold_rows(own) * float(near)
        sums[1] += carry[0]
        square[...] += carry[1]

    def begin():
        centre[...] = dot(own_ref[...], w_ref[:c, :]) - pivot_ref[...]
        zero = (jnp.zeros((8, c), f32), jnp.zeros_like(square[...]))
        return own_ref[...].astype(f32), zero

    @pl.when((step_id > 0) & (step_id < last))
    def _():
        own, zero = begin()

        def body(i, carry):
            for k in range(chunk):
                carry = work(i * chunk + k, own_ref[...].astype(f32), carry)
                pick(i * chunk + k)
            return carry

        finish(own, lax.fori_loop(0, near // chunk, body, zero))

    @pl.when(step_id == last)
    def _():
        own, carry = begin()
        for k in range(near):
            carry = work(k, own, carry)
        finish(own, carry)
        count = float(near * block * (pl.num_programs(0) - 1))
        mean = project(sums[0], sums[1]) / count
        off = mean - pivot_ref[...]
        m2 = jnp.sum(square[...], axis=0, keepdims=True) - count * off * off
        stat_ref[...] = jnp.broadcast_to(jnp.concatenate([mean, m2], axis=0)[None], stat_ref.shape)


def edge_stats(index, pieces, own, weight):
    rows, c = own.shape
    d = weight.shape[1]
    blocks = rows // BLOCK
    near = index.shape[0] // blocks
    total = sum(piece.shape[0] for piece in pieces)
    before = lambda b: jnp.maximum(b - 1, 0)
    whole = lambda x: pl.BlockSpec(x.shape, lambda b: (0,) * len(x.shape))
    stat = jax.ShapeDtypeStruct((lax.axis_size(BOTH), 2, d), f32)
    pivot = jax.ShapeDtypeStruct((1, d), f32)
    return pl.pallas_call(
        functools.partial(edge_kernel, len(pieces)),
        grid=(blocks + 1,),
        out_shape=(
            jax.ShapeDtypeStruct((near, rows, c), bf16),
            jax.ShapeDtypeStruct((near, rows, d), f32),
            stat,
            pivot,
        ),
        in_specs=[smem()]
        + [whole(piece) for piece in pieces]
        + [pl.BlockSpec((BLOCK, c), lambda b: (before(b), 0)), whole(weight)],
        out_specs=(
            pl.BlockSpec((near, BLOCK, c), lambda b: (0, before(b), 0)),
            pl.BlockSpec((near, BLOCK, d), lambda b: (0, before(b), 0)),
            whole(stat),
            whole(pivot),
        ),
        scratch_shapes=[
            pltpu.VMEM((total, LANES), f32),
            pltpu.VMEM((near * BLOCK, LANES), f32),
            pltpu.VMEM((BLOCK, d), f32),
            pltpu.VMEM((2, 8, c), f32),
            pltpu.VMEM((8, d), f32),
        ],
        compiler_params=params(),
        cost_estimate=lasting(22),
        name="edge_stats",
    )(index, *pieces, own, weight)


def moments(stat, edges_each):
    devices = stat.shape[0]
    means = stat[:, 0, :]
    mean = jnp.sum(means, axis=0, keepdims=True) * (1.0 / devices)
    off = means - mean
    m2 = jnp.sum(stat[:, 1, :], axis=0, keepdims=True) + edges_each * jnp.sum(
        off * off, axis=0, keepdims=True
    )
    return mean, lax.rsqrt(m2 * (1.0 / (edges_each * devices)) + EPS)


def pool_kernel(last, edges_each, z_ref, stat_ref, pivot_ref, norm_ref, *refs):
    near, block, d = z_ref.shape
    if last:
        cot_ref, pooled_ref, slope_ref, sums_ref, sums = refs
    else:
        pooled_ref, slope_ref, sum_ref, moment_ref = refs
    mean, inv = moments(stat_ref[...], edges_each)
    half_scale = norm_ref[0:1, :] * inv * 0.5
    half_offset = (pivot_ref[...] - mean) * half_scale + norm_ref[1:2, :] * 0.5
    if last:

        @pl.when(pl.program_id(0) == 0)
        def _():
            sums[...] = jnp.zeros_like(sums)

    for lane in range(0, d, 128):
        lanes = pl.ds(lane, 128)
        scale = jnp.broadcast_to(half_scale[:, lane : lane + 128], (ROWS, 128))
        offset = jnp.broadcast_to(half_offset[:, lane : lane + 128], (ROWS, 128))

        def step(b, carry, lanes=lanes, scale=scale, offset=offset):
            at = pl.ds(pl.multiple_of(b * ROWS, ROWS), ROWS)
            active, bends = [], []
            for k in range(near):
                half = z_ref[k, at, lanes] * scale + offset
                bent = jnp.tanh(half)
                t = 1.0 + bent
                a = half * t
                active.append(a)
                bends.append(t + a * (1.0 - bent))
            top = tree(jnp.maximum, active)
            powers = [jnp.exp2((a - top) * LOG2E) for a in active]
            total = tree(jnp.add, powers)
            pooled = top + jnp.log(total) - math.log(near)
            pooled_ref[at, lanes] = pooled.astype(bf16)
            factor = 0.5 / total
            if last:
                factor = factor * cot_ref[at, lanes].astype(f32)
            halves = [z_ref[k, at, lanes] * scale + offset for k in range(near)]
            slopes = [(powers[k] * factor) * bends[k] for k in range(near)]
            slope_sum = tree(jnp.add, slopes)
            slope_moment = tree(jnp.add, [slopes[k] * halves[k] for k in range(near)])
            for k in range(near):
                slope_ref[k, at, lanes] = slopes[k]
            if not last:
                sum_ref[at, lanes] = slope_sum
                moment_ref[at, lanes] = slope_moment
                return carry
            return (carry[0] + slope_sum, carry[1] + slope_moment)

        zero = jnp.zeros((ROWS, 128), f32)
        carry = lax.fori_loop(0, block // ROWS, step, (zero, zero))
        if last:
            sums[0:1, lanes] += jnp.sum(carry[0], axis=0, keepdims=True)
            sums[1:2, lanes] += jnp.sum(carry[1], axis=0, keepdims=True)
    if last:

        @pl.when(pl.program_id(0) == pl.num_programs(0) - 1)
        def _():
            sums_ref[...] = jnp.broadcast_to(sums[...][None], sums_ref.shape)


def pool(z, stat, pivot, norm, cot=None):
    near, rows, d = z.shape
    whole = lambda x: pl.BlockSpec(x.shape, lambda b: (0,) * len(x.shape))
    by_block = pl.BlockSpec((POOL_BLOCK, d), lambda b: (b, 0))
    by_edge = pl.BlockSpec((near, POOL_BLOCK, d), lambda b: (0, b, 0))
    inputs = [z, stat, pivot, norm]
    in_specs = [by_edge, whole(stat), whole(pivot), whole(norm)]
    row_out = lambda kind: (jax.ShapeDtypeStruct((rows, d), kind), by_block)
    outs = [row_out(bf16), (jax.ShapeDtypeStruct((near, rows, d), f32), by_edge)]
    scratch = []
    if cot is None:
        outs += [row_out(f32), row_out(f32)]
    else:
        inputs.append(cot)
        in_specs.append(by_block)
        sums = jax.ShapeDtypeStruct(stat.shape, f32)
        outs.append((sums, whole(sums)))
        scratch.append(pltpu.VMEM((2, d), f32))
    return pl.pallas_call(
        functools.partial(pool_kernel, cot is not None, float(near * rows)),
        grid=(rows // POOL_BLOCK,),
        out_shape=tuple(o[0] for o in outs),
        in_specs=in_specs,
        out_specs=tuple(o[1] for o in outs),
        scratch_shapes=scratch,
        compiler_params=params(),
        cost_estimate=lasting(12 if cot is None else 20),
        name="pool",
    )(*inputs)


def grads_kernel(
    edges_each,
    inner,
    sends,
    idx_ref,
    slope_ref,
    z_ref,
    back_ref,
    stat_ref,
    pivot_ref,
    norm_ref,
    grads_ref,
    same_ref,
    *refs,
):
    near, block, d = slope_ref.shape
    if inner:
        upstream_ref, diff_ref, line_ref, dz_sum_ref, weight_ref, *send_refs, dz_ref = refs[:-4]
    else:
        line_ref, dz_sum_ref, dz_ref, *send_refs = refs[:-4]
    spread, even, odd, sem = refs[-4:]
    step_id = pl.program_id(0)
    last = pl.num_programs(0) - 1
    total, rows = even.shape[0], dz_sum_ref.shape[0]
    turns = block // 16 * (d // 128)
    share = near * block // turns

    def clear(i, _):
        at = pl.ds(pl.multiple_of(i * 256, 256), 256)
        even[at, :] = jnp.zeros((256, LANES), f32)
        odd[at, :] = jnp.zeros((256, LANES), f32)
        return 0

    def store(waiting, most):
        while len(waiting) > most:
            line, place, row = waiting.pop(0)
            line[place, :] = row

    def add(turn, edges, waiting):
        at = (step_id - 1) * turns + turn
        base = pl.multiple_of(turn * share, 16)
        for e in edges:
            line = (even, odd)[e // GROUP % 2]
            place = pl.ds(idx_ref[at, e], 1)
            waiting.append((line, place, line[place, :] + spread[pl.ds(base + e, 1), :]))
            store(waiting, GROUP)

    def work(adding):
        edges = edges_each * stat_ref.shape[0]
        mean, inv = moments(stat_ref[...], edges_each)
        gain = norm_ref[0:1, :]
        sums = jnp.sum(grads_ref[...], axis=0)
        grad_shift = sums[0:1]
        grad_gain = (2.0 * sums[1:2] - norm_ref[1:2, :] * grad_shift) / gain
        alpha = gain * inv
        rate = alpha * inv * grad_gain * (1.0 / edges)
        constant = alpha * grad_shift * (1.0 / edges) + rate * (pivot_ref[...] - mean)

        for lane in range(0, d, 128):
            lanes = pl.ds(lane, 128)
            wide = lambda x, lane=lane: jnp.broadcast_to(x[:, lane : lane + 128], (16, 128))
            wide_alpha, wide_rate, offset = wide(alpha), wide(rate), wide(constant)

            def step(
                b, _, lane=lane, lanes=lanes, wide_alpha=wide_alpha, wide_rate=wide_rate, offset=offset
            ):
                at = pl.ds(pl.multiple_of(b * 16, 16), 16)
                factor = wide_alpha
                if inner:
                    factor = factor * upstream_ref[at, lanes]
                load = lambda k: (slope_ref[k, at, lanes], z_ref[k, at, lanes])
                loaded = [load(k) for k in range(AHEAD)]
                dzs, waiting = [], []
                each = share // near
                for k in range(near):
                    if adding:
                        turn = lane // 128 * (block // 16) + b
                        add(turn, range(k * each, (k + 1) * each), waiting)
                    if k + AHEAD < near:
                        loaded.append(load(k + AHEAD))
                    slope, z = loaded[k]
                    dzs.append((factor * slope - offset - wide_rate * z).astype(bf16))
                    if k >= AHEAD:
                        dz_ref[k - AHEAD, at, lanes] = dzs[k - AHEAD]
                store(waiting, 0)
                for k in range(near - AHEAD, near):
                    dz_ref[k, at, lanes] = dzs[k]
                row = pl.multiple_of(step_id * block + b * 16, 16)
                dz_sum_ref[pl.ds(row, 16), lanes] = tree(jnp.add, [dz.astype(f32) for dz in dzs])
                return 0

            lax.fori_loop(0, block // 16, step, 0)

        flat = dz_ref[...].reshape(near * block, d)
        back = dot_t(flat, back_ref[...]).astype(bf16).reshape(near, block, LANES)
        for k in range(near):
            spread[pl.ds(k * block, block), :] = dot(same_ref[k], back[k])
        if inner:
            weight_ref[...] += lax.dot_general(
                diff_ref[...].reshape(near * block, diff_ref.shape[2]),
                flat,
                (((0,), (0,)), ((), ())),
                preferred_element_type=f32,
            )

    @pl.when(step_id == 0)
    def _():
        lax.fori_loop(0, total // 256, clear, 0)
        if inner:
            weight_ref[...] = jnp.zeros_like(weight_ref)
        work(False)

    @pl.when((step_id > 0) & (step_id < last))
    def _():
        work(True)

    @pl.when(step_id == last)
    def _():
        def rest(turn, _):
            waiting = []
            add(turn, range(share), waiting)
            store(waiting, 0)
            return 0

        lax.fori_loop(0, turns, rest, 0)

        def join(i, _):
            at = pl.ds(pl.multiple_of(i * 256, 256), 256)
            even[at, :] = even[at, :] + odd[at, :]
            return 0

        lax.fori_loop(0, total // 256, join, 0)
        copy = pltpu.make_async_copy(even, line_ref, sem)
        copy.start()
        for send_ref, slots in zip(send_refs, sends):
            for i, slot in enumerate(slots):
                values = even[pl.ds(slot * rows, rows), : send_ref.shape[1]]
                send_ref[pl.ds(i * rows, rows), :] = values.astype(bf16)
        copy.wait()


def edge_grads(order, slope, z, weight, stat, pivot, norm, grads, same, total, sends, inner=()):
    near, rows, d = slope.shape
    c = weight.shape[0] // 2
    blocks = rows // BLOCK
    now = lambda b: jnp.minimum(b, blocks - 1)
    whole = lambda x: pl.BlockSpec(x.shape, lambda b: (0,) * len(x.shape))
    by_block = lambda width: pl.BlockSpec((BLOCK, width), lambda b: (now(b), 0))
    by_edge = lambda width: pl.BlockSpec((near, BLOCK, width), lambda b: (0, now(b), 0))
    back = jnp.pad(weight[c:], ((0, LANES - c), (0, 0)))
    order = order.reshape(rows // 16 * (d // 128), -1)
    inputs = [order, slope, z, back, stat, pivot, norm, grads, same, *inner]
    in_specs = [
        smem(),
        by_edge(d),
        by_edge(d),
        whole(back),
        whole(stat),
        whole(pivot),
        whole(norm),
        whole(grads),
        by_edge(BLOCK),
    ]
    if inner:
        in_specs += [by_block(d), by_edge(c)]
    body = functools.partial(grads_kernel, float(near * rows), bool(inner), sends)
    dz = jax.ShapeDtypeStruct((near, rows, d), bf16)
    dz_sum = jax.ShapeDtypeStruct((rows, d), f32)
    outs = [
        (jax.ShapeDtypeStruct((total, LANES), f32), pl.BlockSpec(memory_space=pl.ANY)),
        (dz_sum, whole(dz_sum)),
    ]
    scratch = [
        pltpu.VMEM((near * BLOCK, LANES), f32),
        pltpu.VMEM((total, LANES), f32),
        pltpu.VMEM((total, LANES), f32),
        pltpu.SemaphoreType.DMA,
    ]
    if inner:
        part = jax.ShapeDtypeStruct((c, d), f32)
        outs.append((part, whole(part)))
        scratch.insert(0, pltpu.VMEM((near, BLOCK, d), bf16))
    else:
        outs.append((dz, by_edge(d)))
    for slots in sends:
        send = jax.ShapeDtypeStruct((len(slots) * rows, c), bf16)
        outs.append((send, whole(send)))
    return pl.pallas_call(
        body,
        grid=(blocks + 1,),
        out_shape=tuple(o[0] for o in outs),
        in_specs=in_specs,
        out_specs=tuple(o[1] for o in outs),
        scratch_shapes=scratch,
        compiler_params=params(),
        cost_estimate=lasting(40),
        name="edge_grads",
    )(*inputs)


def same_target(index):
    near, rows = index.shape
    blocks = index.reshape(near, rows // BLOCK, BLOCK)
    group = jnp.arange(BLOCK, dtype=jnp.int32) // GROUP
    equal = (blocks[:, :, :, None] == blocks[:, :, None, :]) & (group[:, None] == group[None, :])
    return equal.astype(bf16).reshape(near, rows, BLOCK)


def copies(x):
    return jnp.broadcast_to(x[None], (lax.axis_size(BOTH),) + x.shape)


def shared(x):
    devices = lax.axis_size(BOTH)
    return x.reshape(devices, x.shape[0] // devices, x.shape[1])


def exchange(shares):
    return lax.all_to_all(shares, BOTH, split_axis=0, concat_axis=0, tiled=True)


def everyone(x):
    return exchange(copies(x))


def ring_moves(places):
    ring = list(range(0, places, 2)) + list(range(1, places, 2))[::-1]
    onward = [(ring[i], ring[(i + 1) % places]) for i in range(places)]
    return onward, [(b, a) for a, b in onward]


def ring_place(device, places):
    return jnp.where(device % 2 == 0, device // 2, places - 1 - device // 2)


def line_table(values):
    places = lax.axis_size("pts")
    onward, backward = ring_moves(places)
    rows, far = values.shape[0] // 2, places // 2
    behind, ahead = [values], [values]
    for _ in range(far - 1):
        behind.append(lax.ppermute(behind[-1], "pts", onward))
        ahead.append(lax.ppermute(ahead[-1], "pts", backward))
    farthest = [
        lax.ppermute(behind[-1][:rows], "pts", onward),
        lax.ppermute(ahead[-1][rows:], "pts", backward),
    ]
    return behind + farthest + ahead[:0:-1]


def owners_sum(line, sends, centre):
    places = lax.axis_size("pts")
    onward, backward = ring_moves(places)
    rows, c = centre.shape
    half, far = rows // 2, places // 2
    (first,) = sends

    def slot(j):
        return line[j * rows : (j + 1) * rows, :c]

    forth = lax.ppermute(first[:half], "pts", onward).astype(f32)
    back = lax.ppermute(first[half:], "pts", backward).astype(f32)
    forth = jnp.pad(forth, ((0, half), (0, 0)))
    back = jnp.pad(back, ((half, 0), (0, 0)))
    for j in range(1, far):
        forth, back = (forth + slot(far + j)).astype(bf16), (back + slot(far - j)).astype(bf16)
        forth, back = lax.optimization_barrier((forth, back))
        forth = lax.ppermute(forth, "pts", onward).astype(f32)
        back = lax.ppermute(back, "pts", backward).astype(f32)
    return centre + slot(0) + forth + back


def direct_sum(line, sends, centre):
    places = lax.axis_size("pts")
    onward, _ = ring_moves(places)
    rows, c = centre.shape
    total = centre + line[:rows, :c]
    moves, met = [(a, a) for a, _ in onward], {}
    for far in range(1, places):
        moves = [(a, dict(onward)[b]) for a, b in moves]
        met[far] = lax.ppermute(sends[places - far - 1], "pts", moves)
    for far in range(1, places):
        total = total + met[far].astype(f32)
    return total, met[1]


def centre_grad(dz_sum, weight):
    wide = weight.astype(f32)
    c = weight.shape[0] // 2
    return exact(dz_sum, (wide[:c] - wide[c:]).T)


def per_device(
    points,
    lengths,
    neighbours_one,
    neighbours_two,
    weight_one,
    gain_one,
    shift_one,
    weight_two,
    gain_two,
    shift_two,
    cotangent,
):
    line_devices = lax.axis_size("pts")
    row_count = points.shape[0]
    line_length = line_devices * row_count
    table_one = line_table(points)

    norm_one, norm_two = jnp.stack([gain_one, shift_one]), jnp.stack([gain_two, shift_two])

    cloud_ends = jnp.cumsum(lengths)
    cloud_starts = cloud_ends - lengths
    line_first = lax.axis_index("loc") * line_length
    position = (
        line_first + lax.axis_index("pts") * row_count + jnp.arange(row_count, dtype=jnp.int32)
    )
    begins = (position[:, None] >= cloud_starts[None, :]) & (position[:, None] < cloud_ends[None, :])
    begin = jnp.sum(jnp.where(begins, cloud_starts[None, :], 0), axis=1) - line_first
    here = ring_place(lax.axis_index("pts"), line_devices)

    def slot_rows(neighbours):
        within = neighbours.T + begin[None, :]
        slot = (here - ring_place(within // row_count, line_devices)) % line_devices
        return slot * row_count + within % row_count

    def by_blocks(index):
        blocks = index.reshape(index.shape[0], -1, BLOCK)
        return blocks.transpose(1, 0, 2).reshape(-1, BLOCK)

    index_one = slot_rows(neighbours_one)
    index_two = slot_rows(neighbours_two)
    order_one, order_two = by_blocks(index_one), by_blocks(index_two)
    same_one = same_target(index_one)
    same_two = same_target(index_two)

    diff_one, z_one, stat_one, pivot_one = edge_stats(order_one, table_one, points, weight_one)
    stat_one, order_two = lax.optimization_barrier((exchange(stat_one), order_two))
    act_one, slope_one, slope_sum, slope_moment = pool(z_one, stat_one, pivot_one, norm_one)
    table_two = line_table(act_one)
    diff_two, z_two, stat_two, pivot_two = edge_stats(order_two, table_two, act_one, weight_two)
    stat_two = exchange(stat_two)
    act_two, slope_two, sums_two = pool(z_two, stat_two, pivot_two, norm_two, cotangent)
    sums_two = exchange(sums_two)
    line_two, dz_sum_two, dz_two, *sends_two = edge_grads(
        order_two,
        slope_two,
        z_two,
        weight_two,
        stat_two,
        pivot_two,
        norm_two,
        sums_two,
        same_two,
        line_length,
        [[line_devices // 2]],
    )
    grad_first = owners_sum(line_two, sends_two, centre_grad(dz_sum_two, weight_two))
    grad_first, dz_two, dz_sum_two = lax.optimization_barrier((grad_first, dz_two, dz_sum_two))
    first_two = exact(act_one.astype(f32).T, dz_sum_two)
    second_two = jnp.einsum("kgc,kgd->cd", diff_two, dz_two, preferred_element_type=f32)
    sums_one = jnp.stack(
        [jnp.sum(grad_first * slope_sum, axis=0), jnp.sum(grad_first * slope_moment, axis=0)]
    )
    sums_one = everyone(sums_one)
    line_one, dz_sum_one, second_one, *sends_one = edge_grads(
        order_one,
        slope_one,
        z_one,
        weight_one,
        stat_one,
        pivot_one,
        norm_one,
        sums_one,
        same_one,
        line_length,
        [[slot] for slot in range(1, line_devices)],
        (grad_first, diff_one),
    )
    grad_points, met = direct_sum(line_one, sends_one, centre_grad(dz_sum_one, weight_one))
    first_one = exact(points.astype(f32).T, dz_sum_one)
    weights = jnp.concatenate(
        [first_two.reshape(-1, LANES), second_two.reshape(-1, LANES), first_one, second_one], axis=0
    )
    weights, met = lax.optimization_barrier((weights.astype(bf16), met))
    shares = exchange(shared(weights))
    weights = everyone(jnp.sum(shares.astype(f32), axis=0).astype(bf16))
    weights = weights.reshape(-1, LANES).astype(f32)
    grad_weight_two = weights[: -weight_one.shape[0]].reshape(weight_two.shape)
    grad_weight_one = weights[-weight_one.shape[0] :]

    def norm_grads(sums, gain, shift):
        sums = jnp.sum(sums, axis=0)
        return (2.0 * sums[1] - shift * sums[0]) / gain, sums[0]

    grad_gain_one, grad_shift_one = norm_grads(sums_one, gain_one, shift_one)
    grad_gain_two, grad_shift_two = norm_grads(sums_two, gain_two, shift_two)
    return (
        act_one,
        act_two,
        grad_points,
        grad_weight_one,
        grad_gain_one,
        grad_shift_one,
        grad_weight_two,
        grad_gain_two,
        grad_shift_two,
    )


def solution(mesh):
    rows, copied = P(("pts", "loc"), None), P()
    in_specs = (rows, copied, rows, rows) + (copied,) * 6 + (rows,)
    out_specs = (rows, rows, rows) + (copied,) * 6
    return jax.shard_map(
        per_device, mesh=mesh, in_specs=in_specs, out_specs=out_specs, check_vma=False
    )
```

```python
import functools
import math

import jax
import jax.numpy as jnp
from jax import lax
from jax.experimental import pallas as pl
from jax.experimental.pallas import tpu as pltpu
from jax.sharding import PartitionSpec as P

EPS = 1e-05
BLOCK = 128
POOL_BLOCK = 256
GROUP = 8
LINES = 4
ROWS = 16
AHEAD = 4
LOG2E = 1.0 / math.log(2.0)
LANES = 128
MIB = 1024 * 1024
BOTH = ("pts", "loc")

f32 = jnp.float32
bf16 = jnp.bfloat16


def params():
    return pltpu.CompilerParams(vmem_limit_bytes=52 * MIB)


def lasting(microseconds):
    return pl.CostEstimate(flops=0, transcendentals=0, bytes_accessed=3_000_000 * microseconds)


def smem():
    return pl.BlockSpec(memory_space=pltpu.SMEM)


def fold_rows(x):
    return jnp.sum(x.reshape(x.shape[0] // 8, 8, x.shape[1]), axis=0)


def tree(op, terms):
    while len(terms) > 1:
        pairs = [op(a, b) for a, b in zip(terms[::2], terms[1::2])]
        terms = pairs + terms[len(pairs) * 2 :]
    return terms[0]


def dot(a, b):
    return jnp.dot(a, b, preferred_element_type=f32)


def exact(a, b):
    return jnp.dot(a, b, precision=lax.Precision.HIGHEST, preferred_element_type=f32)


def dot_t(a, b):
    return lax.dot_general(a, b, (((1,), (1,)), ((), ())), preferred_element_type=f32)


def edge_kernel(pieces, *refs):
    table_refs = refs[1 : 1 + pieces]
    idx_ref = refs[0]
    own_ref, w_ref, diff_ref, z_ref, stat_ref, pivot_ref, table, rows, centre, sums, square = refs[
        1 + pieces :
    ]
    near, block, c = diff_ref.shape
    step_id = pl.program_id(0)
    last = pl.num_programs(0) - 1
    chunk = 4

    def project(own_sum, diff_sum):
        weight = w_ref[...].astype(f32)
        both = exact(own_sum, weight[:c]) + exact(diff_sum, weight[c:])
        return jnp.sum(both, axis=0, keepdims=True)

    @pl.when(step_id == 0)
    def _():
        first = 0
        for piece in table_refs:
            for r in range(0, piece.shape[0], 256):
                table[pl.ds(first + r, 256), :c] = piece[pl.ds(r, 256), :].astype(f32)
            first += piece.shape[0]
        sums[...] = jnp.zeros_like(sums)
        square[...] = jnp.zeros_like(square)

    @pl.when(step_id == 1)
    def _():
        own = own_ref[...].astype(f32)
        diff_sum = jnp.zeros((8, c), f32)
        for k in range(near):
            diff_sum = diff_sum + fold_rows(rows[pl.ds(k * block, block), :c] - own)
        own_sum = fold_rows(own) * float(near)
        pivot_ref[...] = project(own_sum, diff_sum) * (1.0 / (near * block))

    def pick(k):
        base = pl.multiple_of(k * block, block)
        at = step_id * near + k
        waiting = []
        for e in range(block + GROUP):
            if e < block:
                waiting.append(table[pl.ds(idx_ref[at, e], 1), :])
            if e >= GROUP:
                rows[pl.ds(base + (e - GROUP), 1), :] = waiting[e - GROUP]

    def work(k, own, carry):
        diff_sum, total = carry
        at = pl.ds(pl.multiple_of(k * block, block), block)
        diff = (rows[at, :c] - own).astype(bf16)
        diff_ref[k] = diff
        diff_sum = diff_sum + fold_rows(diff.astype(f32))
        z = dot(diff, w_ref[c:, :]) + centre[...]
        z_ref[k] = z
        return diff_sum, total + fold_rows(z * z)

    @pl.when(step_id == 0)
    def _():
        def body(i, _):
            pick(i)
            return 0

        lax.fori_loop(0, near, body, 0)

    def finish(own, carry):
        sums[0] += fold_rows(own) * float(near)
        sums[1] += carry[0]
        square[...] += carry[1]

    def begin():
        centre[...] = dot(own_ref[...], w_ref[:c, :]) - pivot_ref[...]
        zero = (jnp.zeros((8, c), f32), jnp.zeros_like(square[...]))
        return own_ref[...].astype(f32), zero

    @pl.when((step_id > 0) & (step_id < last))
    def _():
        own, zero = begin()

        def body(i, carry):
            for k in range(chunk):
                carry = work(i * chunk + k, own_ref[...].astype(f32), carry)
                pick(i * chunk + k)
            return carry

        finish(own, lax.fori_loop(0, near // chunk, body, zero))

    @pl.when(step_id == last)
    def _():
        own, carry = begin()
        for k in range(near):
            carry = work(k, own, carry)
        finish(own, carry)
        count = float(near * block * (pl.num_programs(0) - 1))
        mean = project(sums[0], sums[1]) / count
        off = mean - pivot_ref[...]
        m2 = jnp.sum(square[...], axis=0, keepdims=True) - count * off * off
        stat_ref[...] = jnp.broadcast_to(jnp.concatenate([mean, m2], axis=0)[None], stat_ref.shape)


def edge_stats(index, pieces, own, weight):
    rows, c = own.shape
    d = weight.shape[1]
    blocks = rows // BLOCK
    near = index.shape[0] // blocks
    total = sum(piece.shape[0] for piece in pieces)
    before = lambda b: jnp.maximum(b - 1, 0)
    whole = lambda x: pl.BlockSpec(x.shape, lambda b: (0,) * len(x.shape))
    stat = jax.ShapeDtypeStruct((lax.axis_size(BOTH), 2, d), f32)
    pivot = jax.ShapeDtypeStruct((1, d), f32)
    return pl.pallas_call(
        functools.partial(edge_kernel, len(pieces)),
        grid=(blocks + 1,),
        out_shape=(
            jax.ShapeDtypeStruct((near, rows, c), bf16),
            jax.ShapeDtypeStruct((near, rows, d), f32),
            stat,
            pivot,
        ),
        in_specs=[smem()]
        + [whole(piece) for piece in pieces]
        + [pl.BlockSpec((BLOCK, c), lambda b: (before(b), 0)), whole(weight)],
        out_specs=(
            pl.BlockSpec((near, BLOCK, c), lambda b: (0, before(b), 0)),
            pl.BlockSpec((near, BLOCK, d), lambda b: (0, before(b), 0)),
            whole(stat),
            whole(pivot),
        ),
        scratch_shapes=[
            pltpu.VMEM((total, LANES), f32),
            pltpu.VMEM((near * BLOCK, LANES), f32),
            pltpu.VMEM((BLOCK, d), f32),
            pltpu.VMEM((2, 8, c), f32),
            pltpu.VMEM((8, d), f32),
        ],
        compiler_params=params(),
        cost_estimate=lasting(22),
        name="edge_stats",
    )(index, *pieces, own, weight)


def moments(stat, edges_each):
    devices = stat.shape[0]
    means = stat[:, 0, :]
    mean = jnp.sum(means, axis=0, keepdims=True) * (1.0 / devices)
    off = means - mean
    m2 = jnp.sum(stat[:, 1, :], axis=0, keepdims=True) + edges_each * jnp.sum(
        off * off, axis=0, keepdims=True
    )
    return mean, lax.rsqrt(m2 * (1.0 / (edges_each * devices)) + EPS)


def pool_kernel(last, edges_each, z_ref, stat_ref, pivot_ref, norm_ref, *refs):
    near, block, d = z_ref.shape
    if last:
        cot_ref, pooled_ref, slope_ref, sums_ref, sums = refs
    else:
        pooled_ref, slope_ref, sum_ref, moment_ref = refs
    mean, inv = moments(stat_ref[...], edges_each)
    half_scale = norm_ref[0:1, :] * inv * 0.5
    half_offset = (pivot_ref[...] - mean) * half_scale + norm_ref[1:2, :] * 0.5
    if last:

        @pl.when(pl.program_id(0) == 0)
        def _():
            sums[...] = jnp.zeros_like(sums)

    for lane in range(0, d, 128):
        lanes = pl.ds(lane, 128)
        scale = jnp.broadcast_to(half_scale[:, lane : lane + 128], (ROWS, 128))
        offset = jnp.broadcast_to(half_offset[:, lane : lane + 128], (ROWS, 128))

        def step(b, carry, lanes=lanes, scale=scale, offset=offset):
            at = pl.ds(pl.multiple_of(b * ROWS, ROWS), ROWS)
            active, bends = [], []
            for k in range(near):
                half = z_ref[k, at, lanes] * scale + offset
                bent = jnp.tanh(half)
                t = 1.0 + bent
                a = half * t
                active.append(a)
                bends.append(t + a * (1.0 - bent))
            top = tree(jnp.maximum, active)
            powers = [jnp.exp2((a - top) * LOG2E) for a in active]
            total = tree(jnp.add, powers)
            pooled = top + jnp.log(total) - math.log(near)
            pooled_ref[at, lanes] = pooled.astype(bf16)
            factor = 0.5 / total
            if last:
                factor = factor * cot_ref[at, lanes].astype(f32)
            halves = [z_ref[k, at, lanes] * scale + offset for k in range(near)]
            slopes = [(powers[k] * factor) * bends[k] for k in range(near)]
            slope_sum = tree(jnp.add, slopes)
            slope_moment = tree(jnp.add, [slopes[k] * halves[k] for k in range(near)])
            for k in range(near):
                slope_ref[k, at, lanes] = slopes[k]
            if not last:
                sum_ref[at, lanes] = slope_sum
                moment_ref[at, lanes] = slope_moment
                return carry
            return (carry[0] + slope_sum, carry[1] + slope_moment)

        zero = jnp.zeros((ROWS, 128), f32)
        carry = lax.fori_loop(0, block // ROWS, step, (zero, zero))
        if last:
            sums[0:1, lanes] += jnp.sum(carry[0], axis=0, keepdims=True)
            sums[1:2, lanes] += jnp.sum(carry[1], axis=0, keepdims=True)
    if last:

        @pl.when(pl.program_id(0) == pl.num_programs(0) - 1)
        def _():
            sums_ref[...] = jnp.broadcast_to(sums[...][None], sums_ref.shape)


def pool(z, stat, pivot, norm, cot=None):
    near, rows, d = z.shape
    whole = lambda x: pl.BlockSpec(x.shape, lambda b: (0,) * len(x.shape))
    by_block = pl.BlockSpec((POOL_BLOCK, d), lambda b: (b, 0))
    by_edge = pl.BlockSpec((near, POOL_BLOCK, d), lambda b: (0, b, 0))
    inputs = [z, stat, pivot, norm]
    in_specs = [by_edge, whole(stat), whole(pivot), whole(norm)]
    row_out = lambda kind: (jax.ShapeDtypeStruct((rows, d), kind), by_block)
    outs = [row_out(bf16), (jax.ShapeDtypeStruct((near, rows, d), f32), by_edge)]
    scratch = []
    if cot is None:
        outs += [row_out(f32), row_out(f32)]
    else:
        inputs.append(cot)
        in_specs.append(by_block)
        sums = jax.ShapeDtypeStruct(stat.shape, f32)
        outs.append((sums, whole(sums)))
        scratch.append(pltpu.VMEM((2, d), f32))
    return pl.pallas_call(
        functools.partial(pool_kernel, cot is not None, float(near * rows)),
        grid=(rows // POOL_BLOCK,),
        out_shape=tuple(o[0] for o in outs),
        in_specs=in_specs,
        out_specs=tuple(o[1] for o in outs),
        scratch_shapes=scratch,
        compiler_params=params(),
        cost_estimate=lasting(12 if cot is None else 20),
        name="pool",
    )(*inputs)


def grads_kernel(
    edges_each,
    inner,
    idx_ref,
    slope_ref,
    z_ref,
    back_ref,
    stat_ref,
    pivot_ref,
    norm_ref,
    grads_ref,
    *refs,
):
    near, block, d = slope_ref.shape
    if inner:
        upstream_ref, diff_ref, line_ref, dz_sum_ref, weight_ref, send_ref, dz_ref = refs[: -LINES - 2]
    else:
        line_ref, dz_sum_ref, dz_ref, send_ref = refs[: -LINES - 2]
    spread, sem = refs[-LINES - 2], refs[-1]
    lines = refs[-LINES - 1 : -1]
    step_id = pl.program_id(0)
    last = pl.num_programs(0) - 1
    total, rows = lines[0].shape[0], dz_sum_ref.shape[0]
    turns = block // 16 * (d // 128)
    share = near * block // turns

    def clear(i, _):
        at = pl.ds(pl.multiple_of(i * 256, 256), 256)
        for line in lines:
            line[at, :] = jnp.zeros((256, LANES), f32)
        return 0

    def store(waiting, most):
        while len(waiting) > most:
            line, place, row = waiting.pop(0)
            line[place, :] = row

    def add(turn, edges, waiting):
        at = (step_id - 1) * turns + turn
        base = pl.multiple_of(turn * share, 16)
        for e in edges:
            line = lines[e % LINES]
            place = pl.ds(idx_ref[at, e], 1)
            waiting.append((line, place, line[place, :] + spread[pl.ds(base + e, 1), :]))
            store(waiting, LINES - 1)

    def work(adding):
        edges = edges_each * stat_ref.shape[0]
        mean, inv = moments(stat_ref[...], edges_each)
        gain = norm_ref[0:1, :]
        sums = jnp.sum(grads_ref[...], axis=0)
        grad_shift = sums[0:1]
        grad_gain = (2.0 * sums[1:2] - norm_ref[1:2, :] * grad_shift) / gain
        alpha = gain * inv
        rate = alpha * inv * grad_gain * (1.0 / edges)
        constant = alpha * grad_shift * (1.0 / edges) + rate * (pivot_ref[...] - mean)

        for lane in range(0, d, 128):
            lanes = pl.ds(lane, 128)
            wide = lambda x, lane=lane: jnp.broadcast_to(x[:, lane : lane + 128], (16, 128))
            wide_alpha, wide_rate, offset = wide(alpha), wide(rate), wide(constant)

            def step(
                b, _, lane=lane, lanes=lanes, wide_alpha=wide_alpha, wide_rate=wide_rate, offset=offset
            ):
                at = pl.ds(pl.multiple_of(b * 16, 16), 16)
                factor = wide_alpha
                if inner:
                    factor = factor * upstream_ref[at, lanes]
                load = lambda k: (slope_ref[k, at, lanes], z_ref[k, at, lanes])
                loaded = [load(k) for k in range(AHEAD)]
                dzs, waiting = [], []
                each = share // near
                for k in range(near):
                    if adding:
                        turn = lane // 128 * (block // 16) + b
                        add(turn, range(k * each, (k + 1) * each), waiting)
                    if k + AHEAD < near:
                        loaded.append(load(k + AHEAD))
                    slope, z = loaded[k]
                    dzs.append((factor * slope - offset - wide_rate * z).astype(bf16))
                    if k >= AHEAD:
                        dz_ref[k - AHEAD, at, lanes] = dzs[k - AHEAD]
                store(waiting, 0)
                for k in range(near - AHEAD, near):
                    dz_ref[k, at, lanes] = dzs[k]
                row = pl.multiple_of(step_id * block + b * 16, 16)
                dz_sum_ref[pl.ds(row, 16), lanes] = tree(jnp.add, [dz.astype(f32) for dz in dzs])
                return 0

            lax.fori_loop(0, block // 16, step, 0)

        flat = dz_ref[...].reshape(near * block, d)
        spread[...] = dot_t(flat, back_ref[...]).astype(bf16).astype(f32)
        if inner:
            weight_ref[...] += lax.dot_general(
                diff_ref[...].reshape(near * block, diff_ref.shape[2]),
                flat,
                (((0,), (0,)), ((), ())),
                preferred_element_type=f32,
            )

    @pl.when(step_id == 0)
    def _():
        lax.fori_loop(0, total // 256, clear, 0)
        if inner:
            weight_ref[...] = jnp.zeros_like(weight_ref)
        work(False)

    @pl.when((step_id > 0) & (step_id < last))
    def _():
        work(True)

    @pl.when(step_id == last)
    def _():
        def rest(turn, _):
            waiting = []
            add(turn, range(share), waiting)
            store(waiting, 0)
            return 0

        lax.fori_loop(0, turns, rest, 0)

        def join(i, _):
            at = pl.ds(pl.multiple_of(i * 256, 256), 256)
            lines[0][at, :] = tree(jnp.add, [line[at, :] for line in lines])
            return 0

        lax.fori_loop(0, total // 256, join, 0)
        copy = pltpu.make_async_copy(lines[0], line_ref, sem)
        copy.start()
        send_ref[...] = lines[0][pl.ds(total // 2, rows), : send_ref.shape[1]].astype(bf16)
        copy.wait()


def edge_grads(order, slope, z, weight, stat, pivot, norm, grads, total, inner=()):
    near, rows, d = slope.shape
    c = weight.shape[0] // 2
    blocks = rows // BLOCK
    now = lambda b: jnp.minimum(b, blocks - 1)
    whole = lambda x: pl.BlockSpec(x.shape, lambda b: (0,) * len(x.shape))
    by_block = lambda width: pl.BlockSpec((BLOCK, width), lambda b: (now(b), 0))
    by_edge = lambda width: pl.BlockSpec((near, BLOCK, width), lambda b: (0, now(b), 0))
    back = jnp.pad(weight[c:], ((0, LANES - c), (0, 0)))
    order = order.reshape(rows // 16 * (d // 128), -1)
    inputs = [order, slope, z, back, stat, pivot, norm, grads, *inner]
    in_specs = [
        smem(),
        by_edge(d),
        by_edge(d),
        whole(back),
        whole(stat),
        whole(pivot),
        whole(norm),
        whole(grads),
    ]
    if inner:
        in_specs += [by_block(d), by_edge(c)]
    body = functools.partial(grads_kernel, float(near * rows), bool(inner))
    dz = jax.ShapeDtypeStruct((near, rows, d), bf16)
    dz_sum = jax.ShapeDtypeStruct((rows, d), f32)
    outs = [
        (jax.ShapeDtypeStruct((total, LANES), f32), pl.BlockSpec(memory_space=pl.ANY)),
        (dz_sum, whole(dz_sum)),
    ]
    scratch = [
        pltpu.VMEM((near * BLOCK, LANES), f32),
        *[pltpu.VMEM((total, LANES), f32)] * LINES,
        pltpu.SemaphoreType.DMA,
    ]
    if inner:
        part = jax.ShapeDtypeStruct((c, d), f32)
        outs.append((part, whole(part)))
        scratch.insert(0, pltpu.VMEM((near, BLOCK, d), bf16))
    else:
        outs.append((dz, by_edge(d)))
    send = jax.ShapeDtypeStruct((rows, c), bf16)
    outs.append((send, whole(send)))
    return pl.pallas_call(
        body,
        grid=(blocks + 1,),
        out_shape=tuple(o[0] for o in outs),
        in_specs=in_specs,
        out_specs=tuple(o[1] for o in outs),
        scratch_shapes=scratch,
        compiler_params=params(),
        cost_estimate=lasting(40),
        name="edge_grads",
    )(*inputs)


def copies(x):
    return jnp.broadcast_to(x[None], (lax.axis_size(BOTH),) + x.shape)


def shared(x):
    devices = lax.axis_size(BOTH)
    return x.reshape(devices, x.shape[0] // devices, x.shape[1])


def exchange(shares):
    return lax.all_to_all(shares, BOTH, split_axis=0, concat_axis=0, tiled=True)


def everyone(x):
    return exchange(copies(x))


def ring_moves(places):
    ring = list(range(0, places, 2)) + list(range(1, places, 2))[::-1]
    onward = [(ring[i], ring[(i + 1) % places]) for i in range(places)]
    return onward, [(b, a) for a, b in onward]


def ring_place(device, places):
    return jnp.where(device % 2 == 0, device // 2, places - 1 - device // 2)


def line_table(values):
    places = lax.axis_size("pts")
    onward, backward = ring_moves(places)
    rows, far = values.shape[0] // 2, places // 2
    behind, ahead = [values], [values]
    for _ in range(far - 1):
        behind.append(lax.ppermute(behind[-1], "pts", onward))
        ahead.append(lax.ppermute(ahead[-1], "pts", backward))
    farthest = [
        lax.ppermute(behind[-1][:rows], "pts", onward),
        lax.ppermute(ahead[-1][rows:], "pts", backward),
    ]
    return behind + farthest + ahead[:0:-1]


def owners_sum(line, send, centre, weights=None):
    places = lax.axis_size("pts")
    onward, backward = ring_moves(places)
    rows, c = centre.shape
    half, far = rows // 2, places // 2

    def slot(j):
        return line[j * rows : (j + 1) * rows, :c]

    forth = lax.ppermute(send[:half], "pts", onward)
    back = lax.ppermute(send[half:], "pts", backward)
    if weights is not None:
        forth, back, weights = lax.optimization_barrier((forth, back, weights))
        shares = exchange(shared(weights))
    forth = jnp.pad(forth.astype(f32), ((0, half), (0, 0)))
    back = jnp.pad(back.astype(f32), ((half, 0), (0, 0)))
    for j in range(1, far):
        forth, back = (forth + slot(far + j)).astype(bf16), (back + slot(far - j)).astype(bf16)
        forth, back = lax.optimization_barrier((forth, back))
        if weights is not None and j == far - 1:
            forth, back, shares = lax.optimization_barrier((forth, back, shares))
            weights = everyone(jnp.sum(shares.astype(f32), axis=0).astype(bf16))
        forth = lax.ppermute(forth, "pts", onward).astype(f32)
        back = lax.ppermute(back, "pts", backward).astype(f32)
    return centre + slot(0) + forth + back, weights


def centre_grad(dz_sum, weight):
    wide = weight.astype(f32)
    c = weight.shape[0] // 2
    return exact(dz_sum, (wide[:c] - wide[c:]).T)


def per_device(
    points,
    lengths,
    neighbours_one,
    neighbours_two,
    weight_one,
    gain_one,
    shift_one,
    weight_two,
    gain_two,
    shift_two,
    cotangent,
):
    line_devices = lax.axis_size("pts")
    row_count = points.shape[0]
    line_length = line_devices * row_count
    table_one = line_table(points)

    norm_one, norm_two = jnp.stack([gain_one, shift_one]), jnp.stack([gain_two, shift_two])

    cloud_ends = jnp.cumsum(lengths)
    cloud_starts = cloud_ends - lengths
    line_first = lax.axis_index("loc") * line_length
    position = (
        line_first + lax.axis_index("pts") * row_count + jnp.arange(row_count, dtype=jnp.int32)
    )
    begins = (position[:, None] >= cloud_starts[None, :]) & (position[:, None] < cloud_ends[None, :])
    begin = jnp.sum(jnp.where(begins, cloud_starts[None, :], 0), axis=1) - line_first
    here = ring_place(lax.axis_index("pts"), line_devices)

    def slot_rows(neighbours):
        within = neighbours.T + begin[None, :]
        slot = (here - ring_place(within // row_count, line_devices)) % line_devices
        return slot * row_count + within % row_count

    def by_blocks(index):
        blocks = index.reshape(index.shape[0], -1, BLOCK)
        return blocks.transpose(1, 0, 2).reshape(-1, BLOCK)

    index_one = slot_rows(neighbours_one)
    index_two = slot_rows(neighbours_two)
    order_one, order_two = by_blocks(index_one), by_blocks(index_two)

    diff_one, z_one, stat_one, pivot_one = edge_stats(order_one, table_one, points, weight_one)
    stat_one, order_two = lax.optimization_barrier((exchange(stat_one), order_two))
    act_one, slope_one, slope_sum, slope_moment = pool(z_one, stat_one, pivot_one, norm_one)
    table_two = line_table(act_one)
    diff_two, z_two, stat_two, pivot_two = edge_stats(order_two, table_two, act_one, weight_two)
    stat_two = exchange(stat_two)
    act_two, slope_two, sums_two = pool(z_two, stat_two, pivot_two, norm_two, cotangent)
    sums_two = exchange(sums_two)
    line_two, dz_sum_two, dz_two, send_two = edge_grads(
        order_two,
        slope_two,
        z_two,
        weight_two,
        stat_two,
        pivot_two,
        norm_two,
        sums_two,
        line_length,
    )
    grad_first, _ = owners_sum(line_two, send_two, centre_grad(dz_sum_two, weight_two))
    grad_first, dz_two, dz_sum_two = lax.optimization_barrier((grad_first, dz_two, dz_sum_two))
    first_two = exact(act_one.astype(f32).T, dz_sum_two)
    second_two = jnp.einsum("kgc,kgd->cd", diff_two, dz_two, preferred_element_type=f32)
    sums_one = jnp.stack(
        [jnp.sum(grad_first * slope_sum, axis=0), jnp.sum(grad_first * slope_moment, axis=0)]
    )
    sums_one = everyone(sums_one)
    line_one, dz_sum_one, second_one, send_one = edge_grads(
        order_one,
        slope_one,
        z_one,
        weight_one,
        stat_one,
        pivot_one,
        norm_one,
        sums_one,
        line_length,
        (grad_first, diff_one),
    )
    first_one = exact(points.astype(f32).T, dz_sum_one)
    weights = jnp.concatenate(
        [first_two.reshape(-1, LANES), second_two.reshape(-1, LANES), first_one, second_one], axis=0
    )
    grad_points, weights = owners_sum(
        line_one, send_one, centre_grad(dz_sum_one, weight_one), weights.astype(bf16)
    )
    weights = weights.reshape(-1, LANES).astype(f32)
    grad_weight_two = weights[: -weight_one.shape[0]].reshape(weight_two.shape)
    grad_weight_one = weights[-weight_one.shape[0] :]

    def norm_grads(sums, gain, shift):
        sums = jnp.sum(sums, axis=0)
        return (2.0 * sums[1] - shift * sums[0]) / gain, sums[0]

    grad_gain_one, grad_shift_one = norm_grads(sums_one, gain_one, shift_one)
    grad_gain_two, grad_shift_two = norm_grads(sums_two, gain_two, shift_two)
    return (
        act_one,
        act_two,
        grad_points,
        grad_weight_one,
        grad_gain_one,
        grad_shift_one,
        grad_weight_two,
        grad_gain_two,
        grad_shift_two,
    )


def solution(mesh):
    rows, copied = P(("pts", "loc"), None), P()
    in_specs = (rows, copied, rows, rows) + (copied,) * 6 + (rows,)
    out_specs = (rows, rows, rows) + (copied,) * 6
    return jax.shard_map(
        per_device, mesh=mesh, in_specs=in_specs, out_specs=out_specs, check_vma=False
    )
```

```python
import functools
import math

import jax
import jax.numpy as jnp
from jax import lax
from jax.experimental import pallas as pl
from jax.experimental.pallas import tpu as pltpu
from jax.sharding import PartitionSpec as P

EPS = 1e-05
BLOCK = 128
POOL_BLOCK = 256
GROUP = 8
LINES = 4
POINTS = 16
ROWS = 16
AHEAD = 4
LOG2E = 1.0 / math.log(2.0)
LANES = 128
MIB = 1024 * 1024
BOTH = ("pts", "loc")

f32 = jnp.float32
bf16 = jnp.bfloat16


def params():
    return pltpu.CompilerParams(vmem_limit_bytes=52 * MIB)


def lasting(microseconds):
    return pl.CostEstimate(flops=0, transcendentals=0, bytes_accessed=3_000_000 * microseconds)


def smem():
    return pl.BlockSpec(memory_space=pltpu.SMEM)


def fold_rows(x):
    return jnp.sum(x.reshape(x.shape[0] // 8, 8, x.shape[1]), axis=0)


def tree(op, terms):
    while len(terms) > 1:
        pairs = [op(a, b) for a, b in zip(terms[::2], terms[1::2])]
        terms = pairs + terms[len(pairs) * 2 :]
    return terms[0]


def dot(a, b):
    return jnp.dot(a, b, preferred_element_type=f32)


def exact(a, b):
    return jnp.dot(a, b, precision=lax.Precision.HIGHEST, preferred_element_type=f32)


def dot_t(a, b):
    return lax.dot_general(a, b, (((1,), (1,)), ((), ())), preferred_element_type=f32)


def edge_kernel(pieces, *refs):
    table_refs = refs[1 : 1 + pieces]
    idx_ref = refs[0]
    own_ref, w_ref, diff_ref, z_ref, stat_ref, pivot_ref, table, rows, centre, sums, square = refs[
        1 + pieces :
    ]
    near, block, c = diff_ref.shape
    step_id = pl.program_id(0)
    last = pl.num_programs(0) - 1
    chunk = 4

    def project(own_sum, diff_sum):
        weight = w_ref[...].astype(f32)
        both = exact(own_sum, weight[:c]) + exact(diff_sum, weight[c:])
        return jnp.sum(both, axis=0, keepdims=True)

    @pl.when(step_id == 0)
    def _():
        first = 0
        for piece in table_refs:
            for r in range(0, piece.shape[0], 256):
                table[pl.ds(first + r, 256), :c] = piece[pl.ds(r, 256), :].astype(f32)
            first += piece.shape[0]
        sums[...] = jnp.zeros_like(sums)
        square[...] = jnp.zeros_like(square)

    @pl.when(step_id == 1)
    def _():
        own = own_ref[...].astype(f32)
        diff_sum = jnp.zeros((8, c), f32)
        for k in range(near):
            diff_sum = diff_sum + fold_rows(rows[pl.ds(k * block, block), :c] - own)
        own_sum = fold_rows(own) * float(near)
        pivot_ref[...] = project(own_sum, diff_sum) * (1.0 / (near * block))

    def pick(k):
        base = pl.multiple_of(k * block, block)
        at = step_id * near + k
        waiting = []
        for e in range(block + GROUP):
            if e < block:
                waiting.append(table[pl.ds(idx_ref[at, e], 1), :])
            if e >= GROUP:
                rows[pl.ds(base + (e - GROUP), 1), :] = waiting[e - GROUP]

    def work(k, own, carry):
        diff_sum, total = carry
        at = pl.ds(pl.multiple_of(k * block, block), block)
        diff = (rows[at, :c] - own).astype(bf16)
        diff_ref[k] = diff
        diff_sum = diff_sum + fold_rows(diff.astype(f32))
        z = dot(diff, w_ref[c:, :]) + centre[...]
        z_ref[k] = z
        return diff_sum, total + fold_rows(z * z)

    @pl.when(step_id == 0)
    def _():
        def body(i, _):
            pick(i)
            return 0

        lax.fori_loop(0, near, body, 0)

    def finish(own, carry):
        sums[0] += fold_rows(own) * float(near)
        sums[1] += carry[0]
        square[...] += carry[1]

    def begin():
        centre[...] = dot(own_ref[...], w_ref[:c, :]) - pivot_ref[...]
        zero = (jnp.zeros((8, c), f32), jnp.zeros_like(square[...]))
        return own_ref[...].astype(f32), zero

    @pl.when((step_id > 0) & (step_id < last))
    def _():
        own, zero = begin()

        def body(i, carry):
            for k in range(chunk):
                carry = work(i * chunk + k, own_ref[...].astype(f32), carry)
                pick(i * chunk + k)
            return carry

        finish(own, lax.fori_loop(0, near // chunk, body, zero))

    @pl.when(step_id == last)
    def _():
        own, carry = begin()
        for k in range(near):
            carry = work(k, own, carry)
        finish(own, carry)
        count = float(near * block * (pl.num_programs(0) - 1))
        mean = project(sums[0], sums[1]) / count
        off = mean - pivot_ref[...]
        m2 = jnp.sum(square[...], axis=0, keepdims=True) - count * off * off
        stat_ref[...] = jnp.broadcast_to(jnp.concatenate([mean, m2], axis=0)[None], stat_ref.shape)


def edge_stats(index, pieces, own, weight):
    rows, c = own.shape
    d = weight.shape[1]
    blocks = rows // BLOCK
    near = index.shape[0] // blocks
    total = sum(piece.shape[0] for piece in pieces)
    before = lambda b: jnp.maximum(b - 1, 0)
    whole = lambda x: pl.BlockSpec(x.shape, lambda b: (0,) * len(x.shape))
    stat = jax.ShapeDtypeStruct((lax.axis_size(BOTH), 2, d), f32)
    pivot = jax.ShapeDtypeStruct((1, d), f32)
    return pl.pallas_call(
        functools.partial(edge_kernel, len(pieces)),
        grid=(blocks + 1,),
        out_shape=(
            jax.ShapeDtypeStruct((near, rows, c), bf16),
            jax.ShapeDtypeStruct((near, rows, d), f32),
            stat,
            pivot,
        ),
        in_specs=[smem()]
        + [whole(piece) for piece in pieces]
        + [pl.BlockSpec((BLOCK, c), lambda b: (before(b), 0)), whole(weight)],
        out_specs=(
            pl.BlockSpec((near, BLOCK, c), lambda b: (0, before(b), 0)),
            pl.BlockSpec((near, BLOCK, d), lambda b: (0, before(b), 0)),
            whole(stat),
            whole(pivot),
        ),
        scratch_shapes=[
            pltpu.VMEM((total, LANES), f32),
            pltpu.VMEM((near * BLOCK, LANES), f32),
            pltpu.VMEM((BLOCK, d), f32),
            pltpu.VMEM((2, 8, c), f32),
            pltpu.VMEM((8, d), f32),
        ],
        compiler_params=params(),
        cost_estimate=lasting(22),
        name="edge_stats",
    )(index, *pieces, own, weight)


def moments(stat, edges_each):
    devices = stat.shape[0]
    means = stat[:, 0, :]
    mean = jnp.sum(means, axis=0, keepdims=True) * (1.0 / devices)
    off = means - mean
    m2 = jnp.sum(stat[:, 1, :], axis=0, keepdims=True) + edges_each * jnp.sum(
        off * off, axis=0, keepdims=True
    )
    return mean, lax.rsqrt(m2 * (1.0 / (edges_each * devices)) + EPS)


def pool_kernel(last, edges_each, z_ref, stat_ref, pivot_ref, norm_ref, *refs):
    near, block, d = z_ref.shape
    if last:
        cot_ref, pooled_ref, slope_ref, sums_ref, sums = refs
    else:
        pooled_ref, slope_ref, sum_ref, moment_ref = refs
    mean, inv = moments(stat_ref[...], edges_each)
    half_scale = norm_ref[0:1, :] * inv * 0.5
    half_offset = (pivot_ref[...] - mean) * half_scale + norm_ref[1:2, :] * 0.5
    if last:

        @pl.when(pl.program_id(0) == 0)
        def _():
            sums[...] = jnp.zeros_like(sums)

    for lane in range(0, d, 128):
        lanes = pl.ds(lane, 128)
        scale = jnp.broadcast_to(half_scale[:, lane : lane + 128], (ROWS, 128))
        offset = jnp.broadcast_to(half_offset[:, lane : lane + 128], (ROWS, 128))

        def step(b, carry, lanes=lanes, scale=scale, offset=offset):
            at = pl.ds(pl.multiple_of(b * ROWS, ROWS), ROWS)
            active, bends = [], []
            for k in range(near):
                half = z_ref[k, at, lanes] * scale + offset
                bent = jnp.tanh(half)
                t = 1.0 + bent
                a = half * t
                active.append(a)
                bends.append(t + a * (1.0 - bent))
            top = tree(jnp.maximum, active)
            powers = [jnp.exp2((a - top) * LOG2E) for a in active]
            total = tree(jnp.add, powers)
            pooled = top + jnp.log(total) - math.log(near)
            pooled_ref[at, lanes] = pooled.astype(bf16)
            factor = 0.5 / total
            if last:
                factor = factor * cot_ref[at, lanes].astype(f32)
            halves = [z_ref[k, at, lanes] * scale + offset for k in range(near)]
            slopes = [(powers[k] * factor) * bends[k] for k in range(near)]
            slope_sum = tree(jnp.add, slopes)
            slope_moment = tree(jnp.add, [slopes[k] * halves[k] for k in range(near)])
            for k in range(near):
                slope_ref[k, at, lanes] = slopes[k]
            if not last:
                sum_ref[at, lanes] = slope_sum
                moment_ref[at, lanes] = slope_moment
                return carry
            return (carry[0] + slope_sum, carry[1] + slope_moment)

        zero = jnp.zeros((ROWS, 128), f32)
        carry = lax.fori_loop(0, block // ROWS, step, (zero, zero))
        if last:
            sums[0:1, lanes] += jnp.sum(carry[0], axis=0, keepdims=True)
            sums[1:2, lanes] += jnp.sum(carry[1], axis=0, keepdims=True)
    if last:

        @pl.when(pl.program_id(0) == pl.num_programs(0) - 1)
        def _():
            sums_ref[...] = jnp.broadcast_to(sums[...][None], sums_ref.shape)


def pool(z, stat, pivot, norm, cot=None):
    near, rows, d = z.shape
    whole = lambda x: pl.BlockSpec(x.shape, lambda b: (0,) * len(x.shape))
    by_block = pl.BlockSpec((POOL_BLOCK, d), lambda b: (b, 0))
    by_edge = pl.BlockSpec((near, POOL_BLOCK, d), lambda b: (0, b, 0))
    inputs = [z, stat, pivot, norm]
    in_specs = [by_edge, whole(stat), whole(pivot), whole(norm)]
    row_out = lambda kind: (jax.ShapeDtypeStruct((rows, d), kind), by_block)
    outs = [row_out(bf16), (jax.ShapeDtypeStruct((near, rows, d), f32), by_edge)]
    scratch = []
    if cot is None:
        outs += [row_out(f32), row_out(f32)]
    else:
        inputs.append(cot)
        in_specs.append(by_block)
        sums = jax.ShapeDtypeStruct(stat.shape, f32)
        outs.append((sums, whole(sums)))
        scratch.append(pltpu.VMEM((2, d), f32))
    return pl.pallas_call(
        functools.partial(pool_kernel, cot is not None, float(near * rows)),
        grid=(rows // POOL_BLOCK,),
        out_shape=tuple(o[0] for o in outs),
        in_specs=in_specs,
        out_specs=tuple(o[1] for o in outs),
        scratch_shapes=scratch,
        compiler_params=params(),
        cost_estimate=lasting(12 if cot is None else 20),
        name="pool",
    )(*inputs)


def grads_kernel(
    edges_each,
    inner,
    idx_ref,
    slope_ref,
    z_ref,
    back_ref,
    stat_ref,
    pivot_ref,
    norm_ref,
    grads_ref,
    *refs,
):
    near, block, d = slope_ref.shape
    if inner:
        upstream_ref, diff_ref, line_ref, dz_sum_ref, weight_ref, send_ref, dz_ref = refs[: -LINES - 3]
    else:
        line_ref, dz_sum_ref, dz_ref, send_ref = refs[: -LINES - 3]
    fresh, held, sem = refs[-LINES - 3], refs[-LINES - 2], refs[-1]
    lines = refs[-LINES - 1 : -1]
    step_id = pl.program_id(0)
    last = pl.num_programs(0) - 1
    total, rows = lines[0].shape[0], dz_sum_ref.shape[0]
    turns = block // POINTS
    share = near * POINTS

    def store(waiting, most):
        while len(waiting) > most:
            line, place, row = waiting.pop(0)
            line[place, :] = row

    def add(turn, edges, waiting):
        for e in edges:
            line = lines[e % LINES]
            place = pl.ds(idx_ref[turn, e], 1)
            waiting.append((line, place, line[place, :] + held[pl.ds(e, 1), :]))
            store(waiting, LINES - 1)

    @pl.when(step_id == 0)
    def _():
        def clear(i, _):
            at = pl.ds(pl.multiple_of(i * 256, 256), 256)
            for line in lines:
                line[at, :] = jnp.zeros((256, LANES), f32)
            return 0

        lax.fori_loop(0, total // 256, clear, 0)
        fresh[...] = jnp.zeros_like(fresh)
        if inner:
            weight_ref[...] = jnp.zeros_like(weight_ref)

    edges = edges_each * stat_ref.shape[0]
    mean, inv = moments(stat_ref[...], edges_each)
    gain = norm_ref[0:1, :]
    sums = jnp.sum(grads_ref[...], axis=0)
    grad_shift = sums[0:1]
    grad_gain = (2.0 * sums[1:2] - norm_ref[1:2, :] * grad_shift) / gain
    alpha = gain * inv
    rate = alpha * inv * grad_gain * (1.0 / edges)
    constant = alpha * grad_shift * (1.0 / edges) + rate * (pivot_ref[...] - mean)
    wide = [
        [jnp.broadcast_to(x[:, lane : lane + 128], (POINTS, 128)) for x in (alpha, rate, constant)]
        for lane in range(0, d, 128)
    ]

    def turn(t, _):
        at = pl.ds(pl.multiple_of(t * POINTS, POINTS), POINTS)
        before = jnp.maximum(step_id * turns + t - 1, 0)
        held[...] = fresh[...]
        units = [(k, i) for i in range(d // 128) for k in range(near)]
        factors = [w[0] for w in wide]
        if inner:
            factors = [
                f * upstream_ref[at, pl.ds(i * 128, 128)] for i, f in enumerate(factors)
            ]

        def load(unit):
            k, i = unit
            lanes = pl.ds(i * 128, 128)
            return slope_ref[k, at, lanes], z_ref[k, at, lanes]

        loaded = [load(unit) for unit in units[:AHEAD]]
        dzs, waiting = {}, []
        each = share // 2 // len(units)
        for n, (k, i) in enumerate(units):
            add(before, range(n * each, (n + 1) * each), waiting)
            if n + AHEAD < len(units):
                loaded.append(load(units[n + AHEAD]))
            slope, z = loaded[n]
            dzs[k, i] = (factors[i] * slope - wide[i][2] - wide[i][1] * z).astype(bf16)
            dz_ref[k, at, pl.ds(i * 128, 128)] = dzs[k, i]
        whole = [
            jnp.concatenate([dzs[k, i] for k in range(near)], axis=0) for i in range(d // 128)
        ]
        product = dot_t(jnp.concatenate(whole, axis=1), back_ref[...]).astype(bf16)
        add(before, range(share // 2, share), waiting)
        row = pl.multiple_of(step_id * block + t * POINTS, POINTS)
        for i in range(d // 128):
            dz_sum_ref[pl.ds(row, POINTS), pl.ds(i * 128, 128)] = tree(
                jnp.add, [dzs[k, i].astype(f32) for k in range(near)]
            )
        store(waiting, 0)
        fresh[...] = product.astype(f32)
        return 0

    lax.fori_loop(0, turns, turn, 0)
    if inner:
        weight_ref[...] += lax.dot_general(
            diff_ref[...].reshape(near * block, diff_ref.shape[2]),
            dz_ref[...].reshape(near * block, d),
            (((0,), (0,)), ((), ())),
            preferred_element_type=f32,
        )

    @pl.when(step_id == last)
    def _():
        held[...] = fresh[...]
        waiting = []
        add(rows // POINTS - 1, range(share), waiting)
        store(waiting, 0)

        def join(i, _):
            at = pl.ds(pl.multiple_of(i * 256, 256), 256)
            lines[0][at, :] = tree(jnp.add, [line[at, :] for line in lines])
            return 0

        lax.fori_loop(0, total // 256, join, 0)
        copy = pltpu.make_async_copy(lines[0], line_ref, sem)
        copy.start()
        send_ref[...] = lines[0][pl.ds(total // 2, rows), : send_ref.shape[1]].astype(bf16)
        copy.wait()


def edge_grads(turns, slope, z, weight, stat, pivot, norm, grads, total, inner=()):
    near, rows, d = slope.shape
    c = weight.shape[0] // 2
    whole = lambda x: pl.BlockSpec(x.shape, lambda b: (0,) * len(x.shape))
    by_block = lambda width: pl.BlockSpec((BLOCK, width), lambda b: (b, 0))
    by_edge = lambda width: pl.BlockSpec((near, BLOCK, width), lambda b: (0, b, 0))
    back = jnp.pad(weight[c:], ((0, LANES - c), (0, 0)))
    inputs = [turns, slope, z, back, stat, pivot, norm, grads, *inner]
    in_specs = [
        smem(),
        by_edge(d),
        by_edge(d),
        whole(back),
        whole(stat),
        whole(pivot),
        whole(norm),
        whole(grads),
    ]
    if inner:
        in_specs += [by_block(d), by_edge(c)]
    dz = jax.ShapeDtypeStruct((near, rows, d), bf16)
    dz_sum = jax.ShapeDtypeStruct((rows, d), f32)
    send = jax.ShapeDtypeStruct((rows, c), bf16)
    outs = [
        (jax.ShapeDtypeStruct((total, LANES), f32), pl.BlockSpec(memory_space=pl.ANY)),
        (dz_sum, whole(dz_sum)),
    ]
    scratch = [
        pltpu.VMEM((near * POINTS, LANES), f32),
        pltpu.VMEM((near * POINTS, LANES), f32),
        *[pltpu.VMEM((total, LANES), f32)] * LINES,
        pltpu.SemaphoreType.DMA,
    ]
    if inner:
        part = jax.ShapeDtypeStruct((c, d), f32)
        outs.append((part, whole(part)))
        scratch.insert(0, pltpu.VMEM((near, BLOCK, d), bf16))
    else:
        outs.append((dz, by_edge(d)))
    outs.append((send, whole(send)))
    return pl.pallas_call(
        functools.partial(grads_kernel, float(near * rows), bool(inner)),
        grid=(rows // BLOCK,),
        out_shape=tuple(o[0] for o in outs),
        in_specs=in_specs,
        out_specs=tuple(o[1] for o in outs),
        scratch_shapes=scratch,
        compiler_params=params(),
        cost_estimate=lasting(35),
        name="edge_grads",
    )(*inputs)


def copies(x):
    return jnp.broadcast_to(x[None], (lax.axis_size(BOTH),) + x.shape)


def shared(x):
    devices = lax.axis_size(BOTH)
    return x.reshape(devices, x.shape[0] // devices, x.shape[1])


def exchange(shares):
    return lax.all_to_all(shares, BOTH, split_axis=0, concat_axis=0, tiled=True)


def everyone(x):
    return exchange(copies(x))


def ring_moves(places):
    ring = list(range(0, places, 2)) + list(range(1, places, 2))[::-1]
    onward = [(ring[i], ring[(i + 1) % places]) for i in range(places)]
    return onward, [(b, a) for a, b in onward]


def ring_place(device, places):
    return jnp.where(device % 2 == 0, device // 2, places - 1 - device // 2)


def line_table(values):
    places = lax.axis_size("pts")
    onward, backward = ring_moves(places)
    rows, far = values.shape[0] // 2, places // 2
    behind, ahead = [values], [values]
    for _ in range(far - 1):
        behind.append(lax.ppermute(behind[-1], "pts", onward))
        ahead.append(lax.ppermute(ahead[-1], "pts", backward))
    farthest = [
        lax.ppermute(behind[-1][:rows], "pts", onward),
        lax.ppermute(ahead[-1][rows:], "pts", backward),
    ]
    return behind + farthest + ahead[:0:-1]


def owners_sum(line, send, centre, weights=None):
    places = lax.axis_size("pts")
    onward, backward = ring_moves(places)
    rows, c = centre.shape
    half, far = rows // 2, places // 2

    def slot(j):
        return line[j * rows : (j + 1) * rows, :c]

    forth = lax.ppermute(send[:half], "pts", onward)
    back = lax.ppermute(send[half:], "pts", backward)
    if weights is not None:
        forth, back, weights = lax.optimization_barrier((forth, back, weights))
        shares = exchange(shared(weights))
    forth = jnp.pad(forth.astype(f32), ((0, half), (0, 0)))
    back = jnp.pad(back.astype(f32), ((half, 0), (0, 0)))
    for j in range(1, far):
        forth, back = (forth + slot(far + j)).astype(bf16), (back + slot(far - j)).astype(bf16)
        forth, back = lax.optimization_barrier((forth, back))
        if weights is not None and j == far - 1:
            forth, back, shares = lax.optimization_barrier((forth, back, shares))
            weights = everyone(jnp.sum(shares.astype(f32), axis=0).astype(bf16))
        forth = lax.ppermute(forth, "pts", onward).astype(f32)
        back = lax.ppermute(back, "pts", backward).astype(f32)
    return centre + slot(0) + forth + back, weights


def centre_grad(dz_sum, weight):
    wide = weight.astype(f32)
    c = weight.shape[0] // 2
    return exact(dz_sum, (wide[:c] - wide[c:]).T)


def per_device(
    points,
    lengths,
    neighbours_one,
    neighbours_two,
    weight_one,
    gain_one,
    shift_one,
    weight_two,
    gain_two,
    shift_two,
    cotangent,
):
    line_devices = lax.axis_size("pts")
    row_count = points.shape[0]
    line_length = line_devices * row_count
    table_one = line_table(points)

    norm_one, norm_two = jnp.stack([gain_one, shift_one]), jnp.stack([gain_two, shift_two])

    cloud_ends = jnp.cumsum(lengths)
    cloud_starts = cloud_ends - lengths
    line_first = lax.axis_index("loc") * line_length
    position = (
        line_first + lax.axis_index("pts") * row_count + jnp.arange(row_count, dtype=jnp.int32)
    )
    begins = (position[:, None] >= cloud_starts[None, :]) & (position[:, None] < cloud_ends[None, :])
    begin = jnp.sum(jnp.where(begins, cloud_starts[None, :], 0), axis=1) - line_first
    here = ring_place(lax.axis_index("pts"), line_devices)

    def slot_rows(neighbours):
        within = neighbours.T + begin[None, :]
        slot = (here - ring_place(within // row_count, line_devices)) % line_devices
        return slot * row_count + within % row_count

    def by_blocks(index, points):
        return index.reshape(index.shape[0], -1, points).transpose(1, 0, 2)

    index_one = slot_rows(neighbours_one)
    index_two = slot_rows(neighbours_two)
    order_one = by_blocks(index_one, BLOCK).reshape(-1, BLOCK)
    order_two = by_blocks(index_two, BLOCK).reshape(-1, BLOCK)
    turns_one = by_blocks(index_one, POINTS).reshape(row_count // POINTS, -1)
    turns_two = by_blocks(index_two, POINTS).reshape(row_count // POINTS, -1)

    diff_one, z_one, stat_one, pivot_one = edge_stats(order_one, table_one, points, weight_one)
    stat_one, order_two, turns_one, turns_two = lax.optimization_barrier(
        (exchange(stat_one), order_two, turns_one, turns_two)
    )
    act_one, slope_one, slope_sum, slope_moment = pool(z_one, stat_one, pivot_one, norm_one)
    table_two = line_table(act_one)
    diff_two, z_two, stat_two, pivot_two = edge_stats(order_two, table_two, act_one, weight_two)
    stat_two = exchange(stat_two)
    act_two, slope_two, sums_two = pool(z_two, stat_two, pivot_two, norm_two, cotangent)
    sums_two = exchange(sums_two)
    line_two, dz_sum_two, dz_two, send_two = edge_grads(
        turns_two,
        slope_two,
        z_two,
        weight_two,
        stat_two,
        pivot_two,
        norm_two,
        sums_two,
        line_length,
    )
    grad_first, _ = owners_sum(line_two, send_two, centre_grad(dz_sum_two, weight_two))
    grad_first, dz_two, dz_sum_two = lax.optimization_barrier((grad_first, dz_two, dz_sum_two))
    first_two = exact(act_one.astype(f32).T, dz_sum_two)
    second_two = jnp.einsum("kgc,kgd->cd", diff_two, dz_two, preferred_element_type=f32)
    sums_one = jnp.stack(
        [jnp.sum(grad_first * slope_sum, axis=0), jnp.sum(grad_first * slope_moment, axis=0)]
    )
    sums_one = everyone(sums_one)
    line_one, dz_sum_one, second_one, send_one = edge_grads(
        turns_one,
        slope_one,
        z_one,
        weight_one,
        stat_one,
        pivot_one,
        norm_one,
        sums_one,
        line_length,
        (grad_first, diff_one),
    )
    first_one = exact(points.astype(f32).T, dz_sum_one)
    weights = jnp.concatenate(
        [first_two.reshape(-1, LANES), second_two.reshape(-1, LANES), first_one, second_one], axis=0
    )
    grad_points, weights = owners_sum(
        line_one, send_one, centre_grad(dz_sum_one, weight_one), weights.astype(bf16)
    )
    weights = weights.reshape(-1, LANES).astype(f32)
    grad_weight_two = weights[: -weight_one.shape[0]].reshape(weight_two.shape)
    grad_weight_one = weights[-weight_one.shape[0] :]

    def norm_grads(sums, gain, shift):
        sums = jnp.sum(sums, axis=0)
        return (2.0 * sums[1] - shift * sums[0]) / gain, sums[0]

    grad_gain_one, grad_shift_one = norm_grads(sums_one, gain_one, shift_one)
    grad_gain_two, grad_shift_two = norm_grads(sums_two, gain_two, shift_two)
    return (
        act_one,
        act_two,
        grad_points,
        grad_weight_one,
        grad_gain_one,
        grad_shift_one,
        grad_weight_two,
        grad_gain_two,
        grad_shift_two,
    )


def solution(mesh):
    rows, copied = P(("pts", "loc"), None), P()
    in_specs = (rows, copied, rows, rows) + (copied,) * 6 + (rows,)
    out_specs = (rows, rows, rows) + (copied,) * 6
    return jax.shard_map(
        per_device, mesh=mesh, in_specs=in_specs, out_specs=out_specs, check_vma=False
    )
```

```python
import functools
import math

import jax
import jax.numpy as jnp
from jax import lax
from jax.experimental import pallas as pl
from jax.experimental.pallas import tpu as pltpu
from jax.sharding import PartitionSpec as P

EPS = 1e-05
MIB = 1024 * 1024
BLOCK = 128
POOL_BLOCK = 256
GROUP = 8
LINES = 6
LINE_BYTES = 32 * MIB
POINTS = 16
ROWS = 16
AHEAD = 4
LOG2E = 1.0 / math.log(2.0)
LANES = 128
BOTH = ("pts", "loc")

f32 = jnp.float32
bf16 = jnp.bfloat16


def params():
    return pltpu.CompilerParams(vmem_limit_bytes=52 * MIB)


def lasting(microseconds):
    return pl.CostEstimate(flops=0, transcendentals=0, bytes_accessed=3_000_000 * microseconds)


def smem():
    return pl.BlockSpec(memory_space=pltpu.SMEM)


def fold_rows(x):
    return jnp.sum(x.reshape(x.shape[0] // 8, 8, x.shape[1]), axis=0)


def tree(op, terms):
    while len(terms) > 1:
        pairs = [op(a, b) for a, b in zip(terms[::2], terms[1::2])]
        terms = pairs + terms[len(pairs) * 2 :]
    return terms[0]


def dot(a, b):
    return jnp.dot(a, b, preferred_element_type=f32)


def exact(a, b):
    return jnp.dot(a, b, precision=lax.Precision.HIGHEST, preferred_element_type=f32)


def dot_t(a, b):
    return lax.dot_general(a, b, (((1,), (1,)), ((), ())), preferred_element_type=f32)


def edge_kernel(pieces, *refs):
    table_refs = refs[1 : 1 + pieces]
    idx_ref = refs[0]
    own_ref, w_ref, diff_ref, z_ref, stat_ref, pivot_ref, table, rows, centre, sums, square = refs[
        1 + pieces :
    ]
    near, block, c = diff_ref.shape
    step_id = pl.program_id(0)
    last = pl.num_programs(0) - 1
    chunk = 4

    def project(own_sum, diff_sum):
        weight = w_ref[...].astype(f32)
        both = exact(own_sum, weight[:c]) + exact(diff_sum, weight[c:])
        return jnp.sum(both, axis=0, keepdims=True)

    @pl.when(step_id == 0)
    def _():
        first = 0
        for piece in table_refs:
            for r in range(0, piece.shape[0], 256):
                table[pl.ds(first + r, 256), :c] = piece[pl.ds(r, 256), :].astype(f32)
            first += piece.shape[0]
        sums[...] = jnp.zeros_like(sums)
        square[...] = jnp.zeros_like(square)

    @pl.when(step_id == 1)
    def _():
        own = own_ref[...].astype(f32)
        diff_sum = jnp.zeros((8, c), f32)
        for k in range(near):
            diff_sum = diff_sum + fold_rows(rows[pl.ds(k * block, block), :c] - own)
        own_sum = fold_rows(own) * float(near)
        pivot_ref[...] = project(own_sum, diff_sum) * (1.0 / (near * block))

    def pick(k):
        base = pl.multiple_of(k * block, block)
        at = step_id * near + k
        waiting = []
        for e in range(block + GROUP):
            if e < block:
                waiting.append(table[pl.ds(idx_ref[at, e], 1), :])
            if e >= GROUP:
                rows[pl.ds(base + (e - GROUP), 1), :] = waiting[e - GROUP]

    def work(k, own, carry, between=lambda: None):
        diff_sum, total = carry
        at = pl.ds(pl.multiple_of(k * block, block), block)
        diff = (rows[at, :c] - own).astype(bf16)
        diff_ref[k] = diff
        diff_sum = diff_sum + fold_rows(diff.astype(f32))
        product = dot(diff, w_ref[c:, :])
        between()
        z = product + centre[...]
        z_ref[k] = z
        return diff_sum, total + fold_rows(z * z)

    @pl.when(step_id == 0)
    def _():
        def body(i, _):
            pick(i)
            return 0

        lax.fori_loop(0, near, body, 0)

    def finish(own, carry):
        sums[0] += fold_rows(own) * float(near)
        sums[1] += carry[0]
        square[...] += carry[1]

    def begin():
        centre[...] = dot(own_ref[...], w_ref[:c, :]) - pivot_ref[...]
        zero = (jnp.zeros((8, c), f32), jnp.zeros_like(square[...]))
        return own_ref[...].astype(f32), zero

    @pl.when((step_id > 0) & (step_id < last))
    def _():
        own, zero = begin()

        def body(i, carry):
            for k in range(chunk):
                at = i * chunk + k
                carry = work(at, own_ref[...].astype(f32), carry, functools.partial(pick, at))
            return carry

        finish(own, lax.fori_loop(0, near // chunk, body, zero))

    @pl.when(step_id == last)
    def _():
        own, carry = begin()
        for k in range(near):
            carry = work(k, own, carry)
        finish(own, carry)
        count = float(near * block * (pl.num_programs(0) - 1))
        mean = project(sums[0], sums[1]) / count
        off = mean - pivot_ref[...]
        m2 = jnp.sum(square[...], axis=0, keepdims=True) - count * off * off
        stat_ref[...] = jnp.broadcast_to(jnp.concatenate([mean, m2], axis=0)[None], stat_ref.shape)


def edge_stats(index, pieces, own, weight):
    rows, c = own.shape
    d = weight.shape[1]
    blocks = rows // BLOCK
    near = index.shape[0] // blocks
    total = sum(piece.shape[0] for piece in pieces)
    before = lambda b: jnp.maximum(b - 1, 0)
    whole = lambda x: pl.BlockSpec(x.shape, lambda b: (0,) * len(x.shape))
    stat = jax.ShapeDtypeStruct((lax.axis_size(BOTH), 2, d), f32)
    pivot = jax.ShapeDtypeStruct((1, d), f32)
    return pl.pallas_call(
        functools.partial(edge_kernel, len(pieces)),
        grid=(blocks + 1,),
        out_shape=(
            jax.ShapeDtypeStruct((near, rows, c), bf16),
            jax.ShapeDtypeStruct((near, rows, d), f32),
            stat,
            pivot,
        ),
        in_specs=[smem()]
        + [whole(piece) for piece in pieces]
        + [pl.BlockSpec((BLOCK, c), lambda b: (before(b), 0)), whole(weight)],
        out_specs=(
            pl.BlockSpec((near, BLOCK, c), lambda b: (0, before(b), 0)),
            pl.BlockSpec((near, BLOCK, d), lambda b: (0, before(b), 0)),
            whole(stat),
            whole(pivot),
        ),
        scratch_shapes=[
            pltpu.VMEM((total, LANES), f32),
            pltpu.VMEM((near * BLOCK, LANES), f32),
            pltpu.VMEM((BLOCK, d), f32),
            pltpu.VMEM((2, 8, c), f32),
            pltpu.VMEM((8, d), f32),
        ],
        compiler_params=params(),
        cost_estimate=lasting(22),
        name="edge_stats",
    )(index, *pieces, own, weight)


def moments(stat, edges_each):
    devices = stat.shape[0]
    means = stat[:, 0, :]
    mean = jnp.sum(means, axis=0, keepdims=True) * (1.0 / devices)
    off = means - mean
    m2 = jnp.sum(stat[:, 1, :], axis=0, keepdims=True) + edges_each * jnp.sum(
        off * off, axis=0, keepdims=True
    )
    return mean, lax.rsqrt(m2 * (1.0 / (edges_each * devices)) + EPS)


def pool_kernel(last, edges_each, z_ref, stat_ref, pivot_ref, norm_ref, *refs):
    near, block, d = z_ref.shape
    if last:
        cot_ref, pooled_ref, slope_ref, sums_ref, sums = refs
    else:
        pooled_ref, slope_ref, sum_ref, moment_ref = refs
    mean, inv = moments(stat_ref[...], edges_each)
    half_scale = norm_ref[0:1, :] * inv * 0.5
    half_offset = (pivot_ref[...] - mean) * half_scale + norm_ref[1:2, :] * 0.5
    if last:

        @pl.when(pl.program_id(0) == 0)
        def _():
            sums[...] = jnp.zeros_like(sums)

    for lane in range(0, d, 128):
        lanes = pl.ds(lane, 128)
        scale = jnp.broadcast_to(half_scale[:, lane : lane + 128], (ROWS, 128))
        offset = jnp.broadcast_to(half_offset[:, lane : lane + 128], (ROWS, 128))

        def step(b, carry, lanes=lanes, scale=scale, offset=offset):
            at = pl.ds(pl.multiple_of(b * ROWS, ROWS), ROWS)
            active, bends = [], []
            for k in range(near):
                half = z_ref[k, at, lanes] * scale + offset
                bent = jnp.tanh(half)
                t = 1.0 + bent
                a = half * t
                active.append(a)
                bends.append(t + a * (1.0 - bent))
            top = tree(jnp.maximum, active)
            powers = [jnp.exp2((a - top) * LOG2E) for a in active]
            total = tree(jnp.add, powers)
            pooled = top + jnp.log(total) - math.log(near)
            pooled_ref[at, lanes] = pooled.astype(bf16)
            factor = 0.5 / total
            if last:
                factor = factor * cot_ref[at, lanes].astype(f32)
            halves = [z_ref[k, at, lanes] * scale + offset for k in range(near)]
            slopes = [(powers[k] * factor) * bends[k] for k in range(near)]
            slope_sum = tree(jnp.add, slopes)
            slope_moment = tree(jnp.add, [slopes[k] * halves[k] for k in range(near)])
            for k in range(near):
                slope_ref[k, at, lanes] = slopes[k]
            if not last:
                sum_ref[at, lanes] = slope_sum
                moment_ref[at, lanes] = slope_moment
                return carry
            return (carry[0] + slope_sum, carry[1] + slope_moment)

        zero = jnp.zeros((ROWS, 128), f32)
        carry = lax.fori_loop(0, block // ROWS, step, (zero, zero))
        if last:
            sums[0:1, lanes] += jnp.sum(carry[0], axis=0, keepdims=True)
            sums[1:2, lanes] += jnp.sum(carry[1], axis=0, keepdims=True)
    if last:

        @pl.when(pl.program_id(0) == pl.num_programs(0) - 1)
        def _():
            sums_ref[...] = jnp.broadcast_to(sums[...][None], sums_ref.shape)


def pool(z, stat, pivot, norm, cot=None):
    near, rows, d = z.shape
    whole = lambda x: pl.BlockSpec(x.shape, lambda b: (0,) * len(x.shape))
    by_block = pl.BlockSpec((POOL_BLOCK, d), lambda b: (b, 0))
    by_edge = pl.BlockSpec((near, POOL_BLOCK, d), lambda b: (0, b, 0))
    inputs = [z, stat, pivot, norm]
    in_specs = [by_edge, whole(stat), whole(pivot), whole(norm)]
    row_out = lambda kind: (jax.ShapeDtypeStruct((rows, d), kind), by_block)
    outs = [row_out(bf16), (jax.ShapeDtypeStruct((near, rows, d), f32), by_edge)]
    scratch = []
    if cot is None:
        outs += [row_out(f32), row_out(f32)]
    else:
        inputs.append(cot)
        in_specs.append(by_block)
        sums = jax.ShapeDtypeStruct(stat.shape, f32)
        outs.append((sums, whole(sums)))
        scratch.append(pltpu.VMEM((2, d), f32))
    return pl.pallas_call(
        functools.partial(pool_kernel, cot is not None, float(near * rows)),
        grid=(rows // POOL_BLOCK,),
        out_shape=tuple(o[0] for o in outs),
        in_specs=in_specs,
        out_specs=tuple(o[1] for o in outs),
        scratch_shapes=scratch,
        compiler_params=params(),
        cost_estimate=lasting(12 if cot is None else 20),
        name="pool",
    )(*inputs)


def grads_kernel(
    edges_each,
    inner,
    turn_lines,
    idx_ref,
    slope_ref,
    z_ref,
    back_ref,
    stat_ref,
    pivot_ref,
    norm_ref,
    grads_ref,
    *refs,
):
    near, block, d = slope_ref.shape
    if inner:
        upstream_ref, diff_ref, line_ref, dz_sum_ref, weight_ref, send_ref, dz_ref = refs[: -turn_lines - 3]
    else:
        line_ref, dz_sum_ref, dz_ref, send_ref = refs[: -turn_lines - 3]
    fresh, held, *lines, sem = refs[-turn_lines - 3 :]
    step_id = pl.program_id(0)
    last = pl.num_programs(0) - 1
    total, rows = lines[0].shape[0], dz_sum_ref.shape[0]
    turns = block // POINTS
    share = near * POINTS

    def store(waiting, most):
        while len(waiting) > most:
            line, place, row = waiting.pop(0)
            line[place, :] = row

    def add(turn, edges, waiting):
        for e in edges:
            line = lines[e % turn_lines]
            place = pl.ds(idx_ref[turn, e], 1)
            waiting.append((line, place, line[place, :] + held[pl.ds(e, 1), :]))
            store(waiting, turn_lines - 1)

    @pl.when(step_id == 0)
    def _():
        def clear(i, _):
            at = pl.ds(pl.multiple_of(i * 256, 256), 256)
            for line in lines:
                line[at, :] = jnp.zeros((256, LANES), f32)
            return 0

        lax.fori_loop(0, total // 256, clear, 0)
        fresh[...] = jnp.zeros_like(fresh)
        if inner:
            weight_ref[...] = jnp.zeros_like(weight_ref)

    edges = edges_each * stat_ref.shape[0]
    mean, inv = moments(stat_ref[...], edges_each)
    gain = norm_ref[0:1, :]
    sums = jnp.sum(grads_ref[...], axis=0)
    grad_shift = sums[0:1]
    grad_gain = (2.0 * sums[1:2] - norm_ref[1:2, :] * grad_shift) / gain
    alpha = gain * inv
    rate = alpha * inv * grad_gain * (1.0 / edges)
    constant = alpha * grad_shift * (1.0 / edges) + rate * (pivot_ref[...] - mean)
    wide = [
        [jnp.broadcast_to(x[:, lane : lane + 128], (POINTS, 128)) for x in (alpha, rate, constant)]
        for lane in range(0, d, 128)
    ]

    def turn(t, _):
        at = pl.ds(pl.multiple_of(t * POINTS, POINTS), POINTS)
        before = jnp.maximum(step_id * turns + t - 1, 0)
        held[...] = fresh[...]
        units = [(k, i) for i in range(d // 128) for k in range(near)]
        factors = [w[0] for w in wide]
        if inner:
            factors = [
                f * upstream_ref[at, pl.ds(i * 128, 128)] for i, f in enumerate(factors)
            ]

        def load(unit):
            k, i = unit
            lanes = pl.ds(i * 128, 128)
            return slope_ref[k, at, lanes], z_ref[k, at, lanes]

        loaded = [load(unit) for unit in units[:AHEAD]]
        dzs, waiting = {}, []
        each = share // 2 // len(units)
        for n, (k, i) in enumerate(units):
            add(before, range(n * each, (n + 1) * each), waiting)
            if n + AHEAD < len(units):
                loaded.append(load(units[n + AHEAD]))
            slope, z = loaded[n]
            dzs[k, i] = (factors[i] * slope - wide[i][2] - wide[i][1] * z).astype(bf16)
            dz_ref[k, at, pl.ds(i * 128, 128)] = dzs[k, i]
        whole = [
            jnp.concatenate([dzs[k, i] for k in range(near)], axis=0) for i in range(d // 128)
        ]
        product = dot_t(jnp.concatenate(whole, axis=1), back_ref[...]).astype(bf16)
        add(before, range(share // 2, share), waiting)
        row = pl.multiple_of(step_id * block + t * POINTS, POINTS)
        for i in range(d // 128):
            dz_sum_ref[pl.ds(row, POINTS), pl.ds(i * 128, 128)] = tree(
                jnp.add, [dzs[k, i].astype(f32) for k in range(near)]
            )
        store(waiting, 0)
        fresh[...] = product.astype(f32)
        return 0

    lax.fori_loop(0, turns, turn, 0)
    if inner:
        weight_ref[...] += lax.dot_general(
            diff_ref[...].reshape(near * block, diff_ref.shape[2]),
            dz_ref[...].reshape(near * block, d),
            (((0,), (0,)), ((), ())),
            preferred_element_type=f32,
        )

    @pl.when(step_id == last)
    def _():
        held[...] = fresh[...]
        waiting = []
        add(rows // POINTS - 1, range(share), waiting)
        store(waiting, 0)

        def join(i, _):
            at = pl.ds(pl.multiple_of(i * 256, 256), 256)
            lines[0][at, :] = tree(jnp.add, [line[at, :] for line in lines])
            return 0

        lax.fori_loop(0, total // 256, join, 0)
        copy = pltpu.make_async_copy(lines[0], line_ref, sem)
        copy.start()
        send_ref[...] = lines[0][pl.ds(total // 2, rows), : send_ref.shape[1]].astype(bf16)
        copy.wait()


def edge_grads(turns, slope, z, weight, stat, pivot, norm, grads, total, inner=()):
    near, rows, d = slope.shape
    c = weight.shape[0] // 2
    whole = lambda x: pl.BlockSpec(x.shape, lambda b: (0,) * len(x.shape))
    by_block = lambda width: pl.BlockSpec((BLOCK, width), lambda b: (b, 0))
    by_edge = lambda width: pl.BlockSpec((near, BLOCK, width), lambda b: (0, b, 0))
    turn_lines = min(LINES, LINE_BYTES // (total * LANES * 4))
    back = jnp.pad(weight[c:], ((0, LANES - c), (0, 0)))
    inputs = [turns, slope, z, back, stat, pivot, norm, grads, *inner]
    in_specs = [
        smem(),
        by_edge(d),
        by_edge(d),
        whole(back),
        whole(stat),
        whole(pivot),
        whole(norm),
        whole(grads),
    ]
    if inner:
        in_specs += [by_block(d), by_edge(c)]
    dz = jax.ShapeDtypeStruct((near, rows, d), bf16)
    dz_sum = jax.ShapeDtypeStruct((rows, d), f32)
    send = jax.ShapeDtypeStruct((rows, c), bf16)
    outs = [
        (jax.ShapeDtypeStruct((total, LANES), f32), pl.BlockSpec(memory_space=pl.ANY)),
        (dz_sum, whole(dz_sum)),
    ]
    scratch = [
        pltpu.VMEM((near * POINTS, LANES), f32),
        pltpu.VMEM((near * POINTS, LANES), f32),
        *[pltpu.VMEM((total, LANES), f32)] * turn_lines,
        pltpu.SemaphoreType.DMA,
    ]
    if inner:
        part = jax.ShapeDtypeStruct((c, d), f32)
        outs.append((part, whole(part)))
        scratch.insert(0, pltpu.VMEM((near, BLOCK, d), bf16))
    else:
        outs.append((dz, by_edge(d)))
    outs.append((send, whole(send)))
    return pl.pallas_call(
        functools.partial(grads_kernel, float(near * rows), bool(inner), turn_lines),
        grid=(rows // BLOCK,),
        out_shape=tuple(o[0] for o in outs),
        in_specs=in_specs,
        out_specs=tuple(o[1] for o in outs),
        scratch_shapes=scratch,
        compiler_params=params(),
        cost_estimate=lasting(35),
        name="edge_grads",
    )(*inputs)


def copies(x):
    return jnp.broadcast_to(x[None], (lax.axis_size(BOTH),) + x.shape)


def shared(x):
    devices = lax.axis_size(BOTH)
    return x.reshape(devices, x.shape[0] // devices, x.shape[1])


def exchange(shares):
    return lax.all_to_all(shares, BOTH, split_axis=0, concat_axis=0, tiled=True)


def everyone(x):
    return exchange(copies(x))


def ring_moves(places):
    ring = list(range(0, places, 2)) + list(range(1, places, 2))[::-1]
    onward = [(ring[i], ring[(i + 1) % places]) for i in range(places)]
    return onward, [(b, a) for a, b in onward]


def ring_place(device, places):
    return jnp.where(device % 2 == 0, device // 2, places - 1 - device // 2)


def line_table(values):
    places = lax.axis_size("pts")
    onward, backward = ring_moves(places)
    rows, far = values.shape[0] // 2, places // 2
    behind, ahead = [values], [values]
    for _ in range(far - 1):
        behind.append(lax.ppermute(behind[-1], "pts", onward))
        ahead.append(lax.ppermute(ahead[-1], "pts", backward))
    farthest = [
        lax.ppermute(behind[-1][:rows], "pts", onward),
        lax.ppermute(ahead[-1][rows:], "pts", backward),
    ]
    return behind + farthest + ahead[:0:-1]


def owners_sum(line, send, centre, weights=None):
    places = lax.axis_size("pts")
    onward, backward = ring_moves(places)
    rows, c = centre.shape
    half, far = rows // 2, places // 2

    def slot(j):
        return line[j * rows : (j + 1) * rows, :c]

    forth = lax.ppermute(send[:half], "pts", onward)
    back = lax.ppermute(send[half:], "pts", backward)
    if weights is not None:
        forth, back, weights = lax.optimization_barrier((forth, back, weights))
        shares = exchange(shared(weights))
    forth = jnp.pad(forth.astype(f32), ((0, half), (0, 0)))
    back = jnp.pad(back.astype(f32), ((half, 0), (0, 0)))
    for j in range(1, far):
        forth, back = (forth + slot(far + j)).astype(bf16), (back + slot(far - j)).astype(bf16)
        forth, back = lax.optimization_barrier((forth, back))
        if weights is not None and j == far - 1:
            forth, back, shares = lax.optimization_barrier((forth, back, shares))
            weights = everyone(jnp.sum(shares.astype(f32), axis=0).astype(bf16))
        forth = lax.ppermute(forth, "pts", onward).astype(f32)
        back = lax.ppermute(back, "pts", backward).astype(f32)
    return centre + slot(0) + forth + back, weights


def centre_grad(dz_sum, weight):
    wide = weight.astype(f32)
    c = weight.shape[0] // 2
    return exact(dz_sum, (wide[:c] - wide[c:]).T)


def per_device(
    points,
    lengths,
    neighbours_one,
    neighbours_two,
    weight_one,
    gain_one,
    shift_one,
    weight_two,
    gain_two,
    shift_two,
    cotangent,
):
    line_devices = lax.axis_size("pts")
    row_count = points.shape[0]
    line_length = line_devices * row_count
    table_one = line_table(points)

    norm_one, norm_two = jnp.stack([gain_one, shift_one]), jnp.stack([gain_two, shift_two])

    cloud_ends = jnp.cumsum(lengths)
    cloud_starts = cloud_ends - lengths
    line_first = lax.axis_index("loc") * line_length
    position = (
        line_first + lax.axis_index("pts") * row_count + jnp.arange(row_count, dtype=jnp.int32)
    )
    begins = (position[:, None] >= cloud_starts[None, :]) & (position[:, None] < cloud_ends[None, :])
    begin = jnp.sum(jnp.where(begins, cloud_starts[None, :], 0), axis=1) - line_first
    here = ring_place(lax.axis_index("pts"), line_devices)

    def slot_rows(neighbours):
        within = neighbours.T + begin[None, :]
        slot = (here - ring_place(within // row_count, line_devices)) % line_devices
        return slot * row_count + within % row_count

    def by_blocks(index, points):
        return index.reshape(index.shape[0], -1, points).transpose(1, 0, 2)

    index_one = slot_rows(neighbours_one)
    index_two = slot_rows(neighbours_two)
    order_one = by_blocks(index_one, BLOCK).reshape(-1, BLOCK)
    order_two = by_blocks(index_two, BLOCK).reshape(-1, BLOCK)
    turns_one = by_blocks(index_one, POINTS).reshape(row_count // POINTS, -1)
    turns_two = by_blocks(index_two, POINTS).reshape(row_count // POINTS, -1)

    diff_one, z_one, stat_one, pivot_one = edge_stats(order_one, table_one, points, weight_one)
    stat_one, order_two, turns_one, turns_two = lax.optimization_barrier(
        (exchange(stat_one), order_two, turns_one, turns_two)
    )
    act_one, slope_one, slope_sum, slope_moment = pool(z_one, stat_one, pivot_one, norm_one)
    table_two = line_table(act_one)
    diff_two, z_two, stat_two, pivot_two = edge_stats(order_two, table_two, act_one, weight_two)
    stat_two = exchange(stat_two)
    act_two, slope_two, sums_two = pool(z_two, stat_two, pivot_two, norm_two, cotangent)
    sums_two = exchange(sums_two)
    line_two, dz_sum_two, dz_two, send_two = edge_grads(
        turns_two,
        slope_two,
        z_two,
        weight_two,
        stat_two,
        pivot_two,
        norm_two,
        sums_two,
        line_length,
    )
    grad_first, _ = owners_sum(line_two, send_two, centre_grad(dz_sum_two, weight_two))
    grad_first, dz_two, dz_sum_two = lax.optimization_barrier((grad_first, dz_two, dz_sum_two))
    first_two = exact(act_one.astype(f32).T, dz_sum_two)
    second_two = jnp.einsum("kgc,kgd->cd", diff_two, dz_two, preferred_element_type=f32)
    sums_one = jnp.stack(
        [jnp.sum(grad_first * slope_sum, axis=0), jnp.sum(grad_first * slope_moment, axis=0)]
    )
    sums_one = everyone(sums_one)
    line_one, dz_sum_one, second_one, send_one = edge_grads(
        turns_one,
        slope_one,
        z_one,
        weight_one,
        stat_one,
        pivot_one,
        norm_one,
        sums_one,
        line_length,
        (grad_first, diff_one),
    )
    first_one = exact(points.astype(f32).T, dz_sum_one)
    weights = jnp.concatenate(
        [first_two.reshape(-1, LANES), second_two.reshape(-1, LANES), first_one, second_one], axis=0
    )
    grad_points, weights = owners_sum(
        line_one, send_one, centre_grad(dz_sum_one, weight_one), weights.astype(bf16)
    )
    weights = weights.reshape(-1, LANES).astype(f32)
    grad_weight_two = weights[: -weight_one.shape[0]].reshape(weight_two.shape)
    grad_weight_one = weights[-weight_one.shape[0] :]

    def norm_grads(sums, gain, shift):
        sums = jnp.sum(sums, axis=0)
        return (2.0 * sums[1] - shift * sums[0]) / gain, sums[0]

    grad_gain_one, grad_shift_one = norm_grads(sums_one, gain_one, shift_one)
    grad_gain_two, grad_shift_two = norm_grads(sums_two, gain_two, shift_two)
    return (
        act_one,
        act_two,
        grad_points,
        grad_weight_one,
        grad_gain_one,
        grad_shift_one,
        grad_weight_two,
        grad_gain_two,
        grad_shift_two,
    )


def solution(mesh):
    rows, copied = P(("pts", "loc"), None), P()
    in_specs = (rows, copied, rows, rows) + (copied,) * 6 + (rows,)
    out_specs = (rows, rows, rows) + (copied,) * 6
    return jax.shard_map(
        per_device, mesh=mesh, in_specs=in_specs, out_specs=out_specs, check_vma=False
    )
```

```python
import functools
import math

import jax
import jax.numpy as jnp
from jax import lax
from jax.experimental import pallas as pl
from jax.experimental.pallas import tpu as pltpu
from jax.sharding import PartitionSpec as P

EPS = 1e-05
MIB = 1024 * 1024
BLOCK = 128
POOL_BLOCK = 256
GROUP = 8
LINES = 6
LINE_BYTES = 32 * MIB
POINTS = 32
ROWS = 16
AHEAD = 4
LOG2E = 1.0 / math.log(2.0)
LANES = 128
BOTH = ("pts", "loc")

f32 = jnp.float32
bf16 = jnp.bfloat16


def params():
    return pltpu.CompilerParams(vmem_limit_bytes=52 * MIB)


def lasting(microseconds):
    return pl.CostEstimate(flops=0, transcendentals=0, bytes_accessed=3_000_000 * microseconds)


def smem():
    return pl.BlockSpec(memory_space=pltpu.SMEM)


def fold_rows(x):
    return jnp.sum(x.reshape(x.shape[0] // 8, 8, x.shape[1]), axis=0)


def tree(op, terms):
    while len(terms) > 1:
        pairs = [op(a, b) for a, b in zip(terms[::2], terms[1::2])]
        terms = pairs + terms[len(pairs) * 2 :]
    return terms[0]


def dot(a, b):
    return jnp.dot(a, b, preferred_element_type=f32)


def exact(a, b):
    return jnp.dot(a, b, precision=lax.Precision.HIGHEST, preferred_element_type=f32)


def dot_t(a, b):
    return lax.dot_general(a, b, (((1,), (1,)), ((), ())), preferred_element_type=f32)


def edge_kernel(pieces, *refs):
    table_refs = refs[1 : 1 + pieces]
    idx_ref = refs[0]
    own_ref, w_ref, diff_ref, z_ref, stat_ref, pivot_ref, table, rows, centre, sums, square = refs[
        1 + pieces :
    ]
    near, block, c = diff_ref.shape
    step_id = pl.program_id(0)
    last = pl.num_programs(0) - 1
    chunk = 10

    def project(own_sum, diff_sum):
        weight = w_ref[...].astype(f32)
        both = exact(own_sum, weight[:c]) + exact(diff_sum, weight[c:])
        return jnp.sum(both, axis=0, keepdims=True)

    @pl.when(step_id == 0)
    def _():
        first = 0
        for piece in table_refs:
            for r in range(0, piece.shape[0], 256):
                table[pl.ds(first + r, 256), :c] = piece[pl.ds(r, 256), :].astype(f32)
            first += piece.shape[0]
        sums[...] = jnp.zeros_like(sums)
        square[...] = jnp.zeros_like(square)

    @pl.when(step_id == 1)
    def _():
        own = own_ref[...].astype(f32)
        diff_sum = jnp.zeros((8, c), f32)
        for k in range(near):
            diff_sum = diff_sum + fold_rows(rows[pl.ds(k * block, block), :c] - own)
        own_sum = fold_rows(own) * float(near)
        pivot_ref[...] = project(own_sum, diff_sum) * (1.0 / (near * block))

    def pick(k):
        base = pl.multiple_of(k * block, block)
        at = step_id * near + k
        waiting = []
        for e in range(block + GROUP):
            if e < block:
                waiting.append(table[pl.ds(idx_ref[at, e], 1), :])
            if e >= GROUP:
                rows[pl.ds(base + (e - GROUP), 1), :] = waiting[e - GROUP]

    def work(k, own, carry, between=lambda: None):
        diff_sum, total = carry
        at = pl.ds(pl.multiple_of(k * block, block), block)
        diff = (rows[at, :c] - own).astype(bf16)
        diff_ref[k] = diff
        diff_sum = diff_sum + fold_rows(diff.astype(f32))
        product = dot(diff, w_ref[c:, :])
        between()
        z = product + centre[...]
        z_ref[k] = z
        return diff_sum, total + fold_rows(z * z)

    @pl.when(step_id == 0)
    def _():
        def body(i, _):
            pick(i)
            return 0

        lax.fori_loop(0, near, body, 0)

    def finish(own, carry):
        sums[0] += fold_rows(own) * float(near)
        sums[1] += carry[0]
        square[...] += carry[1]

    def begin():
        centre[...] = dot(own_ref[...], w_ref[:c, :]) - pivot_ref[...]
        zero = (jnp.zeros((8, c), f32), jnp.zeros_like(square[...]))
        return own_ref[...].astype(f32), zero

    @pl.when((step_id > 0) & (step_id < last))
    def _():
        own, zero = begin()

        def body(i, carry):
            for k in range(chunk):
                at = i * chunk + k
                carry = work(at, own_ref[...].astype(f32), carry, functools.partial(pick, at))
            return carry

        finish(own, lax.fori_loop(0, near // chunk, body, zero))

    @pl.when(step_id == last)
    def _():
        own, carry = begin()
        for k in range(near):
            carry = work(k, own, carry)
        finish(own, carry)
        count = float(near * block * (pl.num_programs(0) - 1))
        mean = project(sums[0], sums[1]) / count
        off = mean - pivot_ref[...]
        m2 = jnp.sum(square[...], axis=0, keepdims=True) - count * off * off
        stat_ref[...] = jnp.broadcast_to(jnp.concatenate([mean, m2], axis=0)[None], stat_ref.shape)


def edge_stats(index, pieces, own, weight):
    rows, c = own.shape
    d = weight.shape[1]
    blocks = rows // BLOCK
    near = index.shape[0] // blocks
    total = sum(piece.shape[0] for piece in pieces)
    before = lambda b: jnp.maximum(b - 1, 0)
    whole = lambda x: pl.BlockSpec(x.shape, lambda b: (0,) * len(x.shape))
    stat = jax.ShapeDtypeStruct((lax.axis_size(BOTH), 2, d), f32)
    pivot = jax.ShapeDtypeStruct((1, d), f32)
    return pl.pallas_call(
        functools.partial(edge_kernel, len(pieces)),
        grid=(blocks + 1,),
        out_shape=(
            jax.ShapeDtypeStruct((near, rows, c), bf16),
            jax.ShapeDtypeStruct((near, rows, d), f32),
            stat,
            pivot,
        ),
        in_specs=[smem()]
        + [whole(piece) for piece in pieces]
        + [pl.BlockSpec((BLOCK, c), lambda b: (before(b), 0)), whole(weight)],
        out_specs=(
            pl.BlockSpec((near, BLOCK, c), lambda b: (0, before(b), 0)),
            pl.BlockSpec((near, BLOCK, d), lambda b: (0, before(b), 0)),
            whole(stat),
            whole(pivot),
        ),
        scratch_shapes=[
            pltpu.VMEM((total, LANES), f32),
            pltpu.VMEM((near * BLOCK, LANES), f32),
            pltpu.VMEM((BLOCK, d), f32),
            pltpu.VMEM((2, 8, c), f32),
            pltpu.VMEM((8, d), f32),
        ],
        compiler_params=params(),
        cost_estimate=lasting(22),
        name="edge_stats",
    )(index, *pieces, own, weight)


def moments(stat, edges_each):
    devices = stat.shape[0]
    means = stat[:, 0, :]
    mean = jnp.sum(means, axis=0, keepdims=True) * (1.0 / devices)
    off = means - mean
    m2 = jnp.sum(stat[:, 1, :], axis=0, keepdims=True) + edges_each * jnp.sum(
        off * off, axis=0, keepdims=True
    )
    return mean, lax.rsqrt(m2 * (1.0 / (edges_each * devices)) + EPS)


def pool_kernel(last, edges_each, z_ref, stat_ref, pivot_ref, norm_ref, *refs):
    near, block, d = z_ref.shape
    if last:
        cot_ref, pooled_ref, slope_ref, sums_ref, sums = refs
    else:
        pooled_ref, slope_ref, sum_ref, moment_ref = refs
    mean, inv = moments(stat_ref[...], edges_each)
    half_scale = norm_ref[0:1, :] * inv * 0.5
    half_offset = (pivot_ref[...] - mean) * half_scale + norm_ref[1:2, :] * 0.5
    if last:

        @pl.when(pl.program_id(0) == 0)
        def _():
            sums[...] = jnp.zeros_like(sums)

    for lane in range(0, d, 128):
        lanes = pl.ds(lane, 128)
        scale = jnp.broadcast_to(half_scale[:, lane : lane + 128], (ROWS, 128))
        offset = jnp.broadcast_to(half_offset[:, lane : lane + 128], (ROWS, 128))

        def step(b, carry, lanes=lanes, scale=scale, offset=offset):
            at = pl.ds(pl.multiple_of(b * ROWS, ROWS), ROWS)
            active, bends = [], []
            for k in range(near):
                half = z_ref[k, at, lanes] * scale + offset
                bent = jnp.tanh(half)
                t = 1.0 + bent
                a = half * t
                active.append(a)
                bends.append(t + a * (1.0 - bent))
            top = tree(jnp.maximum, active)
            powers = [jnp.exp2((a - top) * LOG2E) for a in active]
            total = tree(jnp.add, powers)
            pooled = top + jnp.log(total) - math.log(near)
            pooled_ref[at, lanes] = pooled.astype(bf16)
            factor = 0.5 / total
            if last:
                factor = factor * cot_ref[at, lanes].astype(f32)
            halves = [z_ref[k, at, lanes] * scale + offset for k in range(near)]
            slopes = [(powers[k] * factor) * bends[k] for k in range(near)]
            slope_sum = tree(jnp.add, slopes)
            slope_moment = tree(jnp.add, [slopes[k] * halves[k] for k in range(near)])
            for k in range(near):
                slope_ref[k, at, lanes] = slopes[k]
            if not last:
                sum_ref[at, lanes] = slope_sum
                moment_ref[at, lanes] = slope_moment
                return carry
            return (carry[0] + slope_sum, carry[1] + slope_moment)

        zero = jnp.zeros((ROWS, 128), f32)
        carry = lax.fori_loop(0, block // ROWS, step, (zero, zero))
        if last:
            sums[0:1, lanes] += jnp.sum(carry[0], axis=0, keepdims=True)
            sums[1:2, lanes] += jnp.sum(carry[1], axis=0, keepdims=True)
    if last:

        @pl.when(pl.program_id(0) == pl.num_programs(0) - 1)
        def _():
            sums_ref[...] = jnp.broadcast_to(sums[...][None], sums_ref.shape)


def pool(z, stat, pivot, norm, cot=None):
    near, rows, d = z.shape
    whole = lambda x: pl.BlockSpec(x.shape, lambda b: (0,) * len(x.shape))
    by_block = pl.BlockSpec((POOL_BLOCK, d), lambda b: (b, 0))
    by_edge = pl.BlockSpec((near, POOL_BLOCK, d), lambda b: (0, b, 0))
    inputs = [z, stat, pivot, norm]
    in_specs = [by_edge, whole(stat), whole(pivot), whole(norm)]
    row_out = lambda kind: (jax.ShapeDtypeStruct((rows, d), kind), by_block)
    outs = [row_out(bf16), (jax.ShapeDtypeStruct((near, rows, d), f32), by_edge)]
    scratch = []
    if cot is None:
        outs += [row_out(f32), row_out(f32)]
    else:
        inputs.append(cot)
        in_specs.append(by_block)
        sums = jax.ShapeDtypeStruct(stat.shape, f32)
        outs.append((sums, whole(sums)))
        scratch.append(pltpu.VMEM((2, d), f32))
    return pl.pallas_call(
        functools.partial(pool_kernel, cot is not None, float(near * rows)),
        grid=(rows // POOL_BLOCK,),
        out_shape=tuple(o[0] for o in outs),
        in_specs=in_specs,
        out_specs=tuple(o[1] for o in outs),
        scratch_shapes=scratch,
        compiler_params=params(),
        cost_estimate=lasting(12 if cot is None else 20),
        name="pool",
    )(*inputs)


def grads_kernel(
    edges_each,
    inner,
    turn_lines,
    idx_ref,
    slope_ref,
    z_ref,
    back_ref,
    stat_ref,
    pivot_ref,
    norm_ref,
    grads_ref,
    *refs,
):
    near, block, d = slope_ref.shape
    if inner:
        upstream_ref, diff_ref, line_ref, dz_sum_ref, weight_ref, send_ref, dz_ref = refs[: -turn_lines - 3]
    else:
        line_ref, dz_sum_ref, dz_ref, send_ref = refs[: -turn_lines - 3]
    fresh, held, *lines, sem = refs[-turn_lines - 3 :]
    step_id = pl.program_id(0)
    last = pl.num_programs(0) - 1
    total, rows = lines[0].shape[0], dz_sum_ref.shape[0]
    turns = block // POINTS
    share = near * POINTS

    def store(waiting, most):
        while len(waiting) > most:
            line, place, row = waiting.pop(0)
            line[place, :] = row

    def add(turn, edges, waiting):
        for e in edges:
            line = lines[e % turn_lines]
            place = pl.ds(idx_ref[turn, e], 1)
            waiting.append((line, place, line[place, :] + held[pl.ds(e, 1), :]))
            store(waiting, turn_lines - 1)

    @pl.when(step_id == 0)
    def _():
        def clear(i, _):
            at = pl.ds(pl.multiple_of(i * 256, 256), 256)
            for line in lines:
                line[at, :] = jnp.zeros((256, LANES), f32)
            return 0

        lax.fori_loop(0, total // 256, clear, 0)
        fresh[...] = jnp.zeros_like(fresh)
        if inner:
            weight_ref[...] = jnp.zeros_like(weight_ref)

    edges = edges_each * stat_ref.shape[0]
    mean, inv = moments(stat_ref[...], edges_each)
    gain = norm_ref[0:1, :]
    sums = jnp.sum(grads_ref[...], axis=0)
    grad_shift = sums[0:1]
    grad_gain = (2.0 * sums[1:2] - norm_ref[1:2, :] * grad_shift) / gain
    alpha = gain * inv
    rate = alpha * inv * grad_gain * (1.0 / edges)
    constant = alpha * grad_shift * (1.0 / edges) + rate * (pivot_ref[...] - mean)
    wide = [
        [jnp.broadcast_to(x[:, lane : lane + 128], (POINTS, 128)) for x in (alpha, rate, constant)]
        for lane in range(0, d, 128)
    ]

    def turn(t, _):
        at = pl.ds(pl.multiple_of(t * POINTS, POINTS), POINTS)
        before = jnp.maximum(step_id * turns + t - 1, 0)
        held[...] = fresh[...]
        units = [(k, i) for i in range(d // 128) for k in range(near)]
        factors = [w[0] for w in wide]
        if inner:
            factors = [
                f * upstream_ref[at, pl.ds(i * 128, 128)] for i, f in enumerate(factors)
            ]

        def load(unit):
            k, i = unit
            lanes = pl.ds(i * 128, 128)
            return slope_ref[k, at, lanes], z_ref[k, at, lanes]

        loaded = [load(unit) for unit in units[:AHEAD]]
        dzs, waiting = {}, []
        each = share // 2 // len(units)
        for n, (k, i) in enumerate(units):
            add(before, range(n * each, (n + 1) * each), waiting)
            if n + AHEAD < len(units):
                loaded.append(load(units[n + AHEAD]))
            slope, z = loaded[n]
            dzs[k, i] = (factors[i] * slope - wide[i][2] - wide[i][1] * z).astype(bf16)
            dz_ref[k, at, pl.ds(i * 128, 128)] = dzs[k, i]
        whole = [
            jnp.concatenate([dzs[k, i] for k in range(near)], axis=0) for i in range(d // 128)
        ]
        product = dot_t(jnp.concatenate(whole, axis=1), back_ref[...]).astype(bf16)
        add(before, range(share // 2, share), waiting)
        row = pl.multiple_of(step_id * block + t * POINTS, POINTS)
        for i in range(d // 128):
            dz_sum_ref[pl.ds(row, POINTS), pl.ds(i * 128, 128)] = tree(
                jnp.add, [dzs[k, i].astype(f32) for k in range(near)]
            )
        store(waiting, 0)
        fresh[...] = product.astype(f32)
        return 0

    lax.fori_loop(0, turns, turn, 0)
    if inner:
        weight_ref[...] += lax.dot_general(
            diff_ref[...].reshape(near * block, diff_ref.shape[2]),
            dz_ref[...].reshape(near * block, d),
            (((0,), (0,)), ((), ())),
            preferred_element_type=f32,
        )

    @pl.when(step_id == last)
    def _():
        held[...] = fresh[...]
        waiting = []
        add(rows // POINTS - 1, range(share), waiting)
        store(waiting, 0)

        def join(i, _):
            at = pl.ds(pl.multiple_of(i * 256, 256), 256)
            lines[0][at, :] = tree(jnp.add, [line[at, :] for line in lines])
            return 0

        lax.fori_loop(0, total // 256, join, 0)
        copy = pltpu.make_async_copy(lines[0], line_ref, sem)
        copy.start()
        send_ref[...] = lines[0][pl.ds(total // 2, rows), : send_ref.shape[1]].astype(bf16)
        copy.wait()


def edge_grads(turns, slope, z, weight, stat, pivot, norm, grads, total, inner=()):
    near, rows, d = slope.shape
    c = weight.shape[0] // 2
    whole = lambda x: pl.BlockSpec(x.shape, lambda b: (0,) * len(x.shape))
    by_block = lambda width: pl.BlockSpec((BLOCK, width), lambda b: (b, 0))
    by_edge = lambda width: pl.BlockSpec((near, BLOCK, width), lambda b: (0, b, 0))
    turn_lines = min(LINES, LINE_BYTES // (total * LANES * 4))
    back = jnp.pad(weight[c:], ((0, LANES - c), (0, 0)))
    inputs = [turns, slope, z, back, stat, pivot, norm, grads, *inner]
    in_specs = [
        smem(),
        by_edge(d),
        by_edge(d),
        whole(back),
        whole(stat),
        whole(pivot),
        whole(norm),
        whole(grads),
    ]
    if inner:
        in_specs += [by_block(d), by_edge(c)]
    dz = jax.ShapeDtypeStruct((near, rows, d), bf16)
    dz_sum = jax.ShapeDtypeStruct((rows, d), f32)
    send = jax.ShapeDtypeStruct((rows, c), bf16)
    outs = [
        (jax.ShapeDtypeStruct((total, LANES), f32), pl.BlockSpec(memory_space=pl.ANY)),
        (dz_sum, whole(dz_sum)),
    ]
    scratch = [
        pltpu.VMEM((near * POINTS, LANES), f32),
        pltpu.VMEM((near * POINTS, LANES), f32),
        *[pltpu.VMEM((total, LANES), f32)] * turn_lines,
        pltpu.SemaphoreType.DMA,
    ]
    if inner:
        part = jax.ShapeDtypeStruct((c, d), f32)
        outs.append((part, whole(part)))
        scratch.insert(0, pltpu.VMEM((near, BLOCK, d), bf16))
    else:
        outs.append((dz, by_edge(d)))
    outs.append((send, whole(send)))
    return pl.pallas_call(
        functools.partial(grads_kernel, float(near * rows), bool(inner), turn_lines),
        grid=(rows // BLOCK,),
        out_shape=tuple(o[0] for o in outs),
        in_specs=in_specs,
        out_specs=tuple(o[1] for o in outs),
        scratch_shapes=scratch,
        compiler_params=params(),
        cost_estimate=lasting(35),
        name="edge_grads",
    )(*inputs)


def copies(x):
    return jnp.broadcast_to(x[None], (lax.axis_size(BOTH),) + x.shape)


def shared(x):
    devices = lax.axis_size(BOTH)
    return x.reshape(devices, x.shape[0] // devices, x.shape[1])


def exchange(shares):
    return lax.all_to_all(shares, BOTH, split_axis=0, concat_axis=0, tiled=True)


def everyone(x):
    return exchange(copies(x))


def ring_moves(places):
    ring = list(range(0, places, 2)) + list(range(1, places, 2))[::-1]
    onward = [(ring[i], ring[(i + 1) % places]) for i in range(places)]
    return onward, [(b, a) for a, b in onward]


def ring_place(device, places):
    return jnp.where(device % 2 == 0, device // 2, places - 1 - device // 2)


def line_table(values):
    places = lax.axis_size("pts")
    onward, backward = ring_moves(places)
    rows, far = values.shape[0] // 2, places // 2
    behind, ahead = [values], [values]
    for _ in range(far - 1):
        behind.append(lax.ppermute(behind[-1], "pts", onward))
        ahead.append(lax.ppermute(ahead[-1], "pts", backward))
    farthest = [
        lax.ppermute(behind[-1][:rows], "pts", onward),
        lax.ppermute(ahead[-1][rows:], "pts", backward),
    ]
    return behind + farthest + ahead[:0:-1]


def owners_sum(line, send, centre, weights=None):
    places = lax.axis_size("pts")
    onward, backward = ring_moves(places)
    rows, c = centre.shape
    half, far = rows // 2, places // 2

    def slot(j):
        return line[j * rows : (j + 1) * rows, :c]

    forth = lax.ppermute(send[:half], "pts", onward)
    back = lax.ppermute(send[half:], "pts", backward)
    if weights is not None:
        forth, back, weights = lax.optimization_barrier((forth, back, weights))
        shares = exchange(shared(weights))
    forth = jnp.pad(forth.astype(f32), ((0, half), (0, 0)))
    back = jnp.pad(back.astype(f32), ((half, 0), (0, 0)))
    for j in range(1, far):
        forth, back = (forth + slot(far + j)).astype(bf16), (back + slot(far - j)).astype(bf16)
        forth, back = lax.optimization_barrier((forth, back))
        if weights is not None and j == far - 1:
            forth, back, shares = lax.optimization_barrier((forth, back, shares))
            weights = everyone(jnp.sum(shares.astype(f32), axis=0).astype(bf16))
        forth = lax.ppermute(forth, "pts", onward).astype(f32)
        back = lax.ppermute(back, "pts", backward).astype(f32)
    return centre + slot(0) + forth + back, weights


def centre_grad(dz_sum, weight):
    wide = weight.astype(f32)
    c = weight.shape[0] // 2
    return exact(dz_sum, (wide[:c] - wide[c:]).T)


def per_device(
    points,
    lengths,
    neighbours_one,
    neighbours_two,
    weight_one,
    gain_one,
    shift_one,
    weight_two,
    gain_two,
    shift_two,
    cotangent,
):
    line_devices = lax.axis_size("pts")
    row_count = points.shape[0]
    line_length = line_devices * row_count
    table_one = line_table(points)

    norm_one, norm_two = jnp.stack([gain_one, shift_one]), jnp.stack([gain_two, shift_two])

    cloud_ends = jnp.cumsum(lengths)
    cloud_starts = cloud_ends - lengths
    line_first = lax.axis_index("loc") * line_length
    position = (
        line_first + lax.axis_index("pts") * row_count + jnp.arange(row_count, dtype=jnp.int32)
    )
    begins = (position[:, None] >= cloud_starts[None, :]) & (position[:, None] < cloud_ends[None, :])
    begin = jnp.sum(jnp.where(begins, cloud_starts[None, :], 0), axis=1) - line_first
    here = ring_place(lax.axis_index("pts"), line_devices)

    def slot_rows(neighbours):
        within = neighbours.T + begin[None, :]
        slot = (here - ring_place(within // row_count, line_devices)) % line_devices
        return slot * row_count + within % row_count

    def by_blocks(index, points):
        return index.reshape(index.shape[0], -1, points).transpose(1, 0, 2)

    index_one = slot_rows(neighbours_one)
    index_two = slot_rows(neighbours_two)
    order_one = by_blocks(index_one, BLOCK).reshape(-1, BLOCK)
    order_two = by_blocks(index_two, BLOCK).reshape(-1, BLOCK)
    turns_one = by_blocks(index_one, POINTS).reshape(row_count // POINTS, -1)
    turns_two = by_blocks(index_two, POINTS).reshape(row_count // POINTS, -1)

    diff_one, z_one, stat_one, pivot_one = edge_stats(order_one, table_one, points, weight_one)
    stat_one, order_two, turns_one, turns_two = lax.optimization_barrier(
        (exchange(stat_one), order_two, turns_one, turns_two)
    )
    act_one, slope_one, slope_sum, slope_moment = pool(z_one, stat_one, pivot_one, norm_one)
    table_two = line_table(act_one)
    diff_two, z_two, stat_two, pivot_two = edge_stats(order_two, table_two, act_one, weight_two)
    stat_two = exchange(stat_two)
    act_two, slope_two, sums_two = pool(z_two, stat_two, pivot_two, norm_two, cotangent)
    sums_two = exchange(sums_two)
    line_two, dz_sum_two, dz_two, send_two = edge_grads(
        turns_two,
        slope_two,
        z_two,
        weight_two,
        stat_two,
        pivot_two,
        norm_two,
        sums_two,
        line_length,
    )
    grad_first, _ = owners_sum(line_two, send_two, centre_grad(dz_sum_two, weight_two))
    grad_first, dz_two, dz_sum_two = lax.optimization_barrier((grad_first, dz_two, dz_sum_two))
    first_two = exact(act_one.astype(f32).T, dz_sum_two)
    second_two = jnp.einsum("kgc,kgd->cd", diff_two, dz_two, preferred_element_type=f32)
    sums_one = jnp.stack(
        [jnp.sum(grad_first * slope_sum, axis=0), jnp.sum(grad_first * slope_moment, axis=0)]
    )
    sums_one = everyone(sums_one)
    line_one, dz_sum_one, second_one, send_one = edge_grads(
        turns_one,
        slope_one,
        z_one,
        weight_one,
        stat_one,
        pivot_one,
        norm_one,
        sums_one,
        line_length,
        (grad_first, diff_one),
    )
    first_one = exact(points.astype(f32).T, dz_sum_one)
    weights = jnp.concatenate(
        [first_two.reshape(-1, LANES), second_two.reshape(-1, LANES), first_one, second_one], axis=0
    )
    grad_points, weights = owners_sum(
        line_one, send_one, centre_grad(dz_sum_one, weight_one), weights.astype(bf16)
    )
    weights = weights.reshape(-1, LANES).astype(f32)
    grad_weight_two = weights[: -weight_one.shape[0]].reshape(weight_two.shape)
    grad_weight_one = weights[-weight_one.shape[0] :]

    def norm_grads(sums, gain, shift):
        sums = jnp.sum(sums, axis=0)
        return (2.0 * sums[1] - shift * sums[0]) / gain, sums[0]

    grad_gain_one, grad_shift_one = norm_grads(sums_one, gain_one, shift_one)
    grad_gain_two, grad_shift_two = norm_grads(sums_two, gain_two, shift_two)
    return (
        act_one,
        act_two,
        grad_points,
        grad_weight_one,
        grad_gain_one,
        grad_shift_one,
        grad_weight_two,
        grad_gain_two,
        grad_shift_two,
    )


def solution(mesh):
    rows, copied = P(("pts", "loc"), None), P()
    in_specs = (rows, copied, rows, rows) + (copied,) * 6 + (rows,)
    out_specs = (rows, rows, rows) + (copied,) * 6
    return jax.shard_map(
        per_device, mesh=mesh, in_specs=in_specs, out_specs=out_specs, check_vma=False
    )
```

```python
import functools
import math

import jax
import jax.numpy as jnp
from jax import lax
from jax.experimental import pallas as pl
from jax.experimental.pallas import tpu as pltpu
from jax.sharding import PartitionSpec as P

EPS = 1e-05
MIB = 1024 * 1024
BLOCK = 128
POOL_BLOCK = 256
GROUP = 8
LINES = 6
LINE_BYTES = 24 * MIB
POINTS = 32
ROWS = 16
AHEAD = 4
LOG2E = 1.0 / math.log(2.0)
LANES = 128
BOTH = ("pts", "loc")

f32 = jnp.float32
bf16 = jnp.bfloat16


def params():
    return pltpu.CompilerParams(vmem_limit_bytes=52 * MIB)


def lasting(microseconds):
    return pl.CostEstimate(flops=0, transcendentals=0, bytes_accessed=3_000_000 * microseconds)


def smem():
    return pl.BlockSpec(memory_space=pltpu.SMEM)


def fold_rows(x):
    return jnp.sum(x.reshape(x.shape[0] // 8, 8, x.shape[1]), axis=0)


def tree(op, terms):
    while len(terms) > 1:
        pairs = [op(a, b) for a, b in zip(terms[::2], terms[1::2])]
        terms = pairs + terms[len(pairs) * 2 :]
    return terms[0]


def dot(a, b):
    return jnp.dot(a, b, preferred_element_type=f32)


def exact(a, b):
    return jnp.dot(a, b, precision=lax.Precision.HIGHEST, preferred_element_type=f32)


def dot_t(a, b):
    return lax.dot_general(a, b, (((1,), (1,)), ((), ())), preferred_element_type=f32)


def edge_kernel(pieces, *refs):
    table_refs = refs[1 : 1 + pieces]
    idx_ref = refs[0]
    own_ref, w_ref, diff_ref, z_ref, stat_ref, pivot_ref, table, rows, centre, sums, square = refs[
        1 + pieces :
    ]
    near, block, c = diff_ref.shape
    step_id = pl.program_id(0)
    last = pl.num_programs(0) - 1
    chunk = 10

    def project(own_sum, diff_sum):
        weight = w_ref[...].astype(f32)
        both = exact(own_sum, weight[:c]) + exact(diff_sum, weight[c:])
        return jnp.sum(both, axis=0, keepdims=True)

    @pl.when(step_id == 0)
    def _():
        first = 0
        for piece in table_refs:
            for r in range(0, piece.shape[0], 256):
                table[pl.ds(first + r, 256), :c] = piece[pl.ds(r, 256), :].astype(f32)
            first += piece.shape[0]
        sums[...] = jnp.zeros_like(sums)
        square[...] = jnp.zeros_like(square)

    @pl.when(step_id == 1)
    def _():
        own = own_ref[...].astype(f32)
        diff_sum = jnp.zeros((8, c), f32)
        for k in range(near):
            diff_sum = diff_sum + fold_rows(rows[pl.ds(k * block, block), :c] - own)
        own_sum = fold_rows(own) * float(near)
        pivot_ref[...] = project(own_sum, diff_sum) * (1.0 / (near * block))

    def pick(k):
        base = pl.multiple_of(k * block, block)
        at = step_id * near + k
        waiting = []
        for e in range(block + GROUP):
            if e < block:
                waiting.append(table[pl.ds(idx_ref[at, e], 1), :])
            if e >= GROUP:
                rows[pl.ds(base + (e - GROUP), 1), :] = waiting[e - GROUP]

    def work(k, own, carry, between=lambda: None):
        diff_sum, total = carry
        at = pl.ds(pl.multiple_of(k * block, block), block)
        diff = (rows[at, :c] - own).astype(bf16)
        diff_ref[k] = diff
        diff_sum = diff_sum + fold_rows(diff.astype(f32))
        product = dot(diff, w_ref[c:, :])
        between()
        z = product + centre[...]
        z_ref[k] = z
        return diff_sum, total + fold_rows(z * z)

    @pl.when(step_id == 0)
    def _():
        def body(i, _):
            pick(i)
            return 0

        lax.fori_loop(0, near, body, 0)

    def finish(own, carry):
        sums[0] += fold_rows(own) * float(near)
        sums[1] += carry[0]
        square[...] += carry[1]

    def begin():
        centre[...] = dot(own_ref[...], w_ref[:c, :]) - pivot_ref[...]
        zero = (jnp.zeros((8, c), f32), jnp.zeros_like(square[...]))
        return own_ref[...].astype(f32), zero

    @pl.when((step_id > 0) & (step_id < last))
    def _():
        own, zero = begin()

        def body(i, carry):
            for k in range(chunk):
                at = i * chunk + k
                carry = work(at, own_ref[...].astype(f32), carry, functools.partial(pick, at))
            return carry

        finish(own, lax.fori_loop(0, near // chunk, body, zero))

    @pl.when(step_id == last)
    def _():
        own, carry = begin()
        for k in range(near):
            carry = work(k, own, carry)
        finish(own, carry)
        count = float(near * block * (pl.num_programs(0) - 1))
        mean = project(sums[0], sums[1]) / count
        off = mean - pivot_ref[...]
        m2 = jnp.sum(square[...], axis=0, keepdims=True) - count * off * off
        stat_ref[...] = jnp.broadcast_to(jnp.concatenate([mean, m2], axis=0)[None], stat_ref.shape)


def edge_stats(index, pieces, own, weight):
    rows, c = own.shape
    d = weight.shape[1]
    blocks = rows // BLOCK
    near = index.shape[0] // blocks
    total = sum(piece.shape[0] for piece in pieces)
    before = lambda b: jnp.maximum(b - 1, 0)
    whole = lambda x: pl.BlockSpec(x.shape, lambda b: (0,) * len(x.shape))
    stat = jax.ShapeDtypeStruct((lax.axis_size(BOTH), 2, d), f32)
    pivot = jax.ShapeDtypeStruct((1, d), f32)
    return pl.pallas_call(
        functools.partial(edge_kernel, len(pieces)),
        grid=(blocks + 1,),
        out_shape=(
            jax.ShapeDtypeStruct((near, rows, c), bf16),
            jax.ShapeDtypeStruct((near, rows, d), f32),
            stat,
            pivot,
        ),
        in_specs=[smem()]
        + [whole(piece) for piece in pieces]
        + [pl.BlockSpec((BLOCK, c), lambda b: (before(b), 0)), whole(weight)],
        out_specs=(
            pl.BlockSpec((near, BLOCK, c), lambda b: (0, before(b), 0)),
            pl.BlockSpec((near, BLOCK, d), lambda b: (0, before(b), 0)),
            whole(stat),
            whole(pivot),
        ),
        scratch_shapes=[
            pltpu.VMEM((total, LANES), f32),
            pltpu.VMEM((near * BLOCK, LANES), f32),
            pltpu.VMEM((BLOCK, d), f32),
            pltpu.VMEM((2, 8, c), f32),
            pltpu.VMEM((8, d), f32),
        ],
        compiler_params=params(),
        cost_estimate=lasting(22),
        name="edge_stats",
    )(index, *pieces, own, weight)


def moments(stat, edges_each):
    devices = stat.shape[0]
    means = stat[:, 0, :]
    mean = jnp.sum(means, axis=0, keepdims=True) * (1.0 / devices)
    off = means - mean
    m2 = jnp.sum(stat[:, 1, :], axis=0, keepdims=True) + edges_each * jnp.sum(
        off * off, axis=0, keepdims=True
    )
    return mean, lax.rsqrt(m2 * (1.0 / (edges_each * devices)) + EPS)


def pool_kernel(last, edges_each, z_ref, stat_ref, pivot_ref, norm_ref, *refs):
    near, block, d = z_ref.shape
    if last:
        cot_ref, pooled_ref, slope_ref, sums_ref, sums = refs
    else:
        pooled_ref, slope_ref, sum_ref, moment_ref = refs
    mean, inv = moments(stat_ref[...], edges_each)
    half_scale = norm_ref[0:1, :] * inv * 0.5
    half_offset = (pivot_ref[...] - mean) * half_scale + norm_ref[1:2, :] * 0.5
    if last:

        @pl.when(pl.program_id(0) == 0)
        def _():
            sums[...] = jnp.zeros_like(sums)

    for lane in range(0, d, 128):
        lanes = pl.ds(lane, 128)
        scale = jnp.broadcast_to(half_scale[:, lane : lane + 128], (ROWS, 128))
        offset = jnp.broadcast_to(half_offset[:, lane : lane + 128], (ROWS, 128))

        def step(b, carry, lanes=lanes, scale=scale, offset=offset):
            at = pl.ds(pl.multiple_of(b * ROWS, ROWS), ROWS)
            active, bends = [], []
            for k in range(near):
                half = z_ref[k, at, lanes] * scale + offset
                bent = jnp.tanh(half)
                t = 1.0 + bent
                a = half * t
                active.append(a)
                bends.append(t + a * (1.0 - bent))
            top = tree(jnp.maximum, active)
            powers = [jnp.exp2((a - top) * LOG2E) for a in active]
            total = tree(jnp.add, powers)
            pooled = top + jnp.log(total) - math.log(near)
            pooled_ref[at, lanes] = pooled.astype(bf16)
            factor = 0.5 / total
            if last:
                factor = factor * cot_ref[at, lanes].astype(f32)
            halves = [z_ref[k, at, lanes] * scale + offset for k in range(near)]
            slopes = [(powers[k] * factor) * bends[k] for k in range(near)]
            slope_sum = tree(jnp.add, slopes)
            slope_moment = tree(jnp.add, [slopes[k] * halves[k] for k in range(near)])
            for k in range(near):
                slope_ref[k, at, lanes] = slopes[k]
            if not last:
                sum_ref[at, lanes] = slope_sum
                moment_ref[at, lanes] = slope_moment
                return carry
            return (carry[0] + slope_sum, carry[1] + slope_moment)

        zero = jnp.zeros((ROWS, 128), f32)
        carry = lax.fori_loop(0, block // ROWS, step, (zero, zero))
        if last:
            sums[0:1, lanes] += jnp.sum(carry[0], axis=0, keepdims=True)
            sums[1:2, lanes] += jnp.sum(carry[1], axis=0, keepdims=True)
    if last:

        @pl.when(pl.program_id(0) == pl.num_programs(0) - 1)
        def _():
            sums_ref[...] = jnp.broadcast_to(sums[...][None], sums_ref.shape)


def pool(z, stat, pivot, norm, cot=None):
    near, rows, d = z.shape
    whole = lambda x: pl.BlockSpec(x.shape, lambda b: (0,) * len(x.shape))
    by_block = pl.BlockSpec((POOL_BLOCK, d), lambda b: (b, 0))
    by_edge = pl.BlockSpec((near, POOL_BLOCK, d), lambda b: (0, b, 0))
    inputs = [z, stat, pivot, norm]
    in_specs = [by_edge, whole(stat), whole(pivot), whole(norm)]
    row_out = lambda kind: (jax.ShapeDtypeStruct((rows, d), kind), by_block)
    outs = [row_out(bf16), (jax.ShapeDtypeStruct((near, rows, d), f32), by_edge)]
    scratch = []
    if cot is None:
        outs += [row_out(f32), row_out(f32)]
    else:
        inputs.append(cot)
        in_specs.append(by_block)
        sums = jax.ShapeDtypeStruct(stat.shape, f32)
        outs.append((sums, whole(sums)))
        scratch.append(pltpu.VMEM((2, d), f32))
    return pl.pallas_call(
        functools.partial(pool_kernel, cot is not None, float(near * rows)),
        grid=(rows // POOL_BLOCK,),
        out_shape=tuple(o[0] for o in outs),
        in_specs=in_specs,
        out_specs=tuple(o[1] for o in outs),
        scratch_shapes=scratch,
        compiler_params=params(),
        cost_estimate=lasting(12 if cot is None else 20),
        name="pool",
    )(*inputs)


def grads_kernel(
    edges_each,
    inner,
    turn_lines,
    idx_ref,
    slope_ref,
    z_ref,
    back_ref,
    stat_ref,
    pivot_ref,
    norm_ref,
    grads_ref,
    *refs,
):
    near, block, d = slope_ref.shape
    if inner:
        upstream_ref, diff_ref, line_ref, dz_sum_ref, weight_ref, send_ref = refs[: -turn_lines - 2]
    else:
        line_ref, dz_sum_ref, dz_ref, send_ref = refs[: -turn_lines - 2]
    fresh, held, *lines = refs[-turn_lines - 2 :]
    step_id = pl.program_id(0)
    last = pl.num_programs(0) - 1
    total, rows = lines[0].shape[0], dz_sum_ref.shape[0]
    turns = block // POINTS
    share = near * POINTS

    def store(waiting, most):
        while len(waiting) > most:
            line, place, row = waiting.pop(0)
            line[place, :] = row

    def add(turn, edges, waiting):
        for e in edges:
            line = lines[e % turn_lines]
            place = pl.ds(idx_ref[turn, e], 1)
            waiting.append((line, place, line[place, :] + held[pl.ds(e, 1), :]))
            store(waiting, turn_lines - 1)

    @pl.when(step_id == 0)
    def _():
        def clear(i, _):
            at = pl.ds(pl.multiple_of(i * 256, 256), 256)
            for line in lines:
                line[at, :] = jnp.zeros((256, LANES), f32)
            return 0

        lax.fori_loop(0, total // 256, clear, 0)
        fresh[...] = jnp.zeros_like(fresh)
        if inner:
            weight_ref[...] = jnp.zeros_like(weight_ref)

    edges = edges_each * stat_ref.shape[0]
    mean, inv = moments(stat_ref[...], edges_each)
    gain = norm_ref[0:1, :]
    sums = jnp.sum(grads_ref[...], axis=0)
    grad_shift = sums[0:1]
    grad_gain = (2.0 * sums[1:2] - norm_ref[1:2, :] * grad_shift) / gain
    alpha = gain * inv
    rate = alpha * inv * grad_gain * (1.0 / edges)
    constant = alpha * grad_shift * (1.0 / edges) + rate * (pivot_ref[...] - mean)
    wide = [
        [jnp.broadcast_to(x[:, lane : lane + 128], (POINTS, 128)) for x in (alpha, rate, constant)]
        for lane in range(0, d, 128)
    ]

    def turn(t, _):
        at = pl.ds(pl.multiple_of(t * POINTS, POINTS), POINTS)
        before = jnp.maximum(step_id * turns + t - 1, 0)
        held[...] = fresh[...]
        units = [(k, i) for i in range(d // 128) for k in range(near)]
        factors = [w[0] for w in wide]
        if inner:
            factors = [
                f * upstream_ref[at, pl.ds(i * 128, 128)] for i, f in enumerate(factors)
            ]

        def load(unit):
            k, i = unit
            lanes = pl.ds(i * 128, 128)
            return slope_ref[k, at, lanes], z_ref[k, at, lanes]

        loaded = [load(unit) for unit in units[:AHEAD]]
        dzs, waiting = {}, []
        each = share // 2 // len(units)
        for n, (k, i) in enumerate(units):
            add(before, range(n * each, (n + 1) * each), waiting)
            if n + AHEAD < len(units):
                loaded.append(load(units[n + AHEAD]))
            slope, z = loaded[n]
            dzs[k, i] = (factors[i] * slope - wide[i][2] - wide[i][1] * z).astype(bf16)
            if not inner:
                dz_ref[k, at, pl.ds(i * 128, 128)] = dzs[k, i]
        whole = [
            jnp.concatenate([dzs[k, i] for k in range(near)], axis=0) for i in range(d // 128)
        ]
        flat = jnp.concatenate(whole, axis=1)
        product = dot_t(flat, back_ref[...]).astype(bf16)
        if inner:
            weight_ref[...] += lax.dot_general(
                diff_ref[:, at, :].reshape(share, diff_ref.shape[2]),
                flat,
                (((0,), (0,)), ((), ())),
                preferred_element_type=f32,
            )
        add(before, range(share // 2, share), waiting)
        row = pl.multiple_of(step_id * block + t * POINTS, POINTS)
        for i in range(d // 128):
            dz_sum_ref[pl.ds(row, POINTS), pl.ds(i * 128, 128)] = tree(
                jnp.add, [dzs[k, i].astype(f32) for k in range(near)]
            )
        store(waiting, 0)
        fresh[...] = product.astype(f32)
        return 0

    lax.fori_loop(0, turns, turn, 0)
    @pl.when(step_id == last)
    def _():
        held[...] = fresh[...]
        waiting = []
        add(rows // POINTS - 1, range(share), waiting)
        store(waiting, 0)

        def join(i, _):
            at = pl.ds(pl.multiple_of(i * 256, 256), 256)
            joined = tree(jnp.add, [line[at, :] for line in lines])
            line_ref[at, :] = joined[:, : line_ref.shape[1]].astype(bf16)
            return 0

        lax.fori_loop(0, total // 256, join, 0)
        send_ref[...] = line_ref[pl.ds(total // 2, rows), :]


def edge_grads(turns, slope, z, weight, stat, pivot, norm, grads, total, inner=()):
    near, rows, d = slope.shape
    c = weight.shape[0] // 2
    whole = lambda x: pl.BlockSpec(x.shape, lambda b: (0,) * len(x.shape))
    by_block = lambda width: pl.BlockSpec((BLOCK, width), lambda b: (b, 0))
    by_edge = lambda width: pl.BlockSpec((near, BLOCK, width), lambda b: (0, b, 0))
    turn_lines = min(LINES, LINE_BYTES // (total * LANES * 4))
    back = jnp.pad(weight[c:], ((0, LANES - c), (0, 0)))
    inputs = [turns, slope, z, back, stat, pivot, norm, grads, *inner]
    in_specs = [
        smem(),
        by_edge(d),
        by_edge(d),
        whole(back),
        whole(stat),
        whole(pivot),
        whole(norm),
        whole(grads),
    ]
    if inner:
        in_specs += [by_block(d), by_edge(c)]
    dz = jax.ShapeDtypeStruct((near, rows, d), bf16)
    dz_sum = jax.ShapeDtypeStruct((rows, d), f32)
    line = jax.ShapeDtypeStruct((total, c), bf16)
    send = jax.ShapeDtypeStruct((rows, c), bf16)
    outs = [
        (line, whole(line)),
        (dz_sum, whole(dz_sum)),
    ]
    scratch = [
        pltpu.VMEM((near * POINTS, LANES), f32),
        pltpu.VMEM((near * POINTS, LANES), f32),
        *[pltpu.VMEM((total, LANES), f32)] * turn_lines,
    ]
    if inner:
        part = jax.ShapeDtypeStruct((c, d), f32)
        outs.append((part, whole(part)))
    else:
        outs.append((dz, by_edge(d)))
    outs.append((send, whole(send)))
    return pl.pallas_call(
        functools.partial(grads_kernel, float(near * rows), bool(inner), turn_lines),
        grid=(rows // BLOCK,),
        out_shape=tuple(o[0] for o in outs),
        in_specs=in_specs,
        out_specs=tuple(o[1] for o in outs),
        scratch_shapes=scratch,
        compiler_params=params(),
        cost_estimate=lasting(35),
        name="edge_grads",
    )(*inputs)


def copies(x):
    return jnp.broadcast_to(x[None], (lax.axis_size(BOTH),) + x.shape)


def shared(x):
    devices = lax.axis_size(BOTH)
    return x.reshape(devices, x.shape[0] // devices, x.shape[1])


def exchange(shares):
    return lax.all_to_all(shares, BOTH, split_axis=0, concat_axis=0, tiled=True)


def everyone(x):
    return exchange(copies(x))


def ring_moves(places):
    ring = list(range(0, places, 2)) + list(range(1, places, 2))[::-1]
    onward = [(ring[i], ring[(i + 1) % places]) for i in range(places)]
    return onward, [(b, a) for a, b in onward]


def ring_place(device, places):
    return jnp.where(device % 2 == 0, device // 2, places - 1 - device // 2)


def line_table(values):
    places = lax.axis_size("pts")
    onward, backward = ring_moves(places)
    rows, far = values.shape[0] // 2, places // 2
    behind, ahead = [values], [values]
    for _ in range(far - 1):
        behind.append(lax.ppermute(behind[-1], "pts", onward))
        ahead.append(lax.ppermute(ahead[-1], "pts", backward))
    farthest = [
        lax.ppermute(behind[-1][:rows], "pts", onward),
        lax.ppermute(ahead[-1][rows:], "pts", backward),
    ]
    return behind + farthest + ahead[:0:-1]


def owners_sum(line, send, centre, weights=None):
    places = lax.axis_size("pts")
    onward, backward = ring_moves(places)
    rows = centre.shape[0]
    half, far = rows // 2, places // 2

    def slot(j):
        return line[j * rows : (j + 1) * rows].astype(f32)

    forth = lax.ppermute(send[:half], "pts", onward)
    back = lax.ppermute(send[half:], "pts", backward)
    forth, back, centre = lax.optimization_barrier((forth, back, centre))
    if weights is not None:
        forth, back, weights = lax.optimization_barrier((forth, back, weights))
        shares = exchange(shared(weights))
    forth = jnp.pad(forth.astype(f32), ((0, half), (0, 0)))
    back = jnp.pad(back.astype(f32), ((half, 0), (0, 0)))
    for j in range(1, far):
        forth, back = (forth + slot(far + j)).astype(bf16), (back + slot(far - j)).astype(bf16)
        forth, back = lax.optimization_barrier((forth, back))
        if weights is not None and j == far - 1:
            forth, back, shares = lax.optimization_barrier((forth, back, shares))
            weights = everyone(jnp.sum(shares.astype(f32), axis=0).astype(bf16))
        forth = lax.ppermute(forth, "pts", onward).astype(f32)
        back = lax.ppermute(back, "pts", backward).astype(f32)
    return centre + slot(0) + forth + back, weights


def centre_grad(dz_sum, weight):
    wide = weight.astype(f32)
    c = weight.shape[0] // 2
    return exact(dz_sum, (wide[:c] - wide[c:]).T)


def per_device(
    points,
    lengths,
    neighbours_one,
    neighbours_two,
    weight_one,
    gain_one,
    shift_one,
    weight_two,
    gain_two,
    shift_two,
    cotangent,
):
    line_devices = lax.axis_size("pts")
    row_count = points.shape[0]
    line_length = line_devices * row_count
    table_one = line_table(points)

    norm_one, norm_two = jnp.stack([gain_one, shift_one]), jnp.stack([gain_two, shift_two])

    cloud_ends = jnp.cumsum(lengths)
    cloud_starts = cloud_ends - lengths
    line_first = lax.axis_index("loc") * line_length
    position = (
        line_first + lax.axis_index("pts") * row_count + jnp.arange(row_count, dtype=jnp.int32)
    )
    begins = (position[:, None] >= cloud_starts[None, :]) & (position[:, None] < cloud_ends[None, :])
    begin = jnp.sum(jnp.where(begins, cloud_starts[None, :], 0), axis=1) - line_first
    here = ring_place(lax.axis_index("pts"), line_devices)

    def slot_rows(neighbours):
        within = neighbours.T + begin[None, :]
        slot = (here - ring_place(within // row_count, line_devices)) % line_devices
        return slot * row_count + within % row_count

    def by_blocks(index, points):
        return index.reshape(index.shape[0], -1, points).transpose(1, 0, 2)

    index_one = slot_rows(neighbours_one)
    index_two = slot_rows(neighbours_two)
    order_one = by_blocks(index_one, BLOCK).reshape(-1, BLOCK)
    order_two = by_blocks(index_two, BLOCK).reshape(-1, BLOCK)
    turns_one = by_blocks(index_one, POINTS).reshape(row_count // POINTS, -1)
    turns_two = by_blocks(index_two, POINTS).reshape(row_count // POINTS, -1)

    diff_one, z_one, stat_one, pivot_one = edge_stats(order_one, table_one, points, weight_one)
    stat_one, order_two, turns_one, turns_two = lax.optimization_barrier(
        (exchange(stat_one), order_two, turns_one, turns_two)
    )
    act_one, slope_one, slope_sum, slope_moment = pool(z_one, stat_one, pivot_one, norm_one)
    table_two = line_table(act_one)
    diff_two, z_two, stat_two, pivot_two = edge_stats(order_two, table_two, act_one, weight_two)
    stat_two = exchange(stat_two)
    act_two, slope_two, sums_two = pool(z_two, stat_two, pivot_two, norm_two, cotangent)
    sums_two = exchange(sums_two)
    line_two, dz_sum_two, dz_two, send_two = edge_grads(
        turns_two,
        slope_two,
        z_two,
        weight_two,
        stat_two,
        pivot_two,
        norm_two,
        sums_two,
        line_length,
    )
    grad_first, _ = owners_sum(line_two, send_two, centre_grad(dz_sum_two, weight_two))
    grad_first, dz_two, dz_sum_two = lax.optimization_barrier((grad_first, dz_two, dz_sum_two))
    first_two = exact(act_one.astype(f32).T, dz_sum_two)
    second_two = jnp.einsum("kgc,kgd->cd", diff_two, dz_two, preferred_element_type=f32)
    sums_one = jnp.stack(
        [jnp.sum(grad_first * slope_sum, axis=0), jnp.sum(grad_first * slope_moment, axis=0)]
    )
    sums_one = everyone(sums_one)
    line_one, dz_sum_one, second_one, send_one = edge_grads(
        turns_one,
        slope_one,
        z_one,
        weight_one,
        stat_one,
        pivot_one,
        norm_one,
        sums_one,
        line_length,
        (grad_first, diff_one),
    )
    first_one = exact(points.astype(f32).T, dz_sum_one)
    weights = jnp.concatenate(
        [first_two.reshape(-1, LANES), second_two.reshape(-1, LANES), first_one, second_one], axis=0
    )
    grad_points, weights = owners_sum(
        line_one, send_one, centre_grad(dz_sum_one, weight_one), weights.astype(bf16)
    )
    weights = weights.reshape(-1, LANES).astype(f32)
    grad_weight_two = weights[: -weight_one.shape[0]].reshape(weight_two.shape)
    grad_weight_one = weights[-weight_one.shape[0] :]

    def norm_grads(sums, gain, shift):
        sums = jnp.sum(sums, axis=0)
        return (2.0 * sums[1] - shift * sums[0]) / gain, sums[0]

    grad_gain_one, grad_shift_one = norm_grads(sums_one, gain_one, shift_one)
    grad_gain_two, grad_shift_two = norm_grads(sums_two, gain_two, shift_two)
    return (
        act_one,
        act_two,
        grad_points,
        grad_weight_one,
        grad_gain_one,
        grad_shift_one,
        grad_weight_two,
        grad_gain_two,
        grad_shift_two,
    )


def solution(mesh):
    rows, copied = P(("pts", "loc"), None), P()
    in_specs = (rows, copied, rows, rows) + (copied,) * 6 + (rows,)
    out_specs = (rows, rows, rows) + (copied,) * 6
    return jax.shard_map(
        per_device, mesh=mesh, in_specs=in_specs, out_specs=out_specs, check_vma=False
    )
```

```python
import functools
import math

import jax
import jax.numpy as jnp
from jax import lax
from jax.experimental import pallas as pl
from jax.experimental.pallas import tpu as pltpu
from jax.sharding import PartitionSpec as P

EPS = 1e-05
MIB = 1024 * 1024
BLOCK = 128
POOL_BLOCK = 256
GROUP = 8
LINES = 6
LINE_BYTES = 24 * MIB
TURN = 8192
ROWS = 16
AHEAD = 4
LOG2E = 1.0 / math.log(2.0)
LANES = 128
BOTH = ("pts", "loc")

f32 = jnp.float32
bf16 = jnp.bfloat16


def params():
    return pltpu.CompilerParams(vmem_limit_bytes=52 * MIB)


def lasting(microseconds):
    return pl.CostEstimate(flops=0, transcendentals=0, bytes_accessed=3_000_000 * microseconds)


def smem():
    return pl.BlockSpec(memory_space=pltpu.SMEM)


def fold_rows(x):
    return jnp.sum(x.reshape(x.shape[0] // 8, 8, x.shape[1]), axis=0)


def tree(op, terms):
    while len(terms) > 1:
        pairs = [op(a, b) for a, b in zip(terms[::2], terms[1::2])]
        terms = pairs + terms[len(pairs) * 2 :]
    return terms[0]


def dot(a, b):
    return jnp.dot(a, b, preferred_element_type=f32)


def exact(a, b):
    return jnp.dot(a, b, precision=lax.Precision.HIGHEST, preferred_element_type=f32)


def dot_t(a, b):
    return lax.dot_general(a, b, (((1,), (1,)), ((), ())), preferred_element_type=f32)


def edge_kernel(pieces, *refs):
    table_refs = refs[1 : 1 + pieces]
    idx_ref = refs[0]
    own_ref, w_ref, diff_ref, z_ref, stat_ref, pivot_ref, table, rows, centre, sums, square = refs[
        1 + pieces :
    ]
    near, block, c = diff_ref.shape
    step_id = pl.program_id(0)
    last = pl.num_programs(0) - 1
    chunk = 10

    def project(own_sum, diff_sum):
        weight = w_ref[...].astype(f32)
        both = exact(own_sum, weight[:c]) + exact(diff_sum, weight[c:])
        return jnp.sum(both, axis=0, keepdims=True)

    @pl.when(step_id == 0)
    def _():
        first = 0
        for piece in table_refs:
            for r in range(0, piece.shape[0], 256):
                table[pl.ds(first + r, 256), :c] = piece[pl.ds(r, 256), :].astype(f32)
            first += piece.shape[0]
        sums[...] = jnp.zeros_like(sums)
        square[...] = jnp.zeros_like(square)

    @pl.when(step_id == 1)
    def _():
        own = own_ref[...].astype(f32)
        diff_sum = jnp.zeros((8, c), f32)
        for k in range(near):
            diff_sum = diff_sum + fold_rows(rows[pl.ds(k * block, block), :c] - own)
        own_sum = fold_rows(own) * float(near)
        pivot_ref[...] = project(own_sum, diff_sum) * (1.0 / (near * block))

    def pick(k):
        base = pl.multiple_of(k * block, block)
        at = step_id * near + k
        waiting = []
        for e in range(block + GROUP):
            if e < block:
                waiting.append(table[pl.ds(idx_ref[at, e], 1), :])
            if e >= GROUP:
                rows[pl.ds(base + (e - GROUP), 1), :] = waiting[e - GROUP]

    def work(k, own, carry, between=lambda: None):
        diff_sum, total = carry
        at = pl.ds(pl.multiple_of(k * block, block), block)
        diff = (rows[at, :c] - own).astype(bf16)
        diff_ref[k] = diff
        diff_sum = diff_sum + fold_rows(diff.astype(f32))
        product = dot(diff, w_ref[c:, :])
        between()
        z = product + centre[...]
        z_ref[k] = z
        return diff_sum, total + fold_rows(z * z)

    @pl.when(step_id == 0)
    def _():
        def body(i, _):
            pick(i)
            return 0

        lax.fori_loop(0, near, body, 0)

    def finish(own, carry):
        sums[0] += fold_rows(own) * float(near)
        sums[1] += carry[0]
        square[...] += carry[1]

    def begin():
        centre[...] = dot(own_ref[...], w_ref[:c, :]) - pivot_ref[...]
        zero = (jnp.zeros((8, c), f32), jnp.zeros_like(square[...]))
        return own_ref[...].astype(f32), zero

    @pl.when((step_id > 0) & (step_id < last))
    def _():
        own, zero = begin()

        def body(i, carry):
            for k in range(chunk):
                at = i * chunk + k
                carry = work(at, own_ref[...].astype(f32), carry, functools.partial(pick, at))
            return carry

        finish(own, lax.fori_loop(0, near // chunk, body, zero))

    @pl.when(step_id == last)
    def _():
        own, carry = begin()
        for k in range(near):
            carry = work(k, own, carry)
        finish(own, carry)
        count = float(near * block * (pl.num_programs(0) - 1))
        mean = project(sums[0], sums[1]) / count
        off = mean - pivot_ref[...]
        m2 = jnp.sum(square[...], axis=0, keepdims=True) - count * off * off
        stat_ref[...] = jnp.broadcast_to(jnp.concatenate([mean, m2], axis=0)[None], stat_ref.shape)


def edge_stats(index, pieces, own, weight):
    rows, c = own.shape
    d = weight.shape[1]
    blocks = rows // BLOCK
    near = index.shape[0] // blocks
    total = sum(piece.shape[0] for piece in pieces)
    before = lambda b: jnp.maximum(b - 1, 0)
    whole = lambda x: pl.BlockSpec(x.shape, lambda b: (0,) * len(x.shape))
    stat = jax.ShapeDtypeStruct((lax.axis_size(BOTH), 2, d), f32)
    pivot = jax.ShapeDtypeStruct((1, d), f32)
    return pl.pallas_call(
        functools.partial(edge_kernel, len(pieces)),
        grid=(blocks + 1,),
        out_shape=(
            jax.ShapeDtypeStruct((near, rows, c), bf16),
            jax.ShapeDtypeStruct((near, rows, d), f32),
            stat,
            pivot,
        ),
        in_specs=[smem()]
        + [whole(piece) for piece in pieces]
        + [pl.BlockSpec((BLOCK, c), lambda b: (before(b), 0)), whole(weight)],
        out_specs=(
            pl.BlockSpec((near, BLOCK, c), lambda b: (0, before(b), 0)),
            pl.BlockSpec((near, BLOCK, d), lambda b: (0, before(b), 0)),
            whole(stat),
            whole(pivot),
        ),
        scratch_shapes=[
            pltpu.VMEM((total, LANES), f32),
            pltpu.VMEM((near * BLOCK, LANES), f32),
            pltpu.VMEM((BLOCK, d), f32),
            pltpu.VMEM((2, 8, c), f32),
            pltpu.VMEM((8, d), f32),
        ],
        compiler_params=params(),
        cost_estimate=lasting(22),
        name="edge_stats",
    )(index, *pieces, own, weight)


def moments(stat, edges_each):
    devices = stat.shape[0]
    means = stat[:, 0, :]
    mean = jnp.sum(means, axis=0, keepdims=True) * (1.0 / devices)
    off = means - mean
    m2 = jnp.sum(stat[:, 1, :], axis=0, keepdims=True) + edges_each * jnp.sum(
        off * off, axis=0, keepdims=True
    )
    return mean, lax.rsqrt(m2 * (1.0 / (edges_each * devices)) + EPS)


def pool_kernel(last, edges_each, z_ref, stat_ref, pivot_ref, norm_ref, *refs):
    near, block, d = z_ref.shape
    if last:
        cot_ref, pooled_ref, slope_ref, sums_ref, sums = refs
    else:
        pooled_ref, slope_ref, sum_ref, moment_ref = refs
    mean, inv = moments(stat_ref[...], edges_each)
    half_scale = norm_ref[0:1, :] * inv * 0.5
    half_offset = (pivot_ref[...] - mean) * half_scale + norm_ref[1:2, :] * 0.5
    if last:

        @pl.when(pl.program_id(0) == 0)
        def _():
            sums[...] = jnp.zeros_like(sums)

    for lane in range(0, d, 128):
        lanes = pl.ds(lane, 128)
        scale = jnp.broadcast_to(half_scale[:, lane : lane + 128], (ROWS, 128))
        offset = jnp.broadcast_to(half_offset[:, lane : lane + 128], (ROWS, 128))

        def step(b, carry, lanes=lanes, scale=scale, offset=offset):
            at = pl.ds(pl.multiple_of(b * ROWS, ROWS), ROWS)
            active, bends = [], []
            for k in range(near):
                half = z_ref[k, at, lanes] * scale + offset
                bent = jnp.tanh(half)
                t = 1.0 + bent
                a = half * t
                active.append(a)
                bends.append(t + a * (1.0 - bent))
            top = tree(jnp.maximum, active)
            powers = [jnp.exp2((a - top) * LOG2E) for a in active]
            total = tree(jnp.add, powers)
            pooled = top + jnp.log(total) - math.log(near)
            pooled_ref[at, lanes] = pooled.astype(bf16)
            factor = 0.5 / total
            if last:
                factor = factor * cot_ref[at, lanes].astype(f32)
            halves = [z_ref[k, at, lanes] * scale + offset for k in range(near)]
            slopes = [(powers[k] * factor) * bends[k] for k in range(near)]
            slope_sum = tree(jnp.add, slopes)
            slope_moment = tree(jnp.add, [slopes[k] * halves[k] for k in range(near)])
            for k in range(near):
                slope_ref[k, at, lanes] = slopes[k]
            if not last:
                sum_ref[at, lanes] = slope_sum
                moment_ref[at, lanes] = slope_moment
                return carry
            return (carry[0] + slope_sum, carry[1] + slope_moment)

        zero = jnp.zeros((ROWS, 128), f32)
        carry = lax.fori_loop(0, block // ROWS, step, (zero, zero))
        if last:
            sums[0:1, lanes] += jnp.sum(carry[0], axis=0, keepdims=True)
            sums[1:2, lanes] += jnp.sum(carry[1], axis=0, keepdims=True)
    if last:

        @pl.when(pl.program_id(0) == pl.num_programs(0) - 1)
        def _():
            sums_ref[...] = jnp.broadcast_to(sums[...][None], sums_ref.shape)


def pool(z, stat, pivot, norm, cot=None):
    near, rows, d = z.shape
    whole = lambda x: pl.BlockSpec(x.shape, lambda b: (0,) * len(x.shape))
    by_block = pl.BlockSpec((POOL_BLOCK, d), lambda b: (b, 0))
    by_edge = pl.BlockSpec((near, POOL_BLOCK, d), lambda b: (0, b, 0))
    inputs = [z, stat, pivot, norm]
    in_specs = [by_edge, whole(stat), whole(pivot), whole(norm)]
    row_out = lambda kind: (jax.ShapeDtypeStruct((rows, d), kind), by_block)
    outs = [row_out(bf16), (jax.ShapeDtypeStruct((near, rows, d), f32), by_edge)]
    scratch = []
    if cot is None:
        outs += [row_out(f32), row_out(f32)]
    else:
        inputs.append(cot)
        in_specs.append(by_block)
        sums = jax.ShapeDtypeStruct(stat.shape, f32)
        outs.append((sums, whole(sums)))
        scratch.append(pltpu.VMEM((2, d), f32))
    return pl.pallas_call(
        functools.partial(pool_kernel, cot is not None, float(near * rows)),
        grid=(rows // POOL_BLOCK,),
        out_shape=tuple(o[0] for o in outs),
        in_specs=in_specs,
        out_specs=tuple(o[1] for o in outs),
        scratch_shapes=scratch,
        compiler_params=params(),
        cost_estimate=lasting(12 if cot is None else 20),
        name="pool",
    )(*inputs)


def grads_kernel(
    edges_each,
    inner,
    turn_lines,
    idx_ref,
    slope_ref,
    z_ref,
    back_ref,
    stat_ref,
    pivot_ref,
    norm_ref,
    grads_ref,
    *refs,
):
    near, block, d = slope_ref.shape
    if inner:
        upstream_ref, diff_ref, line_ref, dz_sum_ref, weight_ref, send_ref = refs[: -turn_lines - 2]
    else:
        line_ref, dz_sum_ref, dz_ref, send_ref = refs[: -turn_lines - 2]
    fresh, held, *lines = refs[-turn_lines - 2 :]
    step_id = pl.program_id(0)
    last = pl.num_programs(0) - 1
    total, rows = lines[0].shape[0], dz_sum_ref.shape[0]
    points = TURN // d
    turns = block // points
    share = near * points

    def store(waiting, most):
        while len(waiting) > most:
            line, place, row = waiting.pop(0)
            line[place, :] = row

    def add(turn, edges, waiting):
        for e in edges:
            line = lines[e % turn_lines]
            place = pl.ds(idx_ref[turn, e], 1)
            waiting.append((line, place, line[place, :] + held[pl.ds(e, 1), :]))
            store(waiting, turn_lines - 1)

    @pl.when(step_id == 0)
    def _():
        def clear(i, _):
            at = pl.ds(pl.multiple_of(i * 256, 256), 256)
            for line in lines:
                line[at, :] = jnp.zeros((256, LANES), f32)
            return 0

        lax.fori_loop(0, total // 256, clear, 0)
        fresh[...] = jnp.zeros_like(fresh)
        if inner:
            weight_ref[...] = jnp.zeros_like(weight_ref)

    edges = edges_each * stat_ref.shape[0]
    mean, inv = moments(stat_ref[...], edges_each)
    gain = norm_ref[0:1, :]
    sums = jnp.sum(grads_ref[...], axis=0)
    grad_shift = sums[0:1]
    grad_gain = (2.0 * sums[1:2] - norm_ref[1:2, :] * grad_shift) / gain
    alpha = gain * inv
    rate = alpha * inv * grad_gain * (1.0 / edges)
    constant = alpha * grad_shift * (1.0 / edges) + rate * (pivot_ref[...] - mean)
    wide = [
        [jnp.broadcast_to(x[:, lane : lane + 128], (points, 128)) for x in (alpha, rate, constant)]
        for lane in range(0, d, 128)
    ]

    def turn(t, _):
        at = pl.ds(pl.multiple_of(t * points, points), points)
        before = jnp.maximum(step_id * turns + t - 1, 0)
        held[...] = fresh[...]
        units = [(k, i) for i in range(d // 128) for k in range(near)]
        factors = [w[0] for w in wide]
        if inner:
            factors = [
                f * upstream_ref[at, pl.ds(i * 128, 128)] for i, f in enumerate(factors)
            ]

        def load(unit):
            k, i = unit
            lanes = pl.ds(i * 128, 128)
            return slope_ref[k, at, lanes], z_ref[k, at, lanes]

        loaded = [load(unit) for unit in units[:AHEAD]]
        dzs, waiting = {}, []
        each = share // 2 // len(units)
        for n, (k, i) in enumerate(units):
            add(before, range(n * each, (n + 1) * each), waiting)
            if n + AHEAD < len(units):
                loaded.append(load(units[n + AHEAD]))
            slope, z = loaded[n]
            dzs[k, i] = (factors[i] * slope - wide[i][2] - wide[i][1] * z).astype(bf16)
            if not inner:
                dz_ref[k, at, pl.ds(i * 128, 128)] = dzs[k, i]
        whole = [
            jnp.concatenate([dzs[k, i] for k in range(near)], axis=0) for i in range(d // 128)
        ]
        flat = jnp.concatenate(whole, axis=1)
        product = dot_t(flat, back_ref[...]).astype(bf16)
        if inner:
            weight_ref[...] += lax.dot_general(
                diff_ref[:, at, :].reshape(share, diff_ref.shape[2]),
                flat,
                (((0,), (0,)), ((), ())),
                preferred_element_type=f32,
            )
        add(before, range(share // 2, share), waiting)
        row = pl.multiple_of(step_id * block + t * points, points)
        for i in range(d // 128):
            dz_sum_ref[pl.ds(row, points), pl.ds(i * 128, 128)] = tree(
                jnp.add, [dzs[k, i].astype(f32) for k in range(near)]
            )
        store(waiting, 0)
        fresh[...] = product.astype(f32)
        return 0

    lax.fori_loop(0, turns, turn, 0)
    @pl.when(step_id == last)
    def _():
        held[...] = fresh[...]
        waiting = []
        add(rows // points - 1, range(share), waiting)
        store(waiting, 0)

        def join(i, _):
            at = pl.ds(pl.multiple_of(i * 256, 256), 256)
            joined = tree(jnp.add, [line[at, :] for line in lines])
            line_ref[at, :] = joined[:, : line_ref.shape[1]].astype(bf16)
            return 0

        lax.fori_loop(0, total // 256, join, 0)
        send_ref[...] = line_ref[pl.ds(total // 2, rows), :]


def edge_grads(turns, slope, z, weight, stat, pivot, norm, grads, total, inner=()):
    near, rows, d = slope.shape
    c = weight.shape[0] // 2
    whole = lambda x: pl.BlockSpec(x.shape, lambda b: (0,) * len(x.shape))
    by_block = lambda width: pl.BlockSpec((BLOCK, width), lambda b: (b, 0))
    by_edge = lambda width: pl.BlockSpec((near, BLOCK, width), lambda b: (0, b, 0))
    turn_lines = min(LINES, LINE_BYTES // (total * LANES * 4))
    back = jnp.pad(weight[c:], ((0, LANES - c), (0, 0)))
    inputs = [turns, slope, z, back, stat, pivot, norm, grads, *inner]
    in_specs = [
        smem(),
        by_edge(d),
        by_edge(d),
        whole(back),
        whole(stat),
        whole(pivot),
        whole(norm),
        whole(grads),
    ]
    if inner:
        in_specs += [by_block(d), by_edge(c)]
    dz = jax.ShapeDtypeStruct((near, rows, d), bf16)
    dz_sum = jax.ShapeDtypeStruct((rows, d), f32)
    line = jax.ShapeDtypeStruct((total, c), bf16)
    send = jax.ShapeDtypeStruct((rows, c), bf16)
    outs = [
        (line, whole(line)),
        (dz_sum, whole(dz_sum)),
    ]
    scratch = [
        pltpu.VMEM((near * (TURN // d), LANES), f32),
        pltpu.VMEM((near * (TURN // d), LANES), f32),
        *[pltpu.VMEM((total, LANES), f32)] * turn_lines,
    ]
    if inner:
        part = jax.ShapeDtypeStruct((c, d), f32)
        outs.append((part, whole(part)))
    else:
        outs.append((dz, by_edge(d)))
    outs.append((send, whole(send)))
    return pl.pallas_call(
        functools.partial(grads_kernel, float(near * rows), bool(inner), turn_lines),
        grid=(rows // BLOCK,),
        out_shape=tuple(o[0] for o in outs),
        in_specs=in_specs,
        out_specs=tuple(o[1] for o in outs),
        scratch_shapes=scratch,
        compiler_params=params(),
        cost_estimate=lasting(35),
        name="edge_grads",
    )(*inputs)


def copies(x):
    return jnp.broadcast_to(x[None], (lax.axis_size(BOTH),) + x.shape)


def shared(x):
    devices = lax.axis_size(BOTH)
    return x.reshape(devices, x.shape[0] // devices, x.shape[1])


def exchange(shares):
    return lax.all_to_all(shares, BOTH, split_axis=0, concat_axis=0, tiled=True)


def everyone(x):
    return exchange(copies(x))


def ring_moves(places):
    ring = list(range(0, places, 2)) + list(range(1, places, 2))[::-1]
    onward = [(ring[i], ring[(i + 1) % places]) for i in range(places)]
    return onward, [(b, a) for a, b in onward]


def ring_place(device, places):
    return jnp.where(device % 2 == 0, device // 2, places - 1 - device // 2)


def line_table(values):
    places = lax.axis_size("pts")
    onward, backward = ring_moves(places)
    rows, far = values.shape[0] // 2, places // 2
    behind, ahead = [values], [values]
    for _ in range(far - 1):
        behind.append(lax.ppermute(behind[-1], "pts", onward))
        ahead.append(lax.ppermute(ahead[-1], "pts", backward))
    farthest = [
        lax.ppermute(behind[-1][:rows], "pts", onward),
        lax.ppermute(ahead[-1][rows:], "pts", backward),
    ]
    return behind + farthest + ahead[:0:-1]


def owners_sum(line, send, centre, weights=None):
    places = lax.axis_size("pts")
    onward, backward = ring_moves(places)
    rows = centre.shape[0]
    half, far = rows // 2, places // 2

    def slot(j):
        return line[j * rows : (j + 1) * rows].astype(f32)

    forth = lax.ppermute(send[:half], "pts", onward)
    back = lax.ppermute(send[half:], "pts", backward)
    forth, back, centre = lax.optimization_barrier((forth, back, centre))
    if weights is not None:
        shares = exchange(shared(weights))
    forth = jnp.pad(forth.astype(f32), ((0, half), (0, 0)))
    back = jnp.pad(back.astype(f32), ((half, 0), (0, 0)))
    for j in range(1, far):
        forth, back = (forth + slot(far + j)).astype(bf16), (back + slot(far - j)).astype(bf16)
        forth, back = lax.optimization_barrier((forth, back))
        if weights is not None and j == far - 2:
            forth, back, shares = lax.optimization_barrier((forth, back, shares))
            weights = everyone(jnp.sum(shares.astype(f32), axis=0).astype(bf16))
        forth = lax.ppermute(forth, "pts", onward).astype(f32)
        back = lax.ppermute(back, "pts", backward).astype(f32)
    return centre + slot(0) + forth + back, weights


def centre_grad(dz_sum, weight):
    wide = weight.astype(f32)
    c = weight.shape[0] // 2
    return exact(dz_sum, (wide[:c] - wide[c:]).T)


def per_device(
    points,
    lengths,
    neighbours_one,
    neighbours_two,
    weight_one,
    gain_one,
    shift_one,
    weight_two,
    gain_two,
    shift_two,
    cotangent,
):
    line_devices = lax.axis_size("pts")
    row_count = points.shape[0]
    line_length = line_devices * row_count
    table_one = line_table(points)

    norm_one, norm_two = jnp.stack([gain_one, shift_one]), jnp.stack([gain_two, shift_two])

    cloud_ends = jnp.cumsum(lengths)
    cloud_starts = cloud_ends - lengths
    line_first = lax.axis_index("loc") * line_length
    position = (
        line_first + lax.axis_index("pts") * row_count + jnp.arange(row_count, dtype=jnp.int32)
    )
    begins = (position[:, None] >= cloud_starts[None, :]) & (position[:, None] < cloud_ends[None, :])
    begin = jnp.sum(jnp.where(begins, cloud_starts[None, :], 0), axis=1) - line_first
    here = ring_place(lax.axis_index("pts"), line_devices)

    def slot_rows(neighbours):
        within = neighbours.T + begin[None, :]
        slot = (here - ring_place(within // row_count, line_devices)) % line_devices
        return slot * row_count + within % row_count

    def by_blocks(index, points):
        return index.reshape(index.shape[0], -1, points).transpose(1, 0, 2)

    index_one = slot_rows(neighbours_one)
    index_two = slot_rows(neighbours_two)
    order_one = by_blocks(index_one, BLOCK).reshape(-1, BLOCK)
    order_two = by_blocks(index_two, BLOCK).reshape(-1, BLOCK)
    near = neighbours_one.shape[1]
    points_one, points_two = TURN // gain_one.shape[0], TURN // gain_two.shape[0]
    turns_one = by_blocks(index_one, points_one).reshape(-1, near * points_one)
    turns_two = by_blocks(index_two, points_two).reshape(-1, near * points_two)

    diff_one, z_one, stat_one, pivot_one = edge_stats(order_one, table_one, points, weight_one)
    stat_one, order_two, turns_one, turns_two = lax.optimization_barrier(
        (exchange(stat_one), order_two, turns_one, turns_two)
    )
    act_one, slope_one, slope_sum, slope_moment = pool(z_one, stat_one, pivot_one, norm_one)
    table_two = line_table(act_one)
    diff_two, z_two, stat_two, pivot_two = edge_stats(order_two, table_two, act_one, weight_two)
    stat_two = exchange(stat_two)
    act_two, slope_two, sums_two = pool(z_two, stat_two, pivot_two, norm_two, cotangent)
    sums_two = exchange(sums_two)
    line_two, dz_sum_two, dz_two, send_two = edge_grads(
        turns_two,
        slope_two,
        z_two,
        weight_two,
        stat_two,
        pivot_two,
        norm_two,
        sums_two,
        line_length,
    )
    grad_first, _ = owners_sum(line_two, send_two, centre_grad(dz_sum_two, weight_two))
    grad_first, dz_two, dz_sum_two = lax.optimization_barrier((grad_first, dz_two, dz_sum_two))
    first_two = exact(act_one.astype(f32).T, dz_sum_two)
    second_two = jnp.einsum("kgc,kgd->cd", diff_two, dz_two, preferred_element_type=f32)
    sums_one = jnp.stack(
        [jnp.sum(grad_first * slope_sum, axis=0), jnp.sum(grad_first * slope_moment, axis=0)]
    )
    sums_one = everyone(sums_one)
    line_one, dz_sum_one, second_one, send_one = edge_grads(
        turns_one,
        slope_one,
        z_one,
        weight_one,
        stat_one,
        pivot_one,
        norm_one,
        sums_one,
        line_length,
        (grad_first, diff_one),
    )
    first_one = exact(points.astype(f32).T, dz_sum_one)
    weights = jnp.concatenate(
        [first_two.reshape(-1, LANES), second_two.reshape(-1, LANES), first_one, second_one], axis=0
    )
    grad_points, weights = owners_sum(
        line_one, send_one, centre_grad(dz_sum_one, weight_one), weights.astype(bf16)
    )
    weights = weights.reshape(-1, LANES).astype(f32)
    grad_weight_two = weights[: -weight_one.shape[0]].reshape(weight_two.shape)
    grad_weight_one = weights[-weight_one.shape[0] :]

    def norm_grads(sums, gain, shift):
        sums = jnp.sum(sums, axis=0)
        return (2.0 * sums[1] - shift * sums[0]) / gain, sums[0]

    grad_gain_one, grad_shift_one = norm_grads(sums_one, gain_one, shift_one)
    grad_gain_two, grad_shift_two = norm_grads(sums_two, gain_two, shift_two)
    return (
        act_one,
        act_two,
        grad_points,
        grad_weight_one,
        grad_gain_one,
        grad_shift_one,
        grad_weight_two,
        grad_gain_two,
        grad_shift_two,
    )


def solution(mesh):
    rows, copied = P(("pts", "loc"), None), P()
    in_specs = (rows, copied, rows, rows) + (copied,) * 6 + (rows,)
    out_specs = (rows, rows, rows) + (copied,) * 6
    return jax.shard_map(
        per_device, mesh=mesh, in_specs=in_specs, out_specs=out_specs, check_vma=False
    )
```

```python
import functools
import math

import jax
import jax.numpy as jnp
from jax import lax
from jax.experimental import pallas as pl
from jax.experimental.pallas import tpu as pltpu
from jax.sharding import PartitionSpec as P

EPS = 1e-05
MIB = 1024 * 1024
BLOCK = 128
POOL_BLOCK = 256
GROUP = 8
LINES = 6
LINE_BYTES = 24 * MIB
POINTS = 64
ROWS = 16
AHEAD = 4
LOG2E = 1.0 / math.log(2.0)
LANES = 128
BOTH = ("pts", "loc")

f32 = jnp.float32
bf16 = jnp.bfloat16


def params():
    return pltpu.CompilerParams(vmem_limit_bytes=52 * MIB)


def lasting(microseconds):
    return pl.CostEstimate(flops=0, transcendentals=0, bytes_accessed=3_000_000 * microseconds)


def smem():
    return pl.BlockSpec(memory_space=pltpu.SMEM)


def fold_rows(x):
    return jnp.sum(x.reshape(x.shape[0] // 8, 8, x.shape[1]), axis=0)


def tree(op, terms):
    while len(terms) > 1:
        pairs = [op(a, b) for a, b in zip(terms[::2], terms[1::2])]
        terms = pairs + terms[len(pairs) * 2 :]
    return terms[0]


def dot(a, b):
    return jnp.dot(a, b, preferred_element_type=f32)


def exact(a, b):
    return jnp.dot(a, b, precision=lax.Precision.HIGHEST, preferred_element_type=f32)


def dot_t(a, b):
    return lax.dot_general(a, b, (((1,), (1,)), ((), ())), preferred_element_type=f32)


def edge_kernel(pieces, *refs):
    table_refs = refs[1 : 1 + pieces]
    idx_ref = refs[0]
    own_ref, w_ref, diff_ref, z_ref, stat_ref, pivot_ref, table, rows, centre, sums, square = refs[
        1 + pieces :
    ]
    near, block, c = diff_ref.shape
    step_id = pl.program_id(0)
    last = pl.num_programs(0) - 1
    chunk = near

    def project(own_sum, diff_sum):
        weight = w_ref[...].astype(f32)
        both = exact(own_sum, weight[:c]) + exact(diff_sum, weight[c:])
        return jnp.sum(both, axis=0, keepdims=True)

    @pl.when(step_id == 0)
    def _():
        first = 0
        for piece in table_refs:
            for r in range(0, piece.shape[0], 256):
                table[pl.ds(first + r, 256), :c] = piece[pl.ds(r, 256), :].astype(f32)
            first += piece.shape[0]
        sums[...] = jnp.zeros_like(sums)
        square[...] = jnp.zeros_like(square)

    @pl.when(step_id == 1)
    def _():
        own = own_ref[...].astype(f32)
        diff_sum = jnp.zeros((8, c), f32)
        for k in range(near):
            diff_sum = diff_sum + fold_rows(rows[pl.ds(k * block, block), :c] - own)
        own_sum = fold_rows(own) * float(near)
        pivot_ref[...] = project(own_sum, diff_sum) * (1.0 / (near * block))

    def pick(k):
        base = pl.multiple_of(k * block, block)
        at = step_id * near + k
        waiting = []
        for e in range(block + GROUP):
            if e < block:
                waiting.append(table[pl.ds(idx_ref[at, e], 1), :])
            if e >= GROUP:
                rows[pl.ds(base + (e - GROUP), 1), :] = waiting[e - GROUP]

    def work(k, own, carry, between=lambda: None):
        diff_sum, total = carry
        at = pl.ds(pl.multiple_of(k * block, block), block)
        diff = (rows[at, :c] - own).astype(bf16)
        diff_ref[k] = diff
        diff_sum = diff_sum + fold_rows(diff.astype(f32))
        product = dot(diff, w_ref[c:, :])
        between()
        z = product + centre[...]
        z_ref[k] = z
        return diff_sum, total + fold_rows(z * z)

    @pl.when(step_id == 0)
    def _():
        def body(i, _):
            pick(i)
            return 0

        lax.fori_loop(0, near, body, 0)

    def finish(own, carry):
        sums[0] += fold_rows(own) * float(near)
        sums[1] += carry[0]
        square[...] += carry[1]

    def begin():
        centre[...] = dot(own_ref[...], w_ref[:c, :]) - pivot_ref[...]
        zero = (jnp.zeros((8, c), f32), jnp.zeros_like(square[...]))
        return own_ref[...].astype(f32), zero

    @pl.when((step_id > 0) & (step_id < last))
    def _():
        own, zero = begin()

        def body(i, carry):
            for k in range(chunk):
                at = i * chunk + k
                carry = work(at, own_ref[...].astype(f32), carry, functools.partial(pick, at))
            return carry

        finish(own, lax.fori_loop(0, near // chunk, body, zero))

    @pl.when(step_id == last)
    def _():
        own, carry = begin()
        for k in range(near):
            carry = work(k, own, carry)
        finish(own, carry)
        count = float(near * block * (pl.num_programs(0) - 1))
        mean = project(sums[0], sums[1]) / count
        off = mean - pivot_ref[...]
        m2 = jnp.sum(square[...], axis=0, keepdims=True) - count * off * off
        stat_ref[...] = jnp.broadcast_to(jnp.concatenate([mean, m2], axis=0)[None], stat_ref.shape)


def edge_stats(index, pieces, own, weight):
    rows, c = own.shape
    d = weight.shape[1]
    blocks = rows // BLOCK
    near = index.shape[0] // blocks
    total = sum(piece.shape[0] for piece in pieces)
    before = lambda b: jnp.maximum(b - 1, 0)
    whole = lambda x: pl.BlockSpec(x.shape, lambda b: (0,) * len(x.shape))
    stat = jax.ShapeDtypeStruct((lax.axis_size(BOTH), 2, d), f32)
    pivot = jax.ShapeDtypeStruct((1, d), f32)
    return pl.pallas_call(
        functools.partial(edge_kernel, len(pieces)),
        grid=(blocks + 1,),
        out_shape=(
            jax.ShapeDtypeStruct((near, rows, c), bf16),
            jax.ShapeDtypeStruct((near, rows, d), f32),
            stat,
            pivot,
        ),
        in_specs=[smem()]
        + [whole(piece) for piece in pieces]
        + [pl.BlockSpec((BLOCK, c), lambda b: (before(b), 0)), whole(weight)],
        out_specs=(
            pl.BlockSpec((near, BLOCK, c), lambda b: (0, before(b), 0)),
            pl.BlockSpec((near, BLOCK, d), lambda b: (0, before(b), 0)),
            whole(stat),
            whole(pivot),
        ),
        scratch_shapes=[
            pltpu.VMEM((total, LANES), f32),
            pltpu.VMEM((near * BLOCK, LANES), f32),
            pltpu.VMEM((BLOCK, d), f32),
            pltpu.VMEM((2, 8, c), f32),
            pltpu.VMEM((8, d), f32),
        ],
        compiler_params=params(),
        cost_estimate=lasting(22),
        name="edge_stats",
    )(index, *pieces, own, weight)


def moments(stat, edges_each):
    devices = stat.shape[0]
    means = stat[:, 0, :]
    mean = jnp.sum(means, axis=0, keepdims=True) * (1.0 / devices)
    off = means - mean
    m2 = jnp.sum(stat[:, 1, :], axis=0, keepdims=True) + edges_each * jnp.sum(
        off * off, axis=0, keepdims=True
    )
    return mean, lax.rsqrt(m2 * (1.0 / (edges_each * devices)) + EPS)


def pool_kernel(last, edges_each, z_ref, stat_ref, pivot_ref, norm_ref, *refs):
    near, block, d = z_ref.shape
    if last:
        cot_ref, pooled_ref, slope_ref, sums_ref, sums = refs
    else:
        pooled_ref, slope_ref, sum_ref, moment_ref = refs
    mean, inv = moments(stat_ref[...], edges_each)
    half_scale = norm_ref[0:1, :] * inv * 0.5
    half_offset = (pivot_ref[...] - mean) * half_scale + norm_ref[1:2, :] * 0.5
    if last:

        @pl.when(pl.program_id(0) == 0)
        def _():
            sums[...] = jnp.zeros_like(sums)

    for lane in range(0, d, 128):
        lanes = pl.ds(lane, 128)
        scale = jnp.broadcast_to(half_scale[:, lane : lane + 128], (ROWS, 128))
        offset = jnp.broadcast_to(half_offset[:, lane : lane + 128], (ROWS, 128))

        def step(b, carry, lanes=lanes, scale=scale, offset=offset):
            at = pl.ds(pl.multiple_of(b * ROWS, ROWS), ROWS)
            active, bends = [], []
            for k in range(near):
                half = z_ref[k, at, lanes] * scale + offset
                bent = jnp.tanh(half)
                t = 1.0 + bent
                a = half * t
                active.append(a)
                bends.append(t + a * (1.0 - bent))
            top = tree(jnp.maximum, active)
            powers = [jnp.exp2((a - top) * LOG2E) for a in active]
            total = tree(jnp.add, powers)
            pooled = top + jnp.log(total) - math.log(near)
            pooled_ref[at, lanes] = pooled.astype(bf16)
            factor = 0.5 / total
            if last:
                factor = factor * cot_ref[at, lanes].astype(f32)
            halves = [z_ref[k, at, lanes] * scale + offset for k in range(near)]
            slopes = [(powers[k] * factor) * bends[k] for k in range(near)]
            slope_sum = tree(jnp.add, slopes)
            slope_moment = tree(jnp.add, [slopes[k] * halves[k] for k in range(near)])
            for k in range(near):
                slope_ref[k, at, lanes] = slopes[k]
            if not last:
                sum_ref[at, lanes] = slope_sum
                moment_ref[at, lanes] = slope_moment
                return carry
            return (carry[0] + slope_sum, carry[1] + slope_moment)

        zero = jnp.zeros((ROWS, 128), f32)
        carry = lax.fori_loop(0, block // ROWS, step, (zero, zero))
        if last:
            sums[0:1, lanes] += jnp.sum(carry[0], axis=0, keepdims=True)
            sums[1:2, lanes] += jnp.sum(carry[1], axis=0, keepdims=True)
    if last:

        @pl.when(pl.program_id(0) == pl.num_programs(0) - 1)
        def _():
            sums_ref[...] = jnp.broadcast_to(sums[...][None], sums_ref.shape)


def pool(z, stat, pivot, norm, cot=None):
    near, rows, d = z.shape
    whole = lambda x: pl.BlockSpec(x.shape, lambda b: (0,) * len(x.shape))
    by_block = pl.BlockSpec((POOL_BLOCK, d), lambda b: (b, 0))
    by_edge = pl.BlockSpec((near, POOL_BLOCK, d), lambda b: (0, b, 0))
    inputs = [z, stat, pivot, norm]
    in_specs = [by_edge, whole(stat), whole(pivot), whole(norm)]
    row_out = lambda kind: (jax.ShapeDtypeStruct((rows, d), kind), by_block)
    outs = [row_out(bf16), (jax.ShapeDtypeStruct((near, rows, d), f32), by_edge)]
    scratch = []
    if cot is None:
        outs += [row_out(f32), row_out(f32)]
    else:
        inputs.append(cot)
        in_specs.append(by_block)
        sums = jax.ShapeDtypeStruct(stat.shape, f32)
        outs.append((sums, whole(sums)))
        scratch.append(pltpu.VMEM((2, d), f32))
    return pl.pallas_call(
        functools.partial(pool_kernel, cot is not None, float(near * rows)),
        grid=(rows // POOL_BLOCK,),
        out_shape=tuple(o[0] for o in outs),
        in_specs=in_specs,
        out_specs=tuple(o[1] for o in outs),
        scratch_shapes=scratch,
        compiler_params=params(),
        cost_estimate=lasting(12 if cot is None else 20),
        name="pool",
    )(*inputs)


def grads_kernel(
    edges_each,
    inner,
    turn_lines,
    idx_ref,
    slope_ref,
    z_ref,
    back_ref,
    stat_ref,
    pivot_ref,
    norm_ref,
    grads_ref,
    *refs,
):
    near, block, d = slope_ref.shape
    if inner:
        upstream_ref, diff_ref, line_ref, dz_sum_ref, weight_ref, send_ref = refs[: -turn_lines - 2]
    else:
        line_ref, dz_sum_ref, dz_ref, send_ref = refs[: -turn_lines - 2]
    fresh, held, *lines = refs[-turn_lines - 2 :]
    step_id = pl.program_id(0)
    last = pl.num_programs(0) - 1
    total, rows = lines[0].shape[0], dz_sum_ref.shape[0]
    turns = block // POINTS
    share = near * POINTS

    def store(waiting, most):
        while len(waiting) > most:
            line, place, row = waiting.pop(0)
            line[place, :] = row

    def add(turn, edges, waiting):
        for e in edges:
            line = lines[e % turn_lines]
            place = pl.ds(idx_ref[turn, e], 1)
            waiting.append((line, place, line[place, :] + held[pl.ds(e, 1), :]))
            store(waiting, turn_lines - 1)

    @pl.when(step_id == 0)
    def _():
        def clear(i, _):
            at = pl.ds(pl.multiple_of(i * 256, 256), 256)
            for line in lines:
                line[at, :] = jnp.zeros((256, LANES), f32)
            return 0

        lax.fori_loop(0, total // 256, clear, 0)
        fresh[...] = jnp.zeros_like(fresh)
        if inner:
            weight_ref[...] = jnp.zeros_like(weight_ref)

    edges = edges_each * stat_ref.shape[0]
    mean, inv = moments(stat_ref[...], edges_each)
    gain = norm_ref[0:1, :]
    sums = jnp.sum(grads_ref[...], axis=0)
    grad_shift = sums[0:1]
    grad_gain = (2.0 * sums[1:2] - norm_ref[1:2, :] * grad_shift) / gain
    alpha = gain * inv
    rate = alpha * inv * grad_gain * (1.0 / edges)
    constant = alpha * grad_shift * (1.0 / edges) + rate * (pivot_ref[...] - mean)
    wide = [
        [jnp.broadcast_to(x[:, lane : lane + 128], (POINTS, 128)) for x in (alpha, rate, constant)]
        for lane in range(0, d, 128)
    ]

    def turn(t, _):
        at = pl.ds(pl.multiple_of(t * POINTS, POINTS), POINTS)
        before = jnp.maximum(step_id * turns + t - 1, 0)
        held[...] = fresh[...]
        units = [(k, i) for i in range(d // 128) for k in range(near)]
        factors = [w[0] for w in wide]
        if inner:
            factors = [
                f * upstream_ref[at, pl.ds(i * 128, 128)] for i, f in enumerate(factors)
            ]

        def load(unit):
            k, i = unit
            lanes = pl.ds(i * 128, 128)
            return slope_ref[k, at, lanes], z_ref[k, at, lanes]

        loaded = [load(unit) for unit in units[:AHEAD]]
        dzs, waiting = {}, []
        each = share // 2 // len(units)
        for n, (k, i) in enumerate(units):
            add(before, range(n * each, (n + 1) * each), waiting)
            if n + AHEAD < len(units):
                loaded.append(load(units[n + AHEAD]))
            slope, z = loaded[n]
            dzs[k, i] = (factors[i] * slope - wide[i][2] - wide[i][1] * z).astype(bf16)
            if not inner:
                dz_ref[k, at, pl.ds(i * 128, 128)] = dzs[k, i]
        whole = [
            jnp.concatenate([dzs[k, i] for k in range(near)], axis=0) for i in range(d // 128)
        ]
        flat = jnp.concatenate(whole, axis=1)
        product = dot_t(flat, back_ref[...]).astype(bf16)
        if inner:
            weight_ref[...] += lax.dot_general(
                diff_ref[:, at, :].reshape(share, diff_ref.shape[2]),
                flat,
                (((0,), (0,)), ((), ())),
                preferred_element_type=f32,
            )
        add(before, range(share // 2, share), waiting)
        row = pl.multiple_of(step_id * block + t * POINTS, POINTS)
        for i in range(d // 128):
            dz_sum_ref[pl.ds(row, POINTS), pl.ds(i * 128, 128)] = tree(
                jnp.add, [dzs[k, i].astype(f32) for k in range(near)]
            )
        store(waiting, 0)
        fresh[...] = product.astype(f32)
        return 0

    lax.fori_loop(0, turns, turn, 0)
    @pl.when(step_id == last)
    def _():
        held[...] = fresh[...]
        waiting = []
        add(rows // POINTS - 1, range(share), waiting)
        store(waiting, 0)

        def join(i, _):
            at = pl.ds(pl.multiple_of(i * 256, 256), 256)
            joined = tree(jnp.add, [line[at, :] for line in lines])
            line_ref[at, :] = joined[:, : line_ref.shape[1]].astype(bf16)
            return 0

        lax.fori_loop(0, total // 256, join, 0)
        send_ref[...] = line_ref[pl.ds(total // 2, rows), :]


def edge_grads(turns, slope, z, weight, stat, pivot, norm, grads, total, inner=()):
    near, rows, d = slope.shape
    c = weight.shape[0] // 2
    whole = lambda x: pl.BlockSpec(x.shape, lambda b: (0,) * len(x.shape))
    by_block = lambda width: pl.BlockSpec((BLOCK, width), lambda b: (b, 0))
    by_edge = lambda width: pl.BlockSpec((near, BLOCK, width), lambda b: (0, b, 0))
    turn_lines = min(LINES, LINE_BYTES // (total * LANES * 4))
    back = jnp.pad(weight[c:], ((0, LANES - c), (0, 0)))
    inputs = [turns, slope, z, back, stat, pivot, norm, grads, *inner]
    in_specs = [
        smem(),
        by_edge(d),
        by_edge(d),
        whole(back),
        whole(stat),
        whole(pivot),
        whole(norm),
        whole(grads),
    ]
    if inner:
        in_specs += [by_block(d), by_edge(c)]
    dz = jax.ShapeDtypeStruct((near, rows, d), bf16)
    dz_sum = jax.ShapeDtypeStruct((rows, d), f32)
    line = jax.ShapeDtypeStruct((total, c), bf16)
    send = jax.ShapeDtypeStruct((rows, c), bf16)
    outs = [
        (line, whole(line)),
        (dz_sum, whole(dz_sum)),
    ]
    scratch = [
        pltpu.VMEM((near * POINTS, LANES), f32),
        pltpu.VMEM((near * POINTS, LANES), f32),
        *[pltpu.VMEM((total, LANES), f32)] * turn_lines,
    ]
    if inner:
        part = jax.ShapeDtypeStruct((c, d), f32)
        outs.append((part, whole(part)))
    else:
        outs.append((dz, by_edge(d)))
    outs.append((send, whole(send)))
    return pl.pallas_call(
        functools.partial(grads_kernel, float(near * rows), bool(inner), turn_lines),
        grid=(rows // BLOCK,),
        out_shape=tuple(o[0] for o in outs),
        in_specs=in_specs,
        out_specs=tuple(o[1] for o in outs),
        scratch_shapes=scratch,
        compiler_params=params(),
        cost_estimate=lasting(35),
        name="edge_grads",
    )(*inputs)


def copies(x):
    return jnp.broadcast_to(x[None], (lax.axis_size(BOTH),) + x.shape)


def shared(x):
    devices = lax.axis_size(BOTH)
    return x.reshape(devices, x.shape[0] // devices, x.shape[1])


def exchange(shares):
    return lax.all_to_all(shares, BOTH, split_axis=0, concat_axis=0, tiled=True)


def everyone(x):
    return exchange(copies(x))


def ring_moves(places):
    ring = list(range(0, places, 2)) + list(range(1, places, 2))[::-1]
    onward = [(ring[i], ring[(i + 1) % places]) for i in range(places)]
    return onward, [(b, a) for a, b in onward]


def ring_place(device, places):
    return jnp.where(device % 2 == 0, device // 2, places - 1 - device // 2)


def line_table(values):
    places = lax.axis_size("pts")
    onward, backward = ring_moves(places)
    rows, far = values.shape[0] // 2, places // 2
    behind, ahead = [values], [values]
    for _ in range(far - 1):
        behind.append(lax.ppermute(behind[-1], "pts", onward))
        ahead.append(lax.ppermute(ahead[-1], "pts", backward))
    farthest = [
        lax.ppermute(behind[-1][:rows], "pts", onward),
        lax.ppermute(ahead[-1][rows:], "pts", backward),
    ]
    return behind + farthest + ahead[:0:-1]


def owners_sum(line, send, centre, weights=None):
    places = lax.axis_size("pts")
    onward, backward = ring_moves(places)
    rows = centre.shape[0]
    half, far = rows // 2, places // 2

    def slot(j):
        return line[j * rows : (j + 1) * rows].astype(f32)

    forth = lax.ppermute(send[:half], "pts", onward)
    back = lax.ppermute(send[half:], "pts", backward)
    forth, back, centre = lax.optimization_barrier((forth, back, centre))
    if weights is not None:
        forth, back, weights = lax.optimization_barrier((forth, back, weights))
        shares = exchange(shared(weights))
    forth = jnp.pad(forth.astype(f32), ((0, half), (0, 0)))
    back = jnp.pad(back.astype(f32), ((half, 0), (0, 0)))
    for j in range(1, far):
        forth, back = (forth + slot(far + j)).astype(bf16), (back + slot(far - j)).astype(bf16)
        forth, back = lax.optimization_barrier((forth, back))
        if weights is not None and j == far - 1:
            forth, back, shares = lax.optimization_barrier((forth, back, shares))
            weights = everyone(jnp.sum(shares.astype(f32), axis=0).astype(bf16))
        forth = lax.ppermute(forth, "pts", onward).astype(f32)
        back = lax.ppermute(back, "pts", backward).astype(f32)
    return centre + slot(0) + forth + back, weights


def centre_grad(dz_sum, weight):
    wide = weight.astype(f32)
    c = weight.shape[0] // 2
    return exact(dz_sum, (wide[:c] - wide[c:]).T)


def per_device(
    points,
    lengths,
    neighbours_one,
    neighbours_two,
    weight_one,
    gain_one,
    shift_one,
    weight_two,
    gain_two,
    shift_two,
    cotangent,
):
    line_devices = lax.axis_size("pts")
    row_count = points.shape[0]
    line_length = line_devices * row_count
    table_one = line_table(points)

    norm_one, norm_two = jnp.stack([gain_one, shift_one]), jnp.stack([gain_two, shift_two])

    cloud_ends = jnp.cumsum(lengths)
    cloud_starts = cloud_ends - lengths
    line_first = lax.axis_index("loc") * line_length
    position = (
        line_first + lax.axis_index("pts") * row_count + jnp.arange(row_count, dtype=jnp.int32)
    )
    begins = (position[:, None] >= cloud_starts[None, :]) & (position[:, None] < cloud_ends[None, :])
    begin = jnp.sum(jnp.where(begins, cloud_starts[None, :], 0), axis=1) - line_first
    here = ring_place(lax.axis_index("pts"), line_devices)

    def slot_rows(neighbours):
        within = neighbours.T + begin[None, :]
        slot = (here - ring_place(within // row_count, line_devices)) % line_devices
        return slot * row_count + within % row_count

    def by_blocks(index, points):
        return index.reshape(index.shape[0], -1, points).transpose(1, 0, 2)

    index_one = slot_rows(neighbours_one)
    index_two = slot_rows(neighbours_two)
    order_one = by_blocks(index_one, BLOCK).reshape(-1, BLOCK)
    order_two = by_blocks(index_two, BLOCK).reshape(-1, BLOCK)
    near = neighbours_one.shape[1]
    turns_one = by_blocks(index_one, POINTS).reshape(-1, near * POINTS)
    turns_two = by_blocks(index_two, POINTS).reshape(-1, near * POINTS)

    diff_one, z_one, stat_one, pivot_one = edge_stats(order_one, table_one, points, weight_one)
    stat_one, order_two, turns_one, turns_two = lax.optimization_barrier(
        (exchange(stat_one), order_two, turns_one, turns_two)
    )
    act_one, slope_one, slope_sum, slope_moment = pool(z_one, stat_one, pivot_one, norm_one)
    table_two = line_table(act_one)
    diff_two, z_two, stat_two, pivot_two = edge_stats(order_two, table_two, act_one, weight_two)
    stat_two = exchange(stat_two)
    act_two, slope_two, sums_two = pool(z_two, stat_two, pivot_two, norm_two, cotangent)
    sums_two = exchange(sums_two)
    line_two, dz_sum_two, dz_two, send_two = edge_grads(
        turns_two,
        slope_two,
        z_two,
        weight_two,
        stat_two,
        pivot_two,
        norm_two,
        sums_two,
        line_length,
    )
    grad_first, _ = owners_sum(line_two, send_two, centre_grad(dz_sum_two, weight_two))
    grad_first, dz_two, dz_sum_two = lax.optimization_barrier((grad_first, dz_two, dz_sum_two))
    first_two = exact(act_one.astype(f32).T, dz_sum_two)
    second_two = jnp.einsum("kgc,kgd->cd", diff_two, dz_two, preferred_element_type=f32)
    sums_one = jnp.stack(
        [jnp.sum(grad_first * slope_sum, axis=0), jnp.sum(grad_first * slope_moment, axis=0)]
    )
    sums_one = everyone(sums_one)
    line_one, dz_sum_one, second_one, send_one = edge_grads(
        turns_one,
        slope_one,
        z_one,
        weight_one,
        stat_one,
        pivot_one,
        norm_one,
        sums_one,
        line_length,
        (grad_first, diff_one),
    )
    first_one = exact(points.astype(f32).T, dz_sum_one)
    weights = jnp.concatenate(
        [first_two.reshape(-1, LANES), second_two.reshape(-1, LANES), first_one, second_one], axis=0
    )
    grad_points, weights = owners_sum(
        line_one, send_one, centre_grad(dz_sum_one, weight_one), weights.astype(bf16)
    )
    weights = weights.reshape(-1, LANES).astype(f32)
    grad_weight_two = weights[: -weight_one.shape[0]].reshape(weight_two.shape)
    grad_weight_one = weights[-weight_one.shape[0] :]

    def norm_grads(sums, gain, shift):
        sums = jnp.sum(sums, axis=0)
        return (2.0 * sums[1] - shift * sums[0]) / gain, sums[0]

    grad_gain_one, grad_shift_one = norm_grads(sums_one, gain_one, shift_one)
    grad_gain_two, grad_shift_two = norm_grads(sums_two, gain_two, shift_two)
    return (
        act_one,
        act_two,
        grad_points,
        grad_weight_one,
        grad_gain_one,
        grad_shift_one,
        grad_weight_two,
        grad_gain_two,
        grad_shift_two,
    )


def solution(mesh):
    rows, copied = P(("pts", "loc"), None), P()
    in_specs = (rows, copied, rows, rows) + (copied,) * 6 + (rows,)
    out_specs = (rows, rows, rows) + (copied,) * 6
    return jax.shard_map(
        per_device, mesh=mesh, in_specs=in_specs, out_specs=out_specs, check_vma=False
    )
```
